128 devices in a mesh: dp: 16 (over x, y_lo, core), tensor: 8 (over y_hi, z).
Axes of the slice: x: 4, y: 4 (y_hi: 2, y_lo: 2; y = y_hi * 2 + y_lo), z: 4, core: 2. Of those that a mesh axis runs over, the one named last changes fastest.
Arguments:
- tokens: bfloat16 [16384, 2048], P(('dp', 'tensor')), may hold values from -6 to 6
- positions: int32 [16384], P('dp'), may hold values from 0 to 3069, as said below
- w_query: bfloat16 [2048, 2048], P('dp', 'tensor'), may hold values from -0.125 to 0.125
- w_key: bfloat16 [2048, 512], P('dp', 'tensor'), may hold values from -0.125 to 0.125
- w_value: bfloat16 [2048, 512], P('dp', 'tensor'), may hold values from -0.125 to 0.125
- w_out: bfloat16 [2048, 2048], P('tensor', 'dp'), may hold values from -0.75 to 0.75
- attn_gain: bfloat16 [2048], P('dp'), may hold values from 0.5 to 1.5
- w_gate: bfloat16 [2048, 8192], P('dp', 'tensor'), may hold values from -0.125 to 0.125
- w_up: bfloat16 [2048, 8192], P('dp', 'tensor'), may hold values from -0.125 to 0.125
- w_down: bfloat16 [8192, 2048], P('tensor', 'dp'), may hold values from -0.0625 to 0.0625
- mlp_gain: bfloat16 [2048], P('dp'), may hold values from 0.5 to 1.5
- cotangent: bfloat16 [16384, 2048], P(('dp', 'tensor')), may hold values from -6 to 6
Outputs:
- layer_out: bfloat16 [16384, 2048], P(('dp', 'tensor'))
- grad_tokens: bfloat16 [16384, 2048], P(('dp', 'tensor'))
- grad_query: float32 [2048, 2048], P('dp', 'tensor')
- grad_key: float32 [2048, 512], P('dp', 'tensor')
- grad_value: float32 [2048, 512], P('dp', 'tensor')
- grad_out: float32 [2048, 2048], P('tensor', 'dp')
- grad_attn_gain: float32 [2048], P('dp')
- grad_gate: float32 [2048, 8192], P('dp', 'tensor')
- grad_up: float32 [2048, 8192], P('dp', 'tensor')
- grad_down: float32 [8192, 2048], P('tensor', 'dp')
- grad_mlp_gain: float32 [2048], P('dp')
The draws below stay inside these ranges and needn't reach their ends.
Inputs may be any that keep to these rules, and one draw needn't show every extreme that they name: Each sequence of 1024 tokens starts at position 0, and its positions rise by 1 to 3 from one token to the next; in the last sequence they rise by 3 at every token.
All inputs are finite; a program needn't handle non-finite values.
Results may differ from the reference program's by a relative error of at most 0.025.
Values may be sent and summed in bfloat16 or wider, within the bound.
No kernel may reach another device: no remote copies, remote signals or barrier semaphores. Data moves between devices by JAX's collectives and lax.ppermute only.
A program may use at most 192 MiB of HBM per device.

```python
import jax
import jax.numpy as jnp
from jax import lax

D = 2048
H = 32
KV = 8
DH = 64
FF = 8192
SEQ_LEN = 1024
SEQS = 1
TOKENS = 16384
N_DP = 16


def draw_positions(key, part):
    key = jax.random.fold_in(key, 5)
    seq_total = SEQS * N_DP
    steps = jax.random.randint(key, (seq_total, SEQ_LEN), 1, 4).astype(jnp.int32)
    rows = jnp.arange(seq_total, dtype=jnp.int32)[:, None]
    steps = jnp.where(rows == seq_total - 1, jnp.int32(3), steps)
    columns = jnp.arange(SEQ_LEN, dtype=jnp.int32)[None, :]
    steps = jnp.where(columns == 0, jnp.int32(0), steps)
    places = jnp.cumsum(steps, axis=1).astype(jnp.int32)
    return places.reshape(-1).astype(jnp.int32)


def block_scale(key, extent, split, least, largest):
    def one(axis_at, parts):
        steps = jax.random.uniform(jax.random.fold_in(jax.random.fold_in(key, 6), axis_at), (parts,), jnp.float32, least / len(split), largest / len(split))
        return jnp.repeat(jnp.exp(steps), extent[axis_at] // parts).reshape((-1,) + (1,) * (len(extent) - axis_at - 1))

    level = one(*split[0])
    for cut in split[1:]:
        level = level * one(*cut)
    return level


def normal_values(own_key, extent, scale, most, split=(), kind=jnp.bfloat16):
    entries = jax.random.normal(own_key, extent, jnp.float32) * scale
    if len(split) > 0:
        entries = block_scale(own_key, extent, split, -0.22, 0.18) * entries
    return jnp.clip(entries, min=-most, max=most).astype(kind)


def setup_inputs(seed: int = 0) -> dict:
    arg_keys = jax.random.split(jax.random.key(seed), 13)
    tokens = normal_values(arg_keys[0], (TOKENS, D), 1.0, 6.0, ((0, 128),))
    positions = draw_positions(jax.random.fold_in(arg_keys[12], 71), 0)
    w_query = normal_values(arg_keys[2], (D, H * DH), D ** -0.5, 0.125, ((0, 16), (1, 8)))
    w_key = normal_values(arg_keys[3], (D, KV * DH), D ** -0.5, 0.125, ((0, 16), (1, 8)))
    w_value = normal_values(arg_keys[4], (D, KV * DH), D ** -0.5, 0.125, ((0, 16), (1, 8)))
    w_out = normal_values(arg_keys[5], (H * DH, D), (H * DH // 32) ** -0.5, 0.75, ((0, 8), (1, 16)))
    attn_gain = jnp.clip(1.0 + 0.1 * jax.random.normal(arg_keys[6], (D,), jnp.float32), 0.5, 1.5).astype(jnp.bfloat16)
    w_gate = normal_values(arg_keys[7], (D, FF), D ** -0.5, 0.125, ((0, 16), (1, 8)))
    w_up = normal_values(arg_keys[8], (D, FF), D ** -0.5, 0.125, ((0, 16), (1, 8)))
    w_down = normal_values(arg_keys[9], (FF, D), FF ** -0.5, 0.0625, ((0, 8), (1, 16)))
    mlp_gain = jnp.clip(1.0 + 0.1 * jax.random.normal(arg_keys[10], (D,), jnp.float32), 0.5, 1.5).astype(jnp.bfloat16)
    cotangent = normal_values(arg_keys[11], (TOKENS, D), 1.0, 6.0, ((0, 128),))
    return {"tokens": tokens, "positions": positions, "w_query": w_query, "w_key": w_key, "w_value": w_value, "w_out": w_out, "attn_gain": attn_gain, "w_gate": w_gate, "w_up": w_up, "w_down": w_down, "mlp_gain": mlp_gain, "cotangent": cotangent}


@jax.custom_vjp
def low(v):
    return lax.optimization_barrier(v.astype(jnp.bfloat16)).astype(jnp.float32)

@jax.custom_vjp
def low_back(v):
    return v

def low_keep(v):
    return (low(v), None)

def low_pass(kept, grad):
    return (grad,)

def back_keep(v):
    return (v, None)

def back_low(kept, grad):
    return (low(grad),)
low.defvjp(low_keep, low_pass)
low_back.defvjp(back_keep, back_low)
eps = 1e-05
highest = lax.Precision.HIGHEST

def frequencies(head_size):
    pair_index = jnp.arange(head_size // 2).astype(jnp.float32)
    base_freq = 500000.0 ** (-2.0 * pair_index / head_size)
    wavelen = 2.0 * jnp.pi / base_freq
    smooth = (8192.0 / wavelen - 1.0) / 3.0
    blended = (1.0 - smooth) * base_freq / 32.0 + smooth * base_freq
    return jnp.where(wavelen < 2048.0, base_freq, jnp.where(wavelen > 8192.0, base_freq / 32.0, blended))

def rotate(values, cosine, sine_table):
    half_size = values.shape[-1] // 2
    first_half = values[..., :half_size]
    second_half = values[..., half_size:]
    cos_rows = cosine[:, None, :]
    sin_rows = sine_table[:, None, :]
    return jnp.concatenate([first_half * cos_rows - second_half * sin_rows, second_half * cos_rows + first_half * sin_rows], axis=-1)

def rms_norm(values):
    return values * lax.rsqrt(lax.optimization_barrier(jnp.mean(values * values, axis=-1, keepdims=True)) + eps)

def block_forward(inputs, w_query, w_key, w_value, w_out, gain_attn, w_gate, w_up, w_down, gain_mlp, cosine, sine_table):
    seq_len = inputs.shape[0]
    group_size = H // KV
    normed_a = low(rms_norm(inputs) * gain_attn)
    query_pre = low_back(jnp.dot(normed_a, w_query, precision=highest)).reshape(seq_len, H, DH)
    key_pre = low_back(jnp.dot(normed_a, w_key, precision=highest)).reshape(seq_len, KV, DH)
    values_b = low(low_back(jnp.dot(normed_a, w_value, precision=highest))).reshape(seq_len, KV, DH)
    query_rot = low(rotate(query_pre, cosine, sine_table)).reshape(seq_len, KV, group_size, DH)
    key_rot = low(rotate(key_pre, cosine, sine_table))
    scores = low_back(jnp.einsum('qhgd,khd->hgqk', query_rot, key_rot, precision=highest) * DH ** (-0.5))
    causal = jnp.arange(seq_len)[:, None] >= jnp.arange(seq_len)[None, :]
    scores = jnp.where(causal, scores, -1e+30)
    attention = jax.nn.softmax(scores, axis=-1)
    attended = jnp.einsum('hgqk,khd->qhgd', low(attention), values_b, precision=highest)
    attended = low(low_back(attended)).reshape(seq_len, H * DH)
    residual = inputs + low_back(jnp.dot(attended, w_out, precision=highest))
    normed_m = low(rms_norm(residual) * gain_mlp)
    gate_proj = low_back(jnp.dot(normed_m, w_gate, precision=highest))
    up_proj = low_back(jnp.dot(normed_m, w_up, precision=highest))
    activated = low(jax.nn.silu(gate_proj) * up_proj)
    return residual + low_back(jnp.dot(activated, w_down, precision=highest))

def reference(tokens, positions, w_query, w_key, w_value, w_out, attn_gain, w_gate, w_up, w_down, mlp_gain, cotangent):
    weights = tuple((weight.astype(jnp.float32) for weight in (w_query, w_key, w_value, w_out, attn_gain, w_gate, w_up, w_down, mlp_gain)))
    inverse_freq = frequencies(DH)
    seq_count = tokens.shape[0] // SEQ_LEN
    inputs_all = tokens.astype(jnp.float32).reshape(seq_count, SEQ_LEN, D)
    upstream_all = cotangent.astype(jnp.float32).reshape(seq_count, SEQ_LEN, D)
    places_all = positions.reshape(seq_count, SEQ_LEN)

    def per_sequence(summed, element):
        inputs, upstream, places = element
        angles = places.astype(jnp.float32)[:, None] * inverse_freq[None, :]
        cosine = jnp.cos(angles)
        sine_table = jnp.sin(angles)

        def forward(inputs_arg, weights_arg):
            return block_forward(inputs_arg, *weights_arg, cosine, sine_table)
        result, pullback = jax.vjp(forward, inputs, weights)
        grad_inputs, grad_weights = pullback(upstream)
        summed = jax.tree.map(jnp.add, summed, grad_weights)
        return (summed, (result, grad_inputs))
    zero_grads = jax.tree.map(jnp.zeros_like, weights)
    summed, (outputs, input_grads) = lax.scan(per_sequence, zero_grads, (inputs_all, upstream_all, places_all))
    return (outputs.reshape(-1, D).astype(jnp.bfloat16), input_grads.reshape(-1, D).astype(jnp.bfloat16), summed[0], summed[1], summed[2], summed[3], summed[4], summed[5], summed[6], summed[7], summed[8])
```

```python
import itertools

import jax
import jax.numpy as jnp
from jax import lax
from jax.sharding import Mesh, PartitionSpec as P

H = 32
KV = 8
DH = 64
SEQ_LEN = 1024
D = 2048
eps = 1e-05

SIZES = dict(x=4, l=2, c=2, h=2, z=4)
AXES = ("x", "l", "c", "h", "z")


def pairs(axes, move):
    def place(index):
        at = 0
        for a in axes:
            at = at * SIZES[a] + index[a]
        return at

    out = []
    for index in itertools.product(*[range(SIZES[a]) for a in axes]):
        here = dict(zip(axes, index))
        out.append((place(here), place(move(dict(here)))))
    return out


def to_swapped(d):
    d["c"], d["h"] = d["h"], d["c"]
    return d


def to_sibling(d):
    d["c"] = 1 - d["c"]
    return d


def along(axis):
    def move(d):
        step = 1 - 2 * d["c"]
        if axis == "y":
            y = (2 * d["h"] + d["l"] + step) % 4
            d["h"], d["l"] = y // 2, y % 2
        else:
            d[axis] = (d[axis] + step) % 4
        return d

    return move


RING_AXES = dict(x=("x", "c"), y=("l", "c", "h"), z=("c", "z"))


def ring(value, axis):
    axes = RING_AXES[axis]
    return lax.ppermute(value, axes, pairs(axes, along(axis)))


def swapped(value):
    return lax.ppermute(value, ("c", "h"), pairs(("c", "h"), to_swapped))


def sibling(value):
    return lax.ppermute(value, ("c",), pairs(("c",), to_sibling))


def dot(a, b, ca, cb):
    return lax.dot_general(a, b, (((ca,), (cb,)), ((), ())), preferred_element_type=jnp.float32)


def bf(v):
    return v.astype(jnp.bfloat16)


def fl(v):
    return v.astype(jnp.float32)


class Place:
    def __init__(self):
        self.c = lax.axis_index("c")
        self.z = lax.axis_index("z")
        self.x = lax.axis_index("x")
        self.y = 2 * lax.axis_index("h") + lax.axis_index("l")
        self.step = 1 - 2 * self.c

    def source(self, axis, k):
        at = dict(x=self.x, y=self.y, z=self.z)[axis]
        at = lax.rem(at - self.step * k + 4, 4)
        if axis == "y":
            at = 2 * lax.rem(at, 2) + lax.div(at, 2)
        return at


def gather_rows(block, first, me):
    n = block.shape[1]
    stage = jnp.zeros((4, 128, n), block.dtype)
    part = block
    for k in range(4):
        if k:
            part = ring(part, first)
        stage = lax.dynamic_update_slice(stage, part[None], (me.source(first, k), 0, 0))
    whole = jnp.zeros((4, 4, 128, n), block.dtype)
    second = "y" if first == "x" else "x"
    part = stage
    for k in range(4):
        if k:
            part = ring(part, second)
        at = me.source(second, k)
        if second == "x":
            whole = lax.dynamic_update_slice(whole, part[None], (at, 0, 0, 0))
        else:
            whole = lax.dynamic_update_slice(whole, part[:, None], (0, at, 0, 0))
    return whole.reshape(D, n)


def scatter_rows(piece, first, me):
    total = piece(me.source(first, 1))
    for k in (2, 3, 0):
        total = fl(ring(bf(total), first)) + piece(me.source(first, k))
    second = "y" if first == "x" else "x"
    stage = total.reshape(4, 128, -1)

    def at(k):
        return lax.dynamic_index_in_dim(stage, me.source(second, k), 0, keepdims=False)

    total = at(1)
    for k in (2, 3, 0):
        total = fl(ring(bf(total), second)) + at(k)
    return total


def columns_at(rows, first, i):
    if first == "x":
        return lax.dynamic_slice_in_dim(rows, i * 512, 512, axis=1)
    split = rows.reshape(rows.shape[0], 4, 4, 128)
    return lax.dynamic_index_in_dim(split, i, 2, keepdims=False).reshape(rows.shape[0], 512)


def weight_gradient(rows, right, first, me):
    return scatter_rows(lambda i: dot(columns_at(rows, first, i), right, 0, 0), first, me)


def gather_tokens(block):
    out = []
    part = block
    for k in range(4):
        if k:
            part = ring(part, "z")
        out.append(jnp.concatenate([part, sibling(part)], axis=0))
    return out


def scatter_tokens(partial):
    total = None
    for k in (1, 2, 3, 0):
        mine = partial(k)
        mine = mine[:128] + fl(sibling(bf(mine[128:])))
        total = mine if total is None else fl(ring(bf(total), "z")) + mine
    return total


def frequencies(head_size):
    pair_index = jnp.arange(head_size // 2).astype(jnp.float32)
    base_freq = 500000.0 ** (-2.0 * pair_index / head_size)
    wavelen = 2.0 * jnp.pi / base_freq
    smooth = (8192.0 / wavelen - 1.0) / 3.0
    blended = (1.0 - smooth) * base_freq / 32.0 + smooth * base_freq
    return jnp.where(
        wavelen < 2048.0, base_freq, jnp.where(wavelen > 8192.0, base_freq / 32.0, blended)
    )


def rotate(values, cosine, sine_table):
    half_size = values.shape[-1] // 2
    first_half = values[..., :half_size]
    second_half = values[..., half_size:]
    cos_rows = cosine[:, None, :]
    sin_rows = sine_table[:, None, :]
    return jnp.concatenate(
        [
            first_half * cos_rows - second_half * sin_rows,
            second_half * cos_rows + first_half * sin_rows,
        ],
        axis=-1,
    )


def norm_parts(values):
    inverse = lax.rsqrt(jnp.mean(values * values, axis=-1, keepdims=True) + eps)
    return (values * inverse, inverse)


def norm_backward(grad_normed, unit_rows, inverse, gain_rows):
    scaled = grad_normed * gain_rows
    centred = scaled - unit_rows * jnp.mean(scaled * unit_rows, axis=-1, keepdims=True)
    return (inverse * centred, jnp.sum(grad_normed * unit_rows, axis=0))


def causal_mask(first_row, block_rows, key_count):
    rows_here = first_row + jnp.arange(block_rows)[:, None]
    return rows_here >= jnp.arange(key_count)[None, :]


SCALE = DH ** (-0.5)
BLOCK = 512


def block_scores(query_block, keys, first_row):
    key_count = first_row + BLOCK
    scores = (
        jnp.einsum("qgd,kd->gqk", query_block, keys[:key_count], preferred_element_type=jnp.float32)
        * SCALE
    )
    return jnp.where(causal_mask(first_row, BLOCK, key_count), scores, -1e30)


def attend(query, keys, values):
    out_parts = []
    lse_parts = []
    for first_row in range(0, SEQ_LEN, BLOCK):
        key_count = first_row + BLOCK
        scores = block_scores(query[first_row:key_count], keys, first_row)
        row_top = jnp.max(scores, axis=-1, keepdims=True)
        lse = row_top + jnp.log(jnp.sum(jnp.exp(scores - row_top), axis=-1, keepdims=True))
        probs = bf(jnp.exp(scores - lse))
        out_parts.append(
            jnp.einsum("gqk,kd->qgd", probs, values[:key_count], preferred_element_type=jnp.float32)
        )
        lse_parts.append(lse)
    return jnp.concatenate(out_parts, axis=0), jnp.concatenate(lse_parts, axis=1)


def attend_backward(query, keys, values, grad_out, lse):
    grad_query_parts = []
    grad_keys = jnp.zeros((SEQ_LEN, DH), jnp.float32)
    grad_values = jnp.zeros((SEQ_LEN, DH), jnp.float32)
    for first_row in range(0, SEQ_LEN, BLOCK):
        key_count = first_row + BLOCK
        query_block = query[first_row:key_count]
        grad_block = grad_out[first_row:key_count]
        probs = jnp.exp(block_scores(query_block, keys, first_row) - lse[:, first_row:key_count])
        grad_probs = jnp.einsum(
            "qgd,kd->gqk", grad_block, values[:key_count], preferred_element_type=jnp.float32
        )
        grad_values = grad_values.at[:key_count].add(
            jnp.einsum("gqk,qgd->kd", bf(probs), grad_block, preferred_element_type=jnp.float32)
        )
        delta = jnp.sum(grad_probs * probs, axis=-1, keepdims=True)
        grad_scores = bf(probs * (grad_probs - delta))
        grad_query_parts.append(
            SCALE
            * jnp.einsum(
                "gqk,kd->qgd", grad_scores, keys[:key_count], preferred_element_type=jnp.float32
            )
        )
        grad_keys = grad_keys.at[:key_count].add(
            SCALE
            * jnp.einsum("gqk,qgd->kd", grad_scores, query_block, preferred_element_type=jnp.float32)
        )
    return jnp.concatenate(grad_query_parts, axis=0), grad_keys, grad_values


def on_device(
    tokens, positions, w_query, w_key, w_value, w_out, attn_gain, w_gate, w_up, w_down, mlp_gain, cotangent
):
    me = Place()
    h = lax.axis_index("h")

    part_attn = swapped(jnp.concatenate([w_query, w_key, w_value, w_out.T], axis=1))
    attn_a = gather_rows(part_attn[:, :320], "x", me)
    attn_b = gather_rows(part_attn[:, 320:], "y", me)
    w_qkv = jnp.concatenate([attn_a, attn_b[:, :64]], axis=1)
    w_out_t = attn_b[:, 64:]
    gains = lax.all_gather(jnp.stack([attn_gain, mlp_gain]), ("x", "l", "c"), axis=1, tiled=True)
    gain_attn = fl(gains[0])
    gain_mlp = fl(gains[1])

    inputs = fl(swapped(tokens))
    seq_positions = jnp.where(h == me.c, positions, sibling(positions))
    angles = seq_positions.astype(jnp.float32)[:, None] * frequencies(DH)[None, :]
    cosine = jnp.cos(angles)
    sine = jnp.sin(angles)

    def natural(step_blocks):
        n = step_blocks[0].shape[1]
        whole = jnp.zeros((8, 128, n), step_blocks[0].dtype)
        for k in range(4):
            two = step_blocks[k].reshape(2, 128, n)
            at = 4 * me.c + lax.rem(me.z - me.step * k + 4, 4)
            whole = lax.dynamic_update_slice(whole, two[:1], (at, 0, 0))
            at = 4 * (1 - me.c) + lax.rem(me.z + me.step * k + 4, 4)
            whole = lax.dynamic_update_slice(whole, two[1:], (at, 0, 0))
        return whole.reshape(SEQ_LEN, n)

    def ring_order(rows, k):
        blocks = rows.reshape(8, 128, -1)
        own = 4 * me.c + lax.rem(me.z - me.step * k + 4, 4)
        other = 4 * (1 - me.c) + lax.rem(me.z + me.step * k + 4, 4)
        return jnp.concatenate(
            [
                lax.dynamic_index_in_dim(blocks, own, 0, keepdims=False),
                lax.dynamic_index_in_dim(blocks, other, 0, keepdims=False),
            ],
            axis=0,
        )

    unit_attn, inverse_attn = norm_parts(inputs)
    rows_attn = gather_tokens(bf(unit_attn * gain_attn))
    qkv = natural([dot(rows_attn[k], w_qkv, 1, 0) for k in range(4)])
    query = bf(rotate(qkv[:, :256].reshape(SEQ_LEN, 4, DH), cosine, sine))
    keys = bf(rotate(qkv[:, 256:320].reshape(SEQ_LEN, 1, DH), cosine, sine))[:, 0]
    values = bf(qkv[:, 320:])

    part_down = swapped(w_down.T)
    w_down_t = jnp.concatenate(
        [gather_rows(part_down[:, :512], "x", me), gather_rows(part_down[:, 512:], "y", me)], axis=1
    )
    full_gate = gather_rows(swapped(w_gate), "x", me)
    full_up = gather_rows(swapped(w_up), "y", me)
    upstream = swapped(cotangent)
    rows_up = gather_tokens(upstream)
    grad_act = [dot(rows_up[k], w_down_t, 1, 0) for k in range(4)]

    attended, lse = attend(query, keys, values)
    attended = bf(attended.reshape(SEQ_LEN, 256))
    attended_steps = [ring_order(attended, k) for k in range(4)]
    residual = inputs + scatter_tokens(lambda k: dot(attended_steps[k], w_out_t, 1, 1))

    unit_mlp, inverse_mlp = norm_parts(residual)
    rows_mlp = gather_tokens(bf(unit_mlp * gain_mlp))
    activated, grad_gate_pre, grad_up_pre = [], [], []
    for k in range(4):
        gate = dot(rows_mlp[k], full_gate, 1, 0)
        up = dot(rows_mlp[k], full_up, 1, 0)
        sig = jax.nn.sigmoid(gate)
        silu = gate * sig
        activated.append(bf(silu * up))
        grad_gate_pre.append(bf(grad_act[k] * up * sig * (1.0 + gate * (1.0 - sig))))
        grad_up_pre.append(bf(grad_act[k] * silu))

    grad_normed_mlp = scatter_tokens(
        lambda k: dot(grad_gate_pre[k], full_gate, 1, 1) + dot(grad_up_pre[k], full_up, 1, 1)
    )
    grad_norm_mlp, gain_part_mlp = norm_backward(grad_normed_mlp, unit_mlp, inverse_mlp, gain_mlp)
    grad_residual = fl(upstream) + grad_norm_mlp
    rows_gr = gather_tokens(bf(grad_residual))
    layer_out = bf(residual + scatter_tokens(lambda k: dot(activated[k], w_down_t, 1, 1)))

    all_up = jnp.concatenate(rows_up, axis=0)
    all_act = jnp.concatenate(activated, axis=0)
    all_mlp = jnp.concatenate(rows_mlp, axis=0)
    share_down = jnp.concatenate(
        [
            weight_gradient(all_up, all_act[:, :512], "x", me),
            weight_gradient(all_up, all_act[:, 512:], "y", me),
        ],
        axis=1,
    )
    share_gate = weight_gradient(all_mlp, jnp.concatenate(grad_gate_pre, axis=0), "x", me)
    share_up = weight_gradient(all_mlp, jnp.concatenate(grad_up_pre, axis=0), "y", me)

    grad_attended = natural([bf(dot(rows_gr[k], w_out_t, 1, 0)) for k in range(4)])
    grad_query_rot, grad_key_rot, grad_values = attend_backward(
        query, keys, values, grad_attended.reshape(SEQ_LEN, 4, DH), lse
    )
    grad_qkv = jnp.concatenate(
        [
            bf(rotate(grad_query_rot, cosine, -sine)).reshape(SEQ_LEN, 256),
            bf(rotate(grad_key_rot[:, None], cosine, -sine))[:, 0],
            bf(grad_values),
        ],
        axis=1,
    )
    grad_qkv_steps = [ring_order(grad_qkv, k) for k in range(4)]
    grad_normed_attn = scatter_tokens(lambda k: dot(grad_qkv_steps[k], w_qkv, 1, 1))
    grad_norm_attn, gain_part_attn = norm_backward(
        grad_normed_attn, unit_attn, inverse_attn, gain_attn
    )
    grad_tokens = bf(grad_residual + grad_norm_attn)

    all_gr = jnp.concatenate(rows_gr, axis=0)
    all_attn = jnp.concatenate(rows_attn, axis=0)
    all_attended = jnp.concatenate(attended_steps, axis=0)
    all_qkv = jnp.concatenate(grad_qkv_steps, axis=0)

    def piece_b(i):
        return jnp.concatenate(
            [
                dot(columns_at(all_attn, "y", i), all_qkv[:, 320:], 0, 0),
                dot(columns_at(all_gr, "y", i), all_attended, 0, 0),
            ],
            axis=1,
        )

    share_attn = jnp.concatenate(
        [weight_gradient(all_attn, all_qkv[:, :320], "x", me), scatter_rows(piece_b, "y", me)], axis=1
    )

    share_attn = fl(swapped(bf(share_attn)))
    gain_parts = jnp.stack([gain_part_attn, gain_part_mlp])
    gain_sums = lax.psum(gain_parts, AXES)
    rows_at = (4 * me.x + 2 * lax.axis_index("l") + me.c) * 128
    gain_sums = lax.dynamic_slice_in_dim(gain_sums, rows_at, 128, axis=1)
    return (
        swapped(layer_out),
        swapped(grad_tokens),
        share_attn[:, :256],
        share_attn[:, 256:320],
        share_attn[:, 320:384],
        share_attn[:, 384:].T,
        gain_sums[0],
        fl(swapped(bf(share_gate))),
        fl(swapped(bf(share_up))),
        fl(swapped(bf(share_down))).T,
        gain_sums[1],
    )


def solution(mesh):
    split = Mesh(mesh.devices.reshape(4, 2, 2, 2, 4), AXES)
    dp, tensor = ("x", "l", "c"), ("h", "z")
    both = P(AXES, None)
    weight, turned, vector = P(dp, tensor), P(tensor, dp), P(dp)
    in_specs = (
        both, vector, weight, weight, weight, turned, vector, weight, weight, turned, vector, both,
    )
    out_specs = (
        both, both, weight, weight, weight, turned, vector, weight, weight, turned, vector,
    )
    return jax.shard_map(on_device, mesh=split, in_specs=in_specs, out_specs=out_specs, check_vma=False)
```

```python
import functools
import itertools
import math

import jax
import jax.numpy as jnp
from jax import lax
from jax.experimental import pallas as pl
from jax.experimental.pallas import tpu as pltpu
from jax.sharding import Mesh, PartitionSpec as P

H = 32
KV = 8
DH = 64
SEQ_LEN = 1024
D = 2048
eps = 1e-05

SIZES = dict(x=4, l=2, c=2, h=2, z=4)
AXES = ("x", "l", "c", "h", "z")

SCALE = DH ** (-0.5)
SCALE2 = SCALE * math.log2(math.e)
VMEM_LIMIT = 48 * 1024 * 1024


def pairs(axes, move):
    def place(index):
        at = 0
        for a in axes:
            at = at * SIZES[a] + index[a]
        return at

    out = []
    for index in itertools.product(*[range(SIZES[a]) for a in axes]):
        here = dict(zip(axes, index))
        out.append((place(here), place(move(dict(here)))))
    return out


def to_swapped(d):
    d["c"], d["h"] = d["h"], d["c"]
    return d


def to_sibling(d):
    d["c"] = 1 - d["c"]
    return d


def along(axis):
    def move(d):
        step = 1 - 2 * d["c"]
        if axis == "y":
            y = (2 * d["h"] + d["l"] + step) % 4
            d["h"], d["l"] = y // 2, y % 2
        else:
            d[axis] = (d[axis] + step) % 4
        return d

    return move


RING_AXES = dict(x=("x", "c"), y=("l", "c", "h"), z=("c", "z"))


def ring(value, axis):
    axes = RING_AXES[axis]
    return lax.ppermute(value, axes, pairs(axes, along(axis)))


def swapped(value):
    return lax.ppermute(value, ("c", "h"), pairs(("c", "h"), to_swapped))


def sibling(value):
    return lax.ppermute(value, ("c",), pairs(("c",), to_sibling))


def z_flipped(value, bit):
    def move(d):
        d["z"] = d["z"] ^ bit
        return d

    return lax.ppermute(value, ("z",), pairs(("z",), move))


def dot(a, b, ca, cb):
    return lax.dot_general(a, b, (((ca,), (cb,)), ((), ())), preferred_element_type=jnp.float32)


def bf(v):
    return v.astype(jnp.bfloat16)


def fl(v):
    return v.astype(jnp.float32)


def sds(shape, dtype=jnp.bfloat16):
    return jax.ShapeDtypeStruct(shape, dtype)


def cost(flops, bytes_accessed):
    return pl.CostEstimate(flops=int(flops), bytes_accessed=int(bytes_accessed), transcendentals=0)


PARAMS = pltpu.CompilerParams(vmem_limit_bytes=VMEM_LIMIT)
ANY = pl.BlockSpec(memory_space=pl.ANY)
WHOLE = pl.BlockSpec(memory_space=pltpu.VMEM)


class Place:
    def __init__(self):
        self.c = lax.axis_index("c")
        self.z = lax.axis_index("z")
        self.x = lax.axis_index("x")
        self.h = lax.axis_index("h")
        self.y = 2 * self.h + lax.axis_index("l")
        self.step = 1 - 2 * self.c
        order = []
        for k in range(4):
            order.append(4 * self.c + lax.rem(self.z - self.step * k + 4, 4))
            order.append(4 * (1 - self.c) + lax.rem(self.z + self.step * k + 4, 4))
        self.order = jnp.stack(order).astype(jnp.int32)
        self.blocks = {}
        for first, second in (("x", "y"), ("y", "x")):
            out = []
            for k2 in range(4):
                for k1 in range(4):
                    a, b = self.source(first, k1), self.source(second, k2)
                    out.append(4 * a + b if first == "x" else 4 * b + a)
            self.blocks[first] = jnp.stack(out).astype(jnp.int32)

    def source(self, axis, k):
        at = dict(x=self.x, y=self.y, z=self.z)[axis]
        at = lax.rem(at - self.step * k + 4, 4)
        if axis == "y":
            at = 2 * lax.rem(at, 2) + lax.div(at, 2)
        return at


def place_rows(parts, blocks):
    n = parts[0].shape[1]

    def kernel(blocks_ref, p0, p1, p2, p3, out_ref, sems):
        copies = []
        for k2, part in enumerate((p0, p1, p2, p3)):
            for k1 in range(4):
                at = pl.multiple_of(blocks_ref[4 * k2 + k1] * 128, 128)
                copies.append(
                    pltpu.make_async_copy(
                        part.at[pl.ds(128 * k1, 128)], out_ref.at[pl.ds(at, 128)], sems.at[4 * k2 + k1]
                    )
                )
        for copy in copies:
            copy.start()
        for copy in copies:
            copy.wait()

    return pl.pallas_call(
        kernel,
        out_shape=sds((D, n)),
        in_specs=[pl.BlockSpec(memory_space=pltpu.SMEM)] + [ANY] * 4,
        out_specs=ANY,
        scratch_shapes=[pltpu.SemaphoreType.DMA((16,))],
        compiler_params=PARAMS,
        cost_estimate=cost(0, 2 * D * n * 2),
        name="place_rows",
    )(blocks, *parts)


def gather_rows(block, first, me):
    second = "y" if first == "x" else "x"
    parts = [block]
    for _ in range(3):
        parts.append(ring(parts[-1], first))
    parts = [jnp.concatenate(parts, axis=0)]
    for _ in range(3):
        parts.append(ring(parts[-1], second))
    return place_rows(parts, me.blocks[first])


def weight_piece(rows, right, at, first, received):
    n = right.shape[1]
    tile = 256 if n % 256 == 0 else 128
    extra = [] if received is None else [received]

    def kernel(at_ref, a0, a1, a2, a3, right_ref, *rest):
        left = jnp.concatenate([a0[...], a1[...], a2[...], a3[...]], axis=1)
        total = dot(left, right_ref[...], 0, 0)
        if extra:
            total = total + fl(rest[0][...])
        rest[-1][...] = bf(total)

    def column(j):
        if first == "x":
            return pl.BlockSpec((SEQ_LEN, 128), lambda i, s: (0, 4 * s[0] + j))
        return pl.BlockSpec((SEQ_LEN, 128), lambda i, s: (0, 4 * j + s[0]))

    moving = pl.BlockSpec((512, tile), lambda i, s: (0, i))
    return pl.pallas_call(
        kernel,
        grid_spec=pltpu.PrefetchScalarGridSpec(
            num_scalar_prefetch=1,
            grid=(n // tile,),
            in_specs=[column(j) for j in range(4)]
            + [pl.BlockSpec((SEQ_LEN, tile), lambda i, s: (0, i))]
            + [moving] * len(extra),
            out_specs=moving,
        ),
        out_shape=sds((512, n)),
        compiler_params=PARAMS,
        cost_estimate=cost(2 * 512 * SEQ_LEN * n, 2 * (512 * SEQ_LEN + SEQ_LEN * n + 1024 * n)),
        name="weight_piece",
    )(at.reshape(1).astype(jnp.int32), rows, rows, rows, rows, right, *extra)


def weight_gradient(rows, right, first, me):
    total = weight_piece(rows, right, me.source(first, 1), first, None)
    for k in (2, 3, 0):
        total = weight_piece(rows, right, me.source(first, k), first, ring(total, first))
    second = "y" if first == "x" else "x"
    stage = total.reshape(4, 128, -1)

    def at(k):
        return lax.dynamic_index_in_dim(stage, me.source(second, k), 0, keepdims=False)

    total = at(1)
    for k in (2, 3, 0):
        total = fl(ring(bf(total), second)) + fl(at(k))
    return total


def gather_tokens(block):
    out = []
    part = block
    for k in range(4):
        if k:
            part = ring(part, "z")
        out.append((part, sibling(part)))
    return out


def scatter_tokens(partial):
    total = None
    for k in (1, 2, 3, 0):
        mine, other = partial(k)
        mine = fl(mine) + fl(sibling(other))
        total = mine if total is None else fl(ring(bf(total), "z")) + mine
    return total


def partial_sums(k, terms):
    count = len(terms)
    tile = 512

    def kernel(*refs):
        total = None
        for i in range(count):
            one = dot(refs[i][...], refs[count + i][...], 1, 1)
            total = one if total is None else total + one
        refs[-2][...] = bf(total[:128])
        refs[-1][...] = bf(total[128:])

    depth = sum(rows.shape[1] for rows, _ in terms)
    return pl.pallas_call(
        kernel,
        grid=(D // tile,),
        in_specs=[pl.BlockSpec((256, rows.shape[1]), lambda i: (k, 0)) for rows, _ in terms]
        + [pl.BlockSpec((tile, w.shape[1]), lambda i: (i, 0)) for _, w in terms],
        out_specs=[pl.BlockSpec((128, tile), lambda i: (0, i))] * 2,
        out_shape=[sds((128, D))] * 2,
        compiler_params=PARAMS,
        cost_estimate=cost(2 * 256 * depth * D, 2 * (256 * depth + depth * D + 256 * D)),
        name="partial_sums",
    )(*[rows for rows, _ in terms], *[w for _, w in terms])


def row_block(n, k):
    return pl.BlockSpec((256, n), lambda *_: (k, 0))


def project(k, own, other, weight, before, dtype):
    n = weight.shape[1]

    def kernel(own_ref, other_ref, w_ref, *rest):
        rows = jnp.concatenate([own_ref[...], other_ref[...]], axis=0)
        rest[-2][...] = rows
        rest[-1][...] = dot(rows, w_ref[...], 1, 0).astype(dtype)

    before = [] if before is None else list(before)
    return pl.pallas_call(
        kernel,
        grid=(1,),
        in_specs=[
            pl.BlockSpec((128, D), lambda i: (0, 0)),
            pl.BlockSpec((128, D), lambda i: (0, 0)),
            pl.BlockSpec((D, n), lambda i: (0, 0)),
        ]
        + [ANY] * len(before),
        out_specs=[row_block(D, k), row_block(n, k)],
        out_shape=[sds((SEQ_LEN, D)), sds((SEQ_LEN, n), dtype)],
        input_output_aliases={3: 0, 4: 1} if before else {},
        compiler_params=PARAMS,
        cost_estimate=cost(2 * 256 * D * n, 2 * (512 * D + D * n + 256 * n)),
        name="project",
    )(own, other, weight, *before)


def rope(u, cosine, sine):
    lane = lax.broadcasted_iota(jnp.int32, u.shape, 1)
    turned = jnp.where(lane % DH < DH // 2, pltpu.roll(u, 96, 1), pltpu.roll(u, 32, 1))
    return u * cosine + turned * sine


def rope_three(u, cosine, sine):
    lane = lax.broadcasted_iota(jnp.int32, cosine.shape, 1)
    last = u[:, 256:]
    return jnp.concatenate(
        [
            rope(u[:, :128], cosine, sine),
            rope(u[:, 128:256], cosine, sine),
            jnp.where(lane < DH, rope(last, cosine, sine), last),
        ],
        axis=1,
    )


def project_qkv(k, own, other, gain, weight, tables, order, before):
    def kernel(order_ref, own_ref, other_ref, gain_ref, w_ref, c0, c1, s0, s1, *rest):
        x = fl(jnp.concatenate([own_ref[...], other_ref[...]], axis=0))
        inverse = lax.rsqrt(jnp.mean(x * x, axis=1, keepdims=True) + eps)
        rows = bf(x * inverse * gain_ref[...])
        rest[-2][...] = rows
        cosine = jnp.concatenate([c0[...], c1[...]], axis=0)
        sine = jnp.concatenate([s0[...], s1[...]], axis=0)
        rest[-1][...] = bf(rope_three(dot(rows, w_ref[...], 1, 0), cosine, sine))

    before = [] if before is None else list(before)

    def table(j):
        return pl.BlockSpec((128, 128), lambda i, s: (s[2 * k + j], 0))

    return pl.pallas_call(
        kernel,
        grid_spec=pltpu.PrefetchScalarGridSpec(
            num_scalar_prefetch=1,
            grid=(1,),
            in_specs=[
                pl.BlockSpec((128, D), lambda i, s: (0, 0)),
                pl.BlockSpec((128, D), lambda i, s: (0, 0)),
                pl.BlockSpec((1, D), lambda i, s: (0, 0)),
                pl.BlockSpec((D, 384), lambda i, s: (0, 0)),
                table(0),
                table(1),
                table(0),
                table(1),
            ]
            + [ANY] * len(before),
            out_specs=[row_block(D, k), row_block(384, k)],
        ),
        out_shape=[sds((SEQ_LEN, D)), sds((SEQ_LEN, 384))],
        input_output_aliases={9: 0, 10: 1} if before else {},
        compiler_params=PARAMS,
        cost_estimate=cost(2 * 256 * D * 384, 2 * (512 * D + D * 384 + 256 * 384)),
        name="project_qkv",
    )(order, own, other, gain, weight, tables[0], tables[0], tables[1], tables[1], *before)


def block_at(order_ref, p):
    return pl.ds(pl.multiple_of(order_ref[p] * 128, 128), 128)


def scores_t(keys, query, q_at):
    s = dot(keys, query, 1, 1)
    key = lax.broadcasted_iota(jnp.int32, (256, 256), 0)
    column = lax.broadcasted_iota(jnp.int32, (256, 256), 1)
    diagonal = jnp.where(key <= column, s[q_at:], -1e30)
    return diagonal if q_at == 0 else jnp.concatenate([s[:q_at], diagonal], axis=0)


def attend(qkv, order):
    def kernel(order_ref, qkv_ref, out_ref, nat_ref, lse_ref, att_ref):
        for p in range(8):
            nat_ref[block_at(order_ref, p), :] = qkv_ref[128 * p : 128 * p + 128, :]
        kv = nat_ref[:, 256:]
        keys = kv[:, :DH]
        values_t = kv.T[DH:]
        lse_ref[...] = jnp.zeros_like(lse_ref)
        for q_at in range(0, SEQ_LEN, 256):
            end = q_at + 256
            for pair in range(2):
                two = nat_ref[q_at:end, 128 * pair : 128 * pair + 128]
                outs = []
                for i in range(2):
                    s = scores_t(keys[:end], two[:, DH * i : DH * i + DH], q_at)
                    top = jnp.max(s, axis=0, keepdims=True)
                    p = jnp.exp2((s - top) * SCALE2)
                    total = jnp.sum(p, axis=0, keepdims=True)
                    outs.append(dot(values_t[:, :end], bf(p), 1, 0) / total)
                    g = 2 * pair + i
                    lse_ref[g : g + 1, q_at:end] = top * SCALE2 + jnp.log2(total)
                att_ref[q_at:end, 128 * pair : 128 * pair + 128] = bf(jnp.concatenate(outs, axis=0).T)
        for p in range(8):
            out_ref[128 * p : 128 * p + 128, :] = att_ref[block_at(order_ref, p), :]

    return pl.pallas_call(
        kernel,
        in_specs=[pl.BlockSpec(memory_space=pltpu.SMEM), WHOLE],
        out_specs=[WHOLE] * 3,
        out_shape=[sds((SEQ_LEN, 256)), sds((SEQ_LEN, 384)), sds((8, SEQ_LEN), jnp.float32)],
        scratch_shapes=[pltpu.VMEM((SEQ_LEN, 256), jnp.bfloat16)],
        compiler_params=PARAMS,
        cost_estimate=cost(6e9, 3e6),
        name="attend",
    )(order, qkv)


def attend_backward(qkv, lse, grad_out, tables, order):
    def kernel(order_ref, nat_ref, lse_ref, go_ref, cos_ref, sin_ref, out_ref, go_nat, kv_sum, d_nat):
        for p in range(8):
            go_nat[block_at(order_ref, p), :] = go_ref[128 * p : 128 * p + 128, :]
        kv = nat_ref[:, 256:]
        keys = kv[:, :DH]
        values = kv[:, DH:]
        keys_t = kv.T[:DH]
        kv_sum[...] = jnp.zeros_like(kv_sum)
        for q_at in range(0, SEQ_LEN, 256):
            end = q_at + 256
            cosine = cos_ref[q_at:end, :]
            sine = -sin_ref[q_at:end, :]
            for pair in range(2):
                lanes = slice(128 * pair, 128 * pair + 128)
                two = nat_ref[q_at:end, lanes]
                two_grad = go_nat[q_at:end, lanes]
                outs = []
                for i in range(2):
                    query = two[:, DH * i : DH * i + DH]
                    grad = two_grad[:, DH * i : DH * i + DH]
                    g = 2 * pair + i
                    s = scores_t(keys[:end], query, q_at)
                    p = jnp.exp2(s * SCALE2 - lse_ref[g : g + 1, q_at:end])
                    dp = dot(values[:end], grad, 1, 1)
                    delta = jnp.sum(dp * p, axis=0, keepdims=True)
                    ds = bf(p * (dp - delta))
                    kv_sum[:end, :] += jnp.concatenate(
                        [dot(ds, query, 1, 0), dot(bf(p), grad, 1, 0)], axis=1
                    )
                    outs.append(dot(keys_t[:, :end], ds, 1, 0))
                d_query = jnp.concatenate(outs, axis=0).T * SCALE
                d_nat[q_at:end, lanes] = bf(rope(d_query, cosine, sine))
        lane = lax.broadcasted_iota(jnp.int32, (SEQ_LEN, 128), 1)
        total = kv_sum[...]
        turned = rope(total * SCALE, cos_ref[...], -sin_ref[...])
        d_nat[:, 256:] = bf(jnp.where(lane < DH, turned, total))
        for p in range(8):
            out_ref[128 * p : 128 * p + 128, :] = d_nat[block_at(order_ref, p), :]

    return pl.pallas_call(
        kernel,
        in_specs=[pl.BlockSpec(memory_space=pltpu.SMEM)] + [WHOLE] * 5,
        out_specs=WHOLE,
        out_shape=sds((SEQ_LEN, 384)),
        scratch_shapes=[
            pltpu.VMEM((SEQ_LEN, 256), jnp.bfloat16),
            pltpu.VMEM((SEQ_LEN, 128), jnp.float32),
            pltpu.VMEM((SEQ_LEN, 384), jnp.bfloat16),
        ],
        compiler_params=PARAMS,
        cost_estimate=cost(12e9, 5e6),
        name="attend_backward",
    )(order, qkv, lse, grad_out, *tables)


def mlp_step(k, own, other, w_gate, w_up, grad_act, before):
    tile = 256
    width = w_gate.shape[1]

    def kernel(own_ref, other_ref, g_ref, u_ref, ga_ref, *rest):
        rows_ref, act_ref, gg_ref, gu_ref = rest[-4:]
        rows = jnp.concatenate([own_ref[...], other_ref[...]], axis=0)

        @pl.when(pl.program_id(0) == 0)
        def _():
            rows_ref[...] = rows

        gate = dot(rows, g_ref[...], 1, 0)
        up = dot(rows, u_ref[...], 1, 0)
        sig = jax.nn.sigmoid(gate)
        silu = gate * sig
        ga = ga_ref[...]
        act_ref[...] = bf(silu * up)
        gg_ref[...] = bf(ga * up * sig * (1.0 + gate * (1.0 - sig)))
        gu_ref[...] = bf(ga * silu)

    before = [] if before is None else list(before)
    piece = pl.BlockSpec((256, tile), lambda i: (k, i))
    return pl.pallas_call(
        kernel,
        grid=(width // tile,),
        in_specs=[
            pl.BlockSpec((128, D), lambda i: (0, 0)),
            pl.BlockSpec((128, D), lambda i: (0, 0)),
            pl.BlockSpec((D, tile), lambda i: (0, i)),
            pl.BlockSpec((D, tile), lambda i: (0, i)),
            piece,
        ]
        + [ANY] * len(before),
        out_specs=[pl.BlockSpec((256, D), lambda i: (k, 0)), piece, piece, piece],
        out_shape=[sds((SEQ_LEN, D))] + [sds((SEQ_LEN, width))] * 3,
        input_output_aliases={5 + i: i for i in range(len(before))},
        compiler_params=PARAMS,
        cost_estimate=cost(4 * 256 * D * width, 2 * (512 * D + 2 * D * width + 5 * 256 * width)),
        name="mlp_step",
    )(own, other, w_gate, w_up, grad_act, *before)


def frequencies(head_size):
    pair_index = jnp.arange(head_size // 2).astype(jnp.float32)
    base_freq = 500000.0 ** (-2.0 * pair_index / head_size)
    wavelen = 2.0 * jnp.pi / base_freq
    smooth = (8192.0 / wavelen - 1.0) / 3.0
    blended = (1.0 - smooth) * base_freq / 32.0 + smooth * base_freq
    return jnp.where(
        wavelen < 2048.0, base_freq, jnp.where(wavelen > 8192.0, base_freq / 32.0, blended)
    )


def norm_parts(values):
    inverse = lax.rsqrt(jnp.mean(values * values, axis=-1, keepdims=True) + eps)
    return (values * inverse, inverse)


def norm_backward(grad_normed, unit_rows, inverse, gain_rows):
    scaled = grad_normed * gain_rows
    return inverse * (scaled - unit_rows * jnp.mean(scaled * unit_rows, axis=-1, keepdims=True))


def on_device(
    tokens, positions, w_query, w_key, w_value, w_out, attn_gain, w_gate, w_up, w_down, mlp_gain, cotangent
):
    me = Place()
    inputs_b = swapped(tokens)

    gains = jnp.pad(jnp.stack([attn_gain, mlp_gain], axis=1), ((0, 0), (0, 126)))
    part_attn = swapped(jnp.concatenate([w_query, w_key, w_value, w_out.T, gains], axis=1))
    w_qkv = gather_rows(part_attn[:, :384], "x", me)
    out_and_gains = gather_rows(part_attn[:, 384:], "y", me)
    w_out_t = out_and_gains[:, :256]
    gain_rows = fl(out_and_gains[:, 256:258].T)
    gain_attn, gain_mlp = gain_rows[:1], gain_rows[1:]

    seq_positions = jnp.where(me.h == me.c, positions, sibling(positions))
    freq = jnp.tile(frequencies(DH), 4)
    angles = seq_positions.astype(jnp.float32)[:, None] * freq[None, :]
    sign = jnp.where(jnp.arange(128) % DH < DH // 2, -1.0, 1.0)
    tables = (jnp.cos(angles), jnp.sin(angles) * sign[None, :])

    rows_in = gather_tokens(inputs_b)
    state = None
    for k in range(4):
        state = project_qkv(k, *rows_in[k], gain_attn, w_qkv, tables, me.order, state)
    normed_attn, qkv_ring = state

    part_down = swapped(w_down.T)
    w_down_t = jnp.concatenate(
        [gather_rows(part_down[:, :512], "x", me), gather_rows(part_down[:, 512:], "y", me)], axis=1
    )
    part_gate, part_up = swapped(w_gate), swapped(w_up)
    full_gate = gather_rows(part_gate, "x", me)
    full_up = gather_rows(part_up, "y", me)
    upstream = swapped(cotangent)
    rows_up = gather_tokens(upstream)
    state = None
    for k in range(4):
        state = project(k, *rows_up[k], w_down_t, state, jnp.float32)
    all_up, grad_act = state

    attended, qkv, lse = attend(qkv_ring, me.order)
    inputs = fl(inputs_b)
    residual = inputs + scatter_tokens(lambda k: partial_sums(k, [(attended, w_out_t)]))

    unit_mlp, inverse_mlp = norm_parts(residual)
    rows_mlp = gather_tokens(bf(unit_mlp * gain_mlp))
    state = None
    for k in range(4):
        state = mlp_step(k, *rows_mlp[k], full_gate, full_up, grad_act, state)
    all_mlp, activated, grad_gate_pre, grad_up_pre = state

    grad_normed_mlp = scatter_tokens(
        lambda k: partial_sums(k, [(grad_gate_pre, full_gate), (grad_up_pre, full_up)])
    )
    grad_residual = fl(upstream) + norm_backward(grad_normed_mlp, unit_mlp, inverse_mlp, gain_mlp)
    rows_gr = gather_tokens(bf(grad_residual))
    layer_out = bf(residual + scatter_tokens(lambda k: partial_sums(k, [(activated, w_down_t)])))

    share_down = jnp.concatenate(
        [
            weight_gradient(all_up, activated[:, :512], "x", me),
            weight_gradient(all_up, activated[:, 512:], "y", me),
        ],
        axis=1,
    )
    share_gate = weight_gradient(all_mlp, grad_gate_pre, "x", me)
    share_up = weight_gradient(all_mlp, grad_up_pre, "y", me)

    state = None
    for k in range(4):
        state = project(k, *rows_gr[k], w_out_t, state, jnp.bfloat16)
    all_gr, grad_attended = state
    grad_qkv = attend_backward(qkv, lse, grad_attended, tables, me.order)
    grad_normed_attn = scatter_tokens(lambda k: partial_sums(k, [(grad_qkv, w_qkv)]))
    unit_attn, inverse_attn = norm_parts(inputs)
    grad_norm_attn = norm_backward(grad_normed_attn, unit_attn, inverse_attn, gain_attn)
    grad_tokens = bf(grad_residual + grad_norm_attn)

    share_qkv = weight_gradient(normed_attn, grad_qkv, "x", me)
    share_out = weight_gradient(all_gr, attended, "y", me)

    def gain_sum(*terms):
        return sum(jnp.sum(fl(w) * g, axis=1) for w, g in terms)

    gain_sums = jnp.stack(
        [gain_sum((part_attn[:, :384], share_qkv)), gain_sum((part_gate, share_gate), (part_up, share_up))]
    )
    gain_sums = gain_sums / fl(part_attn[:, 640:642].T)
    gain_sums = gain_sums + sibling(gain_sums)
    gain_sums = gain_sums + z_flipped(gain_sums, 1)
    gain_sums = swapped(gain_sums + z_flipped(gain_sums, 2))

    share_attn = fl(swapped(bf(jnp.concatenate([share_qkv, share_out], axis=1))))
    return (
        swapped(layer_out),
        swapped(grad_tokens),
        share_attn[:, :256],
        share_attn[:, 256:320],
        share_attn[:, 320:384],
        share_attn[:, 384:].T,
        gain_sums[0],
        fl(swapped(bf(share_gate))),
        fl(swapped(bf(share_up))),
        fl(swapped(bf(share_down))).T,
        gain_sums[1],
    )


def solution(mesh):
    split = Mesh(mesh.devices.reshape(4, 2, 2, 2, 4), AXES)
    dp, tensor = ("x", "l", "c"), ("h", "z")
    both = P(AXES, None)
    weight, turned, vector = P(dp, tensor), P(tensor, dp), P(dp)
    in_specs = (
        both, vector, weight, weight, weight, turned, vector, weight, weight, turned, vector, both,
    )
    out_specs = (
        both, both, weight, weight, weight, turned, vector, weight, weight, turned, vector,
    )
    return jax.shard_map(on_device, mesh=split, in_specs=in_specs, out_specs=out_specs, check_vma=False)
```

```python
import functools
import itertools
import math

import jax
import jax.numpy as jnp
from jax import lax
from jax.experimental import pallas as pl
from jax.experimental.pallas import tpu as pltpu
from jax.sharding import Mesh, PartitionSpec as P

H = 32
KV = 8
DH = 64
SEQ_LEN = 1024
D = 2048
eps = 1e-05

SIZES = dict(x=4, l=2, c=2, h=2, z=4)
AXES = ("x", "l", "c", "h", "z")

SCALE = DH ** (-0.5)
SCALE2 = SCALE * math.log2(math.e)
VMEM_LIMIT = 20 * 1024 * 1024


def pairs(axes, move):
    def place(index):
        at = 0
        for a in axes:
            at = at * SIZES[a] + index[a]
        return at

    out = []
    for index in itertools.product(*[range(SIZES[a]) for a in axes]):
        here = dict(zip(axes, index))
        out.append((place(here), place(move(dict(here)))))
    return out


def to_swapped(d):
    d["c"], d["h"] = d["h"], d["c"]
    return d


def to_sibling(d):
    d["c"] = 1 - d["c"]
    return d


def along(axis):
    def move(d):
        step = 1 - 2 * d["c"]
        if axis == "y":
            y = (2 * d["h"] + d["l"] + step) % 4
            d["h"], d["l"] = y // 2, y % 2
        else:
            d[axis] = (d[axis] + step) % 4
        return d

    return move


RING_AXES = dict(x=("x", "c"), y=("l", "c", "h"))
Z_STEPS = (0, -1, 1, 2)


def ring(value, axis):
    axes = RING_AXES[axis]
    return lax.ppermute(value, axes, pairs(axes, along(axis)))


def swapped(value):
    return lax.ppermute(value, ("c", "h"), pairs(("c", "h"), to_swapped))


def sibling(value):
    return lax.ppermute(value, ("c",), pairs(("c",), to_sibling))


def z_moved(value, step):
    def move(d):
        d["z"] = (d["z"] + step) % 4
        return d

    return lax.ppermute(value, ("z",), pairs(("z",), move))


def z_flipped(value, bit):
    def move(d):
        d["z"] = d["z"] ^ bit
        return d

    return lax.ppermute(value, ("z",), pairs(("z",), move))


def dot(a, b, ca, cb):
    return lax.dot_general(a, b, (((ca,), (cb,)), ((), ())), preferred_element_type=jnp.float32)


def bf(v):
    return v.astype(jnp.bfloat16)


def fl(v):
    return v.astype(jnp.float32)


def sds(shape, dtype=jnp.bfloat16):
    return jax.ShapeDtypeStruct(shape, dtype)


def cost(flops, bytes_accessed):
    return pl.CostEstimate(flops=int(flops), bytes_accessed=int(bytes_accessed), transcendentals=0)


PARAMS = pltpu.CompilerParams(vmem_limit_bytes=VMEM_LIMIT)
ANY = pl.BlockSpec(memory_space=pl.ANY)
WHOLE = pl.BlockSpec(memory_space=pltpu.VMEM)


class Place:
    def __init__(self):
        self.c = lax.axis_index("c")
        self.z = lax.axis_index("z")
        self.x = lax.axis_index("x")
        self.h = lax.axis_index("h")
        self.y = 2 * self.h + lax.axis_index("l")
        self.step = 1 - 2 * self.c
        order = []
        for step in Z_STEPS:
            at = lax.rem(self.z + step + 4, 4)
            order.append(4 * self.c + at)
            order.append(4 * (1 - self.c) + at)
        self.order = jnp.stack(order).astype(jnp.int32)
        self.blocks = {}
        for first, second in (("x", "y"), ("y", "x")):
            out = []
            for k2 in range(4):
                for k1 in range(4):
                    a, b = self.source(first, k1), self.source(second, k2)
                    out.append(4 * a + b if first == "x" else 4 * b + a)
            self.blocks[first] = jnp.stack(out).astype(jnp.int32)

    def source(self, axis, k):
        at = lax.rem(dict(x=self.x, y=self.y)[axis] - self.step * k + 4, 4)
        if axis == "y":
            at = 2 * lax.rem(at, 2) + lax.div(at, 2)
        return at


SMEM = pl.BlockSpec(memory_space=pltpu.SMEM)


def place_rows(parts, blocks):
    n = parts[0].shape[1]

    def kernel(blocks_ref, p0, p1, p2, p3, out_ref, sems):
        copies = []
        for k2, part in enumerate((p0, p1, p2, p3)):
            for k1 in range(4):
                at = pl.multiple_of(blocks_ref[4 * k2 + k1] * 128, 128)
                copies.append(
                    pltpu.make_async_copy(
                        part.at[pl.ds(128 * k1, 128)], out_ref.at[pl.ds(at, 128)], sems.at[4 * k2 + k1]
                    )
                )
        for copy in copies:
            copy.start()
        for copy in copies:
            copy.wait()

    return pl.pallas_call(
        kernel,
        out_shape=sds((D, n)),
        in_specs=[SMEM] + [ANY] * 4,
        out_specs=WHOLE,
        scratch_shapes=[pltpu.SemaphoreType.DMA((16,))],
        compiler_params=PARAMS,
        cost_estimate=cost(0, 2 * D * n * 2),
        name="place_rows",
    )(blocks, *parts)


def gather_rows(block, first, me):
    second = "y" if first == "x" else "x"
    parts = [block]
    for _ in range(3):
        parts.append(ring(parts[-1], first))
    parts = [jnp.concatenate(parts, axis=0)]
    for _ in range(3):
        parts.append(ring(parts[-1], second))
    return place_rows(parts, me.blocks[first])


def call(kernel, name, outs, args, flops, scratch=()):
    moved = sum(a.size * a.dtype.itemsize for a in args) + sum(o.size * o.dtype.itemsize for o in outs)
    return pl.pallas_call(
        kernel,
        out_shape=outs,
        in_specs=[SMEM if a.dtype == jnp.int32 else WHOLE for a in args],
        out_specs=[WHOLE] * len(outs),
        scratch_shapes=list(scratch),
        compiler_params=PARAMS,
        cost_estimate=cost(flops, moved),
        name=name,
    )(*args)


def weight_piece(rows, right, columns, at, first, received):
    low, high = columns
    args = [at.reshape(1).astype(jnp.int32), *rows, *right] + ([] if received is None else [received])

    def kernel(*refs):
        at = refs[0][0]
        row_refs, right_refs = refs[1 : 1 + len(rows)], refs[1 + len(rows) : 1 + len(rows) + len(right)]
        left = []
        for j in range(4):
            block = 4 * at + j if first == "x" else 4 * j + at
            lanes = pl.ds(pl.multiple_of(block * 128, 128), 128)
            left.append(jnp.concatenate([r[:, lanes] for r in row_refs], axis=0))
        left = jnp.concatenate(left, axis=1)
        for j in range(low, high, 256):
            end = min(j + 256, high)
            total = dot(left, jnp.concatenate([r[:, j:end] for r in right_refs], axis=0), 0, 0)
            here = slice(j - low, end - low)
            if received is not None:
                total = total + fl(refs[-2][:, here])
            refs[-1][:, here] = bf(total)

    n = high - low
    return call(kernel, "weight_piece", [sds((512, n))], args, 2 * 512 * SEQ_LEN * n)[0]


def weight_gradient(rows, right, columns, first, me):
    total = weight_piece(rows, right, columns, me.source(first, 1), first, None)
    for k in (2, 3, 0):
        total = weight_piece(rows, right, columns, me.source(first, k), first, ring(total, first))
    second = "y" if first == "x" else "x"
    stage = total.reshape(4, 128, -1)

    def at(k):
        return lax.dynamic_index_in_dim(stage, me.source(second, k), 0, keepdims=False)

    total = at(1)
    for k in (2, 3, 0):
        total = fl(ring(bf(total), second)) + fl(at(k))
    return total


def gather_tokens(block):
    out = []
    for step in Z_STEPS:
        part = z_moved(block, -step) if step else block
        out.append((part, sibling(part)))
    return out


def scatter_tokens(blocks):
    total = fl(blocks[0])
    for step, block in zip(Z_STEPS[1:], blocks[1:]):
        total = total + fl(z_moved(block, step))
    return total


def partial_sums(pieces, weights):
    count = len(pieces)

    def kernel(*refs):
        for j in range(0, D, 512):
            total = None
            for i in range(count):
                one = dot(refs[i][...], refs[count + i][j : j + 512, :], 1, 1)
                total = one if total is None else total + one
            refs[-2][:, j : j + 512] = bf(total[:128])
            refs[-1][:, j : j + 512] = bf(total[128:])

    depth = sum(p.shape[1] for p in pieces)
    return call(kernel, "partial_sums", [sds((128, D))] * 2, [*pieces, *weights], 2 * 256 * depth * D)


def chip_sums(pieces, weights):
    out = [None] * 4
    for k in (1, 2, 3, 0):
        mine, other = partial_sums(pieces[k], weights)
        out[k] = bf(fl(mine) + fl(sibling(other)))
    return out


def chip_product(own, other, weight, sibling_weight):
    received = sibling(other)

    def kernel(a_ref, b_ref, v_ref, w_ref, *out_refs):
        for j in range(0, D, 512):
            total = dot(a_ref[...], v_ref[j : j + 512, :], 1, 1) + dot(b_ref[...], w_ref[j : j + 512, :], 1, 1)
            for k in range(4):
                out_refs[k][:, j : j + 512] = bf(total[128 * k : 128 * k + 128])

    args = [own, received, weight, sibling_weight]
    return call(kernel, "chip_product", [sds((128, D))] * 4, args, 4 * 512 * own.shape[1] * D)


def project(own, other, weight, dtype):
    n = weight.shape[1]

    def kernel(own_ref, other_ref, w_ref, out_ref):
        rows = jnp.concatenate([own_ref[...], other_ref[...]], axis=0)
        for j in range(0, n, 256):
            out_ref[:, j : j + 256] = dot(rows, w_ref[:, j : j + 256], 1, 0).astype(dtype)

    return call(kernel, "project", [sds((256, n), dtype)], [own, other, weight], 2 * 256 * D * n)[0]


def rope(u, cosine, sine):
    lane = lax.broadcasted_iota(jnp.int32, u.shape, 1)
    turned = jnp.where(lane % DH < DH // 2, pltpu.roll(u, 96, 1), pltpu.roll(u, 32, 1))
    return u * cosine + turned * sine


def rope_three(u, cosine, sine):
    lane = lax.broadcasted_iota(jnp.int32, cosine.shape, 1)
    last = u[:, 256:]
    return jnp.concatenate(
        [
            rope(u[:, :128], cosine, sine),
            rope(u[:, 128:256], cosine, sine),
            jnp.where(lane < DH, rope(last, cosine, sine), last),
        ],
        axis=1,
    )


def block_at(order_ref, p):
    return pl.ds(pl.multiple_of(order_ref[p] * 128, 128), 128)


def project_qkv(k, own, other, gain, weight, tables, order):
    def kernel(order_ref, own_ref, other_ref, gain_ref, w_ref, cos_ref, sin_ref, n0, n1, out_ref):
        x = fl(jnp.concatenate([own_ref[...], other_ref[...]], axis=0))
        inverse = lax.rsqrt(jnp.mean(x * x, axis=1, keepdims=True) + eps)
        rows = bf(x * inverse * gain_ref[...])
        n0[...] = rows[:128]
        n1[...] = rows[128:]
        here = [block_at(order_ref, 2 * k), block_at(order_ref, 2 * k + 1)]
        cosine = jnp.concatenate([cos_ref[at, :] for at in here], axis=0)
        sine = jnp.concatenate([sin_ref[at, :] for at in here], axis=0)
        out_ref[...] = bf(rope_three(dot(rows, w_ref[...], 1, 0), cosine, sine))

    args = [order, own, other, gain, weight, *tables]
    return call(
        kernel, "project_qkv", [sds((128, D)), sds((128, D)), sds((256, 384))], args, 2 * 256 * D * 384
    )


def scores_t(keys, query, q_at):
    s = dot(keys, query, 1, 1)
    key = lax.broadcasted_iota(jnp.int32, (256, 256), 0)
    column = lax.broadcasted_iota(jnp.int32, (256, 256), 1)
    diagonal = jnp.where(key <= column, s[q_at:], -1e30)
    return diagonal if q_at == 0 else jnp.concatenate([s[:q_at], diagonal], axis=0)


def split_rows(from_ref, order_ref, own_ref, other_ref):
    for k in range(4):
        own_ref[128 * k : 128 * k + 128, :] = from_ref[block_at(order_ref, 2 * k), :]
        other_ref[128 * k : 128 * k + 128, :] = from_ref[block_at(order_ref, 2 * k + 1), :]


def attend(qkv, order):
    def kernel(order_ref, q0, q1, q2, q3, own_ref, other_ref, nat_ref, lse_ref, att_ref):
        for k, ref in enumerate((q0, q1, q2, q3)):
            nat_ref[block_at(order_ref, 2 * k), :] = ref[:128, :]
            nat_ref[block_at(order_ref, 2 * k + 1), :] = ref[128:, :]
        kv = nat_ref[:, 256:]
        keys = kv[:, :DH]
        values_t = kv.T[DH:]
        lse_ref[...] = jnp.zeros_like(lse_ref)
        for q_at in range(0, SEQ_LEN, 256):
            end = q_at + 256
            for pair in range(2):
                two = nat_ref[q_at:end, 128 * pair : 128 * pair + 128]
                outs = []
                for i in range(2):
                    s = scores_t(keys[:end], two[:, DH * i : DH * i + DH], q_at)
                    top = jnp.max(s, axis=0, keepdims=True)
                    p = jnp.exp2((s - top) * SCALE2)
                    total = jnp.sum(p, axis=0, keepdims=True)
                    outs.append(dot(values_t[:, :end], bf(p), 1, 0) / total)
                    g = 2 * pair + i
                    lse_ref[g : g + 1, q_at:end] = top * SCALE2 + jnp.log2(total)
                att_ref[q_at:end, 128 * pair : 128 * pair + 128] = bf(jnp.concatenate(outs, axis=0).T)
        split_rows(att_ref, order_ref, own_ref, other_ref)

    outs = [sds((512, 256)), sds((512, 256)), sds((SEQ_LEN, 384)), sds((8, SEQ_LEN), jnp.float32)]
    scratch = [pltpu.VMEM((SEQ_LEN, 256), jnp.bfloat16)]
    return call(kernel, "attend", outs, [order, *qkv], 3e9, scratch)


def attend_backward(qkv, lse, grad_out, tables, order):
    def kernel(order_ref, nat_ref, lse_ref, g0, g1, g2, g3, cos_ref, sin_ref, own_ref, other_ref, go_nat, kv_sum, d_nat):
        for k, ref in enumerate((g0, g1, g2, g3)):
            go_nat[block_at(order_ref, 2 * k), :] = ref[:128, :]
            go_nat[block_at(order_ref, 2 * k + 1), :] = ref[128:, :]
        kv = nat_ref[:, 256:]
        keys = kv[:, :DH]
        values = kv[:, DH:]
        keys_t = kv.T[:DH]
        kv_sum[...] = jnp.zeros_like(kv_sum)
        for q_at in range(0, SEQ_LEN, 256):
            end = q_at + 256
            cosine = cos_ref[q_at:end, :]
            sine = -sin_ref[q_at:end, :]
            for pair in range(2):
                lanes = slice(128 * pair, 128 * pair + 128)
                two = nat_ref[q_at:end, lanes]
                two_grad = go_nat[q_at:end, lanes]
                outs = []
                for i in range(2):
                    query = two[:, DH * i : DH * i + DH]
                    grad = two_grad[:, DH * i : DH * i + DH]
                    g = 2 * pair + i
                    s = scores_t(keys[:end], query, q_at)
                    p = jnp.exp2(s * SCALE2 - lse_ref[g : g + 1, q_at:end])
                    dp = dot(values[:end], grad, 1, 1)
                    delta = jnp.sum(dp * p, axis=0, keepdims=True)
                    ds = bf(p * (dp - delta))
                    kv_sum[:end, :] += jnp.concatenate(
                        [dot(ds, query, 1, 0), dot(bf(p), grad, 1, 0)], axis=1
                    )
                    outs.append(dot(keys_t[:, :end], ds, 1, 0))
                d_query = jnp.concatenate(outs, axis=0).T * SCALE
                d_nat[q_at:end, lanes] = bf(rope(d_query, cosine, sine))
        lane = lax.broadcasted_iota(jnp.int32, (SEQ_LEN, 128), 1)
        total = kv_sum[...]
        turned = rope(total * SCALE, cos_ref[...], -sin_ref[...])
        d_nat[:, 256:] = bf(jnp.where(lane < DH, turned, total))
        split_rows(d_nat, order_ref, own_ref, other_ref)

    scratch = [
        pltpu.VMEM((SEQ_LEN, 256), jnp.bfloat16),
        pltpu.VMEM((SEQ_LEN, 128), jnp.float32),
        pltpu.VMEM((SEQ_LEN, 384), jnp.bfloat16),
    ]
    args = [order, qkv, lse, *grad_out, *tables]
    return call(kernel, "attend_backward", [sds((512, 384))] * 2, args, 6e9, scratch)


def mlp_step(own, other, w_gate, w_up, grad_act):
    width = w_gate.shape[1]

    def kernel(own_ref, other_ref, g_ref, u_ref, ga_ref, act_ref, gg_ref, gu_ref):
        rows = jnp.concatenate([own_ref[...], other_ref[...]], axis=0)
        for j in range(0, width, 256):
            here = slice(j, j + 256)
            gate = dot(rows, g_ref[:, here], 1, 0)
            up = dot(rows, u_ref[:, here], 1, 0)
            sig = jax.nn.sigmoid(gate)
            silu = gate * sig
            ga = ga_ref[:, here]
            act_ref[:, here] = bf(silu * up)
            gg_ref[:, here] = bf(ga * up * sig * (1.0 + gate * (1.0 - sig)))
            gu_ref[:, here] = bf(ga * silu)

    args = [own, other, w_gate, w_up, grad_act]
    return call(kernel, "mlp_step", [sds((256, width))] * 3, args, 4 * 256 * D * width)


def frequencies(head_size):
    pair_index = jnp.arange(head_size // 2).astype(jnp.float32)
    base_freq = 500000.0 ** (-2.0 * pair_index / head_size)
    wavelen = 2.0 * jnp.pi / base_freq
    smooth = (8192.0 / wavelen - 1.0) / 3.0
    blended = (1.0 - smooth) * base_freq / 32.0 + smooth * base_freq
    return jnp.where(
        wavelen < 2048.0, base_freq, jnp.where(wavelen > 8192.0, base_freq / 32.0, blended)
    )


def norm_parts(values):
    inverse = lax.rsqrt(jnp.mean(values * values, axis=-1, keepdims=True) + eps)
    return (values * inverse, inverse)


def norm_backward(grad_normed, unit_rows, inverse, gain_rows):
    scaled = grad_normed * gain_rows
    return inverse * (scaled - unit_rows * jnp.mean(scaled * unit_rows, axis=-1, keepdims=True))


def on_device(
    tokens, positions, w_query, w_key, w_value, w_out, attn_gain, w_gate, w_up, w_down, mlp_gain, cotangent
):
    me = Place()
    inputs_b = swapped(tokens)

    gains = jnp.pad(jnp.stack([attn_gain, mlp_gain], axis=1), ((0, 0), (0, 126)))
    part_attn = swapped(jnp.concatenate([w_query, w_key, w_value, w_out.T, gains], axis=1))
    w_qkv = gather_rows(part_attn[:, :384], "x", me)
    out_and_gains = gather_rows(part_attn[:, 384:], "y", me)
    w_out_t = out_and_gains[:, :256]
    gain_rows = fl(out_and_gains[:, 256:258].T)
    gain_attn, gain_mlp = gain_rows[:1], gain_rows[1:]

    seq_positions = jnp.where(me.h == me.c, positions, sibling(positions))
    freq = jnp.tile(frequencies(DH), 4)
    angles = seq_positions.astype(jnp.float32)[:, None] * freq[None, :]
    sign = jnp.where(jnp.arange(128) % DH < DH // 2, -1.0, 1.0)
    tables = (jnp.cos(angles), jnp.sin(angles) * sign[None, :])

    rows_in = gather_tokens(inputs_b)
    projected = [project_qkv(k, *rows_in[k], gain_attn, w_qkv, tables, me.order) for k in range(4)]
    normed_attn = [p[0] for p in projected] + [p[1] for p in projected]

    part_down = swapped(w_down.T)
    w_down_t = jnp.concatenate(
        [gather_rows(part_down[:, :512], "x", me), gather_rows(part_down[:, 512:], "y", me)], axis=1
    )
    part_gate, part_up = swapped(w_gate), swapped(w_up)
    full_gate = gather_rows(part_gate, "x", me)
    full_up = gather_rows(part_up, "y", me)
    upstream = swapped(cotangent)
    rows_up = gather_tokens(upstream)
    grad_act = [project(*rows_up[k], w_down_t, jnp.float32) for k in range(4)]

    attended, other_attended, qkv, lse = attend([p[2] for p in projected], me.order)
    inputs = fl(inputs_b)
    residual = inputs + scatter_tokens(
        chip_product(attended, other_attended, w_out_t, sibling(w_out_t))
    )

    unit_mlp, inverse_mlp = norm_parts(residual)
    rows_mlp = gather_tokens(bf(unit_mlp * gain_mlp))
    steps = [mlp_step(*rows_mlp[k], full_gate, full_up, grad_act[k]) for k in range(4)]
    activated, grad_gate_pre, grad_up_pre = zip(*steps)

    grad_normed_mlp = scatter_tokens(
        chip_sums(list(zip(grad_gate_pre, grad_up_pre)), [full_gate, full_up])
    )
    grad_residual = fl(upstream) + norm_backward(grad_normed_mlp, unit_mlp, inverse_mlp, gain_mlp)
    rows_gr = gather_tokens(bf(grad_residual))
    layer_out = bf(residual + scatter_tokens(chip_sums([[a] for a in activated], [w_down_t])))

    def by_step(rows):
        return [block for two in rows for block in two]

    def by_core(rows):
        return [two[0] for two in rows] + [two[1] for two in rows]

    all_up, all_mlp = by_step(rows_up), by_step(rows_mlp)
    share_down = jnp.concatenate(
        [
            weight_gradient(all_up, activated, (0, 512), "x", me),
            weight_gradient(all_up, activated, (512, 1024), "y", me),
        ],
        axis=1,
    )
    share_gate = weight_gradient(all_mlp, grad_gate_pre, (0, 1024), "x", me)
    share_up = weight_gradient(all_mlp, grad_up_pre, (0, 1024), "y", me)

    grad_attended = [project(*rows_gr[k], w_out_t, jnp.bfloat16) for k in range(4)]
    grad_qkv, other_grad_qkv = attend_backward(qkv, lse, grad_attended, tables, me.order)
    grad_normed_attn = scatter_tokens(chip_product(grad_qkv, other_grad_qkv, w_qkv, sibling(w_qkv)))
    unit_attn, inverse_attn = norm_parts(inputs)
    grad_norm_attn = norm_backward(grad_normed_attn, unit_attn, inverse_attn, gain_attn)
    grad_tokens = bf(grad_residual + grad_norm_attn)

    share_qkv = weight_gradient(normed_attn, [grad_qkv, other_grad_qkv], (0, 384), "x", me)
    share_out = weight_gradient(by_core(rows_gr), [attended, other_attended], (0, 256), "y", me)

    def gain_sum(*terms):
        return sum(jnp.sum(fl(w) * g, axis=1) for w, g in terms)

    gain_sums = jnp.stack(
        [gain_sum((part_attn[:, :384], share_qkv)), gain_sum((part_gate, share_gate), (part_up, share_up))]
    )
    gain_sums = gain_sums / fl(part_attn[:, 640:642].T)
    gain_sums = gain_sums + sibling(gain_sums)
    gain_sums = gain_sums + z_flipped(gain_sums, 1)
    gain_sums = swapped(gain_sums + z_flipped(gain_sums, 2))

    share_attn = fl(swapped(bf(jnp.concatenate([share_qkv, share_out], axis=1))))
    return (
        swapped(layer_out),
        swapped(grad_tokens),
        share_attn[:, :256],
        share_attn[:, 256:320],
        share_attn[:, 320:384],
        share_attn[:, 384:].T,
        gain_sums[0],
        fl(swapped(bf(share_gate))),
        fl(swapped(bf(share_up))),
        fl(swapped(bf(share_down))).T,
        gain_sums[1],
    )


def solution(mesh):
    split = Mesh(mesh.devices.reshape(4, 2, 2, 2, 4), AXES)
    dp, tensor = ("x", "l", "c"), ("h", "z")
    both = P(AXES, None)
    weight, turned, vector = P(dp, tensor), P(tensor, dp), P(dp)
    in_specs = (
        both, vector, weight, weight, weight, turned, vector, weight, weight, turned, vector, both,
    )
    out_specs = (
        both, both, weight, weight, weight, turned, vector, weight, weight, turned, vector,
    )
    return jax.shard_map(on_device, mesh=split, in_specs=in_specs, out_specs=out_specs, check_vma=False)
```

```python
import functools
import itertools
import math

import jax
import jax.numpy as jnp
from jax import lax
from jax.experimental import pallas as pl
from jax.experimental.pallas import tpu as pltpu
from jax.sharding import Mesh, PartitionSpec as P

H = 32
KV = 8
DH = 64
SEQ_LEN = 1024
D = 2048
eps = 1e-05

SIZES = dict(x=4, l=2, c=2, h=2, z=4)
AXES = ("x", "l", "c", "h", "z")

SCALE = DH ** (-0.5)
SCALE2 = SCALE * math.log2(math.e)
VMEM_LIMIT = 14 * 1024 * 1024


def pairs(axes, move):
    def place(index):
        at = 0
        for a in axes:
            at = at * SIZES[a] + index[a]
        return at

    out = []
    for index in itertools.product(*[range(SIZES[a]) for a in axes]):
        here = dict(zip(axes, index))
        out.append((place(here), place(move(dict(here)))))
    return out


def to_swapped(d):
    d["c"], d["h"] = d["h"], d["c"]
    return d


def to_sibling(d):
    d["c"] = 1 - d["c"]
    return d


def along(axis):
    def move(d):
        step = 1 - 2 * d["c"]
        if axis == "y":
            y = (2 * d["h"] + d["l"] + step) % 4
            d["h"], d["l"] = y // 2, y % 2
        else:
            d[axis] = (d[axis] + step) % 4
        return d

    return move


RING_AXES = dict(x=("x", "c"), y=("l", "c", "h"))


def ring(value, axis):
    axes = RING_AXES[axis]
    return lax.ppermute(value, axes, pairs(axes, along(axis)))


def swapped(value):
    return lax.ppermute(value, ("c", "h"), pairs(("c", "h"), to_swapped))


def sibling(value):
    return lax.ppermute(value, ("c",), pairs(("c",), to_sibling))


def z_flipped(value, bit):
    def move(d):
        d["z"] = d["z"] ^ bit
        return d

    return lax.ppermute(value, ("z",), pairs(("z",), move))


def after(values, *earlier):
    held = lax.optimization_barrier((tuple(values), tuple(earlier)))
    return held[0]


def dot(a, b, ca, cb):
    return lax.dot_general(a, b, (((ca,), (cb,)), ((), ())), preferred_element_type=jnp.float32)


def bf(v):
    return v.astype(jnp.bfloat16)


def fl(v):
    return v.astype(jnp.float32)


def sds(shape, dtype=jnp.bfloat16):
    return jax.ShapeDtypeStruct(shape, dtype)


def cost(flops, bytes_accessed):
    return pl.CostEstimate(flops=int(flops), bytes_accessed=int(bytes_accessed), transcendentals=0)


PARAMS = pltpu.CompilerParams(vmem_limit_bytes=VMEM_LIMIT)
ANY = pl.BlockSpec(memory_space=pl.ANY)
WHOLE = pl.BlockSpec(memory_space=pltpu.VMEM)


class Place:
    def __init__(self):
        self.c = lax.axis_index("c")
        self.x = lax.axis_index("x")
        self.h = lax.axis_index("h")
        self.y = 2 * self.h + lax.axis_index("l")
        self.step = 1 - 2 * self.c
        self.halves = jnp.stack([512 * self.c, 512 * (1 - self.c)]).astype(jnp.int32)
        self.blocks = {}
        for first, second in (("x", "y"), ("y", "x")):
            out = []
            for k2 in range(4):
                for k1 in range(4):
                    a, b = self.source(first, k1), self.source(second, k2)
                    out.append(4 * a + b if first == "x" else 4 * b + a)
            self.blocks[first] = jnp.stack(out).astype(jnp.int32)

    def source(self, axis, k):
        at = lax.rem(dict(x=self.x, y=self.y)[axis] - self.step * k + 4, 4)
        if axis == "y":
            at = 2 * lax.rem(at, 2) + lax.div(at, 2)
        return at


SMEM = pl.BlockSpec(memory_space=pltpu.SMEM)


def place_rows(parts, blocks):
    n = parts[0].shape[1]

    def kernel(blocks_ref, p0, p1, p2, p3, out_ref, sems):
        copies = []
        for k2, part in enumerate((p0, p1, p2, p3)):
            for k1 in range(4):
                at = pl.multiple_of(blocks_ref[4 * k2 + k1] * 128, 128)
                copies.append(
                    pltpu.make_async_copy(
                        part.at[pl.ds(128 * k1, 128)], out_ref.at[pl.ds(at, 128)], sems.at[4 * k2 + k1]
                    )
                )
        for copy in copies:
            copy.start()
        for copy in copies:
            copy.wait()

    return pl.pallas_call(
        kernel,
        out_shape=sds((D, n)),
        in_specs=[SMEM] + [ANY] * 4,
        out_specs=WHOLE,
        scratch_shapes=[pltpu.SemaphoreType.DMA((16,))],
        compiler_params=PARAMS,
        cost_estimate=cost(0, D * n),
        name="place_rows",
    )(blocks, *parts)


def gather_rows(block, first, me, hold=None):
    second = "y" if first == "x" else "x"
    parts = [block]
    for _ in range(3):
        parts.append(ring(parts[-1], first))
    parts = [jnp.concatenate(parts, axis=0)]
    for _ in range(3):
        parts.append(ring(parts[-1], second))
    return place_rows(parts, me.blocks[first]), parts


def call(kernel, name, outs, args, flops, scratch=()):
    return pl.pallas_call(
        kernel,
        out_shape=outs,
        in_specs=[SMEM if a.dtype == jnp.int32 else WHOLE for a in args],
        out_specs=[WHOLE] * len(outs),
        scratch_shapes=list(scratch),
        compiler_params=PARAMS,
        cost_estimate=cost(flops, 0),
        name=name,
    )(*args)


def weight_piece(rows, right, columns, at, first, received, last=None):
    low, high = columns
    n = high - low
    scalars = at.reshape(1).astype(jnp.int32)
    if last is not None:
        scalars = jnp.concatenate([scalars, last])
    args = [scalars, *rows, *right] + ([] if received is None else [received])

    def kernel(*refs):
        at = refs[0][0]
        row_refs, right_refs = refs[1 : 1 + len(rows)], refs[1 + len(rows) : 1 + len(rows) + len(right)]
        left = []
        for j in range(4):
            block = 4 * at + j if first == "x" else 4 * j + at
            lanes = pl.ds(pl.multiple_of(block * 128, 128), 128)
            left.append(jnp.concatenate([r[:, lanes] for r in row_refs], axis=0))
        left = jnp.concatenate(left, axis=1)
        for j in range(low, high, 256):
            end = min(j + 256, high)
            total = dot(left, jnp.concatenate([r[:, j:end] for r in right_refs], axis=0), 0, 0)
            here = slice(j - low, end - low)
            if received is not None:
                total = total + fl(refs[len(args) - 1][:, here])
            refs[len(args) if last is None else -1][:, here] = bf(total)
        if last is not None:
            for k in range(4):
                rows_at = pl.ds(pl.multiple_of(refs[0][1 + k] * 128, 128), 128)
                refs[len(args) + k][...] = refs[-1][rows_at, :]

    flops = 2 * 512 * SEQ_LEN * n
    if last is None:
        return call(kernel, "weight_piece", [sds((512, n))], args, flops)[0]
    scratch = [pltpu.VMEM((512, n), jnp.bfloat16)]
    return call(kernel, "weight_piece", [sds((128, n))] * 4, args, flops, scratch)


def weight_gradient(rows, right, columns, first, me):
    second = "y" if first == "x" else "x"
    last = jnp.stack([me.source(second, k) for k in range(4)]).astype(jnp.int32)
    total = weight_piece(rows, right, columns, me.source(first, 1), first, None)
    for k in (2, 3, 0):
        total = weight_piece(
            rows, right, columns, me.source(first, k), first, ring(total, first), None if k else last
        )
    blocks = total
    total = fl(blocks[1])
    for k in (2, 3, 0):
        total = fl(ring(bf(total), second)) + fl(blocks[k])
    return total


def gather_z(block):
    wide = jnp.broadcast_to(block[None], (4,) + block.shape)
    return lax.all_to_all(wide, "z", split_axis=0, concat_axis=0, tiled=True).reshape(512, block.shape[1])


def gather_tokens(block):
    own = gather_z(block)
    return own, sibling(own)


def scatter_z(sums):
    parts = sums.reshape(4, 128, sums.shape[1])
    arrived = lax.all_to_all(parts, "z", split_axis=0, concat_axis=0, tiled=True)
    return jnp.sum(fl(arrived), axis=0)


def partial_sums(pieces, weights):
    count = len(pieces)

    def kernel(*refs):
        for j in range(0, D, 512):
            total = None
            for i in range(count):
                one = dot(refs[i][...], refs[count + i][j : j + 512, :], 1, 1)
                total = one if total is None else total + one
            refs[-1][:, j : j + 512] = bf(total)

    depth = sum(p.shape[1] for p in pieces)
    return call(kernel, "partial_sums", [sds((512, D))], [*pieces, *weights], 2 * 512 * depth * D)[0]


def chip_sums(own, other, weights):
    received = sibling(partial_sums(other, weights))
    return bf(fl(partial_sums(own, weights)) + fl(received))


def chip_product(own, other, weight, sibling_weight):
    received = sibling(other)
    m = own.shape[1]

    def kernel(a_ref, b_ref, v_ref, w_ref, out_ref):
        for j in range(0, D, 512):
            here = slice(j, j + 512)
            total = dot(a_ref[...], v_ref[here, :m], 1, 1) + dot(b_ref[...], w_ref[here, :m], 1, 1)
            out_ref[:, here] = bf(total)

    args = [own, received, weight, sibling_weight]
    return call(kernel, "chip_product", [sds((512, D))], args, 4 * 512 * m * D)[0]


def project(rows, weight, n, dtype):
    def kernel(rows_ref, w_ref, out_ref):
        for j in range(0, n, 256):
            out_ref[:, j : j + 256] = dot(rows_ref[...], w_ref[:, j : j + 256], 1, 0).astype(dtype)

    return call(kernel, "project", [sds((512, n), dtype)], [rows, weight], 2 * 512 * D * n)[0]


def rope(u, cosine, sine):
    lane = lax.broadcasted_iota(jnp.int32, u.shape, 1)
    turned = jnp.where(lane % DH < DH // 2, pltpu.roll(u, 96, 1), pltpu.roll(u, 32, 1))
    return u * cosine + turned * sine


def rope_three(u, cosine, sine):
    lane = lax.broadcasted_iota(jnp.int32, cosine.shape, 1)
    last = u[:, 256:]
    return jnp.concatenate(
        [
            rope(u[:, :128], cosine, sine),
            rope(u[:, 128:256], cosine, sine),
            jnp.where(lane < DH, rope(last, cosine, sine), last),
        ],
        axis=1,
    )


def half_at(halves_ref, i):
    return pl.ds(pl.multiple_of(halves_ref[i], 512), 512)


def project_qkv(i, rows, gain, weight, tables, halves):
    def kernel(halves_ref, x_ref, gain_ref, w_ref, cos_ref, sin_ref, normed_ref, out_ref):
        x = fl(x_ref[...])
        inverse = lax.rsqrt(jnp.mean(x * x, axis=1, keepdims=True) + eps)
        normed_ref[...] = bf(x * inverse * gain_ref[...])
        here = half_at(halves_ref, i)
        product = dot(normed_ref[...], w_ref[...], 1, 0)
        out_ref[...] = bf(rope_three(product, cos_ref[here, :], sin_ref[here, :]))

    args = [halves, rows, gain, weight, *tables]
    return call(kernel, "project_qkv", [sds((512, D)), sds((512, 384))], args, 2 * 512 * D * 384)


def scores_t(keys, query, q_at):
    s = dot(keys, query, 1, 1)
    key = lax.broadcasted_iota(jnp.int32, (256, 256), 0)
    column = lax.broadcasted_iota(jnp.int32, (256, 256), 1)
    diagonal = jnp.where(key <= column, s[q_at:], -1e30)
    return diagonal if q_at == 0 else jnp.concatenate([s[:q_at], diagonal], axis=0)


def attend(qkv, halves):
    def kernel(halves_ref, q0, q1, own_ref, other_ref, nat_ref, lse_ref, att_ref):
        nat_ref[half_at(halves_ref, 0), :] = q0[...]
        nat_ref[half_at(halves_ref, 1), :] = q1[...]
        kv = nat_ref[:, 256:]
        keys = kv[:, :DH]
        values_t = kv.T[DH:]
        lse_ref[...] = jnp.zeros_like(lse_ref)
        for q_at in range(0, SEQ_LEN, 256):
            end = q_at + 256
            for pair in range(2):
                two = nat_ref[q_at:end, 128 * pair : 128 * pair + 128]
                outs = []
                for i in range(2):
                    s = scores_t(keys[:end], two[:, DH * i : DH * i + DH], q_at)
                    top = jnp.max(s, axis=0, keepdims=True)
                    p = jnp.exp2((s - top) * SCALE2)
                    total = jnp.sum(p, axis=0, keepdims=True)
                    outs.append(dot(values_t[:, :end], bf(p), 1, 0) / total)
                    g = 2 * pair + i
                    lse_ref[g : g + 1, q_at:end] = top * SCALE2 + jnp.log2(total)
                att_ref[q_at:end, 128 * pair : 128 * pair + 128] = bf(jnp.concatenate(outs, axis=0).T)
        own_ref[...] = att_ref[half_at(halves_ref, 0), :]
        other_ref[...] = att_ref[half_at(halves_ref, 1), :]

    outs = [sds((512, 256)), sds((512, 256)), sds((SEQ_LEN, 384)), sds((8, SEQ_LEN), jnp.float32)]
    scratch = [pltpu.VMEM((SEQ_LEN, 256), jnp.bfloat16)]
    return call(kernel, "attend", outs, [halves, *qkv], 3e9, scratch)


def attend_backward(qkv, lse, grad_out, tables, halves):
    def kernel(halves_ref, nat_ref, lse_ref, g0, g1, cos_ref, sin_ref, own_ref, other_ref, go_nat, kv_sum, d_nat):
        go_nat[half_at(halves_ref, 0), :] = g0[...]
        go_nat[half_at(halves_ref, 1), :] = g1[...]
        kv = nat_ref[:, 256:]
        keys = kv[:, :DH]
        values = kv[:, DH:]
        keys_t = kv.T[:DH]
        kv_sum[...] = jnp.zeros_like(kv_sum)
        for q_at in range(0, SEQ_LEN, 256):
            end = q_at + 256
            cosine = cos_ref[q_at:end, :]
            sine = -sin_ref[q_at:end, :]
            for pair in range(2):
                lanes = slice(128 * pair, 128 * pair + 128)
                two = nat_ref[q_at:end, lanes]
                two_grad = go_nat[q_at:end, lanes]
                outs = []
                for i in range(2):
                    query = two[:, DH * i : DH * i + DH]
                    grad = two_grad[:, DH * i : DH * i + DH]
                    g = 2 * pair + i
                    s = scores_t(keys[:end], query, q_at)
                    p = jnp.exp2(s * SCALE2 - lse_ref[g : g + 1, q_at:end])
                    dp = dot(values[:end], grad, 1, 1)
                    delta = jnp.sum(dp * p, axis=0, keepdims=True)
                    ds = bf(p * (dp - delta))
                    kv_sum[:end, :] += jnp.concatenate(
                        [dot(ds, query, 1, 0), dot(bf(p), grad, 1, 0)], axis=1
                    )
                    outs.append(dot(keys_t[:, :end], ds, 1, 0))
                d_query = jnp.concatenate(outs, axis=0).T * SCALE
                d_nat[q_at:end, lanes] = bf(rope(d_query, cosine, sine))
        lane = lax.broadcasted_iota(jnp.int32, (SEQ_LEN, 128), 1)
        total = kv_sum[...]
        turned = rope(total * SCALE, cos_ref[...], -sin_ref[...])
        d_nat[:, 256:] = bf(jnp.where(lane < DH, turned, total))
        own_ref[...] = d_nat[half_at(halves_ref, 0), :]
        other_ref[...] = d_nat[half_at(halves_ref, 1), :]

    scratch = [
        pltpu.VMEM((SEQ_LEN, 256), jnp.bfloat16),
        pltpu.VMEM((SEQ_LEN, 128), jnp.float32),
        pltpu.VMEM((SEQ_LEN, 384), jnp.bfloat16),
    ]
    args = [halves, qkv, lse, *grad_out, *tables]
    return call(kernel, "attend_backward", [sds((512, 384))] * 2, args, 6e9, scratch)


def mlp_step(rows, w_gate, w_up, grad_act):
    width = w_gate.shape[1]

    def kernel(rows_ref, g_ref, u_ref, ga_ref, act_ref, gg_ref, gu_ref):
        for j in range(0, width, 256):
            here = slice(j, j + 256)
            gate = dot(rows_ref[...], g_ref[:, here], 1, 0)
            up = dot(rows_ref[...], u_ref[:, here], 1, 0)
            sig = jax.nn.sigmoid(gate)
            silu = gate * sig
            ga = ga_ref[:, here]
            act_ref[:, here] = bf(silu * up)
            gg_ref[:, here] = bf(ga * up * sig * (1.0 + gate * (1.0 - sig)))
            gu_ref[:, here] = bf(ga * silu)

    args = [rows, w_gate, w_up, grad_act]
    return call(kernel, "mlp_step", [sds((512, width))] * 3, args, 4 * 512 * D * width)


def frequencies(head_size):
    pair_index = jnp.arange(head_size // 2).astype(jnp.float32)
    base_freq = 500000.0 ** (-2.0 * pair_index / head_size)
    wavelen = 2.0 * jnp.pi / base_freq
    smooth = (8192.0 / wavelen - 1.0) / 3.0
    blended = (1.0 - smooth) * base_freq / 32.0 + smooth * base_freq
    return jnp.where(
        wavelen < 2048.0, base_freq, jnp.where(wavelen > 8192.0, base_freq / 32.0, blended)
    )


def norm_parts(values):
    inverse = lax.rsqrt(jnp.mean(values * values, axis=-1, keepdims=True) + eps)
    return (values * inverse, inverse)


def norm_backward(grad_normed, unit_rows, inverse, gain_rows):
    scaled = grad_normed * gain_rows
    return inverse * (scaled - unit_rows * jnp.mean(scaled * unit_rows, axis=-1, keepdims=True))


def on_device(
    tokens, positions, w_query, w_key, w_value, w_out, attn_gain, w_gate, w_up, w_down, mlp_gain, cotangent
):
    me = Place()
    inputs_b = swapped(tokens)
    gains = jnp.pad(jnp.stack([attn_gain, mlp_gain], axis=1), ((0, 0), (0, 126)))
    part_attn = swapped(jnp.concatenate([w_query, w_key, w_value, w_out.T, gains], axis=1))
    seq_positions = jnp.where(me.h == me.c, positions, sibling(positions))

    part_attn, inputs_b = lax.optimization_barrier((part_attn, inputs_b))
    own_in = gather_z(inputs_b)
    w_qkv, parts_a = gather_rows(part_attn[:, :384], "x", me)
    out_and_gains, parts_b = gather_rows(part_attn[:, 384:], "y", me)

    freq = jnp.tile(frequencies(DH), 4)
    angles = seq_positions.astype(jnp.float32)[:, None] * freq[None, :]
    sign = jnp.where(jnp.arange(128) % DH < DH // 2, -1.0, 1.0)
    tables = (jnp.cos(angles), jnp.sin(angles) * sign[None, :])
    pick = bf(jnp.arange(128)[None, :] == jnp.arange(8)[:, None])
    gain_rows = dot(pick, out_and_gains[:, 256:], 1, 1)
    gain_attn, gain_mlp = gain_rows[:1], gain_rows[1:2]

    w_gate, w_up, w_down = after((w_gate, w_up, w_down), inputs_b)
    part_gate, part_up, part_down = swapped(w_gate), swapped(w_up), swapped(w_down.T)
    part_gate, part_up, part_down = after((part_gate, part_up, part_down), parts_a[2], parts_b[2])
    w_down_t = jnp.concatenate(
        [gather_rows(part_down[:, :512], "x", me)[0], gather_rows(part_down[:, 512:], "y", me)[0]], axis=1
    )
    full_gate = gather_rows(part_gate, "x", me)[0]
    full_up = gather_rows(part_up, "y", me)[0]

    rows_in = [own_in, sibling(own_in)]
    projected = [project_qkv(i, rows_in[i], gain_attn, w_qkv, tables, me.halves) for i in range(2)]
    normed_attn = [p[0] for p in projected]

    (cotangent,) = after((cotangent,), inputs_b)
    upstream = swapped(cotangent)
    (own_up,) = after((upstream,), own_in)
    rows_up = gather_tokens(own_up)
    grad_act = [project(r, w_down_t, 1024, jnp.float32) for r in rows_up]

    attended, other_attended, qkv, lse = attend([p[1] for p in projected], me.halves)
    inputs = fl(inputs_b)
    out_sums = chip_product(attended, other_attended, out_and_gains, sibling(out_and_gains))
    (out_sums,) = after((out_sums,), rows_up[0])
    residual = inputs + scatter_z(out_sums)

    unit_mlp, inverse_mlp = norm_parts(residual)
    rows_mlp = gather_tokens(bf(unit_mlp * gain_mlp))
    steps = [mlp_step(r, full_gate, full_up, g) for r, g in zip(rows_mlp, grad_act)]
    activated, grad_gate_pre, grad_up_pre = zip(*steps)

    gate_up = list(zip(grad_gate_pre, grad_up_pre))
    mlp_sums = chip_sums(gate_up[0], gate_up[1], [full_gate, full_up])
    grad_normed_mlp = scatter_z(mlp_sums)
    grad_residual = fl(upstream) + norm_backward(grad_normed_mlp, unit_mlp, inverse_mlp, gain_mlp)
    rows_gr = gather_tokens(bf(grad_residual))

    acts = after(activated, mlp_sums)
    down_sums = chip_sums([acts[0]], [acts[1]], [w_down_t])
    (down_sums,) = after((down_sums,), rows_gr[0])
    layer_out = bf(residual + scatter_z(down_sums))

    share_down = jnp.concatenate(
        [
            weight_gradient(rows_up, acts, (0, 512), "x", me),
            weight_gradient(rows_up, acts, (512, 1024), "y", me),
        ],
        axis=1,
    )
    gg, gu = after((grad_gate_pre, grad_up_pre), mlp_sums)
    share_gate = weight_gradient(rows_mlp, gg, (0, 1024), "x", me)
    share_up = weight_gradient(rows_mlp, gu, (0, 1024), "y", me)

    grad_attended = [project(r, out_and_gains, 256, jnp.bfloat16) for r in rows_gr]
    grad_qkv, other_grad_qkv = attend_backward(qkv, lse, grad_attended, tables, me.halves)
    grad_normed_attn = scatter_z(chip_product(grad_qkv, other_grad_qkv, w_qkv, sibling(w_qkv)))
    unit_attn, inverse_attn = norm_parts(inputs)
    grad_norm_attn = norm_backward(grad_normed_attn, unit_attn, inverse_attn, gain_attn)
    grad_tokens = bf(grad_residual + grad_norm_attn)

    share_qkv = weight_gradient(normed_attn, [grad_qkv, other_grad_qkv], (0, 384), "x", me)
    share_out = weight_gradient(rows_gr, [attended, other_attended], (0, 256), "y", me)

    def gain_sum(*terms):
        return sum(jnp.sum(fl(w) * g, axis=1) for w, g in terms)

    gain_sums = jnp.stack(
        [gain_sum((part_attn[:, :384], share_qkv)), gain_sum((part_gate, share_gate), (part_up, share_up))]
    )
    gain_sums = gain_sums / fl(part_attn[:, 640:642].T)
    gain_sums = gain_sums + sibling(gain_sums)
    gain_sums = gain_sums + z_flipped(gain_sums, 1)
    gain_sums = swapped(gain_sums + z_flipped(gain_sums, 2))

    share_attn = fl(swapped(bf(jnp.concatenate([share_qkv, share_out], axis=1))))
    return (
        swapped(layer_out),
        swapped(grad_tokens),
        share_attn[:, :256],
        share_attn[:, 256:320],
        share_attn[:, 320:384],
        share_attn[:, 384:].T,
        gain_sums[0],
        fl(swapped(bf(share_gate))),
        fl(swapped(bf(share_up))),
        fl(swapped(bf(share_down))).T,
        gain_sums[1],
    )


def solution(mesh):
    split = Mesh(mesh.devices.reshape(4, 2, 2, 2, 4), AXES)
    dp, tensor = ("x", "l", "c"), ("h", "z")
    both = P(AXES, None)
    weight, turned, vector = P(dp, tensor), P(tensor, dp), P(dp)
    in_specs = (
        both, vector, weight, weight, weight, turned, vector, weight, weight, turned, vector, both,
    )
    out_specs = (
        both, both, weight, weight, weight, turned, vector, weight, weight, turned, vector,
    )
    return jax.shard_map(on_device, mesh=split, in_specs=in_specs, out_specs=out_specs, check_vma=False)
```

```python
import functools
import itertools
import math

import jax
import jax.numpy as jnp
from jax import lax
from jax.experimental import pallas as pl
from jax.experimental.pallas import tpu as pltpu
from jax.sharding import Mesh, PartitionSpec as P

H = 32
KV = 8
DH = 64
SEQ_LEN = 1024
D = 2048
eps = 1e-05

SIZES = dict(x=4, l=2, c=2, h=2, z=4)
AXES = ("x", "l", "c", "h", "z")

SCALE = DH ** (-0.5)
SCALE2 = SCALE * math.log2(math.e)
VMEM_LIMIT = 14 * 1024 * 1024


def pairs(axes, move):
    def place(index):
        at = 0
        for a in axes:
            at = at * SIZES[a] + index[a]
        return at

    out = []
    for index in itertools.product(*[range(SIZES[a]) for a in axes]):
        here = dict(zip(axes, index))
        out.append((place(here), place(move(dict(here)))))
    return out


def to_swapped(d):
    d["c"], d["h"] = d["h"], d["c"]
    return d


def to_sibling(d):
    d["c"] = 1 - d["c"]
    return d


def along(axis):
    def move(d):
        step = 1 - 2 * d["c"]
        if axis == "y":
            y = (2 * d["h"] + d["l"] + step) % 4
            d["h"], d["l"] = y // 2, y % 2
        else:
            d[axis] = (d[axis] + step) % 4
        return d

    return move


RING_AXES = dict(x=("x", "c"), y=("l", "c", "h"))


def ring(value, axis):
    axes = RING_AXES[axis]
    return lax.ppermute(value, axes, pairs(axes, along(axis)))


def swapped(value):
    return lax.ppermute(value, ("c", "h"), pairs(("c", "h"), to_swapped))


def sibling(value):
    return lax.ppermute(value, ("c",), pairs(("c",), to_sibling))


def z_moved(value, step):
    def move(d):
        d["z"] = (d["z"] + step) % 4
        return d

    return lax.ppermute(value, ("z",), pairs(("z",), move))


def swapped_across(value):
    def move(d):
        c, h = d["c"], d["h"]
        d["h"], d["c"] = 1 - c, h
        return d

    return lax.ppermute(value, ("c", "h"), pairs(("c", "h"), move))


def after(values, *earlier):
    held = lax.optimization_barrier((tuple(values), tuple(earlier)))
    return held[0]


def dot(a, b, ca, cb):
    return lax.dot_general(a, b, (((ca,), (cb,)), ((), ())), preferred_element_type=jnp.float32)


def bf(v):
    return v.astype(jnp.bfloat16)


def fl(v):
    return v.astype(jnp.float32)


def sds(shape, dtype=jnp.bfloat16):
    return jax.ShapeDtypeStruct(shape, dtype)


def cost(flops):
    return pl.CostEstimate(flops=int(flops), bytes_accessed=1, transcendentals=0)


PARAMS = pltpu.CompilerParams(vmem_limit_bytes=VMEM_LIMIT)
ANY = pl.BlockSpec(memory_space=pl.ANY)
WHOLE = pl.BlockSpec(memory_space=pltpu.VMEM)


class Place:
    def __init__(self):
        self.c = lax.axis_index("c")
        self.x = lax.axis_index("x")
        self.h = lax.axis_index("h")
        self.y = 2 * self.h + lax.axis_index("l")
        self.step = 1 - 2 * self.c
        self.halves = jnp.stack([512 * self.c, 512 * (1 - self.c)]).astype(jnp.int32)
        self.blocks = {}
        for first, second in (("x", "y"), ("y", "x")):
            out = []
            for k2 in range(4):
                for k1 in range(4):
                    a, b = self.source(first, k1), self.source(second, k2)
                    out.append(4 * a + b if first == "x" else 4 * b + a)
            self.blocks[first] = jnp.stack(out).astype(jnp.int32)

    def source(self, axis, k):
        at = lax.rem(dict(x=self.x, y=self.y)[axis] - self.step * k + 4, 4)
        if axis == "y":
            at = 2 * lax.rem(at, 2) + lax.div(at, 2)
        return at


SMEM = pl.BlockSpec(memory_space=pltpu.SMEM)


def place_rows(parts, blocks):
    n = parts[0].shape[1]

    def kernel(blocks_ref, p0, p1, p2, p3, out_ref, sems):
        copies = []
        for k2, part in enumerate((p0, p1, p2, p3)):
            for k1 in range(4):
                at = pl.multiple_of(blocks_ref[4 * k2 + k1] * 128, 128)
                copies.append(
                    pltpu.make_async_copy(
                        part.at[pl.ds(128 * k1, 128)], out_ref.at[pl.ds(at, 128)], sems.at[4 * k2 + k1]
                    )
                )
        for copy in copies:
            copy.start()
        for copy in copies:
            copy.wait()

    return pl.pallas_call(
        kernel,
        out_shape=sds((D, n)),
        in_specs=[SMEM] + [ANY] * 4,
        out_specs=WHOLE,
        scratch_shapes=[pltpu.SemaphoreType.DMA((16,))],
        compiler_params=PARAMS,
        cost_estimate=cost(1),
        name="place_rows",
    )(blocks, *parts)


def stepped(value, axis, steps):
    def move(d):
        for _ in range(steps):
            d = along(axis)(d)
        return d

    axes = RING_AXES[axis]
    return lax.ppermute(value, axes, pairs(axes, move))


def first_stage(block, first, direct):
    parts = [block]
    for k in range(1, 4):
        parts.append(stepped(block, first, k) if direct else ring(parts[-1], first))
    return jnp.concatenate(parts, axis=0)


def second_stage(stage, first, holds=(None, None, None)):
    second = "y" if first == "x" else "x"
    parts = [stage]
    for hold in holds:
        part = parts[-1] if hold is None else after((parts[-1],), hold)[0]
        parts.append(ring(part, second))
    return parts


def gather_rows(block, first, me, direct=False):
    parts = second_stage(first_stage(block, first, direct), first)
    return place_rows(parts, me.blocks[first]), parts


LONG = ("attend", "attend_backward")


def call(kernel, name, outs, args, flops, scratch=()):
    return pl.pallas_call(
        kernel,
        out_shape=outs,
        in_specs=[SMEM if a.dtype == jnp.int32 else WHOLE for a in args],
        out_specs=[WHOLE] * len(outs),
        scratch_shapes=list(scratch),
        compiler_params=PARAMS,
        cost_estimate=cost(flops if name in LONG else 1),
        name=name,
    )(*args)


def weight_piece(rows, right, columns, at, first, received, last=None):
    low, high = columns
    n = high - low
    scalars = at.reshape(1).astype(jnp.int32)
    if last is not None:
        scalars = jnp.concatenate([scalars, last])
    args = [scalars, *rows, *right] + ([] if received is None else [received])

    def kernel(*refs):
        at = refs[0][0]
        row_refs, right_refs = refs[1 : 1 + len(rows)], refs[1 + len(rows) : 1 + len(rows) + len(right)]
        left = []
        for j in range(4):
            block = 4 * at + j if first == "x" else 4 * j + at
            lanes = pl.ds(pl.multiple_of(block * 128, 128), 128)
            left.append(jnp.concatenate([r[:, lanes] for r in row_refs], axis=0))
        left = jnp.concatenate(left, axis=1)
        for j in range(low, high, 256):
            end = min(j + 256, high)
            total = dot(left, jnp.concatenate([r[:, j:end] for r in right_refs], axis=0), 0, 0)
            here = slice(j - low, end - low)
            if received is not None:
                total = total + fl(refs[len(args) - 1][:, here])
            refs[len(args) if last is None else -1][:, here] = bf(total)
        if last is not None:
            for k in range(4):
                rows_at = pl.ds(pl.multiple_of(refs[0][1 + k] * 128, 128), 128)
                refs[len(args) + k][...] = refs[-1][rows_at, :]

    flops = 2 * 512 * SEQ_LEN * n
    if last is None:
        return call(kernel, "weight_piece", [sds((512, n))], args, flops)[0]
    scratch = [pltpu.VMEM((512, n), jnp.bfloat16)]
    return call(kernel, "weight_piece", [sds((128, n))] * 4, args, flops, scratch)


def weight_product(rows, right):
    n = right[0].shape[1]

    def kernel(*refs):
        row_refs, right_refs = refs[: len(rows)], refs[len(rows) : -1]
        for i in range(0, D, 512):
            left = jnp.concatenate([r[:, i : i + 512] for r in row_refs], axis=0)
            for j in range(0, n, 256):
                total = dot(left, jnp.concatenate([r[:, j : j + 256] for r in right_refs], axis=0), 0, 0)
                refs[-1][i : i + 512, j : j + 256] = bf(total)

    return call(kernel, "weight_product", [sds((D, n))], [*rows, *right], 2 * D * SEQ_LEN * n)[0]


class WeightGradient:
    def __init__(self, rows, right, columns, first, me):
        self.args = (rows, right, columns)
        self.first, self.second = first, "y" if first == "x" else "x"
        self.me = me
        self.total = self.received = None

    def send(self):
        if self.received is None:
            self.received = ring(self.total, self.first)
        return self.received

    def piece(self, k, *holds):
        rows, right, columns = self.args
        at = self.me.source(self.first, k)
        received = None if k == 1 else self.send()
        self.received = None
        if holds and received is None:
            right = after(right, *holds)
        elif holds:
            (received,) = after((received,), *holds)
        last = None
        if k == 0:
            last = jnp.stack([self.me.source(self.second, i) for i in range(4)]).astype(jnp.int32)
        self.total = weight_piece(rows, right, columns, at, self.first, received, last)
        return self.total

    def finish(self, *holds):
        if holds:
            self.total = after(self.total, *holds)
        total = fl(self.total[1])
        for k in (2, 3, 0):
            total = fl(ring(bf(total), self.second)) + fl(self.total[k])
        return total


def sum_blocks(parts, order):
    n = parts[0].shape[1]

    def kernel(order_ref, p0, p1, p2, p3, *out_refs):
        for k in range(4):
            at = pl.ds(pl.multiple_of(order_ref[k] * 128, 128), 128)
            out_refs[k][...] = bf(fl(p0[at, :]) + fl(p1[at, :]) + fl(p2[at, :]) + fl(p3[at, :]))

    return call(kernel, "sum_blocks", [sds((128, n))] * 4, [order, *parts], 0)


def direct_pieces(rows, right, columns, first, me):
    parts = []
    for k in (2, 1, 3, 0):
        made = weight_piece(rows, right, columns, me.source(first, k), first, None)
        parts.append(stepped(made, first, 4 - k) if k else made)
    return parts


def direct_sums(parts, first, me):
    second = "y" if first == "x" else "x"
    order = jnp.stack([me.source(second, i) for i in range(4)]).astype(jnp.int32)
    blocks = sum_blocks(parts, order)
    total = fl(blocks[0])
    for k in (2, 1, 3):
        total = total + fl(stepped(blocks[k], second, 4 - k))
    return total


def gather_z(block):
    wide = jnp.broadcast_to(block[None], (4,) + block.shape)
    return lax.all_to_all(wide, "z", split_axis=0, concat_axis=0, tiled=True).reshape(512, block.shape[1])


def gather_tokens(block):
    own = gather_z(block)
    return own, sibling(own)


def arrive_z(sums):
    parts = sums.reshape(4, 128, sums.shape[1])
    return lax.all_to_all(parts, "z", split_axis=0, concat_axis=0, tiled=True)


def scatter_z(sums):
    return jnp.sum(fl(arrive_z(sums)), axis=0)


def partial_sums(pieces, weights):
    count = len(pieces)

    def kernel(*refs):
        for j in range(0, D, 512):
            total = None
            for i in range(count):
                one = dot(refs[i][...], refs[count + i][j : j + 512, :], 1, 1)
                total = one if total is None else total + one
            refs[-1][:, j : j + 512] = bf(total)

    depth = sum(p.shape[1] for p in pieces)
    return call(kernel, "partial_sums", [sds((512, D))], [*pieces, *weights], 2 * 512 * depth * D)[0]


def chip_sums(own, other, weights):
    received = sibling(partial_sums(other, weights))
    return bf(fl(partial_sums(own, weights)) + fl(received))


def chip_product(own, other, weight, sibling_weight):
    received = sibling(other)
    m = own.shape[1]

    def kernel(a_ref, b_ref, v_ref, w_ref, out_ref):
        for j in range(0, D, 512):
            here = slice(j, j + 512)
            total = dot(a_ref[...], v_ref[here, :m], 1, 1) + dot(b_ref[...], w_ref[here, :m], 1, 1)
            out_ref[:, here] = bf(total)

    args = [own, received, weight, sibling_weight]
    return call(kernel, "chip_product", [sds((512, D))], args, 4 * 512 * m * D)[0]


def project(rows, weight, n, dtype):
    def kernel(rows_ref, w_ref, out_ref):
        for j in range(0, n, 256):
            out_ref[:, j : j + 256] = dot(rows_ref[...], w_ref[:, j : j + 256], 1, 0).astype(dtype)

    return call(kernel, "project", [sds((512, n), dtype)], [rows, weight], 2 * 512 * D * n)[0]


def rope(u, cosine, sine):
    lane = lax.broadcasted_iota(jnp.int32, u.shape, 1)
    turned = jnp.where(lane % DH < DH // 2, pltpu.roll(u, 96, 1), pltpu.roll(u, 32, 1))
    return u * cosine + turned * sine


def rope_three(u, cosine, sine):
    lane = lax.broadcasted_iota(jnp.int32, cosine.shape, 1)
    last = u[:, 256:]
    return jnp.concatenate(
        [
            rope(u[:, :128], cosine, sine),
            rope(u[:, 128:256], cosine, sine),
            jnp.where(lane < DH, rope(last, cosine, sine), last),
        ],
        axis=1,
    )


def half_at(halves_ref, i):
    return pl.ds(pl.multiple_of(halves_ref[i], 512), 512)


def project_qkv(i, rows, gain, weight, tables, halves):
    def kernel(halves_ref, x_ref, gain_ref, w_ref, cos_ref, sin_ref, normed_ref, out_ref):
        x = fl(x_ref[...])
        inverse = lax.rsqrt(jnp.mean(x * x, axis=1, keepdims=True) + eps)
        normed_ref[...] = bf(x * inverse * gain_ref[...])
        here = half_at(halves_ref, i)
        product = dot(normed_ref[...], w_ref[...], 1, 0)
        out_ref[...] = bf(rope_three(product, cos_ref[here, :], sin_ref[here, :]))

    args = [halves, rows, gain, weight, *tables]
    return call(kernel, "project_qkv", [sds((512, D)), sds((512, 384))], args, 2 * 512 * D * 384)


def scores_t(keys, query, q_at):
    s = dot(keys, query, 1, 1)
    key = lax.broadcasted_iota(jnp.int32, (256, 256), 0)
    column = lax.broadcasted_iota(jnp.int32, (256, 256), 1)
    diagonal = jnp.where(key <= column, s[q_at:], -1e30)
    return diagonal if q_at == 0 else jnp.concatenate([s[:q_at], diagonal], axis=0)


def attend(qkv, halves):
    def kernel(halves_ref, q0, q1, own_ref, other_ref, nat_ref, lse_ref, att_ref):
        nat_ref[half_at(halves_ref, 0), :] = q0[...]
        nat_ref[half_at(halves_ref, 1), :] = q1[...]
        kv = nat_ref[:, 256:]
        keys = kv[:, :DH]
        values_t = kv.T[DH:]
        lse_ref[...] = jnp.zeros_like(lse_ref)
        for q_at in range(0, SEQ_LEN, 256):
            end = q_at + 256
            for pair in range(2):
                two = nat_ref[q_at:end, 128 * pair : 128 * pair + 128]
                outs = []
                for i in range(2):
                    s = scores_t(keys[:end], two[:, DH * i : DH * i + DH], q_at)
                    top = jnp.max(s, axis=0, keepdims=True)
                    p = jnp.exp2((s - top) * SCALE2)
                    total = jnp.sum(p, axis=0, keepdims=True)
                    outs.append(dot(values_t[:, :end], bf(p), 1, 0) / total)
                    g = 2 * pair + i
                    lse_ref[g : g + 1, q_at:end] = top * SCALE2 + jnp.log2(total)
                att_ref[q_at:end, 128 * pair : 128 * pair + 128] = bf(jnp.concatenate(outs, axis=0).T)
        own_ref[...] = att_ref[half_at(halves_ref, 0), :]
        other_ref[...] = att_ref[half_at(halves_ref, 1), :]

    outs = [sds((512, 256)), sds((512, 256)), sds((SEQ_LEN, 384)), sds((8, SEQ_LEN), jnp.float32)]
    scratch = [pltpu.VMEM((SEQ_LEN, 256), jnp.bfloat16)]
    return call(kernel, "attend", outs, [halves, *qkv], 3e9, scratch)


def attend_backward(qkv, lse, grad_out, tables, halves):
    def kernel(halves_ref, nat_ref, lse_ref, g0, g1, cos_ref, sin_ref, own_ref, other_ref, go_nat, kv_sum, d_nat):
        go_nat[half_at(halves_ref, 0), :] = g0[...]
        go_nat[half_at(halves_ref, 1), :] = g1[...]
        kv = nat_ref[:, 256:]
        keys = kv[:, :DH]
        values = kv[:, DH:]
        keys_t = kv.T[:DH]
        kv_sum[...] = jnp.zeros_like(kv_sum)
        for q_at in range(0, SEQ_LEN, 256):
            end = q_at + 256
            cosine = cos_ref[q_at:end, :]
            sine = -sin_ref[q_at:end, :]
            for pair in range(2):
                lanes = slice(128 * pair, 128 * pair + 128)
                two = nat_ref[q_at:end, lanes]
                two_grad = go_nat[q_at:end, lanes]
                outs = []
                for i in range(2):
                    query = two[:, DH * i : DH * i + DH]
                    grad = two_grad[:, DH * i : DH * i + DH]
                    g = 2 * pair + i
                    s = scores_t(keys[:end], query, q_at)
                    p = jnp.exp2(s * SCALE2 - lse_ref[g : g + 1, q_at:end])
                    dp = dot(values[:end], grad, 1, 1)
                    delta = jnp.sum(dp * p, axis=0, keepdims=True)
                    ds = bf(p * (dp - delta))
                    kv_sum[:end, :] += jnp.concatenate(
                        [dot(ds, query, 1, 0), dot(bf(p), grad, 1, 0)], axis=1
                    )
                    outs.append(dot(keys_t[:, :end], ds, 1, 0))
                d_query = jnp.concatenate(outs, axis=0).T * SCALE
                d_nat[q_at:end, lanes] = bf(rope(d_query, cosine, sine))
        lane = lax.broadcasted_iota(jnp.int32, (SEQ_LEN, 128), 1)
        total = kv_sum[...]
        turned = rope(total * SCALE, cos_ref[...], -sin_ref[...])
        d_nat[:, 256:] = bf(jnp.where(lane < DH, turned, total))
        own_ref[...] = d_nat[half_at(halves_ref, 0), :]
        other_ref[...] = d_nat[half_at(halves_ref, 1), :]

    scratch = [
        pltpu.VMEM((SEQ_LEN, 256), jnp.bfloat16),
        pltpu.VMEM((SEQ_LEN, 128), jnp.float32),
        pltpu.VMEM((SEQ_LEN, 384), jnp.bfloat16),
    ]
    args = [halves, qkv, lse, *grad_out, *tables]
    return call(kernel, "attend_backward", [sds((512, 384))] * 2, args, 6e9, scratch)


def mlp_step(rows, w_gate, w_up, grad_act):
    width = w_gate.shape[1]

    def kernel(rows_ref, g_ref, u_ref, ga_ref, act_ref, gg_ref, gu_ref):
        for j in range(0, width, 256):
            here = slice(j, j + 256)
            gate = dot(rows_ref[...], g_ref[:, here], 1, 0)
            up = dot(rows_ref[...], u_ref[:, here], 1, 0)
            sig = jax.nn.sigmoid(gate)
            silu = gate * sig
            ga = ga_ref[:, here]
            act_ref[:, here] = bf(silu * up)
            gg_ref[:, here] = bf(ga * up * sig * (1.0 + gate * (1.0 - sig)))
            gu_ref[:, here] = bf(ga * silu)

    args = [rows, w_gate, w_up, grad_act]
    return call(kernel, "mlp_step", [sds((512, width))] * 3, args, 4 * 512 * D * width)


def frequencies(head_size):
    pair_index = jnp.arange(head_size // 2).astype(jnp.float32)
    base_freq = 500000.0 ** (-2.0 * pair_index / head_size)
    wavelen = 2.0 * jnp.pi / base_freq
    smooth = (8192.0 / wavelen - 1.0) / 3.0
    blended = (1.0 - smooth) * base_freq / 32.0 + smooth * base_freq
    return jnp.where(
        wavelen < 2048.0, base_freq, jnp.where(wavelen > 8192.0, base_freq / 32.0, blended)
    )


def norm_parts(values):
    inverse = lax.rsqrt(jnp.mean(values * values, axis=-1, keepdims=True) + eps)
    return (values * inverse, inverse)


def norm_backward(grad_normed, unit_rows, inverse, gain_rows):
    scaled = grad_normed * gain_rows
    return inverse * (scaled - unit_rows * jnp.mean(scaled * unit_rows, axis=-1, keepdims=True))


def on_device(
    tokens, positions, w_query, w_key, w_value, w_out, attn_gain, w_gate, w_up, w_down, mlp_gain, cotangent
):
    me = Place()
    plane = ("x", "l", "h")
    inputs_b = swapped(tokens)
    gains = jnp.pad(jnp.stack([attn_gain, mlp_gain], axis=1), ((0, 0), (0, 126)))
    part_attn = swapped(jnp.concatenate([w_query, w_key, w_value, w_out.T, gains], axis=1))
    seq_positions = jnp.where(me.h == me.c, positions, sibling(positions))

    part_attn, inputs_b = lax.optimization_barrier((part_attn, inputs_b))
    own_in = gather_z(inputs_b)
    w_down, cotangent = after((w_down, cotangent), inputs_b)
    part_down = swapped(w_down.T)
    upstream = swapped(cotangent)
    w_qkv, parts_a = gather_rows(part_attn[:, :384], "x", me, direct=True)
    out_and_gains, parts_b = gather_rows(part_attn[:, 384:], "y", me, direct=True)
    (part_down,) = after((part_down,), parts_a[1])
    w_down_t = lax.all_gather(part_down, plane, axis=0, tiled=True)

    freq = jnp.tile(frequencies(DH), 4)
    angles = seq_positions.astype(jnp.float32)[:, None] * freq[None, :]
    sign = jnp.where(jnp.arange(128) % DH < DH // 2, -1.0, 1.0)
    tables = (jnp.cos(angles), jnp.sin(angles) * sign[None, :])
    pick = bf(jnp.arange(128)[None, :] == jnp.arange(8)[:, None])
    gain_rows = dot(pick, out_and_gains[:, 256:], 1, 1)
    gain_attn, gain_mlp = gain_rows[:1], gain_rows[1:2]

    w_gate, w_up = after((w_gate, w_up), parts_a[1], parts_b[1])
    part_gate, part_up = swapped(w_gate), swapped(w_up)
    part_gate, part_up = after((part_gate, part_up), parts_a[2], parts_b[2])
    stage_gate, stage_up = first_stage(part_gate, "x", False), first_stage(part_up, "y", False)

    (own_in,) = after((own_in,), upstream)
    rows_in = [own_in, sibling(own_in)]
    projected = [project_qkv(i, rows_in[i], gain_attn, w_qkv, tables, me.halves) for i in range(2)]
    normed_attn = [p[0] for p in projected]

    (own_up,) = after((upstream,), own_in)
    rows_up = gather_tokens(own_up)

    attended, other_attended, qkv, lse = attend([p[1] for p in projected], me.halves)
    inputs = fl(inputs_b)
    out_sums = chip_product(attended, other_attended, out_and_gains, sibling(out_and_gains))
    (out_sums,) = after((out_sums,), rows_up[0], stage_gate, stage_up)
    residual = inputs + scatter_z(out_sums)

    parts_gate = second_stage(stage_gate, "x")
    parts_up = second_stage(stage_up, "y")
    full_gate = place_rows(parts_gate, me.blocks["x"])
    full_up = place_rows(parts_up, me.blocks["y"])

    (residual,) = after((residual,), parts_gate[2], parts_up[2])
    unit_mlp, inverse_mlp = norm_parts(residual)
    normed_mlp = bf(unit_mlp * gain_mlp)
    own_mlp = gather_z(normed_mlp)
    up_held = after(rows_up, normed_mlp)
    grad_act = [project(r, w_down_t, 1024, jnp.float32) for r in up_held]
    (own_mlp,) = after((own_mlp,), full_gate, full_up, *grad_act)
    rows_mlp = [own_mlp, sibling(own_mlp)]
    steps = [mlp_step(r, full_gate, full_up, g) for r, g in zip(rows_mlp, grad_act)]
    activated, grad_gate_pre, grad_up_pre = zip(*steps)

    gate_up = list(zip(grad_gate_pre, grad_up_pre))
    mlp_sums = chip_sums(gate_up[0], gate_up[1], [full_gate, full_up])
    grad_normed_mlp = scatter_z(mlp_sums)

    grad_gate = WeightGradient(rows_mlp, grad_gate_pre, (0, 1024), "x", me)
    grad_up = WeightGradient(rows_mlp, grad_up_pre, (0, 1024), "y", me)
    grad_gate.piece(1, mlp_sums), grad_up.piece(1, mlp_sums)
    gate_1, up_1 = grad_gate.send(), grad_up.send()
    grad_down = weight_product(rows_up, after(activated, mlp_sums))
    share_down = fl(lax.psum_scatter(grad_down, plane, scatter_dimension=0, tiled=True))
    (grad_normed_mlp,) = after((grad_normed_mlp,), gate_1, up_1, grad_down)
    grad_residual = fl(upstream) + norm_backward(grad_normed_mlp, unit_mlp, inverse_mlp, gain_mlp)
    grad_residual_b = bf(grad_residual)

    own_gr = gather_z(grad_residual_b)
    made = grad_gate.piece(2, grad_residual_b), grad_up.piece(2, grad_residual_b)
    gate_2, up_2 = grad_gate.send(), grad_up.send()
    acts = after(activated, *made)
    down_own, down_other = (partial_sums([a], [w_down_t]) for a in acts)
    (own_gr,) = after((own_gr,), gate_2, up_2, down_own, down_other)
    rows_gr = [own_gr, sibling(own_gr)]
    (down_other,) = after((down_other,), own_gr)
    arrived = arrive_z(bf(fl(down_own) + fl(sibling(down_other))))

    grad_attended = [project(r, out_and_gains, 256, jnp.bfloat16) for r in rows_gr]
    grad_out = WeightGradient(rows_gr, [attended, other_attended], (0, 256), "y", me)
    out_1 = grad_out.piece(1, *grad_attended)
    gate_3, up_3 = grad_gate.piece(3, own_gr), grad_up.piece(3, own_gr)
    grad_attended = after(grad_attended, out_1, gate_3, up_3)
    grad_qkv, other_grad_qkv = attend_backward(qkv, lse, grad_attended, tables, me.halves)
    out_2 = grad_out.piece(2, grad_qkv)
    (arrived,) = after((arrived,), grad_qkv)
    layer_out = bf(residual + jnp.sum(fl(arrived), axis=0))
    attn_sums = chip_product(grad_qkv, other_grad_qkv, w_qkv, sibling(w_qkv))
    (attn_sums,) = after((attn_sums,), layer_out, grad_gate.send(), grad_up.send(), out_2)
    grad_normed_attn = scatter_z(attn_sums)

    d_qkv = after((grad_qkv, other_grad_qkv), attn_sums)
    parts_in = direct_pieces(normed_attn, d_qkv, (0, 384), "x", me)
    made = grad_gate.piece(0, attn_sums), grad_up.piece(0, attn_sums)
    out_3 = grad_out.piece(3, attn_sums)
    (grad_normed_attn,) = after((grad_normed_attn,), out_3, *made[0], *made[1], parts_in[-1])
    out_0 = grad_out.piece(0, grad_normed_attn)
    unit_attn, inverse_attn = norm_parts(inputs)
    grad_norm_attn = norm_backward(grad_normed_attn, unit_attn, inverse_attn, gain_attn)
    grad_tokens = bf(grad_residual + grad_norm_attn)
    share_gate, share_up = grad_gate.finish(grad_normed_attn), grad_up.finish(grad_normed_attn)
    share_qkv = direct_sums(after(parts_in, grad_normed_attn), "x", me)
    share_out = grad_out.finish()

    def gain_sum(*terms):
        return sum(jnp.sum(fl(w) * g, axis=1) for w, g in terms)

    gain_sums = jnp.stack(
        [gain_sum((part_attn[:, :384], share_qkv)), gain_sum((part_gate, share_gate), (part_up, share_up))]
    )
    gain_sums = gain_sums / fl(part_attn[:, 640:642].T)
    gain_sums = gain_sums + z_moved(gain_sums, 1) + z_moved(gain_sums, 2) + z_moved(gain_sums, 3)
    gain_sums = swapped(gain_sums) + swapped_across(gain_sums)

    share_attn = fl(swapped(bf(jnp.concatenate([share_qkv, share_out], axis=1))))
    return (
        swapped(layer_out),
        swapped(grad_tokens),
        share_attn[:, :256],
        share_attn[:, 256:320],
        share_attn[:, 320:384],
        share_attn[:, 384:].T,
        gain_sums[0],
        fl(swapped(bf(share_gate))),
        fl(swapped(bf(share_up))),
        fl(swapped(bf(share_down))).T,
        gain_sums[1],
    )


def solution(mesh):
    split = Mesh(mesh.devices.reshape(4, 2, 2, 2, 4), AXES)
    dp, tensor = ("x", "l", "c"), ("h", "z")
    both = P(AXES, None)
    weight, turned, vector = P(dp, tensor), P(tensor, dp), P(dp)
    in_specs = (
        both, vector, weight, weight, weight, turned, vector, weight, weight, turned, vector, both,
    )
    out_specs = (
        both, both, weight, weight, weight, turned, vector, weight, weight, turned, vector,
    )
    return jax.shard_map(on_device, mesh=split, in_specs=in_specs, out_specs=out_specs, check_vma=False)
```

```python
import functools
import itertools
import math

import jax
import jax.numpy as jnp
from jax import lax
from jax.experimental import pallas as pl
from jax.experimental.pallas import tpu as pltpu
from jax.sharding import Mesh, PartitionSpec as P

H = 32
KV = 8
DH = 64
SEQ_LEN = 1024
D = 2048
eps = 1e-05

SIZES = dict(x=4, l=2, c=2, h=2, z=4)
AXES = ("x", "l", "c", "h", "z")

SCALE = DH ** (-0.5)
SCALE2 = SCALE * math.log2(math.e)
VMEM_LIMIT = 14 * 1024 * 1024


def pairs(axes, move):
    def place(index):
        at = 0
        for a in axes:
            at = at * SIZES[a] + index[a]
        return at

    out = []
    for index in itertools.product(*[range(SIZES[a]) for a in axes]):
        here = dict(zip(axes, index))
        out.append((place(here), place(move(dict(here)))))
    return out


def to_swapped(d):
    d["c"], d["h"] = d["h"], d["c"]
    return d


def to_sibling(d):
    d["c"] = 1 - d["c"]
    return d


def along(axis):
    def move(d):
        step = 1 - 2 * d["c"]
        if axis == "y":
            y = (2 * d["h"] + d["l"] + step) % 4
            d["h"], d["l"] = y // 2, y % 2
        else:
            d[axis] = (d[axis] + step) % 4
        return d

    return move


RING_AXES = dict(x=("x", "c"), y=("l", "c", "h"))


def ring(value, axis):
    axes = RING_AXES[axis]
    return lax.ppermute(value, axes, pairs(axes, along(axis)))


def swapped(value):
    return lax.ppermute(value, ("c", "h"), pairs(("c", "h"), to_swapped))


def sibling(value):
    return lax.ppermute(value, ("c",), pairs(("c",), to_sibling))


def z_moved(value, step):
    def move(d):
        d["z"] = (d["z"] + step) % 4
        return d

    return lax.ppermute(value, ("z",), pairs(("z",), move))


def swapped_across(value):
    def move(d):
        c, h = d["c"], d["h"]
        d["h"], d["c"] = 1 - c, h
        return d

    return lax.ppermute(value, ("c", "h"), pairs(("c", "h"), move))


def after(values, *earlier):
    held = lax.optimization_barrier((tuple(values), tuple(earlier)))
    return held[0]


def dot(a, b, ca, cb):
    return lax.dot_general(a, b, (((ca,), (cb,)), ((), ())), preferred_element_type=jnp.float32)


def bf(v):
    return v.astype(jnp.bfloat16)


def fl(v):
    return v.astype(jnp.float32)


def sds(shape, dtype=jnp.bfloat16):
    return jax.ShapeDtypeStruct(shape, dtype)


def cost(flops):
    return pl.CostEstimate(flops=int(flops), bytes_accessed=1, transcendentals=0)


PARAMS = pltpu.CompilerParams(vmem_limit_bytes=VMEM_LIMIT)
ANY = pl.BlockSpec(memory_space=pl.ANY)
WHOLE = pl.BlockSpec(memory_space=pltpu.VMEM)


class Place:
    def __init__(self):
        self.c = lax.axis_index("c")
        self.x = lax.axis_index("x")
        self.h = lax.axis_index("h")
        self.y = 2 * self.h + lax.axis_index("l")
        self.step = 1 - 2 * self.c
        self.halves = jnp.stack([512 * self.c, 512 * (1 - self.c)]).astype(jnp.int32)
        self.blocks = {}
        for first, second in (("x", "y"), ("y", "x")):
            out = []
            for k2 in range(4):
                for k1 in range(4):
                    a, b = self.source(first, k1), self.source(second, k2)
                    out.append(4 * a + b if first == "x" else 4 * b + a)
            self.blocks[first] = jnp.stack(out).astype(jnp.int32)

    def source(self, axis, k):
        at = lax.rem(dict(x=self.x, y=self.y)[axis] - self.step * k + 4, 4)
        if axis == "y":
            at = 2 * lax.rem(at, 2) + lax.div(at, 2)
        return at


SMEM = pl.BlockSpec(memory_space=pltpu.SMEM)


def place_rows(parts, blocks, columns=None):
    low, high = columns or (0, parts[0].shape[1])
    n = high - low

    def kernel(blocks_ref, p0, p1, p2, p3, out_ref, sems):
        copies = []
        for k2, part in enumerate((p0, p1, p2, p3)):
            for k1 in range(4):
                at = pl.multiple_of(blocks_ref[4 * k2 + k1] * 128, 128)
                copies.append(
                    pltpu.make_async_copy(
                        part.at[pl.ds(128 * k1, 128), pl.ds(low, n)],
                        out_ref.at[pl.ds(at, 128)],
                        sems.at[4 * k2 + k1],
                    )
                )
        for copy in copies:
            copy.start()
        for copy in copies:
            copy.wait()

    return pl.pallas_call(
        kernel,
        out_shape=sds((D, n)),
        in_specs=[SMEM] + [ANY] * 4,
        out_specs=WHOLE,
        scratch_shapes=[pltpu.SemaphoreType.DMA((16,))],
        compiler_params=PARAMS,
        cost_estimate=cost(1),
        name="place_rows",
    )(blocks, *parts)


def stepped(value, axis, steps):
    def move(d):
        for _ in range(steps):
            d = along(axis)(d)
        return d

    axes = RING_AXES[axis]
    return lax.ppermute(value, axes, pairs(axes, move))


def first_stage(block, first, direct):
    parts = [block]
    for k in range(1, 4):
        parts.append(stepped(block, first, k) if direct else ring(parts[-1], first))
    return jnp.concatenate(parts, axis=0)


def second_stage(stage, first, holds=(None, None, None)):
    second = "y" if first == "x" else "x"
    parts = [stage]
    for hold in holds:
        part = parts[-1] if hold is None else after((parts[-1],), hold)[0]
        parts.append(ring(part, second))
    return parts


def gather_rows(block, first, me, direct=False):
    parts = second_stage(first_stage(block, first, direct), first)
    return place_rows(parts, me.blocks[first]), parts


def call(kernel, name, outs, args, flops, scratch=()):
    return pl.pallas_call(
        kernel,
        out_shape=outs,
        in_specs=[SMEM if a.dtype == jnp.int32 else WHOLE for a in args],
        out_specs=[WHOLE] * len(outs),
        scratch_shapes=list(scratch),
        compiler_params=PARAMS,
        cost_estimate=cost(flops),
        name=name,
    )(*args)


def weight_piece(rows, right, columns, at, first, received, last=None):
    low, high = columns
    n = high - low
    scalars = at.reshape(1).astype(jnp.int32)
    if last is not None:
        scalars = jnp.concatenate([scalars, last])
    args = [scalars, *rows, *right] + ([] if received is None else [received])

    def kernel(*refs):
        at = refs[0][0]
        row_refs, right_refs = refs[1 : 1 + len(rows)], refs[1 + len(rows) : 1 + len(rows) + len(right)]
        left = []
        for j in range(4):
            block = 4 * at + j if first == "x" else 4 * j + at
            lanes = pl.ds(pl.multiple_of(block * 128, 128), 128)
            left.append(jnp.concatenate([r[:, lanes] for r in row_refs], axis=0))
        left = jnp.concatenate(left, axis=1)
        for j in range(low, high, 256):
            end = min(j + 256, high)
            total = dot(left, jnp.concatenate([r[:, j:end] for r in right_refs], axis=0), 0, 0)
            here = slice(j - low, end - low)
            if received is not None:
                total = total + fl(refs[len(args) - 1][:, here])
            refs[len(args) if last is None else -1][:, here] = bf(total)
        if last is not None:
            for k in range(4):
                rows_at = pl.ds(pl.multiple_of(refs[0][1 + k] * 128, 128), 128)
                refs[len(args) + k][...] = refs[-1][rows_at, :]

    flops = 2 * 512 * SEQ_LEN * n
    if last is None:
        return call(kernel, "weight_piece", [sds((512, n))], args, flops)[0]
    scratch = [pltpu.VMEM((512, n), jnp.bfloat16)]
    return call(kernel, "weight_piece", [sds((128, n))] * 4, args, flops, scratch)


class WeightGradient:
    def __init__(self, rows, right, columns, first, me):
        self.args = (rows, right, columns)
        self.first, self.second = first, "y" if first == "x" else "x"
        self.me = me
        self.total = self.received = None

    def send(self):
        if self.received is None:
            self.received = ring(self.total, self.first)
        return self.received

    def piece(self, k, *holds):
        rows, right, columns = self.args
        at = self.me.source(self.first, k)
        received = None if k == 1 else self.send()
        self.received = None
        if holds and received is None:
            right = after(right, *holds)
        elif holds:
            (received,) = after((received,), *holds)
        last = None
        if k == 0:
            last = jnp.stack([self.me.source(self.second, i) for i in range(4)]).astype(jnp.int32)
        self.total = weight_piece(rows, right, columns, at, self.first, received, last)
        return self.total

    def finish(self, *holds):
        if holds:
            self.total = after(self.total, *holds)
        total = fl(self.total[1])
        for k in (2, 3, 0):
            total = fl(ring(bf(total), self.second)) + fl(self.total[k])
        return total


def sum_blocks(parts, order):
    n = parts[0].shape[1]

    def kernel(order_ref, p0, p1, p2, p3, *out_refs):
        for k in range(4):
            at = pl.ds(pl.multiple_of(order_ref[k] * 128, 128), 128)
            out_refs[k][...] = bf(fl(p0[at, :]) + fl(p1[at, :]) + fl(p2[at, :]) + fl(p3[at, :]))

    return call(kernel, "sum_blocks", [sds((128, n))] * 4, [order, *parts], 0)


def direct_pieces(rows, right, columns, first, me):
    parts = []
    for k in (2, 1, 3, 0):
        made = weight_piece(rows, right, columns, me.source(first, k), first, None)
        parts.append(stepped(made, first, 4 - k) if k else made)
    return parts


def direct_sums(parts, first, me):
    second = "y" if first == "x" else "x"
    order = jnp.stack([me.source(second, i) for i in range(4)]).astype(jnp.int32)
    blocks = sum_blocks(parts, order)
    total = fl(blocks[0])
    for k in (2, 1, 3):
        total = total + fl(stepped(blocks[k], second, 4 - k))
    return total


def gather_z(block):
    wide = jnp.broadcast_to(block[None], (4,) + block.shape)
    return lax.all_to_all(wide, "z", split_axis=0, concat_axis=0, tiled=True).reshape(512, block.shape[1])


def gather_tokens(block):
    own = gather_z(block)
    return own, sibling(own)


def arrive_z(sums):
    parts = sums.reshape(4, 128, sums.shape[1])
    return lax.all_to_all(parts, "z", split_axis=0, concat_axis=0, tiled=True)


def scatter_z(sums):
    return jnp.sum(fl(arrive_z(sums)), axis=0)


def partial_sums(pieces, weights):
    count = len(pieces)

    def kernel(*refs):
        for j in range(0, D, 512):
            total = None
            for i in range(count):
                one = dot(refs[i][...], refs[count + i][j : j + 512, :], 1, 1)
                total = one if total is None else total + one
            refs[-1][:, j : j + 512] = bf(total)

    depth = sum(p.shape[1] for p in pieces)
    return call(kernel, "partial_sums", [sds((512, D))], [*pieces, *weights], 2 * 512 * depth * D)[0]


def chip_sums(own, other, weights):
    received = sibling(partial_sums(other, weights))
    return bf(fl(partial_sums(own, weights)) + fl(received))


def chip_product(own, other, weight, sibling_weight):
    received = sibling(other)
    m = own.shape[1]

    def kernel(a_ref, b_ref, v_ref, w_ref, out_ref):
        for j in range(0, D, 512):
            here = slice(j, j + 512)
            total = dot(a_ref[...], v_ref[here, :m], 1, 1) + dot(b_ref[...], w_ref[here, :m], 1, 1)
            out_ref[:, here] = bf(total)

    args = [own, received, weight, sibling_weight]
    return call(kernel, "chip_product", [sds((512, D))], args, 4 * 512 * m * D)[0]


def project(rows, weights, dtype, width=None):
    width = width or weights[0].shape[1]
    n = width * len(weights)

    def kernel(rows_ref, *refs):
        for i, w_ref in enumerate(refs[:-1]):
            for j in range(0, width, 256):
                product = dot(rows_ref[...], w_ref[:, j : j + 256], 1, 0)
                refs[-1][:, i * width + j : i * width + j + 256] = product.astype(dtype)

    return call(kernel, "project", [sds((512, n), dtype)], [rows, *weights], 2 * 512 * D * n)[0]


def down_products(rows, weights):
    def kernel(rows_ref, w0, w1, out_ref):
        for j in range(0, D, 512):
            here = slice(j, j + 512)
            total = dot(rows_ref[:, :512], w0[here, :], 1, 1) + dot(rows_ref[:, 512:], w1[here, :], 1, 1)
            out_ref[:, here] = bf(total)

    return call(kernel, "down_products", [sds((512, D))], [rows, *weights], 2 * 512 * 1024 * D)[0]


def rope(u, cosine, sine):
    lane = lax.broadcasted_iota(jnp.int32, u.shape, 1)
    turned = jnp.where(lane % DH < DH // 2, pltpu.roll(u, 96, 1), pltpu.roll(u, 32, 1))
    return u * cosine + turned * sine


def rope_three(u, cosine, sine):
    lane = lax.broadcasted_iota(jnp.int32, cosine.shape, 1)
    last = u[:, 256:]
    return jnp.concatenate(
        [
            rope(u[:, :128], cosine, sine),
            rope(u[:, 128:256], cosine, sine),
            jnp.where(lane < DH, rope(last, cosine, sine), last),
        ],
        axis=1,
    )


def half_at(halves_ref, i):
    return pl.ds(pl.multiple_of(halves_ref[i], 512), 512)


def project_qkv(i, rows, gain, weight, tables, halves):
    def kernel(halves_ref, x_ref, gain_ref, w_ref, cos_ref, sin_ref, normed_ref, out_ref):
        x = fl(x_ref[...])
        inverse = lax.rsqrt(jnp.mean(x * x, axis=1, keepdims=True) + eps)
        normed_ref[...] = bf(x * inverse * gain_ref[...])
        here = half_at(halves_ref, i)
        product = dot(normed_ref[...], w_ref[...], 1, 0)
        out_ref[...] = bf(rope_three(product, cos_ref[here, :], sin_ref[here, :]))

    args = [halves, rows, gain, weight, *tables]
    return call(kernel, "project_qkv", [sds((512, D)), sds((512, 384))], args, 2 * 512 * D * 384)


def scores_t(keys, query, q_at):
    s = dot(keys, query, 1, 1)
    key = lax.broadcasted_iota(jnp.int32, (256, 256), 0)
    column = lax.broadcasted_iota(jnp.int32, (256, 256), 1)
    diagonal = jnp.where(key <= column, s[q_at:], -1e30)
    return diagonal if q_at == 0 else jnp.concatenate([s[:q_at], diagonal], axis=0)


def attend(qkv, halves):
    def kernel(halves_ref, q0, q1, own_ref, other_ref, nat_ref, lse_ref, att_ref):
        nat_ref[half_at(halves_ref, 0), :] = q0[...]
        nat_ref[half_at(halves_ref, 1), :] = q1[...]
        kv = nat_ref[:, 256:]
        keys = kv[:, :DH]
        values_t = kv.T[DH:]
        lse_ref[...] = jnp.zeros_like(lse_ref)
        for q_at in range(0, SEQ_LEN, 256):
            end = q_at + 256
            for pair in range(2):
                two = nat_ref[q_at:end, 128 * pair : 128 * pair + 128]
                outs = []
                for i in range(2):
                    s = scores_t(keys[:end], two[:, DH * i : DH * i + DH], q_at)
                    top = jnp.max(s, axis=0, keepdims=True)
                    p = jnp.exp2((s - top) * SCALE2)
                    total = jnp.sum(p, axis=0, keepdims=True)
                    outs.append(dot(values_t[:, :end], bf(p), 1, 0) / total)
                    g = 2 * pair + i
                    lse_ref[g : g + 1, q_at:end] = top * SCALE2 + jnp.log2(total)
                att_ref[q_at:end, 128 * pair : 128 * pair + 128] = bf(jnp.concatenate(outs, axis=0).T)
        own_ref[...] = att_ref[half_at(halves_ref, 0), :]
        other_ref[...] = att_ref[half_at(halves_ref, 1), :]

    outs = [sds((512, 256)), sds((512, 256)), sds((SEQ_LEN, 384)), sds((8, SEQ_LEN), jnp.float32)]
    scratch = [pltpu.VMEM((SEQ_LEN, 256), jnp.bfloat16)]
    return call(kernel, "attend", outs, [halves, *qkv], 3e9, scratch)


def attend_backward(qkv, lse, grad_out, tables, halves):
    def kernel(halves_ref, nat_ref, lse_ref, g0, g1, cos_ref, sin_ref, own_ref, other_ref, go_nat, kv_sum, d_nat):
        go_nat[half_at(halves_ref, 0), :] = g0[...]
        go_nat[half_at(halves_ref, 1), :] = g1[...]
        kv = nat_ref[:, 256:]
        keys = kv[:, :DH]
        values = kv[:, DH:]
        keys_t = kv.T[:DH]
        kv_sum[...] = jnp.zeros_like(kv_sum)
        for q_at in range(0, SEQ_LEN, 256):
            end = q_at + 256
            cosine = cos_ref[q_at:end, :]
            sine = -sin_ref[q_at:end, :]
            for pair in range(2):
                lanes = slice(128 * pair, 128 * pair + 128)
                two = nat_ref[q_at:end, lanes]
                two_grad = go_nat[q_at:end, lanes]
                outs = []
                for i in range(2):
                    query = two[:, DH * i : DH * i + DH]
                    grad = two_grad[:, DH * i : DH * i + DH]
                    g = 2 * pair + i
                    s = scores_t(keys[:end], query, q_at)
                    p = jnp.exp2(s * SCALE2 - lse_ref[g : g + 1, q_at:end])
                    dp = dot(values[:end], grad, 1, 1)
                    delta = jnp.sum(dp * p, axis=0, keepdims=True)
                    ds = bf(p * (dp - delta))
                    kv_sum[:end, :] += jnp.concatenate(
                        [dot(ds, query, 1, 0), dot(bf(p), grad, 1, 0)], axis=1
                    )
                    outs.append(dot(keys_t[:, :end], ds, 1, 0))
                d_query = jnp.concatenate(outs, axis=0).T * SCALE
                d_nat[q_at:end, lanes] = bf(rope(d_query, cosine, sine))
        lane = lax.broadcasted_iota(jnp.int32, (SEQ_LEN, 128), 1)
        total = kv_sum[...]
        turned = rope(total * SCALE, cos_ref[...], -sin_ref[...])
        d_nat[:, 256:] = bf(jnp.where(lane < DH, turned, total))
        own_ref[...] = d_nat[half_at(halves_ref, 0), :]
        other_ref[...] = d_nat[half_at(halves_ref, 1), :]

    scratch = [
        pltpu.VMEM((SEQ_LEN, 256), jnp.bfloat16),
        pltpu.VMEM((SEQ_LEN, 128), jnp.float32),
        pltpu.VMEM((SEQ_LEN, 384), jnp.bfloat16),
    ]
    args = [halves, qkv, lse, *grad_out, *tables]
    return call(kernel, "attend_backward", [sds((512, 384))] * 2, args, 6e9, scratch)


def mlp_step(rows, w_gate, w_up, grad_act):
    width = w_gate.shape[1]

    def kernel(rows_ref, g_ref, u_ref, ga_ref, act_ref, gg_ref, gu_ref):
        for j in range(0, width, 256):
            here = slice(j, j + 256)
            gate = dot(rows_ref[...], g_ref[:, here], 1, 0)
            up = dot(rows_ref[...], u_ref[:, here], 1, 0)
            sig = jax.nn.sigmoid(gate)
            silu = gate * sig
            ga = ga_ref[:, here]
            act_ref[:, here] = bf(silu * up)
            gg_ref[:, here] = bf(ga * up * sig * (1.0 + gate * (1.0 - sig)))
            gu_ref[:, here] = bf(ga * silu)

    args = [rows, w_gate, w_up, grad_act]
    return call(kernel, "mlp_step", [sds((512, width))] * 3, args, 4 * 512 * D * width)


def frequencies(head_size):
    pair_index = jnp.arange(head_size // 2).astype(jnp.float32)
    base_freq = 500000.0 ** (-2.0 * pair_index / head_size)
    wavelen = 2.0 * jnp.pi / base_freq
    smooth = (8192.0 / wavelen - 1.0) / 3.0
    blended = (1.0 - smooth) * base_freq / 32.0 + smooth * base_freq
    return jnp.where(
        wavelen < 2048.0, base_freq, jnp.where(wavelen > 8192.0, base_freq / 32.0, blended)
    )


def norm_parts(values):
    inverse = lax.rsqrt(jnp.mean(values * values, axis=-1, keepdims=True) + eps)
    return (values * inverse, inverse)


def norm_backward(grad_normed, unit_rows, inverse, gain_rows):
    scaled = grad_normed * gain_rows
    return inverse * (scaled - unit_rows * jnp.mean(scaled * unit_rows, axis=-1, keepdims=True))


def on_device(
    tokens, positions, w_query, w_key, w_value, w_out, attn_gain, w_gate, w_up, w_down, mlp_gain, cotangent
):
    me = Place()
    inputs_b = swapped(tokens)
    gains = jnp.pad(jnp.stack([attn_gain, mlp_gain], axis=1), ((0, 0), (0, 126)))
    part_attn = swapped(jnp.concatenate([w_query, w_key, w_value, w_out.T, gains], axis=1))
    seq_positions = jnp.where(me.h == me.c, positions, sibling(positions))

    part_attn, inputs_b = lax.optimization_barrier((part_attn, inputs_b))
    own_in = gather_z(inputs_b)
    w_gate, w_up, w_down = after((w_gate, w_up, w_down), inputs_b)
    down_rows = w_down.T
    part_a = swapped(jnp.concatenate([w_gate, down_rows[:, :512]], axis=1))
    part_b = swapped(jnp.concatenate([w_up, down_rows[:, 512:]], axis=1))
    w_qkv, parts_qkv = gather_rows(part_attn[:, :384], "x", me)
    out_and_gains, parts_out = gather_rows(part_attn[:, 384:], "y", me)
    (cotangent,) = after((cotangent,), parts_qkv[0], parts_out[0])
    upstream = swapped(cotangent)

    freq = jnp.tile(frequencies(DH), 4)
    angles = seq_positions.astype(jnp.float32)[:, None] * freq[None, :]
    sign = jnp.where(jnp.arange(128) % DH < DH // 2, -1.0, 1.0)
    tables = (jnp.cos(angles), jnp.sin(angles) * sign[None, :])
    pick = bf(jnp.arange(128)[None, :] == jnp.arange(8)[:, None])
    gain_rows = dot(pick, out_and_gains[:, 256:], 1, 1)
    gain_attn, gain_mlp = gain_rows[:1], gain_rows[1:2]

    part_a, part_b = after((part_a, part_b), parts_qkv[2], parts_out[2])
    stage_a, stage_b = first_stage(part_a, "x", False), first_stage(part_b, "y", False)

    (own_in,) = after((own_in,), upstream)
    rows_in = [own_in, sibling(own_in)]
    projected = [project_qkv(i, rows_in[i], gain_attn, w_qkv, tables, me.halves) for i in range(2)]
    normed_attn = [p[0] for p in projected]

    (own_up,) = after((upstream,), own_in)
    rows_up = gather_tokens(own_up)

    attended, other_attended, qkv, lse = attend([p[1] for p in projected], me.halves)
    inputs = fl(inputs_b)
    out_sums = chip_product(attended, other_attended, out_and_gains, sibling(out_and_gains))
    (out_sums,) = after((out_sums,), rows_up[0], stage_a, stage_b)
    residual = inputs + scatter_z(out_sums)

    parts_a = second_stage(stage_a, "x")
    parts_b = second_stage(stage_b, "y")
    full_gate = place_rows(parts_a, me.blocks["x"], (0, 1024))
    full_up = place_rows(parts_b, me.blocks["y"], (0, 1024))
    full_down = [
        place_rows(parts_a, me.blocks["x"], (1024, 1536)),
        place_rows(parts_b, me.blocks["y"], (1024, 1536)),
    ]

    (residual,) = after((residual,), parts_a[1], parts_b[1])
    unit_mlp, inverse_mlp = norm_parts(residual)
    normed_mlp = bf(unit_mlp * gain_mlp)
    own_mlp = gather_z(normed_mlp)
    up_held = after(rows_up, normed_mlp)
    grad_act = [project(r, full_down, jnp.float32) for r in up_held]
    (own_mlp,) = after((own_mlp,), parts_a[2], parts_b[2])
    rows_mlp = [own_mlp, sibling(own_mlp)]
    steps = [mlp_step(r, full_gate, full_up, g) for r, g in zip(rows_mlp, grad_act)]
    activated, grad_gate_pre, grad_up_pre = zip(*steps)

    gate_up = list(zip(grad_gate_pre, grad_up_pre))
    mlp_sums = chip_sums(gate_up[0], gate_up[1], [full_gate, full_up])
    grad_normed_mlp = scatter_z(mlp_sums)

    grad_gate = WeightGradient(rows_mlp, grad_gate_pre, (0, 1024), "x", me)
    grad_up = WeightGradient(rows_mlp, grad_up_pre, (0, 1024), "y", me)
    grad_gate.piece(1, mlp_sums), grad_up.piece(1, mlp_sums)
    grad_down_a = WeightGradient(rows_up, activated, (0, 512), "x", me)
    grad_down_b = WeightGradient(rows_up, activated, (512, 1024), "y", me)
    grad_down_a.piece(1, mlp_sums), grad_down_b.piece(1, mlp_sums)
    sent = [g.send() for g in (grad_gate, grad_up, grad_down_a, grad_down_b)]
    (grad_normed_mlp,) = after((grad_normed_mlp,), *sent)
    grad_residual = fl(upstream) + norm_backward(grad_normed_mlp, unit_mlp, inverse_mlp, gain_mlp)
    grad_residual_b = bf(grad_residual)

    own_gr = gather_z(grad_residual_b)
    weights = (grad_gate, grad_up, grad_down_a, grad_down_b)
    made = [g.piece(2, grad_residual_b) for g in weights]
    sent = [g.send() for g in weights]
    acts = after(activated, *made)
    down_own, down_other = (down_products(a, full_down) for a in acts)
    (own_gr,) = after((own_gr,), *sent, down_own, down_other)
    rows_gr = [own_gr, sibling(own_gr)]
    (down_other,) = after((down_other,), own_gr)
    arrived = arrive_z(bf(fl(down_own) + fl(sibling(down_other))))

    grad_attended = [project(r, [out_and_gains], jnp.bfloat16, 256) for r in rows_gr]
    grad_out = WeightGradient(rows_gr, [attended, other_attended], (0, 256), "y", me)
    out_1 = grad_out.piece(1, *grad_attended)
    made = [g.piece(3, own_gr) for g in weights]
    grad_attended = after(grad_attended, out_1, *made)
    grad_qkv, other_grad_qkv = attend_backward(qkv, lse, grad_attended, tables, me.halves)
    out_2 = grad_out.piece(2, grad_qkv)
    (arrived,) = after((arrived,), grad_qkv)
    layer_out = bf(residual + jnp.sum(fl(arrived), axis=0))
    attn_sums = chip_product(grad_qkv, other_grad_qkv, w_qkv, sibling(w_qkv))
    (attn_sums,) = after((attn_sums,), layer_out, *[g.send() for g in weights], out_2)
    grad_normed_attn = scatter_z(attn_sums)

    d_qkv = after((grad_qkv, other_grad_qkv), attn_sums)
    parts_in = direct_pieces(normed_attn, d_qkv, (0, 384), "x", me)
    made = [block for g in weights for block in g.piece(0, attn_sums)]
    out_3 = grad_out.piece(3, attn_sums)
    (grad_normed_attn,) = after((grad_normed_attn,), out_3, *made, parts_in[-1])
    out_0 = grad_out.piece(0, grad_normed_attn)
    unit_attn, inverse_attn = norm_parts(inputs)
    grad_norm_attn = norm_backward(grad_normed_attn, unit_attn, inverse_attn, gain_attn)
    grad_tokens = bf(grad_residual + grad_norm_attn)
    share_gate, share_up, *share_down = [g.finish(grad_normed_attn) for g in weights]
    share_qkv = direct_sums(after(parts_in, grad_normed_attn), "x", me)
    share_out = grad_out.finish()

    def gain_sum(*terms):
        return sum(jnp.sum(fl(w) * g, axis=1) for w, g in terms)

    gain_sums = jnp.stack(
        [gain_sum((part_attn[:, :384], share_qkv)), gain_sum((part_a[:, :1024], share_gate), (part_b[:, :1024], share_up))]
    )
    gain_sums = gain_sums / fl(part_attn[:, 640:642].T)
    gain_sums = gain_sums + z_moved(gain_sums, 1) + z_moved(gain_sums, 2) + z_moved(gain_sums, 3)
    gain_sums = swapped(gain_sums) + swapped_across(gain_sums)

    share_attn = fl(swapped(bf(jnp.concatenate([share_qkv, share_out], axis=1))))
    return (
        swapped(layer_out),
        swapped(grad_tokens),
        share_attn[:, :256],
        share_attn[:, 256:320],
        share_attn[:, 320:384],
        share_attn[:, 384:].T,
        gain_sums[0],
        fl(swapped(bf(share_gate))),
        fl(swapped(bf(share_up))),
        fl(swapped(bf(jnp.concatenate(share_down, axis=1)))).T,
        gain_sums[1],
    )


def solution(mesh):
    split = Mesh(mesh.devices.reshape(4, 2, 2, 2, 4), AXES)
    dp, tensor = ("x", "l", "c"), ("h", "z")
    both = P(AXES, None)
    weight, turned, vector = P(dp, tensor), P(tensor, dp), P(dp)
    in_specs = (
        both, vector, weight, weight, weight, turned, vector, weight, weight, turned, vector, both,
    )
    out_specs = (
        both, both, weight, weight, weight, turned, vector, weight, weight, turned, vector,
    )
    return jax.shard_map(on_device, mesh=split, in_specs=in_specs, out_specs=out_specs, check_vma=False)
```

```python
import functools
import itertools
import math

import jax
import jax.numpy as jnp
from jax import lax
from jax.experimental import pallas as pl
from jax.experimental.pallas import tpu as pltpu
from jax.sharding import Mesh, PartitionSpec as P

H = 32
KV = 8
DH = 64
SEQ_LEN = 1024
D = 2048
eps = 1e-05

SIZES = dict(x=4, l=2, c=2, h=2, z=4)
AXES = ("x", "l", "c", "h", "z")

SCALE = DH ** (-0.5)
SCALE2 = SCALE * math.log2(math.e)
VMEM_LIMIT = 14 * 1024 * 1024


def pairs(axes, move):
    def place(index):
        at = 0
        for a in axes:
            at = at * SIZES[a] + index[a]
        return at

    out = []
    for index in itertools.product(*[range(SIZES[a]) for a in axes]):
        here = dict(zip(axes, index))
        out.append((place(here), place(move(dict(here)))))
    return out


def to_swapped(d):
    d["c"], d["h"] = d["h"], d["c"]
    return d


def to_sibling(d):
    d["c"] = 1 - d["c"]
    return d


def along(axis):
    def move(d):
        step = 1 - 2 * d["c"]
        if axis == "y":
            y = (2 * d["h"] + d["l"] + step) % 4
            d["h"], d["l"] = y // 2, y % 2
        else:
            d[axis] = (d[axis] + step) % 4
        return d

    return move


RING_AXES = dict(x=("x", "c"), y=("l", "c", "h"))


def ring(value, axis):
    axes = RING_AXES[axis]
    return lax.ppermute(value, axes, pairs(axes, along(axis)))


def swapped(value):
    return lax.ppermute(value, ("c", "h"), pairs(("c", "h"), to_swapped))


def sibling(value):
    return lax.ppermute(value, ("c",), pairs(("c",), to_sibling))


def z_moved(value, step):
    def move(d):
        d["z"] = (d["z"] + step) % 4
        return d

    return lax.ppermute(value, ("z",), pairs(("z",), move))


def swapped_across(value):
    def move(d):
        c, h = d["c"], d["h"]
        d["h"], d["c"] = 1 - c, h
        return d

    return lax.ppermute(value, ("c", "h"), pairs(("c", "h"), move))


def after(values, *earlier):
    held = lax.optimization_barrier((tuple(values), tuple(earlier)))
    return held[0]


def dot(a, b, ca, cb):
    return lax.dot_general(a, b, (((ca,), (cb,)), ((), ())), preferred_element_type=jnp.float32)


def bf(v):
    return v.astype(jnp.bfloat16)


def fl(v):
    return v.astype(jnp.float32)


def sds(shape, dtype=jnp.bfloat16):
    return jax.ShapeDtypeStruct(shape, dtype)


def cost(flops):
    return pl.CostEstimate(flops=int(flops), bytes_accessed=1, transcendentals=0)


PARAMS = pltpu.CompilerParams(vmem_limit_bytes=VMEM_LIMIT)
ANY = pl.BlockSpec(memory_space=pl.ANY)
WHOLE = pl.BlockSpec(memory_space=pltpu.VMEM)


class Place:
    def __init__(self):
        self.c = lax.axis_index("c")
        self.x = lax.axis_index("x")
        self.h = lax.axis_index("h")
        self.y = 2 * self.h + lax.axis_index("l")
        self.step = 1 - 2 * self.c
        self.halves = jnp.stack([512 * self.c, 512 * (1 - self.c)]).astype(jnp.int32)
        self.blocks = {}
        for first, second in (("x", "y"), ("y", "x")):
            out = []
            for k2 in range(4):
                for k1 in range(4):
                    a, b = self.source(first, k1), self.source(second, k2)
                    out.append(4 * a + b if first == "x" else 4 * b + a)
            self.blocks[first] = jnp.stack(out).astype(jnp.int32)

    def source(self, axis, k):
        at = lax.rem(dict(x=self.x, y=self.y)[axis] - self.step * k + 4, 4)
        if axis == "y":
            at = 2 * lax.rem(at, 2) + lax.div(at, 2)
        return at


SMEM = pl.BlockSpec(memory_space=pltpu.SMEM)


def place_rows(parts, blocks, columns=None):
    low, high = columns or (0, parts[0].shape[1])
    n = high - low

    def kernel(blocks_ref, p0, p1, p2, p3, out_ref, sems):
        copies = []
        for k2, part in enumerate((p0, p1, p2, p3)):
            for k1 in range(4):
                at = pl.multiple_of(blocks_ref[4 * k2 + k1] * 128, 128)
                copies.append(
                    pltpu.make_async_copy(
                        part.at[pl.ds(128 * k1, 128), pl.ds(low, n)],
                        out_ref.at[pl.ds(at, 128)],
                        sems.at[4 * k2 + k1],
                    )
                )
        for copy in copies:
            copy.start()
        for copy in copies:
            copy.wait()

    return pl.pallas_call(
        kernel,
        out_shape=sds((D, n)),
        in_specs=[SMEM] + [ANY] * 4,
        out_specs=WHOLE,
        scratch_shapes=[pltpu.SemaphoreType.DMA((16,))],
        compiler_params=PARAMS,
        cost_estimate=cost(1),
        name="place_rows",
    )(blocks, *parts)


def stepped(value, axis, steps):
    def move(d):
        for _ in range(steps):
            d = along(axis)(d)
        return d

    axes = RING_AXES[axis]
    return lax.ppermute(value, axes, pairs(axes, move))


def first_stage(block, first, direct):
    parts = [block]
    for k in range(1, 4):
        parts.append(stepped(block, first, k) if direct else ring(parts[-1], first))
    return jnp.concatenate(parts, axis=0)


def second_stage(stage, first, holds=(None, None, None)):
    second = "y" if first == "x" else "x"
    parts = [stage]
    for hold in holds:
        part = parts[-1] if hold is None else after((parts[-1],), hold)[0]
        parts.append(ring(part, second))
    return parts


def call(kernel, name, outs, args, flops, scratch=()):
    return pl.pallas_call(
        kernel,
        out_shape=outs,
        in_specs=[SMEM if a.dtype == jnp.int32 else WHOLE for a in args],
        out_specs=[WHOLE] * len(outs),
        scratch_shapes=list(scratch),
        compiler_params=PARAMS,
        cost_estimate=cost(flops),
        name=name,
    )(*args)


def weight_piece(terms, at, first, received=None, last=None):
    tile = 256 if all((high - low) % 256 == 0 for _, _, low, high in terms) else 384
    starts = [0]
    for _, _, low, high in terms:
        starts.append(starts[-1] + (high - low) // tile)
    n = starts[-1] * tile
    scalars = at.reshape(1).astype(jnp.int32)
    if last is not None:
        scalars = jnp.concatenate([scalars, last])

    def column(j):
        if first == "x":
            return pl.BlockSpec((512, 128), lambda i, s: (0, 4 * s[0] + j))
        return pl.BlockSpec((512, 128), lambda i, s: (0, 4 * j + s[0]))

    def right_tile(t):
        _, _, low, _ = terms[t]
        here, end = starts[t], starts[t + 1] - 1
        return pl.BlockSpec((512, tile), lambda i, s: (0, low // tile + jnp.clip(i, here, end) - here))

    args, specs = [], []
    for t, (rows, right, _, _) in enumerate(terms):
        for r in rows:
            args += [r] * 4
            specs += [column(j) for j in range(4)]
        args += list(right)
        specs += [right_tile(t)] * 2
    moving = pl.BlockSpec((512, tile), lambda i, s: (0, i))
    if received is not None:
        args.append(received)
        specs.append(moving)
    count = len(terms)

    def kernel(order_ref, *refs):
        left_refs = refs[len(refs) - count :]
        out_refs = refs[len(args) : len(refs) - count - (last is not None)]
        for t in range(count):
            at_t = 10 * t
            i = pl.program_id(0)

            @pl.when(i == starts[t])
            def _(at_t=at_t, t=t):
                halves = [
                    jnp.concatenate([r[...] for r in refs[at_t + 4 * u : at_t + 4 * u + 4]], axis=1) for u in range(2)
                ]
                left_refs[t][...] = jnp.concatenate(halves, axis=0).T

            @pl.when((i >= starts[t]) & (i < starts[t + 1]))
            def _(at_t=at_t, t=t):
                total = dot(left_refs[t][:, :512], refs[at_t + 8][...], 1, 0)
                total = total + dot(left_refs[t][:, 512:], refs[at_t + 9][...], 1, 0)
                if received is not None:
                    total = total + fl(refs[len(args) - 1][...])
                if last is None:
                    out_refs[0][...] = bf(total)
                else:
                    whole = refs[len(refs) - count - 1]
                    whole[...] = bf(total)
                    for k in range(4):
                        rows_at = pl.ds(pl.multiple_of(order_ref[1 + k] * 128, 128), 128)
                        out_refs[k][...] = whole[rows_at, :]

    scratch = [] if last is None else [pltpu.VMEM((512, tile), jnp.bfloat16)]
    scratch += [pltpu.VMEM((512, SEQ_LEN), jnp.bfloat16)] * count
    out = pl.pallas_call(
        kernel,
        grid_spec=pltpu.PrefetchScalarGridSpec(
            num_scalar_prefetch=1,
            grid=(n // tile,),
            in_specs=specs,
            out_specs=[moving] if last is None else [pl.BlockSpec((128, tile), lambda i, s: (0, i))] * 4,
            scratch_shapes=scratch,
        ),
        out_shape=[sds((512, n))] if last is None else [sds((128, n))] * 4,
        compiler_params=PARAMS,
        cost_estimate=cost(2 * 512 * SEQ_LEN * n),
        name="weight_piece",
    )(scalars, *args)
    return out[0] if last is None else out


class WeightGradient:
    def __init__(self, terms, first, me):
        self.terms = terms
        self.first, self.second = first, "y" if first == "x" else "x"
        self.me = me
        self.total = self.received = None

    def send(self):
        if self.received is None:
            self.received = ring(self.total, self.first)
        return self.received

    def piece(self, k, *holds):
        at = self.me.source(self.first, k)
        received = None if k == 1 else self.send()
        self.received = None
        if received is None:
            (at,) = after((at,), *holds)
        else:
            (received,) = after((received,), *holds)
        last = None
        if k == 0:
            last = jnp.stack([self.me.source(self.second, i) for i in range(4)]).astype(jnp.int32)
        self.total = weight_piece(self.terms, at, self.first, received, last)
        return self.total

    def finish(self, *holds):
        total = fl(self.total[1])
        for k in (2, 3, 0):
            sent = bf(total)
            if k == 0:
                (sent,) = after((sent,), holds[1])
            arrived = ring(sent, self.second)
            if k == 2:
                (arrived,) = after((arrived,), holds[0])
            total = fl(arrived) + fl(self.total[k])
        return total


def sum_blocks(parts, order):
    n = parts[0].shape[1]

    def kernel(order_ref, p0, p1, p2, p3, *out_refs):
        for k in range(4):
            at = pl.ds(pl.multiple_of(order_ref[k] * 128, 128), 128)
            out_refs[k][...] = bf(fl(p0[at, :]) + fl(p1[at, :]) + fl(p2[at, :]) + fl(p3[at, :]))

    return call(kernel, "sum_blocks", [sds((128, n))] * 4, [order, *parts], 0)


def direct_pieces(terms, first, me):
    parts = []
    for k in (2, 1, 3, 0):
        made = weight_piece(terms, me.source(first, k), first)
        parts.append(stepped(made, first, 4 - k) if k else made)
    return parts


def direct_sums(parts, first, me):
    second = "y" if first == "x" else "x"
    order = jnp.stack([me.source(second, i) for i in range(4)]).astype(jnp.int32)
    blocks = sum_blocks(parts, order)
    total = fl(blocks[0])
    for k in (2, 1, 3):
        total = total + fl(stepped(blocks[k], second, 4 - k))
    return total


def gather_z(block):
    wide = jnp.broadcast_to(block[None], (4,) + block.shape)
    return lax.all_to_all(wide, "z", split_axis=0, concat_axis=0, tiled=True).reshape(512, block.shape[1])


def gather_tokens(block):
    own = gather_z(block)
    return own, sibling(own)


def arrive_z(sums):
    parts = sums.reshape(4, 128, sums.shape[1])
    return lax.all_to_all(parts, "z", split_axis=0, concat_axis=0, tiled=True)


def scatter_z(sums):
    return jnp.sum(fl(arrive_z(sums)), axis=0)


def partial_sums(pieces, weights):
    count = len(pieces)

    def kernel(*refs):
        for j in range(0, D, 512):
            total = None
            for i in range(count):
                one = dot(refs[i][...], refs[count + i][j : j + 512, :], 1, 1)
                total = one if total is None else total + one
            refs[-1][:, j : j + 512] = bf(total)

    depth = sum(p.shape[1] for p in pieces)
    return call(kernel, "partial_sums", [sds((512, D))], [*pieces, *weights], 2 * 512 * depth * D)[0]


def chip_sums(own, other, weights):
    received = sibling(partial_sums(other, weights))
    return bf(fl(partial_sums(own, weights)) + fl(received))


def chip_product(own, other, weight, sibling_weight):
    received = sibling(other)
    m = own.shape[1]

    def kernel(a_ref, b_ref, v_ref, w_ref, out_ref):
        for j in range(0, D, 512):
            here = slice(j, j + 512)
            total = dot(a_ref[...], v_ref[here, :m], 1, 1) + dot(b_ref[...], w_ref[here, :m], 1, 1)
            out_ref[:, here] = bf(total)

    args = [own, received, weight, sibling_weight]
    return call(kernel, "chip_product", [sds((512, D))], args, 4 * 512 * m * D)[0]


def project(rows, weights, dtype, width=None):
    width = width or weights[0].shape[1]
    n = width * len(weights)

    def kernel(rows_ref, *refs):
        for i, w_ref in enumerate(refs[:-1]):
            for j in range(0, width, 256):
                product = dot(rows_ref[...], w_ref[:, j : j + 256], 1, 0)
                refs[-1][:, i * width + j : i * width + j + 256] = product.astype(dtype)

    return call(kernel, "project", [sds((512, n), dtype)], [rows, *weights], 2 * 512 * D * n)[0]


def down_products(rows, weights):
    def kernel(rows_ref, w0, w1, out_ref):
        for j in range(0, D, 512):
            here = slice(j, j + 512)
            total = dot(rows_ref[:, :512], w0[here, :], 1, 1) + dot(rows_ref[:, 512:], w1[here, :], 1, 1)
            out_ref[:, here] = bf(total)

    return call(kernel, "down_products", [sds((512, D))], [rows, *weights], 2 * 512 * 1024 * D)[0]


def rope(u, cosine, sine):
    lane = lax.broadcasted_iota(jnp.int32, u.shape, 1)
    turned = jnp.where(lane % DH < DH // 2, pltpu.roll(u, 96, 1), pltpu.roll(u, 32, 1))
    return u * cosine + turned * sine


def rope_three(u, cosine, sine):
    lane = lax.broadcasted_iota(jnp.int32, cosine.shape, 1)
    last = u[:, 256:]
    return jnp.concatenate(
        [
            rope(u[:, :128], cosine, sine),
            rope(u[:, 128:256], cosine, sine),
            jnp.where(lane < DH, rope(last, cosine, sine), last),
        ],
        axis=1,
    )


def half_at(halves_ref, i):
    return pl.ds(pl.multiple_of(halves_ref[i], 512), 512)


def project_qkv(i, rows, gain, weight, tables, halves):
    def kernel(halves_ref, x_ref, gain_ref, w_ref, cos_ref, sin_ref, normed_ref, out_ref):
        x = fl(x_ref[...])
        inverse = lax.rsqrt(jnp.mean(x * x, axis=1, keepdims=True) + eps)
        normed_ref[...] = bf(x * inverse * gain_ref[...])
        here = half_at(halves_ref, i)
        product = dot(normed_ref[...], w_ref[...], 1, 0)
        out_ref[...] = bf(rope_three(product, cos_ref[here, :], sin_ref[here, :]))

    args = [halves, rows, gain, weight, *tables]
    return call(kernel, "project_qkv", [sds((512, D)), sds((512, 384))], args, 2 * 512 * D * 384)


def scores_t(keys, query, q_at):
    s = dot(keys, query, 1, 1)
    key = lax.broadcasted_iota(jnp.int32, (256, 256), 0)
    column = lax.broadcasted_iota(jnp.int32, (256, 256), 1)
    diagonal = jnp.where(key <= column, s[q_at:], -1e30)
    return diagonal if q_at == 0 else jnp.concatenate([s[:q_at], diagonal], axis=0)


def attend(qkv, halves):
    def kernel(halves_ref, q0, q1, own_ref, other_ref, nat_ref, lse_ref, att_ref):
        nat_ref[half_at(halves_ref, 0), :] = q0[...]
        nat_ref[half_at(halves_ref, 1), :] = q1[...]
        kv = nat_ref[:, 256:]
        keys = kv[:, :DH]
        values_t = kv.T[DH:]
        lse_ref[...] = jnp.zeros_like(lse_ref)
        for q_at in range(0, SEQ_LEN, 256):
            end = q_at + 256
            for pair in range(2):
                two = nat_ref[q_at:end, 128 * pair : 128 * pair + 128]
                outs = []
                for i in range(2):
                    s = scores_t(keys[:end], two[:, DH * i : DH * i + DH], q_at)
                    top = jnp.max(s, axis=0, keepdims=True)
                    p = jnp.exp2((s - top) * SCALE2)
                    total = jnp.sum(p, axis=0, keepdims=True)
                    outs.append(dot(values_t[:, :end], bf(p), 1, 0) / total)
                    g = 2 * pair + i
                    lse_ref[g : g + 1, q_at:end] = top * SCALE2 + jnp.log2(total)
                att_ref[q_at:end, 128 * pair : 128 * pair + 128] = bf(jnp.concatenate(outs, axis=0).T)
        own_ref[...] = att_ref[half_at(halves_ref, 0), :]
        other_ref[...] = att_ref[half_at(halves_ref, 1), :]

    outs = [sds((512, 256)), sds((512, 256)), sds((SEQ_LEN, 384)), sds((8, SEQ_LEN), jnp.float32)]
    scratch = [pltpu.VMEM((SEQ_LEN, 256), jnp.bfloat16)]
    return call(kernel, "attend", outs, [halves, *qkv], 3e9, scratch)


def attend_backward(qkv, lse, grad_out, tables, halves):
    def kernel(halves_ref, nat_ref, lse_ref, g0, g1, cos_ref, sin_ref, own_ref, other_ref, go_nat, kv_sum, d_nat):
        go_nat[half_at(halves_ref, 0), :] = g0[...]
        go_nat[half_at(halves_ref, 1), :] = g1[...]
        kv = nat_ref[:, 256:]
        keys = kv[:, :DH]
        values = kv[:, DH:]
        keys_t = kv.T[:DH]
        kv_sum[...] = jnp.zeros_like(kv_sum)
        for q_at in range(0, SEQ_LEN, 256):
            end = q_at + 256
            cosine = cos_ref[q_at:end, :]
            sine = -sin_ref[q_at:end, :]
            for pair in range(2):
                lanes = slice(128 * pair, 128 * pair + 128)
                two = nat_ref[q_at:end, lanes]
                two_grad = go_nat[q_at:end, lanes]
                outs = []
                for i in range(2):
                    query = two[:, DH * i : DH * i + DH]
                    grad = two_grad[:, DH * i : DH * i + DH]
                    g = 2 * pair + i
                    s = scores_t(keys[:end], query, q_at)
                    p = jnp.exp2(s * SCALE2 - lse_ref[g : g + 1, q_at:end])
                    dp = dot(values[:end], grad, 1, 1)
                    delta = jnp.sum(dp * p, axis=0, keepdims=True)
                    ds = bf(p * (dp - delta))
                    kv_sum[:end, :] += jnp.concatenate(
                        [dot(ds, query, 1, 0), dot(bf(p), grad, 1, 0)], axis=1
                    )
                    outs.append(dot(keys_t[:, :end], ds, 1, 0))
                d_query = jnp.concatenate(outs, axis=0).T * SCALE
                d_nat[q_at:end, lanes] = bf(rope(d_query, cosine, sine))
        lane = lax.broadcasted_iota(jnp.int32, (SEQ_LEN, 128), 1)
        total = kv_sum[...]
        turned = rope(total * SCALE, cos_ref[...], -sin_ref[...])
        d_nat[:, 256:] = bf(jnp.where(lane < DH, turned, total))
        own_ref[...] = d_nat[half_at(halves_ref, 0), :]
        other_ref[...] = d_nat[half_at(halves_ref, 1), :]

    scratch = [
        pltpu.VMEM((SEQ_LEN, 256), jnp.bfloat16),
        pltpu.VMEM((SEQ_LEN, 128), jnp.float32),
        pltpu.VMEM((SEQ_LEN, 384), jnp.bfloat16),
    ]
    args = [halves, qkv, lse, *grad_out, *tables]
    return call(kernel, "attend_backward", [sds((512, 384))] * 2, args, 6e9, scratch)


def mlp_step(rows, w_gate, w_up, grad_act):
    width = w_gate.shape[1]

    def kernel(rows_ref, g_ref, u_ref, ga_ref, act_ref, gg_ref, gu_ref):
        for j in range(0, width, 256):
            here = slice(j, j + 256)
            gate = dot(rows_ref[...], g_ref[:, here], 1, 0)
            up = dot(rows_ref[...], u_ref[:, here], 1, 0)
            sig = jax.nn.sigmoid(gate)
            silu = gate * sig
            ga = ga_ref[:, here]
            act_ref[:, here] = bf(silu * up)
            gg_ref[:, here] = bf(ga * up * sig * (1.0 + gate * (1.0 - sig)))
            gu_ref[:, here] = bf(ga * silu)

    args = [rows, w_gate, w_up, grad_act]
    return call(kernel, "mlp_step", [sds((512, width))] * 3, args, 4 * 512 * D * width)


def frequencies(head_size):
    pair_index = jnp.arange(head_size // 2).astype(jnp.float32)
    base_freq = 500000.0 ** (-2.0 * pair_index / head_size)
    wavelen = 2.0 * jnp.pi / base_freq
    smooth = (8192.0 / wavelen - 1.0) / 3.0
    blended = (1.0 - smooth) * base_freq / 32.0 + smooth * base_freq
    return jnp.where(
        wavelen < 2048.0, base_freq, jnp.where(wavelen > 8192.0, base_freq / 32.0, blended)
    )


def norm_parts(values):
    inverse = lax.rsqrt(jnp.mean(values * values, axis=-1, keepdims=True) + eps)
    return (values * inverse, inverse)


def norm_backward(grad_normed, unit_rows, inverse, gain_rows):
    scaled = grad_normed * gain_rows
    return inverse * (scaled - unit_rows * jnp.mean(scaled * unit_rows, axis=-1, keepdims=True))


def on_device(
    tokens, positions, w_query, w_key, w_value, w_out, attn_gain, w_gate, w_up, w_down, mlp_gain, cotangent
):
    me = Place()
    inputs_b = swapped(tokens)
    places = jnp.concatenate([(positions // 256).reshape(128, 8), (positions % 256).reshape(128, 8)], axis=1)
    extra = jnp.concatenate([attn_gain[:, None], mlp_gain[:, None], bf(places)], axis=1)
    extra = jnp.pad(extra, ((0, 0), (0, 110)))
    part_attn = swapped(jnp.concatenate([w_query, w_key, w_value, w_out.T, extra], axis=1))

    part_attn, inputs_b = lax.optimization_barrier((part_attn, inputs_b))
    own_in = gather_z(inputs_b)
    w_gate, w_up, w_down, cotangent = after((w_gate, w_up, w_down, cotangent), inputs_b)
    down_rows = w_down.T
    part_a = swapped(jnp.concatenate([w_gate, down_rows[:, :512]], axis=1))
    part_b = swapped(jnp.concatenate([w_up, down_rows[:, 512:]], axis=1))
    upstream = swapped(cotangent)
    stage_qkv = first_stage(part_attn[:, :384], "x", False)
    stage_out = first_stage(part_attn[:, 384:], "y", False)
    stage_qkv, stage_out = after((stage_qkv, stage_out), part_a, part_b)
    parts_qkv, parts_out = second_stage(stage_qkv, "x"), second_stage(stage_out, "y")
    w_qkv = place_rows(parts_qkv, me.blocks["x"])
    out_and_gains = place_rows(parts_out, me.blocks["y"])

    place = fl(part_attn[:, 642:658])
    seq_positions = (256.0 * place[:, :8] + place[:, 8:]).reshape(SEQ_LEN)
    freq = jnp.tile(frequencies(DH), 4)
    angles = seq_positions[:, None] * freq[None, :]
    sign = jnp.where(jnp.arange(128) % DH < DH // 2, -1.0, 1.0)
    tables = (jnp.cos(angles), jnp.sin(angles) * sign[None, :])
    pick = bf(jnp.arange(128)[None, :] == jnp.arange(8)[:, None])
    gain_rows = dot(pick, out_and_gains[:, 256:], 1, 1)
    gain_attn, gain_mlp = gain_rows[:1], gain_rows[1:2]

    part_a, part_b = after((part_a, part_b), parts_qkv[2], parts_out[2])
    stage_a, stage_b = first_stage(part_a, "x", False), first_stage(part_b, "y", False)

    (own_in,) = after((own_in,), upstream)
    rows_in = [own_in, sibling(own_in)]
    projected = [project_qkv(i, rows_in[i], gain_attn, w_qkv, tables, me.halves) for i in range(2)]
    normed_attn = [p[0] for p in projected]

    (own_up,) = after((upstream,), own_in)
    rows_up = gather_tokens(own_up)

    attended, other_attended, qkv, lse = attend([p[1] for p in projected], me.halves)
    inputs = fl(inputs_b)
    out_sums = chip_product(attended, other_attended, out_and_gains, sibling(out_and_gains))
    (out_sums,) = after((out_sums,), rows_up[0], stage_a, stage_b)
    residual = inputs + scatter_z(out_sums)

    parts_a = second_stage(stage_a, "x")
    parts_b = second_stage(stage_b, "y")
    full_gate = place_rows(parts_a, me.blocks["x"], (0, 1024))
    full_up = place_rows(parts_b, me.blocks["y"], (0, 1024))
    full_down = [
        place_rows(parts_a, me.blocks["x"], (1024, 1536)),
        place_rows(parts_b, me.blocks["y"], (1024, 1536)),
    ]

    (residual,) = after((residual,), parts_a[2], parts_b[2])
    unit_mlp, inverse_mlp = norm_parts(residual)
    normed_mlp = bf(unit_mlp * gain_mlp)
    own_mlp = gather_z(normed_mlp)
    up_held = after(rows_up, normed_mlp)
    grad_act = [project(r, full_down, jnp.float32) for r in up_held]
    (own_mlp,) = after((own_mlp,), full_gate, full_up, *full_down)
    rows_mlp = [own_mlp, sibling(own_mlp)]
    steps = [mlp_step(r, full_gate, full_up, g) for r, g in zip(rows_mlp, grad_act)]
    activated, grad_gate_pre, grad_up_pre = zip(*steps)

    gate_up = list(zip(grad_gate_pre, grad_up_pre))
    mlp_sums = chip_sums(gate_up[0], gate_up[1], [full_gate, full_up])
    grad_normed_mlp = scatter_z(mlp_sums)

    grad_a = WeightGradient([(rows_mlp, grad_gate_pre, 0, 1024), (rows_up, activated, 0, 512)], "x", me)
    grad_b = WeightGradient([(rows_mlp, grad_up_pre, 0, 1024), (rows_up, activated, 512, 1024)], "y", me)
    acts = after(activated, mlp_sums)
    down_other = down_products(acts[1], full_down)
    made = [g.piece(1, down_other) for g in (grad_a, grad_b)]
    sent = [g.send() for g in (grad_a, grad_b)]
    down_sums = bf(fl(down_products(acts[0], full_down)) + fl(sibling(down_other)))
    (grad_normed_mlp,) = after((grad_normed_mlp,), *made, down_sums)
    grad_residual = fl(upstream) + norm_backward(grad_normed_mlp, unit_mlp, inverse_mlp, gain_mlp)
    grad_residual_b = bf(grad_residual)

    own_gr = gather_z(grad_residual_b)
    made = [g.piece(2, grad_residual_b) for g in (grad_a, grad_b)]
    sent = [g.send() for g in (grad_a, grad_b)]
    (own_gr,) = after((own_gr,), *made)
    rows_gr = [own_gr, sibling(own_gr)]
    (down_sums,) = after((down_sums,), own_gr)
    arrived = arrive_z(down_sums)

    grad_attended = [project(r, [out_and_gains], jnp.bfloat16, 256) for r in rows_gr]
    made = [g.piece(3, own_gr) for g in (grad_a, grad_b)]
    grad_attended = after(grad_attended, *made)
    grad_qkv, other_grad_qkv = attend_backward(qkv, lse, grad_attended, tables, me.halves)
    made = [block for g in (grad_a, grad_b) for block in g.piece(0, grad_qkv)]
    attn_sums = chip_product(grad_qkv, other_grad_qkv, w_qkv, sibling(w_qkv))
    (attn_sums,) = after((attn_sums,), arrived, *made)
    grad_normed_attn = scatter_z(attn_sums)

    (arrived,) = after((arrived,), attn_sums)
    layer_out = bf(residual + jnp.sum(fl(arrived), axis=0))
    d_qkv = after((grad_qkv, other_grad_qkv), attn_sums)
    att = after((attended, other_attended), attn_sums)
    parts_in = direct_pieces([(normed_attn, d_qkv, 0, 384)], "x", me)
    parts_wo = direct_pieces([(rows_gr, att, 0, 256)], "y", me)
    (grad_normed_attn,) = after((grad_normed_attn,), parts_in[-1], parts_wo[-1], layer_out)
    unit_attn, inverse_attn = norm_parts(inputs)
    grad_norm_attn = norm_backward(grad_normed_attn, unit_attn, inverse_attn, gain_attn)
    grad_tokens = bf(grad_residual + grad_norm_attn)
    share_a, share_b = (g.finish(attn_sums, grad_normed_attn) for g in (grad_a, grad_b))
    share_qkv = direct_sums(after(parts_in, grad_normed_attn), "x", me)
    share_out = direct_sums(after(parts_wo, grad_normed_attn), "y", me)

    def gain_sum(*terms):
        return sum(jnp.sum(fl(w) * g, axis=1) for w, g in terms)

    gain_sums = jnp.stack(
        [
            gain_sum((part_attn[:, :384], share_qkv)),
            gain_sum((part_a[:, :1024], share_a[:, :1024]), (part_b[:, :1024], share_b[:, :1024])),
        ]
    )
    gain_sums = gain_sums / fl(part_attn[:, 640:642].T)
    gain_sums = gain_sums + z_moved(gain_sums, 1) + z_moved(gain_sums, 2) + z_moved(gain_sums, 3)
    gain_sums = swapped(gain_sums) + swapped_across(gain_sums)

    share_attn = fl(swapped(bf(jnp.concatenate([share_qkv, share_out], axis=1))))
    share_a, share_b = fl(swapped(bf(share_a))), fl(swapped(bf(share_b)))
    return (
        swapped(layer_out),
        swapped(grad_tokens),
        share_attn[:, :256],
        share_attn[:, 256:320],
        share_attn[:, 320:384],
        share_attn[:, 384:].T,
        gain_sums[0],
        share_a[:, :1024],
        share_b[:, :1024],
        jnp.concatenate([share_a[:, 1024:], share_b[:, 1024:]], axis=1).T,
        gain_sums[1],
    )


def solution(mesh):
    split = Mesh(mesh.devices.reshape(4, 2, 2, 2, 4), AXES)
    dp, tensor = ("x", "l", "c"), ("h", "z")
    both = P(AXES, None)
    weight, turned, vector = P(dp, tensor), P(tensor, dp), P(dp)
    in_specs = (
        both, vector, weight, weight, weight, turned, vector, weight, weight, turned, vector, both,
    )
    out_specs = (
        both, both, weight, weight, weight, turned, vector, weight, weight, turned, vector,
    )
    return jax.shard_map(on_device, mesh=split, in_specs=in_specs, out_specs=out_specs, check_vma=False)
```

```python
import functools
import itertools
import math

import jax
import jax.numpy as jnp
from jax import lax
from jax.experimental import pallas as pl
from jax.experimental.pallas import tpu as pltpu
from jax.sharding import Mesh, PartitionSpec as P

H = 32
KV = 8
DH = 64
SEQ_LEN = 1024
D = 2048
eps = 1e-05

SIZES = dict(x=4, l=2, c=2, h=2, z=4)
AXES = ("x", "l", "c", "h", "z")

SCALE = DH ** (-0.5)
SCALE2 = SCALE * math.log2(math.e)
VMEM_LIMIT = 14 * 1024 * 1024


def pairs(axes, move):
    def place(index):
        at = 0
        for a in axes:
            at = at * SIZES[a] + index[a]
        return at

    out = []
    for index in itertools.product(*[range(SIZES[a]) for a in axes]):
        here = dict(zip(axes, index))
        out.append((place(here), place(move(dict(here)))))
    return out


def to_swapped(d):
    d["c"], d["h"] = d["h"], d["c"]
    return d


def to_sibling(d):
    d["c"] = 1 - d["c"]
    return d


def along(axis):
    def move(d):
        step = 1 - 2 * d["c"]
        if axis == "y":
            y = (2 * d["h"] + d["l"] + step) % 4
            d["h"], d["l"] = y // 2, y % 2
        else:
            d[axis] = (d[axis] + step) % 4
        return d

    return move


RING_AXES = dict(x=("x", "c"), y=("l", "c", "h"))
Z_STEPS = (0, 1, 3, 2)
PIECES = (1, 3, 2, 0)


def ring(value, axis):
    axes = RING_AXES[axis]
    return lax.ppermute(value, axes, pairs(axes, along(axis)))


def swapped(value):
    return lax.ppermute(value, ("c", "h"), pairs(("c", "h"), to_swapped))


def sibling(value):
    return lax.ppermute(value, ("c",), pairs(("c",), to_sibling))


def z_moved(value, step):
    def move(d):
        d["z"] = (d["z"] + step) % 4
        return d

    return lax.ppermute(value, ("z",), pairs(("z",), move))


def swapped_across(value):
    def move(d):
        c, h = d["c"], d["h"]
        d["h"], d["c"] = 1 - c, h
        return d

    return lax.ppermute(value, ("c", "h"), pairs(("c", "h"), move))


def after(values, *earlier):
    held = lax.optimization_barrier((tuple(values), tuple(earlier)))
    return held[0]


def dot(a, b, ca, cb):
    return lax.dot_general(a, b, (((ca,), (cb,)), ((), ())), preferred_element_type=jnp.float32)


def bf(v):
    return v.astype(jnp.bfloat16)


def fl(v):
    return v.astype(jnp.float32)


def sds(shape, dtype=jnp.bfloat16):
    return jax.ShapeDtypeStruct(shape, dtype)


def cost(flops):
    return pl.CostEstimate(flops=int(flops), bytes_accessed=1, transcendentals=0)


PARAMS = pltpu.CompilerParams(vmem_limit_bytes=VMEM_LIMIT)
ANY = pl.BlockSpec(memory_space=pl.ANY)
WHOLE = pl.BlockSpec(memory_space=pltpu.VMEM)


class Place:
    def __init__(self):
        self.c = lax.axis_index("c")
        self.x = lax.axis_index("x")
        self.h = lax.axis_index("h")
        self.y = 2 * self.h + lax.axis_index("l")
        self.step = 1 - 2 * self.c
        self.halves = jnp.stack([512 * self.c, 512 * (1 - self.c)]).astype(jnp.int32)
        z = lax.axis_index("z")
        self.z_order = jnp.stack([lax.rem(z - step + 4, 4) for step in Z_STEPS]).astype(jnp.int32)
        self.blocks = {}
        for first, second in (("x", "y"), ("y", "x")):
            out = []
            for k2 in range(4):
                for k1 in range(4):
                    a, b = self.source(first, k1), self.source(second, k2)
                    out.append(4 * a + b if first == "x" else 4 * b + a)
            self.blocks[first] = jnp.stack(out).astype(jnp.int32)

    def source(self, axis, k):
        at = lax.rem(dict(x=self.x, y=self.y)[axis] - self.step * k + 4, 4)
        if axis == "y":
            at = 2 * lax.rem(at, 2) + lax.div(at, 2)
        return at


SMEM = pl.BlockSpec(memory_space=pltpu.SMEM)


def place_rows(parts, blocks, widths):
    def kernel(blocks_ref, p0, p1, p2, p3, *rest):
        sems = rest[-1]
        copies = []
        for k2, part in enumerate((p0, p1, p2, p3)):
            for k1 in range(4):
                at = pl.multiple_of(blocks_ref[4 * k2 + k1] * 128, 128)
                low = 0
                for i, width in enumerate(widths):
                    copies.append(
                        pltpu.make_async_copy(
                            part.at[pl.ds(128 * k1, 128), pl.ds(low, width)],
                            rest[i].at[pl.ds(at, 128)],
                            sems.at[len(widths) * (4 * k2 + k1) + i],
                        )
                    )
                    low += width
        for copy in copies:
            copy.start()
        for copy in copies:
            copy.wait()

    return pl.pallas_call(
        kernel,
        out_shape=[pltpu.VMEM((D, width), jnp.bfloat16) for width in widths],
        in_specs=[SMEM] + [ANY] * 4,
        out_specs=[WHOLE] * len(widths),
        scratch_shapes=[pltpu.SemaphoreType.DMA((16 * len(widths),))],
        compiler_params=PARAMS,
        cost_estimate=cost(1),
        name="place_rows",
    )(blocks, *parts)


def stepped(value, axis, steps):
    def move(d):
        for _ in range(steps):
            d = along(axis)(d)
        return d

    axes = RING_AXES[axis]
    return lax.ppermute(value, axes, pairs(axes, move))


def chain(block, axis, holds):
    parts = [block]
    for hold in holds:
        part = ring(parts[-1], axis)
        parts.append(part if hold is None else after((part,), hold)[0])
    return parts


def gather_plane(block):
    wide = jnp.broadcast_to(block[None], (16,) + block.shape)
    return lax.all_to_all(wide, ("x", "l", "h"), split_axis=0, concat_axis=0, tiled=True).reshape(D, block.shape[1])


def call(kernel, name, outs, args, flops, scratch=()):
    return pl.pallas_call(
        kernel,
        out_shape=outs,
        in_specs=[SMEM if a.dtype == jnp.int32 else WHOLE for a in args],
        out_specs=[WHOLE] * len(outs),
        scratch_shapes=list(scratch),
        compiler_params=PARAMS,
        cost_estimate=cost(flops),
        name=name,
    )(*args)


def weight_product(terms, first, me):
    tile = 256 if all(width % 256 == 0 for _, _, _, width in terms) else 384
    starts = [0]
    for _, _, _, width in terms:
        starts.append(starts[-1] + width // tile)
    steps = starts[-1]
    count = len(terms)
    order = jnp.stack([me.source(first, k) for k in PIECES]).astype(jnp.int32)

    def column(j):
        if first == "x":
            return pl.BlockSpec((512, 128), lambda p, i, s: (0, 4 * s[p] + j))
        return pl.BlockSpec((512, 128), lambda p, i, s: (0, 4 * j + s[p]))

    def right_spec(block, width):
        return pl.BlockSpec((512, width), lambda p, i, s: (0, block), pipeline_mode=pl.Buffered(1))

    def out_spec(mine):
        def at(p, i, s):
            return 0, jnp.where(p == mine, i, jnp.where(p < mine, 0, steps - 1))

        return pl.BlockSpec((512, tile), at)

    args, specs = [], []
    for rows, right, block, width in terms:
        for r in rows:
            args += [r] * 4
            specs += [column(j) for j in range(4)]
        args += list(right)
        specs += [right_spec(block, width)] * 2

    def kernel(order_ref, *refs):
        out_refs, left_refs = refs[len(args) : len(args) + 4], refs[len(args) + 4 :]
        p, i = pl.program_id(0), pl.program_id(1)
        for t in range(count):

            @pl.when(i == starts[t])
            def _(t=t):
                halves = [
                    jnp.concatenate([r[...] for r in refs[10 * t + 4 * u : 10 * t + 4 * u + 4]], axis=1)
                    for u in range(2)
                ]
                left_refs[t][...] = jnp.concatenate(halves, axis=0).T

            @pl.when((i >= starts[t]) & (i < starts[t + 1]))
            def _(t=t):
                here = pl.ds(pl.multiple_of((i - starts[t]) * tile, tile), tile)
                total = dot(left_refs[t][:, :512], refs[10 * t + 8][:, here], 1, 0)
                total = total + dot(left_refs[t][:, 512:], refs[10 * t + 9][:, here], 1, 0)
                for mine in range(4):

                    @pl.when(p == mine)
                    def _(mine=mine):
                        out_refs[mine][...] = bf(total)

    return pl.pallas_call(
        kernel,
        grid_spec=pltpu.PrefetchScalarGridSpec(
            num_scalar_prefetch=1,
            grid=(4, steps),
            in_specs=specs,
            out_specs=[out_spec(mine) for mine in range(4)],
            scratch_shapes=[pltpu.VMEM((512, SEQ_LEN), jnp.bfloat16)] * count,
        ),
        out_shape=[sds((512, steps * tile))] * 4,
        compiler_params=PARAMS,
        cost_estimate=cost(2 * D * SEQ_LEN * steps * tile),
        name="weight_product",
    )(order, *args)


def sum_blocks(parts, order):
    n = parts[0].shape[1]

    def kernel(order_ref, p0, p1, p2, p3, *out_refs):
        for k in range(4):
            at = pl.ds(pl.multiple_of(order_ref[k] * 128, 128), 128)
            out_refs[k][...] = bf(fl(p0[at, :]) + fl(p1[at, :]) + fl(p2[at, :]) + fl(p3[at, :]))

    return call(kernel, "sum_blocks", [sds((128, n))] * 4, [order, *parts], 0)


def send_pieces(made, first):
    return [stepped(piece, first, 4 - k) if k else piece for k, piece in zip(PIECES, made)]


def plane_sums(parts, first, me):
    second = "y" if first == "x" else "x"
    order = jnp.stack([me.source(second, k) for k in PIECES]).astype(jnp.int32)
    blocks = sum_blocks(parts, order)
    total = fl(blocks[-1])
    for part in send_pieces(blocks, second)[:-1]:
        total = total + fl(part)
    return total


def send_z(block):
    return [z_moved(block, step) if step else block for step in Z_STEPS]


def place_tokens(blocks, me):
    def kernel(order_ref, b0, b1, b2, b3, out_ref):
        for k, ref in enumerate((b0, b1, b2, b3)):
            out_ref[pl.ds(pl.multiple_of(order_ref[k] * 128, 128), 128), :] = ref[...]

    return call(kernel, "place_tokens", [sds((512, D))], [me.z_order, *blocks], 1)[0]


def norm_tokens(blocks, gain, me):
    def kernel(order_ref, b0, b1, b2, b3, gain_ref, out_ref):
        for k, ref in enumerate((b0, b1, b2, b3)):
            x = fl(ref[...])
            inverse = lax.rsqrt(jnp.mean(x * x, axis=1, keepdims=True) + eps)
            out_ref[pl.ds(pl.multiple_of(order_ref[k] * 128, 128), 128), :] = bf(x * inverse * gain_ref[...])

    return call(kernel, "norm_tokens", [sds((512, D))], [me.z_order, *blocks, gain], 1)[0]


def gather_z(block):
    wide = jnp.broadcast_to(block[None], (4,) + block.shape)
    return lax.all_to_all(wide, "z", split_axis=0, concat_axis=0, tiled=True).reshape(512, block.shape[1])


def arrive_z(sums):
    parts = sums.reshape(4, 128, sums.shape[1])
    return lax.all_to_all(parts, "z", split_axis=0, concat_axis=0, tiled=True)


def scatter_z(sums):
    return jnp.sum(fl(arrive_z(sums)), axis=0)


def partial_sums(pieces, weights):
    count = len(pieces)

    def kernel(*refs):
        for j in range(0, D, 512):
            total = None
            for i in range(count):
                one = dot(refs[i][...], refs[count + i][j : j + 512, :], 1, 1)
                total = one if total is None else total + one
            refs[-1][:, j : j + 512] = bf(total)

    depth = sum(p.shape[1] for p in pieces)
    return call(kernel, "partial_sums", [sds((512, D))], [*pieces, *weights], 2 * 512 * depth * D)[0]


def chip_sums(own, other, weights):
    received = sibling(partial_sums(other, weights))
    return bf(fl(partial_sums(own, weights)) + fl(received))


def chip_product(own, other, weight, sibling_weight):
    received = sibling(other)
    m = own.shape[1]

    def kernel(a_ref, b_ref, v_ref, w_ref, out_ref):
        for j in range(0, D, 512):
            here = slice(j, j + 512)
            total = dot(a_ref[...], v_ref[here, :m], 1, 1) + dot(b_ref[...], w_ref[here, :m], 1, 1)
            out_ref[:, here] = bf(total)

    args = [own, received, weight, sibling_weight]
    return call(kernel, "chip_product", [sds((512, D))], args, 4 * 512 * m * D)[0]


def project(rows, weights, dtype, width=None):
    width = width or weights[0].shape[1]
    n = width * len(weights)

    def kernel(rows_ref, *refs):
        for i, w_ref in enumerate(refs[:-1]):
            for j in range(0, width, 256):
                product = dot(rows_ref[...], w_ref[:, j : j + 256], 1, 0)
                refs[-1][:, i * width + j : i * width + j + 256] = product.astype(dtype)

    return call(kernel, "project", [sds((512, n), dtype)], [rows, *weights], 2 * 512 * D * n)[0]


def down_products(rows, weights):
    def kernel(rows_ref, w0, w1, out_ref):
        for j in range(0, D, 512):
            here = slice(j, j + 512)
            total = dot(rows_ref[:, :512], w0[here, :], 1, 1) + dot(rows_ref[:, 512:], w1[here, :], 1, 1)
            out_ref[:, here] = bf(total)

    return call(kernel, "down_products", [sds((512, D))], [rows, *weights], 2 * 512 * 1024 * D)[0]


def rope(u, cosine, sine):
    lane = lax.broadcasted_iota(jnp.int32, u.shape, 1)
    turned = jnp.where(lane % DH < DH // 2, pltpu.roll(u, 96, 1), pltpu.roll(u, 32, 1))
    return u * cosine + turned * sine


def rope_three(u, cosine, sine):
    lane = lax.broadcasted_iota(jnp.int32, cosine.shape, 1)
    last = u[:, 256:]
    return jnp.concatenate(
        [
            rope(u[:, :128], cosine, sine),
            rope(u[:, 128:256], cosine, sine),
            jnp.where(lane < DH, rope(last, cosine, sine), last),
        ],
        axis=1,
    )


def half_at(halves_ref, i):
    return pl.ds(pl.multiple_of(halves_ref[i], 512), 512)


def project_qkv(i, rows, weight, tables, halves):
    def kernel(halves_ref, rows_ref, w_ref, cos_ref, sin_ref, out_ref):
        here = half_at(halves_ref, i)
        product = dot(rows_ref[...], w_ref[:, :384], 1, 0)
        out_ref[...] = bf(rope_three(product, cos_ref[here, :], sin_ref[here, :]))

    args = [halves, rows, weight, *tables]
    return call(kernel, "project_qkv", [sds((512, 384))], args, 2 * 512 * D * 384)[0]


def scores_t(keys, query, q_at):
    s = dot(keys, query, 1, 1)
    key = lax.broadcasted_iota(jnp.int32, (256, 256), 0)
    column = lax.broadcasted_iota(jnp.int32, (256, 256), 1)
    diagonal = jnp.where(key <= column, s[q_at:], -1e30)
    return diagonal if q_at == 0 else jnp.concatenate([s[:q_at], diagonal], axis=0)


def attend(qkv, halves):
    def kernel(halves_ref, q0, q1, own_ref, other_ref, nat_ref, lse_ref, att_ref):
        nat_ref[half_at(halves_ref, 0), :] = q0[...]
        nat_ref[half_at(halves_ref, 1), :] = q1[...]
        kv = nat_ref[:, 256:]
        keys = kv[:, :DH]
        values_t = kv.T[DH:]
        lse_ref[...] = jnp.zeros_like(lse_ref)
        for q_at in range(0, SEQ_LEN, 256):
            end = q_at + 256
            for pair in range(2):
                two = nat_ref[q_at:end, 128 * pair : 128 * pair + 128]
                outs = []
                for i in range(2):
                    s = scores_t(keys[:end], two[:, DH * i : DH * i + DH], q_at)
                    top = jnp.max(s, axis=0, keepdims=True)
                    p = jnp.exp2((s - top) * SCALE2)
                    total = jnp.sum(p, axis=0, keepdims=True)
                    outs.append(dot(values_t[:, :end], bf(p), 1, 0) / total)
                    g = 2 * pair + i
                    lse_ref[g : g + 1, q_at:end] = top * SCALE2 + jnp.log2(total)
                att_ref[q_at:end, 128 * pair : 128 * pair + 128] = bf(jnp.concatenate(outs, axis=0).T)
        own_ref[...] = att_ref[half_at(halves_ref, 0), :]
        other_ref[...] = att_ref[half_at(halves_ref, 1), :]

    outs = [sds((512, 256)), sds((512, 256)), sds((SEQ_LEN, 384)), sds((8, SEQ_LEN), jnp.float32)]
    scratch = [pltpu.VMEM((SEQ_LEN, 256), jnp.bfloat16)]
    return call(kernel, "attend", outs, [halves, *qkv], 20e9, scratch)


def attend_backward(qkv, lse, grad_out, tables, halves):
    def kernel(halves_ref, nat_ref, lse_ref, g0, g1, cos_ref, sin_ref, own_ref, other_ref, go_nat, kv_sum, d_nat):
        go_nat[half_at(halves_ref, 0), :] = g0[...]
        go_nat[half_at(halves_ref, 1), :] = g1[...]
        kv = nat_ref[:, 256:]
        keys = kv[:, :DH]
        values = kv[:, DH:]
        keys_t = kv.T[:DH]
        kv_sum[...] = jnp.zeros_like(kv_sum)
        for q_at in range(0, SEQ_LEN, 256):
            end = q_at + 256
            cosine = cos_ref[q_at:end, :]
            sine = -sin_ref[q_at:end, :]
            for pair in range(2):
                lanes = slice(128 * pair, 128 * pair + 128)
                two = nat_ref[q_at:end, lanes]
                two_grad = go_nat[q_at:end, lanes]
                outs = []
                for i in range(2):
                    query = two[:, DH * i : DH * i + DH]
                    grad = two_grad[:, DH * i : DH * i + DH]
                    g = 2 * pair + i
                    s = scores_t(keys[:end], query, q_at)
                    p = jnp.exp2(s * SCALE2 - lse_ref[g : g + 1, q_at:end])
                    dp = dot(values[:end], grad, 1, 1)
                    delta = jnp.sum(dp * p, axis=0, keepdims=True)
                    ds = bf(p * (dp - delta))
                    kv_sum[:end, :] += jnp.concatenate(
                        [dot(ds, query, 1, 0), dot(bf(p), grad, 1, 0)], axis=1
                    )
                    outs.append(dot(keys_t[:, :end], ds, 1, 0))
                d_query = jnp.concatenate(outs, axis=0).T * SCALE
                d_nat[q_at:end, lanes] = bf(rope(d_query, cosine, sine))
        lane = lax.broadcasted_iota(jnp.int32, (SEQ_LEN, 128), 1)
        total = kv_sum[...]
        turned = rope(total * SCALE, cos_ref[...], -sin_ref[...])
        d_nat[:, 256:] = bf(jnp.where(lane < DH, turned, total))
        own_ref[...] = d_nat[half_at(halves_ref, 0), :]
        other_ref[...] = d_nat[half_at(halves_ref, 1), :]

    scratch = [
        pltpu.VMEM((SEQ_LEN, 256), jnp.bfloat16),
        pltpu.VMEM((SEQ_LEN, 128), jnp.float32),
        pltpu.VMEM((SEQ_LEN, 384), jnp.bfloat16),
    ]
    args = [halves, qkv, lse, *grad_out, *tables]
    return call(kernel, "attend_backward", [sds((512, 384))] * 2, args, 30e9, scratch)


def mlp_step(rows, w_gate, w_up, grad_act):
    width = w_gate.shape[1]

    def kernel(rows_ref, g_ref, u_ref, ga_ref, act_ref, gg_ref, gu_ref):
        for j in range(0, width, 256):
            here = slice(j, j + 256)
            gate = dot(rows_ref[...], g_ref[:, here], 1, 0)
            up = dot(rows_ref[...], u_ref[:, here], 1, 0)
            sig = jax.nn.sigmoid(gate)
            silu = gate * sig
            ga = ga_ref[:, here]
            act_ref[:, here] = bf(silu * up)
            gg_ref[:, here] = bf(ga * up * sig * (1.0 + gate * (1.0 - sig)))
            gu_ref[:, here] = bf(ga * silu)

    args = [rows, w_gate, w_up, grad_act]
    return call(kernel, "mlp_step", [sds((512, width))] * 3, args, 4 * 512 * D * width)


def frequencies(head_size):
    pair_index = jnp.arange(head_size // 2).astype(jnp.float32)
    base_freq = 500000.0 ** (-2.0 * pair_index / head_size)
    wavelen = 2.0 * jnp.pi / base_freq
    smooth = (8192.0 / wavelen - 1.0) / 3.0
    blended = (1.0 - smooth) * base_freq / 32.0 + smooth * base_freq
    return jnp.where(
        wavelen < 2048.0, base_freq, jnp.where(wavelen > 8192.0, base_freq / 32.0, blended)
    )


def norm_parts(values):
    inverse = lax.rsqrt(jnp.mean(values * values, axis=-1, keepdims=True) + eps)
    return (values * inverse, inverse)


def norm_backward(grad_normed, unit_rows, inverse, gain_rows):
    scaled = grad_normed * gain_rows
    return inverse * (scaled - unit_rows * jnp.mean(scaled * unit_rows, axis=-1, keepdims=True))


def on_device(
    tokens, positions, w_query, w_key, w_value, w_out, attn_gain, w_gate, w_up, w_down, mlp_gain, cotangent
):
    me = Place()
    inputs_b = swapped(tokens)
    places = jnp.concatenate([(positions // 256).reshape(128, 8), (positions % 256).reshape(128, 8)], axis=1)
    extra = jnp.concatenate([attn_gain[:, None], mlp_gain[:, None], bf(places)], axis=1)
    extra = jnp.pad(extra, ((0, 0), (0, 110)))
    part_attn = swapped(jnp.concatenate([w_query, w_key, w_value, extra, w_out.T], axis=1))
    part_attn, inputs_b = lax.optimization_barrier((part_attn, inputs_b))

    blocks_in = send_z(inputs_b)
    w_qkv = gather_plane(part_attn[:, :512])
    w_gate, w_up, w_down, cotangent = after((w_gate, w_up, w_down, cotangent), inputs_b)
    down_rows = w_down.T
    part_a = swapped(jnp.concatenate([w_gate, down_rows[:, :512]], axis=1))
    part_b = swapped(jnp.concatenate([w_up, down_rows[:, 512:]], axis=1))
    upstream = swapped(cotangent)

    place = fl(part_attn[:, 386:402])
    seq_positions = (256.0 * place[:, :8] + place[:, 8:]).reshape(SEQ_LEN)
    freq = jnp.tile(frequencies(DH), 4)
    angles = seq_positions[:, None] * freq[None, :]
    sign = jnp.where(jnp.arange(128) % DH < DH // 2, -1.0, 1.0)
    tables = (jnp.cos(angles), jnp.sin(angles) * sign[None, :])
    pick = bf(jnp.arange(128)[None, :] == jnp.arange(8)[:, None])
    gain_rows = dot(pick, w_qkv[:, 384:], 1, 1)
    gain_attn, gain_mlp = gain_rows[:1], gain_rows[1:2]

    (part_out,) = after((part_attn[:, 512:],), w_qkv)
    w_out_t = gather_plane(part_out)
    blocks_in = after(blocks_in, part_a, part_b, upstream)
    own_normed = norm_tokens(blocks_in, gain_attn, me)
    normed_attn = [own_normed, sibling(own_normed)]
    own_qkv = project_qkv(0, normed_attn[0], w_qkv, tables, me.halves)
    projected = [own_qkv, project_qkv(1, normed_attn[1], w_qkv, tables, me.halves)]

    (own_up,) = after((upstream,), *blocks_in)
    blocks_up = send_z(own_up)

    projected = after(projected, blocks_up[1])
    attended, other_attended, qkv, lse = attend(projected, me.halves)
    inputs = fl(inputs_b)
    out_sums = chip_product(attended, other_attended, w_out_t, sibling(w_out_t))
    (out_sums,) = after((out_sums,), *blocks_up)

    holds = (own_qkv, attended, out_sums)
    stage_a, stage_b = (jnp.concatenate(chain(p, axis, holds), axis=0) for p, axis in ((part_a, "x"), (part_b, "y")))

    own_up = place_tokens(blocks_up, me)
    rows_up = [own_up, sibling(own_up)]
    residual = inputs + scatter_z(out_sums)

    parts_a, parts_b = chain(stage_a, "y", (None, None, None)), chain(stage_b, "x", (None, None, None))
    full_gate, down_a = place_rows(parts_a, me.blocks["x"], (1024, 512))
    full_up, down_b = place_rows(parts_b, me.blocks["y"], (1024, 512))
    full_down = [down_a, down_b]

    (residual,) = after((residual,), parts_a[2], parts_b[2], *rows_up)
    unit_mlp, inverse_mlp = norm_parts(residual)
    normed_mlp = bf(unit_mlp * gain_mlp)
    own_mlp = gather_z(normed_mlp)
    up_held = after(rows_up, normed_mlp)
    grad_act = [project(r, full_down, jnp.float32) for r in up_held]
    (own_mlp,) = after((own_mlp,), full_gate, full_up, grad_act[0])
    rows_mlp = [own_mlp, sibling(own_mlp)]
    steps = [mlp_step(r, full_gate, full_up, g) for r, g in zip(rows_mlp, grad_act)]
    activated, grad_gate_pre, grad_up_pre = zip(*steps)

    gate_up = list(zip(grad_gate_pre, grad_up_pre))
    mlp_sums = chip_sums(gate_up[0], gate_up[1], [full_gate, full_up])
    grad_normed_mlp = scatter_z(mlp_sums)

    gg, gu = after((grad_gate_pre, grad_up_pre), mlp_sums)
    made_a = weight_product([(rows_mlp, gg, 0, 1024), (rows_up, activated, 0, 512)], "x", me)
    made_b = weight_product([(rows_mlp, gu, 0, 1024), (rows_up, activated, 1, 512)], "y", me)
    sent_a, sent_b = send_pieces(made_a, "x"), send_pieces(made_b, "y")
    acts = after(activated, made_a[-1], made_b[-1])
    down_other = down_products(acts[1], full_down)
    down_own = down_products(acts[0], full_down)
    (grad_normed_mlp,) = after((grad_normed_mlp,), down_own)
    grad_residual = fl(upstream) + norm_backward(grad_normed_mlp, unit_mlp, inverse_mlp, gain_mlp)
    grad_residual_b = bf(grad_residual)

    own_gr = gather_z(grad_residual_b)
    (down_arrived,) = after((sibling(down_other),), grad_residual_b)
    down_sums = bf(fl(down_own) + fl(down_arrived))
    (own_gr,) = after((own_gr,), down_sums, *sent_a[:2], *sent_b[:2])
    rows_gr = [own_gr, sibling(own_gr)]
    (down_sums,) = after((down_sums,), own_gr)
    arrived = arrive_z(down_sums)

    grad_attended = [project(r, [w_out_t], jnp.bfloat16) for r in rows_gr]
    grad_qkv, other_grad_qkv = attend_backward(qkv, lse, grad_attended, tables, me.halves)
    attn_sums = chip_product(grad_qkv, other_grad_qkv, w_qkv, sibling(w_qkv))
    (attn_sums,) = after((attn_sums,), arrived)
    grad_normed_attn = scatter_z(attn_sums)

    (arrived,) = after((arrived,), attn_sums)
    layer_out = bf(residual + jnp.sum(fl(arrived), axis=0))
    d_qkv = after((grad_qkv, other_grad_qkv), attn_sums)
    att = after((attended, other_attended), attn_sums)
    made_in = weight_product([(normed_attn, d_qkv, 0, 384)], "x", me)
    made_out = weight_product([(rows_gr, att, 0, 256)], "y", me)
    sent_a, sent_b = after(sent_a, made_out[-1]), after(sent_b, made_out[-1])
    share_a, share_b = plane_sums(sent_a, "x", me), plane_sums(sent_b, "y", me)
    (grad_normed_attn,) = after((grad_normed_attn,), made_in[-1], made_out[-1], layer_out)
    unit_attn, inverse_attn = norm_parts(inputs)
    grad_norm_attn = norm_backward(grad_normed_attn, unit_attn, inverse_attn, gain_attn)
    grad_tokens = bf(grad_residual + grad_norm_attn)
    share_qkv = plane_sums(after(send_pieces(made_in, "x"), grad_normed_attn), "x", me)
    share_out = plane_sums(after(send_pieces(made_out, "y"), grad_normed_attn), "y", me)

    def gain_sum(*terms):
        return sum(jnp.sum(fl(w) * g, axis=1) for w, g in terms)

    gain_sums = jnp.stack(
        [
            gain_sum((part_attn[:, :384], share_qkv)),
            gain_sum((part_a[:, :1024], share_a[:, :1024]), (part_b[:, :1024], share_b[:, :1024])),
        ]
    )
    gain_sums = gain_sums / fl(part_attn[:, 384:386].T)
    gain_sums = gain_sums + z_moved(gain_sums, 1) + z_moved(gain_sums, 2) + z_moved(gain_sums, 3)
    gain_sums = swapped(gain_sums) + swapped_across(gain_sums)

    share_attn = fl(swapped(bf(jnp.concatenate([share_qkv, share_out], axis=1))))
    share_a, share_b = fl(swapped(bf(share_a))), fl(swapped(bf(share_b)))
    return (
        swapped(layer_out),
        swapped(grad_tokens),
        share_attn[:, :256],
        share_attn[:, 256:320],
        share_attn[:, 320:384],
        share_attn[:, 384:].T,
        gain_sums[0],
        share_a[:, :1024],
        share_b[:, :1024],
        jnp.concatenate([share_a[:, 1024:], share_b[:, 1024:]], axis=1).T,
        gain_sums[1],
    )


def solution(mesh):
    split = Mesh(mesh.devices.reshape(4, 2, 2, 2, 4), AXES)
    dp, tensor = ("x", "l", "c"), ("h", "z")
    both = P(AXES, None)
    weight, turned, vector = P(dp, tensor), P(tensor, dp), P(dp)
    in_specs = (
        both, vector, weight, weight, weight, turned, vector, weight, weight, turned, vector, both,
    )
    out_specs = (
        both, both, weight, weight, weight, turned, vector, weight, weight, turned, vector,
    )
    return jax.shard_map(on_device, mesh=split, in_specs=in_specs, out_specs=out_specs, check_vma=False)
```

```python
import functools
import itertools
import math

import jax
import jax.numpy as jnp
from jax import lax
from jax.experimental import pallas as pl
from jax.experimental.pallas import tpu as pltpu
from jax.sharding import Mesh, PartitionSpec as P

H = 32
KV = 8
DH = 64
SEQ_LEN = 1024
D = 2048
eps = 1e-05

SIZES = dict(x=4, l=2, c=2, h=2, z=4)
AXES = ("x", "l", "c", "h", "z")

SCALE = DH ** (-0.5)
SCALE2 = SCALE * math.log2(math.e)
VMEM_LIMIT = 14 * 1024 * 1024


def pairs(axes, move):
    def place(index):
        at = 0
        for a in axes:
            at = at * SIZES[a] + index[a]
        return at

    out = []
    for index in itertools.product(*[range(SIZES[a]) for a in axes]):
        here = dict(zip(axes, index))
        out.append((place(here), place(move(dict(here)))))
    return out


def to_swapped(d):
    d["c"], d["h"] = d["h"], d["c"]
    return d


def to_sibling(d):
    d["c"] = 1 - d["c"]
    return d


def along(axis):
    def move(d):
        step = 1 - 2 * d["c"]
        if axis == "y":
            y = (2 * d["h"] + d["l"] + step) % 4
            d["h"], d["l"] = y // 2, y % 2
        else:
            d[axis] = (d[axis] + step) % 4
        return d

    return move


RING_AXES = dict(x=("x", "c"), y=("l", "c", "h"))
Z_STEPS = (0, 1, 3, 2)
PIECES = (1, 2, 3, 0)


def ring(value, axis):
    axes = RING_AXES[axis]
    return lax.ppermute(value, axes, pairs(axes, along(axis)))


def swapped(value):
    return lax.ppermute(value, ("c", "h"), pairs(("c", "h"), to_swapped))


def sibling(value):
    return lax.ppermute(value, ("c",), pairs(("c",), to_sibling))


def z_moved(value, step):
    def move(d):
        d["z"] = (d["z"] + step) % 4
        return d

    return lax.ppermute(value, ("z",), pairs(("z",), move))


def h_flipped(value):
    def move(d):
        d["h"] = 1 - d["h"]
        return d

    return lax.ppermute(value, ("h",), pairs(("h",), move))


def after(values, *earlier):
    held = lax.optimization_barrier((tuple(values), tuple(earlier)))
    return held[0]


def dot(a, b, ca, cb):
    return lax.dot_general(a, b, (((ca,), (cb,)), ((), ())), preferred_element_type=jnp.float32)


def bf(v):
    return v.astype(jnp.bfloat16)


def fl(v):
    return v.astype(jnp.float32)


def sds(shape, dtype=jnp.bfloat16):
    return jax.ShapeDtypeStruct(shape, dtype)


def cost(flops):
    return pl.CostEstimate(flops=int(flops), bytes_accessed=1, transcendentals=0)


PARAMS = pltpu.CompilerParams(vmem_limit_bytes=VMEM_LIMIT)
ANY = pl.BlockSpec(memory_space=pl.ANY)
WHOLE = pl.BlockSpec(memory_space=pltpu.VMEM)


class Place:
    def __init__(self):
        self.c = lax.axis_index("c")
        self.x = lax.axis_index("x")
        self.h = lax.axis_index("h")
        self.y = 2 * self.h + lax.axis_index("l")
        self.step = 1 - 2 * self.c
        self.halves = jnp.stack([512 * self.c, 512 * (1 - self.c)]).astype(jnp.int32)
        z = lax.axis_index("z")
        self.z_order = jnp.stack([lax.rem(z - step + 4, 4) for step in Z_STEPS]).astype(jnp.int32)
        self.blocks = {}
        for first, second in (("x", "y"), ("y", "x")):
            out = []
            for k2 in range(4):
                for k1 in range(4):
                    a, b = self.source(first, k1), self.source(second, k2)
                    out.append(4 * a + b if first == "x" else 4 * b + a)
            self.blocks[first] = jnp.stack(out).astype(jnp.int32)

    def source(self, axis, k):
        at = lax.rem(dict(x=self.x, y=self.y)[axis] - self.step * k + 4, 4)
        if axis == "y":
            at = 2 * lax.rem(at, 2) + lax.div(at, 2)
        return at


SMEM = pl.BlockSpec(memory_space=pltpu.SMEM)


def pinned(value):
    return pltpu.with_memory_space_constraint(value, pltpu.VMEM)


def place_rows(parts, blocks, widths):
    def kernel(blocks_ref, p0, p1, p2, p3, *rest):
        sems = rest[-1]
        copies = []
        for k2, part in enumerate((p0, p1, p2, p3)):
            for k1 in range(4):
                at = pl.multiple_of(blocks_ref[4 * k2 + k1] * 128, 128)
                low = 0
                for i, width in enumerate(widths):
                    copies.append(
                        pltpu.make_async_copy(
                            part.at[pl.ds(128 * k1, 128), pl.ds(low, width)],
                            rest[i].at[pl.ds(at, 128)],
                            sems.at[len(widths) * (4 * k2 + k1) + i],
                        )
                    )
                    low += width
        for copy in copies:
            copy.start()
        for copy in copies:
            copy.wait()

    return pl.pallas_call(
        kernel,
        out_shape=[pltpu.VMEM((D, width), jnp.bfloat16) for width in widths],
        in_specs=[SMEM] + [ANY] * 4,
        out_specs=[WHOLE] * len(widths),
        scratch_shapes=[pltpu.SemaphoreType.DMA((16 * len(widths),))],
        compiler_params=PARAMS,
        cost_estimate=cost(1),
        name="place_rows",
    )(blocks, *parts)


def stepped(value, axis, steps):
    def move(d):
        for _ in range(steps):
            d = along(axis)(d)
        return d

    axes = RING_AXES[axis]
    return lax.ppermute(value, axes, pairs(axes, move))


def chain(block, axis, holds):
    parts = [block]
    for hold in holds:
        part = ring(parts[-1], axis)
        parts.append(part if hold is None else after((part,), hold)[0])
    return parts


def gather_plane(block):
    wide = jnp.broadcast_to(block[None], (16,) + block.shape)
    return lax.all_to_all(wide, ("x", "l", "h"), split_axis=0, concat_axis=0, tiled=True).reshape(D, block.shape[1])


def call(kernel, name, outs, args, flops, scratch=(), limit=VMEM_LIMIT):
    return pl.pallas_call(
        kernel,
        out_shape=outs,
        in_specs=[SMEM if a.dtype == jnp.int32 else WHOLE for a in args],
        out_specs=[WHOLE] * len(outs),
        scratch_shapes=list(scratch),
        compiler_params=pltpu.CompilerParams(vmem_limit_bytes=limit),
        cost_estimate=cost(flops),
        name=name,
    )(*args)


def weight_product(terms, first, me):
    order = jnp.stack([me.source(first, k) for k in PIECES]).astype(jnp.int32)
    n = sum(high - low for _, _, low, high in terms)
    args = [order]
    for rows, right, _, _ in terms:
        args += [*rows, *right]

    def kernel(order_ref, *refs):
        for p in range(4):
            at = 0
            for t, (_, _, low, high) in enumerate(terms):
                rows, right = refs[4 * t : 4 * t + 2], refs[4 * t + 2 : 4 * t + 4]
                left = []
                for r in rows:
                    lanes = []
                    for j in range(4):
                        block = 4 * order_ref[p] + j if first == "x" else 4 * j + order_ref[p]
                        lanes.append(r[:, pl.ds(pl.multiple_of(block * 128, 128), 128)])
                    left.append(jnp.concatenate(lanes, axis=1))
                for j in range(low, high, 256):
                    end = min(j + 256, high)
                    total = dot(left[0], right[0][:, j:end], 0, 0) + dot(left[1], right[1][:, j:end], 0, 0)
                    refs[4 * len(terms) + p][:, at : at + end - j] = bf(total)
                    at += end - j

    return call(
        kernel, "weight_product", [sds((512, n))] * 4, args, 2 * D * SEQ_LEN * n, limit=28 * 1024 * 1024
    )


def sum_blocks(parts, order):
    n = parts[0].shape[1]

    def kernel(order_ref, *refs):
        for k in range(4):
            at = pl.ds(pl.multiple_of(order_ref[k] * 128, 128), 128)
            refs[len(parts) + k][...] = bf(sum(fl(ref[at, :]) for ref in refs[: len(parts)]))

    return call(kernel, "sum_blocks", [sds((128, n))] * 4, [order, *parts], 1)


def send_pieces(made, first):
    return [stepped(piece, first, 4 - k) if k else piece for k, piece in zip(PIECES, made)]


def homeward(value, k):
    def move(d):
        y = (2 * d["h"] + d["l"] - k * (1 - 2 * d["c"])) % 4
        d["l"], d["h"], d["c"] = y % 2, d["c"], y // 2
        return d

    axes = ("l", "c", "h")
    return lax.ppermute(value, axes, pairs(axes, move))


def add(one, other):
    def kernel(a_ref, b_ref, out_ref):
        out_ref[...] = bf(fl(a_ref[...]) + fl(b_ref[...]))

    return call(kernel, "add", [sds(one.shape)], [one, other], 1)[0]


def second_blocks(parts, first, me):
    second = "y" if first == "x" else "x"
    return sum_blocks(parts, jnp.stack([me.source(second, k) for k in PIECES]).astype(jnp.int32))


def second_stage(blocks, first):
    if first == "x":
        return [homeward(block, k) for k, block in zip(PIECES, blocks)]
    return send_pieces(blocks, "x")


def summed(parts, hold):
    return sum(fl(part) for part in after(parts, hold))


def send_z(block):
    return [z_moved(block, step) if step else block for step in Z_STEPS]


def place_tokens(blocks, me):
    def kernel(order_ref, b0, b1, b2, b3, out_ref):
        for k, ref in enumerate((b0, b1, b2, b3)):
            out_ref[pl.ds(pl.multiple_of(order_ref[k] * 128, 128), 128), :] = ref[...]

    return call(kernel, "place_tokens", [sds((512, D))], [me.z_order, *blocks], 1)[0]


def norm_tokens(blocks, gain, me):
    def kernel(order_ref, b0, b1, b2, b3, gain_ref, out_ref):
        for k, ref in enumerate((b0, b1, b2, b3)):
            x = fl(ref[...])
            inverse = lax.rsqrt(jnp.mean(x * x, axis=1, keepdims=True) + eps)
            out_ref[pl.ds(pl.multiple_of(order_ref[k] * 128, 128), 128), :] = bf(x * inverse * gain_ref[...])

    return call(kernel, "norm_tokens", [sds((512, D))], [me.z_order, *blocks, gain], 1)[0]


def gather_z(wide_block):
    whole = lax.all_to_all(wide_block, "z", split_axis=0, concat_axis=0, tiled=True)
    return whole.reshape(512, whole.shape[2])


def arrive_z(sums):
    parts = sums.reshape(4, 128, sums.shape[1])
    return lax.all_to_all(parts, "z", split_axis=0, concat_axis=0, tiled=True)


def partial_sums(pieces, weights):
    count = len(pieces)

    def kernel(*refs):
        for j in range(0, D, 512):
            total = None
            for i in range(count):
                one = dot(refs[i][...], refs[count + i][j : j + 512, :], 1, 1)
                total = one if total is None else total + one
            refs[-1][:, j : j + 512] = bf(total)

    depth = sum(p.shape[1] for p in pieces)
    return call(kernel, "partial_sums", [sds((512, D))], [*pieces, *map(pinned, weights)], 2 * 512 * depth * D)[0]


def chip_sums(own, other, weights):
    received = sibling(partial_sums(other, weights))
    return bf(fl(partial_sums(own, weights)) + fl(received))


def chip_product(own, other, weight, sibling_weight):
    received = sibling(other)
    m = own.shape[1]

    def kernel(a_ref, b_ref, v_ref, w_ref, out_ref):
        for j in range(0, D, 512):
            here = slice(j, j + 512)
            total = dot(a_ref[...], v_ref[here, :m], 1, 1) + dot(b_ref[...], w_ref[here, :m], 1, 1)
            out_ref[:, here] = bf(total)

    args = [own, received, weight, sibling_weight]
    return call(kernel, "chip_product", [sds((512, D))], args, 4 * 512 * m * D)[0]


def project(rows, weights, dtype, width=None):
    width = width or weights[0].shape[1]
    n = width * len(weights)

    def kernel(rows_ref, *refs):
        for i, w_ref in enumerate(refs[:-1]):
            for j in range(0, width, 256):
                product = dot(rows_ref[...], w_ref[:, j : j + 256], 1, 0)
                refs[-1][:, i * width + j : i * width + j + 256] = product.astype(dtype)

    return call(kernel, "project", [sds((512, n), dtype)], [rows, *weights], 2 * 512 * D * n)[0]


def down_products(rows, weights):
    def kernel(rows_ref, w0, w1, out_ref):
        for j in range(0, D, 512):
            here = slice(j, j + 512)
            total = dot(rows_ref[:, :512], w0[here, :], 1, 1) + dot(rows_ref[:, 512:], w1[here, :], 1, 1)
            out_ref[:, here] = bf(total)

    return call(kernel, "down_products", [sds((512, D))], [rows, *map(pinned, weights)], 2 * 512 * 1024 * D)[0]


def rope(u, cosine, sine):
    lane = lax.broadcasted_iota(jnp.int32, u.shape, 1)
    turned = jnp.where(lane % DH < DH // 2, pltpu.roll(u, 96, 1), pltpu.roll(u, 32, 1))
    return u * cosine + turned * sine


def rope_three(u, cosine, sine):
    lane = lax.broadcasted_iota(jnp.int32, cosine.shape, 1)
    last = u[:, 256:]
    return jnp.concatenate(
        [
            rope(u[:, :128], cosine, sine),
            rope(u[:, 128:256], cosine, sine),
            jnp.where(lane < DH, rope(last, cosine, sine), last),
        ],
        axis=1,
    )


def half_at(halves_ref, i):
    return pl.ds(pl.multiple_of(halves_ref[i], 512), 512)


def project_qkv(i, rows, weight, tables, halves):
    def kernel(halves_ref, rows_ref, w_ref, cos_ref, sin_ref, out_ref):
        here = half_at(halves_ref, i)
        product = dot(rows_ref[...], w_ref[:, :384], 1, 0)
        out_ref[...] = bf(rope_three(product, cos_ref[here, :], sin_ref[here, :]))

    args = [halves, rows, weight, *tables]
    return call(kernel, "project_qkv", [sds((512, 384))], args, 2 * 512 * D * 384)[0]


def scores_t(keys, query, q_at):
    s = dot(keys, query, 1, 1)
    key = lax.broadcasted_iota(jnp.int32, (256, 256), 0)
    column = lax.broadcasted_iota(jnp.int32, (256, 256), 1)
    diagonal = jnp.where(key <= column, s[q_at:], -1e30)
    return diagonal if q_at == 0 else jnp.concatenate([s[:q_at], diagonal], axis=0)


def attend(qkv, halves):
    def kernel(halves_ref, q0, q1, own_ref, other_ref, nat_ref, lse_ref, att_ref):
        nat_ref[half_at(halves_ref, 0), :] = q0[...]
        nat_ref[half_at(halves_ref, 1), :] = q1[...]
        kv = nat_ref[:, 256:]
        keys = kv[:, :DH]
        values_t = kv.T[DH:]
        lse_ref[...] = jnp.zeros_like(lse_ref)
        for q_at in range(0, SEQ_LEN, 256):
            end = q_at + 256
            for pair in range(2):
                two = nat_ref[q_at:end, 128 * pair : 128 * pair + 128]
                outs = []
                for i in range(2):
                    s = scores_t(keys[:end], two[:, DH * i : DH * i + DH], q_at)
                    top = jnp.max(s, axis=0, keepdims=True)
                    p = jnp.exp2((s - top) * SCALE2)
                    total = jnp.sum(p, axis=0, keepdims=True)
                    outs.append(dot(values_t[:, :end], bf(p), 1, 0) / total)
                    g = 2 * pair + i
                    lse_ref[g : g + 1, q_at:end] = top * SCALE2 + jnp.log2(total)
                att_ref[q_at:end, 128 * pair : 128 * pair + 128] = bf(jnp.concatenate(outs, axis=0).T)
        own_ref[...] = att_ref[half_at(halves_ref, 0), :]
        other_ref[...] = att_ref[half_at(halves_ref, 1), :]

    outs = [sds((512, 256)), sds((512, 256)), sds((SEQ_LEN, 384)), sds((8, SEQ_LEN), jnp.float32)]
    scratch = [pltpu.VMEM((SEQ_LEN, 256), jnp.bfloat16)]
    return call(kernel, "attend", outs, [halves, *qkv], 20e9, scratch)


def attend_backward(qkv, lse, grad_out, tables, halves):
    def kernel(halves_ref, nat_ref, lse_ref, g0, g1, cos_ref, sin_ref, own_ref, other_ref, go_nat, kv_sum, d_nat):
        go_nat[half_at(halves_ref, 0), :] = g0[...]
        go_nat[half_at(halves_ref, 1), :] = g1[...]
        kv = nat_ref[:, 256:]
        keys = kv[:, :DH]
        values = kv[:, DH:]
        keys_t = kv.T[:DH]
        kv_sum[...] = jnp.zeros_like(kv_sum)
        for q_at in range(0, SEQ_LEN, 256):
            end = q_at + 256
            cosine = cos_ref[q_at:end, :]
            sine = -sin_ref[q_at:end, :]
            for pair in range(2):
                lanes = slice(128 * pair, 128 * pair + 128)
                two = nat_ref[q_at:end, lanes]
                two_grad = go_nat[q_at:end, lanes]
                outs = []
                for i in range(2):
                    query = two[:, DH * i : DH * i + DH]
                    grad = two_grad[:, DH * i : DH * i + DH]
                    g = 2 * pair + i
                    s = scores_t(keys[:end], query, q_at)
                    p = jnp.exp2(s * SCALE2 - lse_ref[g : g + 1, q_at:end])
                    dp = dot(values[:end], grad, 1, 1)
                    delta = jnp.sum(dp * p, axis=0, keepdims=True)
                    ds = bf(p * (dp - delta))
                    kv_sum[:end, :] += jnp.concatenate(
                        [dot(ds, query, 1, 0), dot(bf(p), grad, 1, 0)], axis=1
                    )
                    outs.append(dot(keys_t[:, :end], ds, 1, 0))
                d_query = jnp.concatenate(outs, axis=0).T * SCALE
                d_nat[q_at:end, lanes] = bf(rope(d_query, cosine, sine))
        lane = lax.broadcasted_iota(jnp.int32, (SEQ_LEN, 128), 1)
        total = kv_sum[...]
        turned = rope(total * SCALE, cos_ref[...], -sin_ref[...])
        d_nat[:, 256:] = bf(jnp.where(lane < DH, turned, total))
        own_ref[...] = d_nat[half_at(halves_ref, 0), :]
        other_ref[...] = d_nat[half_at(halves_ref, 1), :]

    scratch = [
        pltpu.VMEM((SEQ_LEN, 256), jnp.bfloat16),
        pltpu.VMEM((SEQ_LEN, 128), jnp.float32),
        pltpu.VMEM((SEQ_LEN, 384), jnp.bfloat16),
    ]
    args = [halves, qkv, lse, *grad_out, *tables]
    return call(kernel, "attend_backward", [sds((512, 384))] * 2, args, 30e9, scratch)


def mlp_step(rows, w_gate, w_up, grad_act):
    width = w_gate.shape[1]

    def kernel(rows_ref, g_ref, u_ref, ga_ref, act_ref, gg_ref, gu_ref):
        for j in range(0, width, 256):
            here = slice(j, j + 256)
            gate = dot(rows_ref[...], g_ref[:, here], 1, 0)
            up = dot(rows_ref[...], u_ref[:, here], 1, 0)
            sig = jax.nn.sigmoid(gate)
            silu = gate * sig
            ga = ga_ref[:, here]
            act_ref[:, here] = bf(silu * up)
            gg_ref[:, here] = bf(ga * up * sig * (1.0 + gate * (1.0 - sig)))
            gu_ref[:, here] = bf(ga * silu)

    args = [rows, pinned(w_gate), pinned(w_up), grad_act]
    return call(kernel, "mlp_step", [sds((512, width))] * 3, args, 4 * 512 * D * width)


def frequencies(head_size):
    pair_index = jnp.arange(head_size // 2).astype(jnp.float32)
    base_freq = 500000.0 ** (-2.0 * pair_index / head_size)
    wavelen = 2.0 * jnp.pi / base_freq
    smooth = (8192.0 / wavelen - 1.0) / 3.0
    blended = (1.0 - smooth) * base_freq / 32.0 + smooth * base_freq
    return jnp.where(
        wavelen < 2048.0, base_freq, jnp.where(wavelen > 8192.0, base_freq / 32.0, blended)
    )


LONG = 60e9


def wide(out_ref, value):
    for k in range(4):
        out_ref[k] = value


def arrived_sum(ref):
    return fl(ref[0]) + fl(ref[1]) + fl(ref[2]) + fl(ref[3])


def mlp_norm(inputs, arrived, gain):
    def kernel(x_ref, a_ref, gain_ref, residual_ref, out_ref):
        residual = fl(x_ref[...]) + arrived_sum(a_ref)
        residual_ref[...] = residual
        inverse = lax.rsqrt(jnp.mean(residual * residual, axis=1, keepdims=True) + eps)
        wide(out_ref, bf(residual * inverse * gain_ref[...]))

    outs = [sds((128, D), jnp.float32), sds((4, 128, D))]
    return call(kernel, "mlp_norm", outs, [inputs, arrived, gain], LONG)


def norm_grad(grad, values, gain):
    inverse = lax.rsqrt(jnp.mean(values * values, axis=1, keepdims=True) + eps)
    unit = values * inverse
    scaled = grad * gain
    return inverse * (scaled - unit * jnp.mean(scaled * unit, axis=1, keepdims=True))


def mlp_norm_backward(upstream, arrived, residual, gain):
    def kernel(g_ref, a_ref, r_ref, gain_ref, grad_ref, out_ref):
        grad = fl(g_ref[...]) + norm_grad(arrived_sum(a_ref), r_ref[...], gain_ref[...])
        grad_ref[...] = grad
        wide(out_ref, bf(grad))

    outs = [sds((128, D), jnp.float32), sds((4, 128, D))]
    return call(kernel, "mlp_norm_backward", outs, [upstream, arrived, residual, gain], LONG)


def attn_norm_backward(grad_residual, arrived, inputs, gain):
    def kernel(g_ref, a_ref, x_ref, gain_ref, out_ref):
        out_ref[...] = bf(g_ref[...] + norm_grad(arrived_sum(a_ref), fl(x_ref[...]), gain_ref[...]))

    return call(kernel, "attn_norm_backward", [sds((128, D))], [grad_residual, arrived, inputs, gain], LONG)[0]


def layer_output(residual, arrived):
    def kernel(r_ref, a_ref, out_ref):
        out_ref[...] = bf(r_ref[...] + arrived_sum(a_ref))

    return call(kernel, "layer_output", [sds((128, D))], [residual, arrived], 1)[0]


def on_device(
    tokens, positions, w_query, w_key, w_value, w_out, attn_gain, w_gate, w_up, w_down, mlp_gain, cotangent
):
    me = Place()
    inputs_b = swapped(tokens)
    places = jnp.concatenate([(positions // 256).reshape(128, 8), (positions % 256).reshape(128, 8)], axis=1)
    extra = jnp.concatenate([attn_gain[:, None], mlp_gain[:, None], bf(places)], axis=1)
    extra = jnp.pad(extra, ((0, 0), (0, 110)))
    part_attn = swapped(jnp.concatenate([w_query, w_key, w_value, extra, w_out.T], axis=1))
    part_attn, inputs_b = lax.optimization_barrier((part_attn, inputs_b))

    blocks_in = send_z(inputs_b)
    w_qkv = gather_plane(part_attn[:, :512])
    (cotangent,) = after((cotangent,), inputs_b)
    upstream = swapped(cotangent)
    w_gate, w_up, w_down = after((w_gate, w_up, w_down), w_qkv)
    down_rows = w_down.T
    part_ab = swapped(jnp.concatenate([w_gate, down_rows[:, :512], w_up, down_rows[:, 512:]], axis=1))

    place = fl(part_attn[:, 386:402])
    seq_positions = (256.0 * place[:, :8] + place[:, 8:]).reshape(SEQ_LEN)
    freq = jnp.tile(frequencies(DH), 4)
    angles = seq_positions[:, None] * freq[None, :]
    sign = jnp.where(jnp.arange(128) % DH < DH // 2, -1.0, 1.0)
    tables = (jnp.cos(angles), jnp.sin(angles) * sign[None, :])
    pick = bf(jnp.arange(128)[None, :] == jnp.arange(8)[:, None])
    gain_rows = dot(pick, w_qkv[:, 384:], 1, 1)
    gain_attn, gain_mlp = gain_rows[:1], gain_rows[1:2]

    blocks_in = after(blocks_in, *tables, upstream)
    own_normed = norm_tokens(blocks_in, gain_attn, me)
    normed_attn = [own_normed, sibling(own_normed)]
    own_qkv = project_qkv(0, normed_attn[0], w_qkv, tables, me.halves)
    projected = [own_qkv, project_qkv(1, normed_attn[1], w_qkv, tables, me.halves)]

    (own_up,) = after((upstream,), own_normed)
    blocks_up = send_z(own_up)
    (part_out,) = after((part_attn[:, 512:],), own_qkv)
    w_out_t = gather_plane(part_out)

    projected = after(projected, *blocks_up[1:3])
    attended, other_attended, qkv, lse = attend(projected, me.halves)
    (w_out_t,) = after((w_out_t,), attended, blocks_up[3])
    out_sums = chip_product(attended, other_attended, w_out_t, sibling(w_out_t))
    (out_sums,) = after((out_sums,), *blocks_up)

    (part_ab,) = after((part_ab,), projected[1])
    part_a, part_b = part_ab[:, :1536], part_ab[:, 1536:]
    holds = (attended, out_sums, None)
    stage_a, stage_b = (jnp.concatenate(chain(p, axis, holds), axis=0) for p, axis in ((part_a, "x"), (part_b, "y")))

    own_up = place_tokens(blocks_up, me)
    rows_up = [own_up, sibling(own_up)]
    arrived = arrive_z(out_sums)

    parts_a, parts_b = chain(stage_a, "y", (None, None, None)), chain(stage_b, "x", (None, None, None))
    full_gate, down_a = place_rows(parts_a, me.blocks["x"], (1024, 512))
    full_up, down_b = place_rows(parts_b, me.blocks["y"], (1024, 512))
    full_down = [down_a, down_b]

    (arrived,) = after((arrived,), parts_a[2], parts_b[2], *rows_up)
    residual, normed_mlp = mlp_norm(inputs_b, arrived, gain_mlp)
    own_mlp = gather_z(normed_mlp)
    up_held = after(rows_up, normed_mlp)
    grad_act = [project(r, [pinned(w) for w in full_down], jnp.float32) for r in up_held]
    (own_mlp,) = after((own_mlp,), full_gate, full_up, grad_act[0])
    rows_mlp = [own_mlp, sibling(own_mlp)]
    steps = [mlp_step(r, full_gate, full_up, g) for r, g in zip(rows_mlp, grad_act)]
    activated, grad_gate_pre, grad_up_pre = zip(*steps)

    gate_up = list(zip(grad_gate_pre, grad_up_pre))
    mlp_sums = chip_sums(gate_up[0], gate_up[1], [full_gate, full_up])
    arrived = arrive_z(mlp_sums)

    gg, gu = after((grad_gate_pre, grad_up_pre), mlp_sums)
    made_a = weight_product([(rows_mlp, gg, 0, 1024), (rows_up, activated, 0, 512)], "x", me)
    made_b = weight_product([(rows_mlp, gu, 0, 1024), (rows_up, activated, 512, 1024)], "y", me)
    sums = [made_a[0], made_b[0]]
    rings = [ring(total, axis) for total, axis in zip(sums, "xy")]
    acts = after(activated, made_a[-1], made_b[-1])
    down_other = down_products(acts[1], full_down)
    down_own = down_products(acts[0], full_down)
    (arrived,) = after((arrived,), down_own)
    grad_residual, grad_residual_b = mlp_norm_backward(upstream, arrived, residual, gain_mlp)

    own_gr = gather_z(grad_residual_b)
    (down_arrived,) = after((sibling(down_other),), grad_residual_b)
    down_sums = bf(fl(down_own) + fl(down_arrived))
    rings = after(rings, grad_residual_b)
    sums = [add(received, made[1]) for received, made in zip(rings, (made_a, made_b))]
    rings = [ring(total, axis) for total, axis in zip(sums, "xy")]
    (own_gr,) = after((own_gr,), down_sums, *rings)
    rows_gr = [own_gr, sibling(own_gr)]
    (down_sums,) = after((down_sums,), own_gr)
    arrived = arrive_z(down_sums)

    rings = after(rings, own_gr)
    sums = [add(received, made[2]) for received, made in zip(rings, (made_a, made_b))]
    rings = [ring(total, axis) for total, axis in zip(sums, "xy")]
    grad_attended = [project(r, [w_out_t], jnp.bfloat16) for r in after(rows_gr, *sums)]
    grad_qkv, other_grad_qkv = attend_backward(qkv, lse, grad_attended, tables, me.halves)
    rings = after(rings, grad_qkv)
    blocks_a, blocks_b = (
        second_blocks([received, made[3]], first, me)
        for received, made, first in zip(rings, (made_a, made_b), "xy")
    )
    parts_b = second_stage(blocks_b, "y")
    attn_sums = chip_product(grad_qkv, other_grad_qkv, w_qkv, sibling(w_qkv))
    (attn_sums,) = after((attn_sums,), arrived, blocks_a[0], blocks_b[0])
    grad_arrived = arrive_z(attn_sums)

    (arrived,) = after((arrived,), attn_sums)
    layer_out = layer_output(residual, arrived)
    parts_a = second_stage(after(blocks_a, layer_out), "x")
    d_qkv = after((grad_qkv, other_grad_qkv), attn_sums)
    made_in = weight_product([(normed_attn, d_qkv, 0, 384)], "x", me)
    sent_in = send_pieces(made_in, "x")
    att = after((attended, other_attended), made_in[-1])
    made_out = weight_product([(rows_gr, att, 0, 256)], "y", me)
    sent_out = send_pieces(made_out, "y")
    (grad_arrived,) = after((grad_arrived,), made_out[-1], layer_out)
    grad_tokens = attn_norm_backward(grad_residual, grad_arrived, inputs_b, gain_attn)
    share_a, share_b = summed(parts_a, attn_sums), summed(parts_b, attn_sums)
    share_b = fl(swapped(bf(share_b)))
    blocks_in = second_blocks(after(sent_in, grad_tokens), "x", me)
    share_in = summed(second_stage(blocks_in, "x"), grad_tokens)
    blocks_out = second_blocks(after(sent_out, grad_tokens), "y", me)
    share_out = fl(swapped(bf(summed(second_stage(blocks_out, "y"), grad_tokens))))

    def gain_sum(*terms):
        return sum(jnp.sum(fl(w) * g, axis=1) for w, g in terms)

    gain_sums = jnp.stack(
        [
            gain_sum((jnp.concatenate([w_query, w_key, w_value], axis=1), share_in)),
            gain_sum((w_gate, share_a[:, :1024]), (w_up, share_b[:, :1024])),
        ]
    )
    gain_sums = gain_sums / fl(jnp.stack([attn_gain, mlp_gain]))
    gain_sums = gain_sums + z_moved(gain_sums, 1) + z_moved(gain_sums, 2) + z_moved(gain_sums, 3)
    gain_sums = gain_sums + h_flipped(gain_sums)
    return (
        swapped(layer_out),
        swapped(grad_tokens),
        share_in[:, :256],
        share_in[:, 256:320],
        share_in[:, 320:384],
        share_out.T,
        gain_sums[0],
        share_a[:, :1024],
        share_b[:, :1024],
        jnp.concatenate([share_a[:, 1024:], share_b[:, 1024:]], axis=1).T,
        gain_sums[1],
    )


def solution(mesh):
    split = Mesh(mesh.devices.reshape(4, 2, 2, 2, 4), AXES)
    dp, tensor = ("x", "l", "c"), ("h", "z")
    both = P(AXES, None)
    weight, turned, vector = P(dp, tensor), P(tensor, dp), P(dp)
    in_specs = (
        both, vector, weight, weight, weight, turned, vector, weight, weight, turned, vector, both,
    )
    out_specs = (
        both, both, weight, weight, weight, turned, vector, weight, weight, turned, vector,
    )
    return jax.shard_map(on_device, mesh=split, in_specs=in_specs, out_specs=out_specs, check_vma=False)
```

```python
import functools
import itertools
import math

import jax
import jax.numpy as jnp
from jax import lax
from jax.experimental import pallas as pl
from jax.experimental.pallas import tpu as pltpu
from jax.sharding import Mesh, PartitionSpec as P

H = 32
KV = 8
DH = 64
SEQ_LEN = 1024
D = 2048
eps = 1e-05

SIZES = dict(x=4, l=2, c=2, h=2, z=4)
AXES = ("x", "l", "c", "h", "z")

SCALE = DH ** (-0.5)
SCALE2 = SCALE * math.log2(math.e)
VMEM_LIMIT = 12 * 1024 * 1024


def pairs(axes, move):
    def place(index):
        at = 0
        for a in axes:
            at = at * SIZES[a] + index[a]
        return at

    out = []
    for index in itertools.product(*[range(SIZES[a]) for a in axes]):
        here = dict(zip(axes, index))
        out.append((place(here), place(move(dict(here)))))
    return out


def to_swapped(d):
    d["c"], d["h"] = d["h"], d["c"]
    return d


def to_sibling(d):
    d["c"] = 1 - d["c"]
    return d


def along(axis):
    def move(d):
        step = 1 - 2 * d["c"]
        if axis == "y":
            y = (2 * d["h"] + d["l"] + step) % 4
            d["h"], d["l"] = y // 2, y % 2
        else:
            d[axis] = (d[axis] + step) % 4
        return d

    return move


RING_AXES = dict(x=("x", "c"), y=("l", "c", "h"))
Z_STEPS = (0, 1, 3, 2)
PIECES = (1, 2, 3, 0)


def ring(value, axis):
    axes = RING_AXES[axis]
    return lax.ppermute(value, axes, pairs(axes, along(axis)))


def swapped(value):
    return lax.ppermute(value, ("c", "h"), pairs(("c", "h"), to_swapped))


def sibling(value):
    return lax.ppermute(value, ("c",), pairs(("c",), to_sibling))


def z_moved(value, step):
    def move(d):
        d["z"] = (d["z"] + step) % 4
        return d

    return lax.ppermute(value, ("z",), pairs(("z",), move))


def h_flipped(value):
    def move(d):
        d["h"] = 1 - d["h"]
        return d

    return lax.ppermute(value, ("h",), pairs(("h",), move))


def after(values, *earlier):
    held = lax.optimization_barrier((tuple(values), tuple(earlier)))
    return held[0]


def dot(a, b, ca, cb):
    return lax.dot_general(a, b, (((ca,), (cb,)), ((), ())), preferred_element_type=jnp.float32)


def bf(v):
    return v.astype(jnp.bfloat16)


def fl(v):
    return v.astype(jnp.float32)


def sds(shape, dtype=jnp.bfloat16):
    return jax.ShapeDtypeStruct(shape, dtype)


def cost(flops):
    return pl.CostEstimate(flops=int(flops), bytes_accessed=1, transcendentals=0)


PARAMS = pltpu.CompilerParams(vmem_limit_bytes=VMEM_LIMIT)
ANY = pl.BlockSpec(memory_space=pl.ANY)
WHOLE = pl.BlockSpec(memory_space=pltpu.VMEM)


class Place:
    def __init__(self):
        self.c = lax.axis_index("c")
        self.x = lax.axis_index("x")
        self.h = lax.axis_index("h")
        self.y = 2 * self.h + lax.axis_index("l")
        self.step = 1 - 2 * self.c
        self.halves = jnp.stack([512 * self.c, 512 * (1 - self.c)]).astype(jnp.int32)
        z = lax.axis_index("z")
        self.z_order = jnp.stack([lax.rem(z - step + 4, 4) for step in Z_STEPS]).astype(jnp.int32)
        self.blocks = {}
        for first, second in (("x", "y"), ("y", "x")):
            out = []
            for k2 in range(4):
                for k1 in range(4):
                    a, b = self.source(first, k1), self.source(second, k2)
                    out.append(4 * a + b if first == "x" else 4 * b + a)
            self.blocks[first] = jnp.stack(out).astype(jnp.int32)

    def source(self, axis, k):
        at = lax.rem(dict(x=self.x, y=self.y)[axis] - self.step * k + 4, 4)
        if axis == "y":
            at = 2 * lax.rem(at, 2) + lax.div(at, 2)
        return at


SMEM = pl.BlockSpec(memory_space=pltpu.SMEM)


def pinned(value):
    return pltpu.with_memory_space_constraint(value, pltpu.VMEM)


def place_rows(parts, blocks, widths):
    def kernel(blocks_ref, p0, p1, p2, p3, *rest):
        sems = rest[-1]
        copies = []
        for k2, part in enumerate((p0, p1, p2, p3)):
            for k1 in range(4):
                at = pl.multiple_of(blocks_ref[4 * k2 + k1] * 128, 128)
                low = 0
                for i, width in enumerate(widths):
                    copies.append(
                        pltpu.make_async_copy(
                            part.at[pl.ds(128 * k1, 128), pl.ds(low, width)],
                            rest[i].at[pl.ds(at, 128)],
                            sems.at[len(widths) * (4 * k2 + k1) + i],
                        )
                    )
                    low += width
        for copy in copies:
            copy.start()
        for copy in copies:
            copy.wait()

    return pl.pallas_call(
        kernel,
        out_shape=[pltpu.VMEM((D, width), jnp.bfloat16) for width in widths],
        in_specs=[SMEM] + [ANY] * 4,
        out_specs=[WHOLE] * len(widths),
        scratch_shapes=[pltpu.SemaphoreType.DMA((16 * len(widths),))],
        compiler_params=PARAMS,
        cost_estimate=cost(1),
        name="place_rows",
    )(blocks, *parts)


def stepped(value, axis, steps):
    def move(d):
        for _ in range(steps):
            d = along(axis)(d)
        return d

    axes = RING_AXES[axis]
    return lax.ppermute(value, axes, pairs(axes, move))


def chain(block, axis, holds):
    parts = [block]
    for hold in holds:
        part = ring(parts[-1], axis)
        parts.append(part if hold is None else after((part,), hold)[0])
    return parts


def gather_plane(block):
    wide = jnp.broadcast_to(block[None], (16,) + block.shape)
    return lax.all_to_all(wide, ("x", "l", "h"), split_axis=0, concat_axis=0, tiled=True).reshape(D, block.shape[1])


def call(kernel, name, outs, args, flops, scratch=(), limit=VMEM_LIMIT):
    return pl.pallas_call(
        kernel,
        out_shape=outs,
        in_specs=[SMEM if a.dtype == jnp.int32 else WHOLE for a in args],
        out_specs=[WHOLE] * len(outs),
        scratch_shapes=list(scratch),
        compiler_params=pltpu.CompilerParams(vmem_limit_bytes=limit),
        cost_estimate=cost(flops),
        name=name,
    )(*args)


def weight_product(terms, first, me, cuts=1):
    order = jnp.stack([me.source(first, k) for k in PIECES]).astype(jnp.int32)
    n = sum(high - low for _, _, low, high in terms) // cuts
    args = [order]
    for rows, right, _, _ in terms:
        args += [*rows, *right]

    def kernel(order_ref, *refs):
        for p in range(4):
            at = 0
            for t, (_, _, low, high) in enumerate(terms):
                rows, right = refs[4 * t : 4 * t + 2], refs[4 * t + 2 : 4 * t + 4]
                left = []
                for r in rows:
                    lanes = []
                    for j in range(4):
                        block = 4 * order_ref[p] + j if first == "x" else 4 * j + order_ref[p]
                        lanes.append(r[:, pl.ds(pl.multiple_of(block * 128, 128), 128)])
                    left.append(jnp.concatenate(lanes, axis=1))
                for j in range(low, high, 256):
                    end = min(j + 256, high)
                    total = dot(left[0], right[0][:, j:end], 0, 0) + dot(left[1], right[1][:, j:end], 0, 0)
                    out_ref = refs[4 * len(terms) + cuts * p + at // n]
                    out_ref[:, at % n : at % n + end - j] = bf(total)
                    at += end - j

    made = call(kernel, "weight_product", [sds((512, n))] * (4 * cuts), args, 2 * D * SEQ_LEN * n * cuts)
    return [made[cuts * p : cuts * p + cuts] for p in range(4)]


def sum_blocks(parts, order):
    cuts = len(parts[0])
    n = parts[0][0].shape[1]

    def kernel(order_ref, *refs):
        for k in range(4):
            at = pl.ds(pl.multiple_of(order_ref[k] * 128, 128), 128)
            for i in range(cuts):
                total = sum(fl(refs[cuts * j + i][at, :]) for j in range(len(parts)))
                refs[cuts * len(parts) + k][:, n * i : n * i + n] = bf(total)

    args = [order, *[cut for part in parts for cut in part]]
    return call(kernel, "sum_blocks", [sds((128, n * cuts))] * 4, args, 1)


def send_pieces(made, first):
    return [stepped(piece, first, 4 - k) if k else piece for k, piece in zip(PIECES, made)]


def homeward(value, k):
    def move(d):
        y = (2 * d["h"] + d["l"] - k * (1 - 2 * d["c"])) % 4
        d["l"], d["h"], d["c"] = y % 2, d["c"], y // 2
        return d

    axes = ("l", "c", "h")
    return lax.ppermute(value, axes, pairs(axes, move))


def add(one, other):
    count = len(one)

    def kernel(*refs):
        for i in range(count):
            refs[2 * count + i][...] = bf(fl(refs[i][...]) + fl(refs[count + i][...]))

    return call(kernel, "add", [sds(a.shape) for a in one], [*one, *other], 1)


def ring_cuts(cuts, axis):
    return [ring(cut, axis) for cut in cuts]


def second_blocks(parts, first, me):
    second = "y" if first == "x" else "x"
    return sum_blocks(parts, jnp.stack([me.source(second, k) for k in PIECES]).astype(jnp.int32))


def second_stage(blocks, first):
    if first == "x":
        return [homeward(block, k) for k, block in zip(PIECES, blocks)]
    return send_pieces(blocks, "x")


def summed(parts, hold):
    return sum(fl(part) for part in after(parts, hold))


def send_z(block):
    return [z_moved(block, step) if step else block for step in Z_STEPS]


def place_tokens(blocks, me):
    def kernel(order_ref, b0, b1, b2, b3, out_ref):
        for k, ref in enumerate((b0, b1, b2, b3)):
            out_ref[pl.ds(pl.multiple_of(order_ref[k] * 128, 128), 128), :] = ref[...]

    return call(kernel, "place_tokens", [sds((512, D))], [me.z_order, *blocks], 1)[0]


def norm_tokens(blocks, gain, me):
    def kernel(order_ref, b0, b1, b2, b3, gain_ref, out_ref):
        for k, ref in enumerate((b0, b1, b2, b3)):
            x = fl(ref[...])
            inverse = lax.rsqrt(jnp.mean(x * x, axis=1, keepdims=True) + eps)
            out_ref[pl.ds(pl.multiple_of(order_ref[k] * 128, 128), 128), :] = bf(x * inverse * gain_ref[...])

    return call(kernel, "norm_tokens", [sds((512, D))], [me.z_order, *blocks, gain], 1)[0]


def gather_z(wide_block):
    whole = lax.all_to_all(wide_block, "z", split_axis=0, concat_axis=0, tiled=True)
    return whole.reshape(512, whole.shape[2])


def arrive_z(sums):
    parts = sums.reshape(4, 128, sums.shape[1])
    return lax.all_to_all(parts, "z", split_axis=0, concat_axis=0, tiled=True)


def partial_sums(pieces, weights):
    count = len(pieces)

    def kernel(*refs):
        for j in range(0, D, 512):
            total = None
            for i in range(count):
                one = dot(refs[i][...], refs[count + i][j : j + 512, :], 1, 1)
                total = one if total is None else total + one
            refs[-1][:, j : j + 512] = bf(total)

    depth = sum(p.shape[1] for p in pieces)
    return call(kernel, "partial_sums", [sds((512, D))], [*pieces, *map(pinned, weights)], 2 * 512 * depth * D)[0]


def chip_sums(own, other, weights):
    received = sibling(partial_sums(other, weights))
    return bf(fl(partial_sums(own, weights)) + fl(received))


def chip_product(own, other, weight, sibling_weight):
    received = sibling(other)
    m = own.shape[1]

    def kernel(a_ref, b_ref, v_ref, w_ref, out_ref):
        for j in range(0, D, 512):
            here = slice(j, j + 512)
            total = dot(a_ref[...], v_ref[here, :m], 1, 1) + dot(b_ref[...], w_ref[here, :m], 1, 1)
            out_ref[:, here] = bf(total)

    args = [own, received, weight, sibling_weight]
    return call(kernel, "chip_product", [sds((512, D))], args, 4 * 512 * m * D)[0]


def project(rows, weights, dtype, width=None):
    width = width or weights[0].shape[1]
    n = width * len(weights)

    def kernel(rows_ref, *refs):
        for i, w_ref in enumerate(refs[:-1]):
            for j in range(0, width, 256):
                product = dot(rows_ref[...], w_ref[:, j : j + 256], 1, 0)
                refs[-1][:, i * width + j : i * width + j + 256] = product.astype(dtype)

    return call(kernel, "project", [sds((512, n), dtype)], [rows, *weights], 2 * 512 * D * n)[0]


def down_products(rows, weights):
    def kernel(rows_ref, w0, w1, out_ref):
        for j in range(0, D, 512):
            here = slice(j, j + 512)
            total = dot(rows_ref[:, :512], w0[here, :], 1, 1) + dot(rows_ref[:, 512:], w1[here, :], 1, 1)
            out_ref[:, here] = bf(total)

    return call(kernel, "down_products", [sds((512, D))], [rows, *map(pinned, weights)], 2 * 512 * 1024 * D)[0]


def rope(u, cosine, sine):
    lane = lax.broadcasted_iota(jnp.int32, u.shape, 1)
    turned = jnp.where(lane % DH < DH // 2, pltpu.roll(u, 96, 1), pltpu.roll(u, 32, 1))
    return u * cosine + turned * sine


def rope_three(u, cosine, sine):
    lane = lax.broadcasted_iota(jnp.int32, cosine.shape, 1)
    last = u[:, 256:]
    return jnp.concatenate(
        [
            rope(u[:, :128], cosine, sine),
            rope(u[:, 128:256], cosine, sine),
            jnp.where(lane < DH, rope(last, cosine, sine), last),
        ],
        axis=1,
    )


def half_at(halves_ref, i):
    return pl.ds(pl.multiple_of(halves_ref[i], 512), 512)


def project_qkv(i, rows, weight, tables, halves):
    def kernel(halves_ref, rows_ref, w_ref, cos_ref, sin_ref, out_ref):
        here = half_at(halves_ref, i)
        product = dot(rows_ref[...], w_ref[:, :384], 1, 0)
        out_ref[...] = bf(rope_three(product, cos_ref[here, :], sin_ref[here, :]))

    args = [halves, rows, weight, *tables]
    return call(kernel, "project_qkv", [sds((512, 384))], args, 2 * 512 * D * 384)[0]


def scores_t(keys, query, q_at):
    s = dot(keys, query, 1, 1)
    key = lax.broadcasted_iota(jnp.int32, (256, 256), 0)
    column = lax.broadcasted_iota(jnp.int32, (256, 256), 1)
    diagonal = jnp.where(key <= column, s[q_at:], -1e30)
    return diagonal if q_at == 0 else jnp.concatenate([s[:q_at], diagonal], axis=0)


def attend(qkv, halves):
    def kernel(halves_ref, q0, q1, own_ref, other_ref, nat_ref, lse_ref, att_ref):
        nat_ref[half_at(halves_ref, 0), :] = q0[...]
        nat_ref[half_at(halves_ref, 1), :] = q1[...]
        kv = nat_ref[:, 256:]
        keys = kv[:, :DH]
        values_t = kv.T[DH:]
        lse_ref[...] = jnp.zeros_like(lse_ref)
        for q_at in range(0, SEQ_LEN, 256):
            end = q_at + 256
            for pair in range(2):
                two = nat_ref[q_at:end, 128 * pair : 128 * pair + 128]
                outs = []
                for i in range(2):
                    s = scores_t(keys[:end], two[:, DH * i : DH * i + DH], q_at)
                    top = jnp.max(s, axis=0, keepdims=True)
                    p = jnp.exp2((s - top) * SCALE2)
                    total = jnp.sum(p, axis=0, keepdims=True)
                    outs.append(dot(values_t[:, :end], bf(p), 1, 0) / total)
                    g = 2 * pair + i
                    lse_ref[g : g + 1, q_at:end] = top * SCALE2 + jnp.log2(total)
                att_ref[q_at:end, 128 * pair : 128 * pair + 128] = bf(jnp.concatenate(outs, axis=0).T)
        own_ref[...] = att_ref[half_at(halves_ref, 0), :]
        other_ref[...] = att_ref[half_at(halves_ref, 1), :]

    outs = [sds((512, 256)), sds((512, 256)), sds((SEQ_LEN, 384)), sds((8, SEQ_LEN), jnp.float32)]
    scratch = [pltpu.VMEM((SEQ_LEN, 256), jnp.bfloat16)]
    return call(kernel, "attend", outs, [halves, *qkv], 20e9, scratch)


def attend_backward(qkv, lse, grad_out, tables, halves):
    def kernel(halves_ref, nat_ref, lse_ref, g0, g1, cos_ref, sin_ref, own_ref, other_ref, go_nat, kv_sum, d_nat):
        go_nat[half_at(halves_ref, 0), :] = g0[...]
        go_nat[half_at(halves_ref, 1), :] = g1[...]
        kv = nat_ref[:, 256:]
        keys = kv[:, :DH]
        values = kv[:, DH:]
        keys_t = kv.T[:DH]
        kv_sum[...] = jnp.zeros_like(kv_sum)
        for q_at in range(0, SEQ_LEN, 256):
            end = q_at + 256
            cosine = cos_ref[q_at:end, :]
            sine = -sin_ref[q_at:end, :]
            for pair in range(2):
                lanes = slice(128 * pair, 128 * pair + 128)
                two = nat_ref[q_at:end, lanes]
                two_grad = go_nat[q_at:end, lanes]
                outs = []
                for i in range(2):
                    query = two[:, DH * i : DH * i + DH]
                    grad = two_grad[:, DH * i : DH * i + DH]
                    g = 2 * pair + i
                    s = scores_t(keys[:end], query, q_at)
                    p = jnp.exp2(s * SCALE2 - lse_ref[g : g + 1, q_at:end])
                    dp = dot(values[:end], grad, 1, 1)
                    delta = jnp.sum(dp * p, axis=0, keepdims=True)
                    ds = bf(p * (dp - delta))
                    kv_sum[:end, :] += jnp.concatenate(
                        [dot(ds, query, 1, 0), dot(bf(p), grad, 1, 0)], axis=1
                    )
                    outs.append(dot(keys_t[:, :end], ds, 1, 0))
                d_query = jnp.concatenate(outs, axis=0).T * SCALE
                d_nat[q_at:end, lanes] = bf(rope(d_query, cosine, sine))
        lane = lax.broadcasted_iota(jnp.int32, (SEQ_LEN, 128), 1)
        total = kv_sum[...]
        turned = rope(total * SCALE, cos_ref[...], -sin_ref[...])
        d_nat[:, 256:] = bf(jnp.where(lane < DH, turned, total))
        own_ref[...] = d_nat[half_at(halves_ref, 0), :]
        other_ref[...] = d_nat[half_at(halves_ref, 1), :]

    scratch = [
        pltpu.VMEM((SEQ_LEN, 256), jnp.bfloat16),
        pltpu.VMEM((SEQ_LEN, 128), jnp.float32),
        pltpu.VMEM((SEQ_LEN, 384), jnp.bfloat16),
    ]
    args = [halves, qkv, lse, *grad_out, *tables]
    return call(kernel, "attend_backward", [sds((512, 384))] * 2, args, 30e9, scratch)


def mlp_step(rows, w_gate, w_up, grad_act):
    width = w_gate.shape[1]

    def kernel(rows_ref, g_ref, u_ref, ga_ref, act_ref, gg_ref, gu_ref):
        for j in range(0, width, 256):
            here = slice(j, j + 256)
            gate = dot(rows_ref[...], g_ref[:, here], 1, 0)
            up = dot(rows_ref[...], u_ref[:, here], 1, 0)
            sig = jax.nn.sigmoid(gate)
            silu = gate * sig
            ga = fl(ga_ref[:, here])
            act_ref[:, here] = bf(silu * up)
            gg_ref[:, here] = bf(ga * up * sig * (1.0 + gate * (1.0 - sig)))
            gu_ref[:, here] = bf(ga * silu)

    args = [rows, pinned(w_gate), pinned(w_up), grad_act]
    return call(kernel, "mlp_step", [sds((512, width))] * 3, args, 4 * 512 * D * width)


def frequencies(head_size):
    pair_index = jnp.arange(head_size // 2).astype(jnp.float32)
    base_freq = 500000.0 ** (-2.0 * pair_index / head_size)
    wavelen = 2.0 * jnp.pi / base_freq
    smooth = (8192.0 / wavelen - 1.0) / 3.0
    blended = (1.0 - smooth) * base_freq / 32.0 + smooth * base_freq
    return jnp.where(
        wavelen < 2048.0, base_freq, jnp.where(wavelen > 8192.0, base_freq / 32.0, blended)
    )


LONG = 60e9


def wide(out_ref, value):
    for k in range(4):
        out_ref[k] = value


def arrived_sum(ref):
    return fl(ref[0]) + fl(ref[1]) + fl(ref[2]) + fl(ref[3])


def mlp_norm(inputs, arrived, gain):
    def kernel(x_ref, a_ref, gain_ref, residual_ref, out_ref):
        residual = fl(x_ref[...]) + arrived_sum(a_ref)
        residual_ref[...] = residual
        inverse = lax.rsqrt(jnp.mean(residual * residual, axis=1, keepdims=True) + eps)
        wide(out_ref, bf(residual * inverse * gain_ref[...]))

    outs = [sds((128, D), jnp.float32), sds((4, 128, D))]
    return call(kernel, "mlp_norm", outs, [inputs, arrived, gain], LONG)


def norm_grad(grad, values, gain):
    inverse = lax.rsqrt(jnp.mean(values * values, axis=1, keepdims=True) + eps)
    unit = values * inverse
    scaled = grad * gain
    return inverse * (scaled - unit * jnp.mean(scaled * unit, axis=1, keepdims=True))


def mlp_norm_backward(upstream, arrived, residual, gain):
    def kernel(g_ref, a_ref, r_ref, gain_ref, grad_ref, out_ref):
        grad = fl(g_ref[...]) + norm_grad(arrived_sum(a_ref), r_ref[...], gain_ref[...])
        grad_ref[...] = grad
        wide(out_ref, bf(grad))

    outs = [sds((128, D), jnp.float32), sds((4, 128, D))]
    return call(kernel, "mlp_norm_backward", outs, [upstream, arrived, residual, gain], LONG)


def attn_norm_backward(grad_residual, arrived, inputs, gain):
    def kernel(g_ref, a_ref, x_ref, gain_ref, out_ref):
        out_ref[...] = bf(g_ref[...] + norm_grad(arrived_sum(a_ref), fl(x_ref[...]), gain_ref[...]))

    return call(kernel, "attn_norm_backward", [sds((128, D))], [grad_residual, arrived, inputs, gain], LONG)[0]


def layer_output(residual, arrived):
    def kernel(r_ref, a_ref, out_ref):
        out_ref[...] = bf(r_ref[...] + arrived_sum(a_ref))

    return call(kernel, "layer_output", [sds((128, D))], [residual, arrived], 1)[0]


def on_device(
    tokens, positions, w_query, w_key, w_value, w_out, attn_gain, w_gate, w_up, w_down, mlp_gain, cotangent
):
    me = Place()
    inputs_b = swapped(tokens)
    places = jnp.concatenate([(positions // 256).reshape(128, 8), (positions % 256).reshape(128, 8)], axis=1)
    extra = jnp.concatenate([attn_gain[:, None], mlp_gain[:, None], bf(places)], axis=1)
    extra = jnp.pad(extra, ((0, 0), (0, 110)))
    part_attn = swapped(jnp.concatenate([w_query, w_key, w_value, extra, w_out.T], axis=1))
    part_attn, inputs_b = lax.optimization_barrier((part_attn, inputs_b))

    blocks_in = send_z(inputs_b)
    w_qkv = gather_plane(part_attn[:, :512])
    w_gate, w_up, w_down, cotangent = after((w_gate, w_up, w_down, cotangent), inputs_b)
    upstream = swapped(cotangent)
    down_rows = w_down.T
    part_ab = swapped(jnp.concatenate([w_gate, down_rows[:, :512], w_up, down_rows[:, 512:]], axis=1))

    place = fl(part_attn[:, 386:402])
    seq_positions = (256.0 * place[:, :8] + place[:, 8:]).reshape(SEQ_LEN)
    freq = jnp.tile(frequencies(DH), 4)
    angles = seq_positions[:, None] * freq[None, :]
    sign = jnp.where(jnp.arange(128) % DH < DH // 2, -1.0, 1.0)
    tables = (jnp.cos(angles), jnp.sin(angles) * sign[None, :])
    pick = bf(jnp.arange(128)[None, :] == jnp.arange(8)[:, None])
    gain_rows = dot(pick, w_qkv[:, 384:], 1, 1)
    gain_attn, gain_mlp = gain_rows[:1], gain_rows[1:2]

    blocks_in = after(blocks_in, *tables, upstream, part_ab)
    own_normed = norm_tokens(blocks_in, gain_attn, me)
    normed_attn = [own_normed, sibling(own_normed)]
    own_qkv = project_qkv(0, normed_attn[0], w_qkv, tables, me.halves)
    projected = [own_qkv, project_qkv(1, normed_attn[1], w_qkv, tables, me.halves)]

    (own_up,) = after((upstream,), own_normed)
    blocks_up = send_z(own_up)
    (part_out,) = after((part_attn[:, 512:],), own_qkv)
    w_out_t = gather_plane(part_out)

    projected = after(projected, *blocks_up[1:3])
    attended, other_attended, qkv, lse = attend(projected, me.halves)
    (w_out_t,) = after((w_out_t,), attended, blocks_up[3])
    out_sums = chip_product(attended, other_attended, w_out_t, sibling(w_out_t))
    (out_sums,) = after((out_sums,), *blocks_up)

    (part_ab,) = after((part_ab,), own_normed)
    part_a, part_b = part_ab[:, :1536], part_ab[:, 1536:]
    holds = (attended, out_sums, None)
    stage_a, stage_b = (jnp.concatenate(chain(p, axis, holds), axis=0) for p, axis in ((part_a, "x"), (part_b, "y")))

    own_up = place_tokens(blocks_up, me)
    rows_up = [own_up, sibling(own_up)]
    arrived = arrive_z(out_sums)

    parts_a, parts_b = chain(stage_a, "y", (None, None, None)), chain(stage_b, "x", (None, None, None))
    full_gate, down_a = place_rows(parts_a, me.blocks["x"], (1024, 512))
    full_up, down_b = place_rows(parts_b, me.blocks["y"], (1024, 512))
    full_down = [down_a, down_b]

    (arrived,) = after((arrived,), parts_a[2], parts_b[2], *rows_up)
    residual, normed_mlp = mlp_norm(inputs_b, arrived, gain_mlp)
    own_mlp = gather_z(normed_mlp)
    up_held = after(rows_up, normed_mlp)
    grad_act = [project(r, [pinned(w) for w in full_down], jnp.bfloat16) for r in up_held]
    (own_mlp,) = after((own_mlp,), full_gate, full_up, grad_act[0])
    rows_mlp = [own_mlp, sibling(own_mlp)]
    steps = [mlp_step(r, full_gate, full_up, g) for r, g in zip(rows_mlp, grad_act)]
    activated, grad_gate_pre, grad_up_pre = zip(*steps)

    gate_up = list(zip(grad_gate_pre, grad_up_pre))
    mlp_sums = chip_sums(gate_up[0], gate_up[1], [full_gate, full_up])
    arrived = arrive_z(mlp_sums)

    gg, gu = after((grad_gate_pre, grad_up_pre), mlp_sums)
    made_a = weight_product([(rows_mlp, gg, 0, 1024), (rows_up, activated, 0, 512)], "x", me, 2)
    made_b = weight_product([(rows_mlp, gu, 0, 1024), (rows_up, activated, 512, 1024)], "y", me, 2)
    sums = [made_a[0], made_b[0]]
    rings = [ring_cuts(total, axis) for total, axis in zip(sums, "xy")]
    acts = after(activated, made_a[-1][0], made_b[-1][0])
    down_other = down_products(acts[1], full_down)
    down_own = down_products(acts[0], full_down)
    (arrived,) = after((arrived,), down_own)
    grad_residual, grad_residual_b = mlp_norm_backward(upstream, arrived, residual, gain_mlp)

    own_gr = gather_z(grad_residual_b)
    (down_arrived,) = after((sibling(down_other),), grad_residual_b)
    down_sums = bf(fl(down_own) + fl(down_arrived))
    rings = [after(cuts, down_sums) for cuts in rings]
    sums = [add(received, made[1]) for received, made in zip(rings, (made_a, made_b))]
    rings = [ring_cuts(total, axis) for total, axis in zip(sums, "xy")]
    (own_gr,) = after((own_gr,), down_sums, *rings[0], *rings[1])
    rows_gr = [own_gr, sibling(own_gr)]
    rings = [after(cuts, own_gr) for cuts in rings]
    sums = [add(received, made[2]) for received, made in zip(rings, (made_a, made_b))]
    rings = [ring_cuts(total, axis) for total, axis in zip(sums, "xy")]
    (down_sums,) = after((down_sums,), sums[0][0], sums[1][0])
    arrived = arrive_z(down_sums)
    grad_attended = [project(r, [w_out_t], jnp.bfloat16) for r in after(rows_gr, sums[0][0], sums[1][0])]
    grad_qkv, other_grad_qkv = attend_backward(qkv, lse, grad_attended, tables, me.halves)
    blocks_a = second_blocks([after(rings[0], grad_qkv), made_a[3]], "x", me)
    parts_a = second_stage(blocks_a, "x")
    attn_sums = chip_product(grad_qkv, other_grad_qkv, w_qkv, sibling(w_qkv))
    (attn_sums,) = after((attn_sums,), arrived, blocks_a[0])
    grad_arrived = arrive_z(attn_sums)

    d_qkv = after((grad_qkv, other_grad_qkv), attn_sums)
    made_in = weight_product([(normed_attn, d_qkv, 0, 384)], "x", me)
    sent_in = send_pieces([cut for (cut,) in made_in], "x")
    att = after((attended, other_attended), *made_in[-1])
    made_out = weight_product([(rows_gr, att, 0, 256)], "y", me)
    blocks_b = second_blocks([after(rings[1], *made_out[-1]), made_b[3]], "y", me)
    (arrived,) = after((arrived,), blocks_b[0])
    layer_out = layer_output(residual, arrived)
    share_a = summed(parts_a, layer_out)
    parts_b = second_stage(after(blocks_b, share_a), "y")
    (grad_arrived,) = after((grad_arrived,), share_a)
    grad_tokens = attn_norm_backward(grad_residual, grad_arrived, inputs_b, gain_attn)
    blocks_in = second_blocks([[part] for part in after(sent_in, grad_tokens)], "x", me)
    share_in = summed(second_stage(blocks_in, "x"), grad_tokens)
    sent_out = send_pieces(after([cut for (cut,) in made_out], grad_tokens), "y")
    share_b = fl(swapped(bf(summed(parts_b, grad_tokens))))
    blocks_out = second_blocks([[part] for part in after(sent_out, grad_tokens)], "y", me)
    share_out = fl(swapped(bf(summed(second_stage(blocks_out, "y"), grad_tokens))))

    def gain_sum(*terms):
        return sum(jnp.sum(fl(w) * g, axis=1) for w, g in terms)

    gain_sums = jnp.stack(
        [
            gain_sum((jnp.concatenate([w_query, w_key, w_value], axis=1), share_in)),
            gain_sum((w_gate, share_a[:, :1024]), (w_up, share_b[:, :1024])),
        ]
    )
    gain_sums = gain_sums / fl(jnp.stack([attn_gain, mlp_gain]))
    gain_sums = gain_sums + z_moved(gain_sums, 1) + z_moved(gain_sums, 2) + z_moved(gain_sums, 3)
    gain_sums = gain_sums + h_flipped(gain_sums)
    return (
        swapped(layer_out),
        swapped(grad_tokens),
        share_in[:, :256],
        share_in[:, 256:320],
        share_in[:, 320:384],
        share_out.T,
        gain_sums[0],
        share_a[:, :1024],
        share_b[:, :1024],
        jnp.concatenate([share_a[:, 1024:], share_b[:, 1024:]], axis=1).T,
        gain_sums[1],
    )


def solution(mesh):
    split = Mesh(mesh.devices.reshape(4, 2, 2, 2, 4), AXES)
    dp, tensor = ("x", "l", "c"), ("h", "z")
    both = P(AXES, None)
    weight, turned, vector = P(dp, tensor), P(tensor, dp), P(dp)
    in_specs = (
        both, vector, weight, weight, weight, turned, vector, weight, weight, turned, vector, both,
    )
    out_specs = (
        both, both, weight, weight, weight, turned, vector, weight, weight, turned, vector,
    )
    return jax.shard_map(on_device, mesh=split, in_specs=in_specs, out_specs=out_specs, check_vma=False)
```

```python
import functools
import itertools
import math

import jax
import jax.numpy as jnp
from jax import lax
from jax.experimental import pallas as pl
from jax.experimental.pallas import tpu as pltpu
from jax.sharding import Mesh, PartitionSpec as P

H = 32
KV = 8
DH = 64
SEQ_LEN = 1024
D = 2048
eps = 1e-05

SIZES = dict(x=4, l=2, c=2, h=2, z=4)
AXES = ("x", "l", "c", "h", "z")

SCALE = DH ** (-0.5)
SCALE2 = SCALE * math.log2(math.e)
VMEM_LIMIT = 12 * 1024 * 1024


def pairs(axes, move):
    def place(index):
        at = 0
        for a in axes:
            at = at * SIZES[a] + index[a]
        return at

    out = []
    for index in itertools.product(*[range(SIZES[a]) for a in axes]):
        here = dict(zip(axes, index))
        out.append((place(here), place(move(dict(here)))))
    return out


def to_swapped(d):
    d["c"], d["h"] = d["h"], d["c"]
    return d


def to_sibling(d):
    d["c"] = 1 - d["c"]
    return d


def along(axis):
    def move(d):
        step = 1 - 2 * d["c"]
        if axis == "y":
            y = (2 * d["h"] + d["l"] + step) % 4
            d["h"], d["l"] = y // 2, y % 2
        else:
            d[axis] = (d[axis] + step) % 4
        return d

    return move


RING_AXES = dict(x=("x", "c"), y=("l", "c", "h"))
Z_STEPS = (0, 1, 3, 2)
PIECES = (1, 2, 3, 0)


def ring(value, axis):
    axes = RING_AXES[axis]
    return lax.ppermute(value, axes, pairs(axes, along(axis)))


def swapped(value):
    return lax.ppermute(value, ("c", "h"), pairs(("c", "h"), to_swapped))


def sibling(value):
    return lax.ppermute(value, ("c",), pairs(("c",), to_sibling))


def z_moved(value, step):
    def move(d):
        d["z"] = (d["z"] + step) % 4
        return d

    return lax.ppermute(value, ("z",), pairs(("z",), move))


def h_flipped(value):
    def move(d):
        d["h"] = 1 - d["h"]
        return d

    return lax.ppermute(value, ("h",), pairs(("h",), move))


def after(values, *earlier):
    held = lax.optimization_barrier((tuple(values), tuple(earlier)))
    return held[0]


def dot(a, b, ca, cb):
    return lax.dot_general(a, b, (((ca,), (cb,)), ((), ())), preferred_element_type=jnp.float32)


def bf(v):
    return v.astype(jnp.bfloat16)


def fl(v):
    return v.astype(jnp.float32)


def sds(shape, dtype=jnp.bfloat16):
    return jax.ShapeDtypeStruct(shape, dtype)


def cost(flops):
    return pl.CostEstimate(flops=int(flops), bytes_accessed=1, transcendentals=0)


PARAMS = pltpu.CompilerParams(vmem_limit_bytes=VMEM_LIMIT)
ANY = pl.BlockSpec(memory_space=pl.ANY)
WHOLE = pl.BlockSpec(memory_space=pltpu.VMEM)


class Place:
    def __init__(self):
        self.c = lax.axis_index("c")
        self.x = lax.axis_index("x")
        self.h = lax.axis_index("h")
        self.y = 2 * self.h + lax.axis_index("l")
        self.step = 1 - 2 * self.c
        self.halves = jnp.stack([512 * self.c, 512 * (1 - self.c)]).astype(jnp.int32)
        z = lax.axis_index("z")
        self.z_order = jnp.stack([lax.rem(z - step + 4, 4) for step in Z_STEPS]).astype(jnp.int32)
        self.blocks = {}
        for first, second in (("x", "y"), ("y", "x")):
            out = []
            for k2 in range(4):
                for k1 in range(4):
                    a, b = self.source(first, k1), self.source(second, k2)
                    out.append(4 * a + b if first == "x" else 4 * b + a)
            self.blocks[first] = jnp.stack(out).astype(jnp.int32)

    def source(self, axis, k):
        at = lax.rem(dict(x=self.x, y=self.y)[axis] - self.step * k + 4, 4)
        if axis == "y":
            at = 2 * lax.rem(at, 2) + lax.div(at, 2)
        return at


SMEM = pl.BlockSpec(memory_space=pltpu.SMEM)


def pinned(value):
    return pltpu.with_memory_space_constraint(value, pltpu.VMEM)


def place_rows(parts, blocks, widths):
    def kernel(blocks_ref, p0, p1, p2, p3, *rest):
        sems = rest[-1]
        copies = []
        for k2, part in enumerate((p0, p1, p2, p3)):
            for k1 in range(4):
                at = pl.multiple_of(blocks_ref[4 * k2 + k1] * 128, 128)
                low = 0
                for i, width in enumerate(widths):
                    copies.append(
                        pltpu.make_async_copy(
                            part.at[pl.ds(128 * k1, 128), pl.ds(low, width)],
                            rest[i].at[pl.ds(at, 128)],
                            sems.at[len(widths) * (4 * k2 + k1) + i],
                        )
                    )
                    low += width
        for copy in copies:
            copy.start()
        for copy in copies:
            copy.wait()

    return pl.pallas_call(
        kernel,
        out_shape=[pltpu.VMEM((D, width), jnp.bfloat16) for width in widths],
        in_specs=[SMEM] + [ANY] * 4,
        out_specs=[WHOLE] * len(widths),
        scratch_shapes=[pltpu.SemaphoreType.DMA((16 * len(widths),))],
        compiler_params=PARAMS,
        cost_estimate=cost(1),
        name="place_rows",
    )(blocks, *parts)


def stepped(value, axis, steps):
    def move(d):
        for _ in range(steps):
            d = along(axis)(d)
        return d

    axes = RING_AXES[axis]
    return lax.ppermute(value, axes, pairs(axes, move))


def chain(block, axis, holds):
    parts = [block]
    for hold in holds:
        part = ring(parts[-1], axis)
        parts.append(part if hold is None else after((part,), hold)[0])
    return parts


def gather_plane(block):
    wide = jnp.broadcast_to(block[None], (16,) + block.shape)
    return lax.all_to_all(wide, ("x", "l", "h"), split_axis=0, concat_axis=0, tiled=True).reshape(D, block.shape[1])


def call(kernel, name, outs, args, flops, scratch=(), limit=VMEM_LIMIT):
    return pl.pallas_call(
        kernel,
        out_shape=outs,
        in_specs=[SMEM if a.dtype == jnp.int32 else WHOLE for a in args],
        out_specs=[WHOLE] * len(outs),
        scratch_shapes=list(scratch),
        compiler_params=pltpu.CompilerParams(vmem_limit_bytes=limit),
        cost_estimate=cost(flops),
        name=name,
    )(*args)


def weight_product(terms, first, me, cuts=1):
    order = jnp.stack([me.source(first, k) for k in PIECES]).astype(jnp.int32)
    n = sum(high - low for _, _, low, high in terms) // cuts
    args = [order]
    for rows, right, _, _ in terms:
        args += [*rows, *right]

    def kernel(order_ref, *refs):
        for p in range(4):
            at = 0
            for t, (_, _, low, high) in enumerate(terms):
                rows, right = refs[4 * t : 4 * t + 2], refs[4 * t + 2 : 4 * t + 4]
                left = []
                for r in rows:
                    lanes = []
                    for j in range(4):
                        block = 4 * order_ref[p] + j if first == "x" else 4 * j + order_ref[p]
                        lanes.append(r[:, pl.ds(pl.multiple_of(block * 128, 128), 128)])
                    left.append(jnp.concatenate(lanes, axis=1))
                for j in range(low, high, 256):
                    end = min(j + 256, high)
                    total = dot(left[0], right[0][:, j:end], 0, 0) + dot(left[1], right[1][:, j:end], 0, 0)
                    out_ref = refs[4 * len(terms) + cuts * p + at // n]
                    out_ref[:, at % n : at % n + end - j] = bf(total)
                    at += end - j

    made = call(kernel, "weight_product", [sds((512, n))] * (4 * cuts), args, 2 * D * SEQ_LEN * n * cuts)
    return [made[cuts * p : cuts * p + cuts] for p in range(4)]


def sum_blocks(parts, order):
    cuts = len(parts[0])
    n = parts[0][0].shape[1]

    def kernel(order_ref, *refs):
        for k in range(4):
            at = pl.ds(pl.multiple_of(order_ref[k] * 128, 128), 128)
            for i in range(cuts):
                total = sum(fl(refs[cuts * j + i][at, :]) for j in range(len(parts)))
                refs[cuts * len(parts) + k][:, n * i : n * i + n] = bf(total)

    args = [order, *[cut for part in parts for cut in part]]
    return call(kernel, "sum_blocks", [sds((128, n * cuts))] * 4, args, 1)


def send_pieces(made, first):
    return [stepped(piece, first, 4 - k) if k else piece for k, piece in zip(PIECES, made)]


def homeward(value, k):
    def move(d):
        y = (2 * d["h"] + d["l"] - k * (1 - 2 * d["c"])) % 4
        d["l"], d["h"], d["c"] = y % 2, d["c"], y // 2
        return d

    axes = ("l", "c", "h")
    return lax.ppermute(value, axes, pairs(axes, move))


def add(one, other):
    count = len(one)

    def kernel(*refs):
        for i in range(count):
            refs[2 * count + i][...] = bf(fl(refs[i][...]) + fl(refs[count + i][...]))

    return call(kernel, "add", [sds(a.shape) for a in one], [*one, *other], 1)


def ring_cuts(cuts, axis):
    return [ring(cut, axis) for cut in cuts]


def second_blocks(parts, first, me):
    second = "y" if first == "x" else "x"
    return sum_blocks(parts, jnp.stack([me.source(second, k) for k in PIECES]).astype(jnp.int32))


def second_stage(blocks, first):
    if first == "x":
        return [homeward(block, k) for k, block in zip(PIECES, blocks)]
    return send_pieces(blocks, "x")


def summed(parts, hold):
    return sum(fl(part) for part in after(parts, hold))


def send_z(block):
    return [z_moved(block, step) if step else block for step in Z_STEPS]


def place_tokens(blocks, me):
    def kernel(order_ref, b0, b1, b2, b3, out_ref):
        for k, ref in enumerate((b0, b1, b2, b3)):
            out_ref[pl.ds(pl.multiple_of(order_ref[k] * 128, 128), 128), :] = ref[...]

    return call(kernel, "place_tokens", [sds((512, D))], [me.z_order, *blocks], 1)[0]


def norm_tokens(blocks, gain, me):
    def kernel(order_ref, b0, b1, b2, b3, gain_ref, out_ref):
        for k, ref in enumerate((b0, b1, b2, b3)):
            x = fl(ref[...])
            inverse = lax.rsqrt(jnp.mean(x * x, axis=1, keepdims=True) + eps)
            out_ref[pl.ds(pl.multiple_of(order_ref[k] * 128, 128), 128), :] = bf(x * inverse * gain_ref[...])

    return call(kernel, "norm_tokens", [sds((512, D))], [me.z_order, *blocks, gain], 1)[0]


def gather_z(wide_block):
    whole = lax.all_to_all(wide_block, "z", split_axis=0, concat_axis=0, tiled=True)
    return whole.reshape(512, whole.shape[2])


def arrive_z(sums):
    parts = sums.reshape(4, 128, sums.shape[1])
    return lax.all_to_all(parts, "z", split_axis=0, concat_axis=0, tiled=True)


def partial_sums(pieces, weights):
    count = len(pieces)

    def kernel(*refs):
        for j in range(0, D, 512):
            total = None
            for i in range(count):
                one = dot(refs[i][...], refs[count + i][j : j + 512, :], 1, 1)
                total = one if total is None else total + one
            refs[-1][:, j : j + 512] = bf(total)

    depth = sum(p.shape[1] for p in pieces)
    return call(kernel, "partial_sums", [sds((512, D))], [*pieces, *map(pinned, weights)], 2 * 512 * depth * D)[0]


def chip_sums(own, other, weights):
    received = sibling(partial_sums(other, weights))
    return bf(fl(partial_sums(own, weights)) + fl(received))


def chip_product(own, other, weight, sibling_weight):
    received = sibling(other)
    m = own.shape[1]

    def kernel(a_ref, b_ref, v_ref, w_ref, out_ref):
        for j in range(0, D, 512):
            here = slice(j, j + 512)
            total = dot(a_ref[...], v_ref[here, :m], 1, 1) + dot(b_ref[...], w_ref[here, :m], 1, 1)
            out_ref[:, here] = bf(total)

    args = [own, received, weight, sibling_weight]
    return call(kernel, "chip_product", [sds((512, D))], args, 4 * 512 * m * D)[0]


def project(rows, weights, dtype, width=None):
    width = width or weights[0].shape[1]
    n = width * len(weights)

    def kernel(rows_ref, *refs):
        for i, w_ref in enumerate(refs[:-1]):
            for j in range(0, width, 256):
                product = dot(rows_ref[...], w_ref[:, j : j + 256], 1, 0)
                refs[-1][:, i * width + j : i * width + j + 256] = product.astype(dtype)

    return call(kernel, "project", [sds((512, n), dtype)], [rows, *weights], 2 * 512 * D * n)[0]


def down_products(rows, weights):
    def kernel(rows_ref, w0, w1, *out_refs):
        for j in range(0, D, 512):
            here = slice(j, j + 512)
            total = dot(rows_ref[:, :512], w0[here, :], 1, 1) + dot(rows_ref[:, 512:], w1[here, :], 1, 1)
            out_refs[j // 1024][:, j % 1024 : j % 1024 + 512] = bf(total)

    args = [rows, *map(pinned, weights)]
    return call(kernel, "down_products", [sds((512, D // 2))] * 2, args, 2 * 512 * 1024 * D)


def join_sums(one, other):
    def kernel(a0, a1, b0, b1, out_ref):
        out_ref[:, :1024] = bf(fl(a0[...]) + fl(b0[...]))
        out_ref[:, 1024:] = bf(fl(a1[...]) + fl(b1[...]))

    return call(kernel, "join_sums", [sds((512, D))], [*one, *other], 1)[0]


def rope(u, cosine, sine):
    lane = lax.broadcasted_iota(jnp.int32, u.shape, 1)
    turned = jnp.where(lane % DH < DH // 2, pltpu.roll(u, 96, 1), pltpu.roll(u, 32, 1))
    return u * cosine + turned * sine


def rope_three(u, cosine, sine):
    lane = lax.broadcasted_iota(jnp.int32, cosine.shape, 1)
    last = u[:, 256:]
    return jnp.concatenate(
        [
            rope(u[:, :128], cosine, sine),
            rope(u[:, 128:256], cosine, sine),
            jnp.where(lane < DH, rope(last, cosine, sine), last),
        ],
        axis=1,
    )


def half_at(halves_ref, i):
    return pl.ds(pl.multiple_of(halves_ref[i], 512), 512)


def project_qkv(i, rows, weight, tables, halves):
    def kernel(halves_ref, rows_ref, w_ref, cos_ref, sin_ref, out_ref):
        here = half_at(halves_ref, i)
        product = dot(rows_ref[...], w_ref[:, :384], 1, 0)
        out_ref[...] = bf(rope_three(product, cos_ref[here, :], sin_ref[here, :]))

    args = [halves, rows, weight, *tables]
    return call(kernel, "project_qkv", [sds((512, 384))], args, 2 * 512 * D * 384)[0]


def scores_t(keys, query, q_at):
    s = dot(keys, query, 1, 1)
    key = lax.broadcasted_iota(jnp.int32, (256, 256), 0)
    column = lax.broadcasted_iota(jnp.int32, (256, 256), 1)
    diagonal = jnp.where(key <= column, s[q_at:], -1e30)
    return diagonal if q_at == 0 else jnp.concatenate([s[:q_at], diagonal], axis=0)


def attend(qkv, halves):
    def kernel(halves_ref, q0, q1, own_ref, other_ref, nat_ref, lse_ref, att_ref):
        nat_ref[half_at(halves_ref, 0), :] = q0[...]
        nat_ref[half_at(halves_ref, 1), :] = q1[...]
        kv = nat_ref[:, 256:]
        keys = kv[:, :DH]
        values_t = kv.T[DH:]
        lse_ref[...] = jnp.zeros_like(lse_ref)
        for q_at in range(0, SEQ_LEN, 256):
            end = q_at + 256
            for pair in range(2):
                two = nat_ref[q_at:end, 128 * pair : 128 * pair + 128]
                outs = []
                for i in range(2):
                    s = scores_t(keys[:end], two[:, DH * i : DH * i + DH], q_at)
                    top = jnp.max(s, axis=0, keepdims=True)
                    p = jnp.exp2((s - top) * SCALE2)
                    total = jnp.sum(p, axis=0, keepdims=True)
                    outs.append(dot(values_t[:, :end], bf(p), 1, 0) / total)
                    g = 2 * pair + i
                    lse_ref[g : g + 1, q_at:end] = top * SCALE2 + jnp.log2(total)
                att_ref[q_at:end, 128 * pair : 128 * pair + 128] = bf(jnp.concatenate(outs, axis=0).T)
        own_ref[...] = att_ref[half_at(halves_ref, 0), :]
        other_ref[...] = att_ref[half_at(halves_ref, 1), :]

    outs = [sds((512, 256)), sds((512, 256)), sds((SEQ_LEN, 384)), sds((8, SEQ_LEN), jnp.float32)]
    scratch = [pltpu.VMEM((SEQ_LEN, 256), jnp.bfloat16)]
    return call(kernel, "attend", outs, [halves, *qkv], 20e9, scratch)


def attend_backward(qkv, lse, grad_out, tables, halves):
    def kernel(halves_ref, nat_ref, lse_ref, g0, g1, cos_ref, sin_ref, own_ref, other_ref, go_nat, kv_sum, d_nat):
        go_nat[half_at(halves_ref, 0), :] = g0[...]
        go_nat[half_at(halves_ref, 1), :] = g1[...]
        kv = nat_ref[:, 256:]
        keys = kv[:, :DH]
        values = kv[:, DH:]
        keys_t = kv.T[:DH]
        kv_sum[...] = jnp.zeros_like(kv_sum)
        for q_at in range(0, SEQ_LEN, 256):
            end = q_at + 256
            cosine = cos_ref[q_at:end, :]
            sine = -sin_ref[q_at:end, :]
            for pair in range(2):
                lanes = slice(128 * pair, 128 * pair + 128)
                two = nat_ref[q_at:end, lanes]
                two_grad = go_nat[q_at:end, lanes]
                outs = []
                for i in range(2):
                    query = two[:, DH * i : DH * i + DH]
                    grad = two_grad[:, DH * i : DH * i + DH]
                    g = 2 * pair + i
                    s = scores_t(keys[:end], query, q_at)
                    p = jnp.exp2(s * SCALE2 - lse_ref[g : g + 1, q_at:end])
                    dp = dot(values[:end], grad, 1, 1)
                    delta = jnp.sum(dp * p, axis=0, keepdims=True)
                    ds = bf(p * (dp - delta))
                    kv_sum[:end, :] += jnp.concatenate(
                        [dot(ds, query, 1, 0), dot(bf(p), grad, 1, 0)], axis=1
                    )
                    outs.append(dot(keys_t[:, :end], ds, 1, 0))
                d_query = jnp.concatenate(outs, axis=0).T * SCALE
                d_nat[q_at:end, lanes] = bf(rope(d_query, cosine, sine))
        lane = lax.broadcasted_iota(jnp.int32, (SEQ_LEN, 128), 1)
        total = kv_sum[...]
        turned = rope(total * SCALE, cos_ref[...], -sin_ref[...])
        d_nat[:, 256:] = bf(jnp.where(lane < DH, turned, total))
        own_ref[...] = d_nat[half_at(halves_ref, 0), :]
        other_ref[...] = d_nat[half_at(halves_ref, 1), :]

    scratch = [
        pltpu.VMEM((SEQ_LEN, 256), jnp.bfloat16),
        pltpu.VMEM((SEQ_LEN, 128), jnp.float32),
        pltpu.VMEM((SEQ_LEN, 384), jnp.bfloat16),
    ]
    args = [halves, qkv, lse, *grad_out, *tables]
    return call(kernel, "attend_backward", [sds((512, 384))] * 2, args, 30e9, scratch)


def mlp_step(rows, w_gate, w_up, grad_act):
    width = w_gate.shape[1]

    def kernel(rows_ref, g_ref, u_ref, ga_ref, act_ref, gg_ref, gu_ref):
        for j in range(0, width, 256):
            here = slice(j, j + 256)
            gate = dot(rows_ref[...], g_ref[:, here], 1, 0)
            up = dot(rows_ref[...], u_ref[:, here], 1, 0)
            sig = jax.nn.sigmoid(gate)
            silu = gate * sig
            ga = fl(ga_ref[:, here])
            act_ref[:, here] = bf(silu * up)
            gg_ref[:, here] = bf(ga * up * sig * (1.0 + gate * (1.0 - sig)))
            gu_ref[:, here] = bf(ga * silu)

    args = [rows, pinned(w_gate), pinned(w_up), grad_act]
    return call(kernel, "mlp_step", [sds((512, width))] * 3, args, 4 * 512 * D * width)


def frequencies(head_size):
    pair_index = jnp.arange(head_size // 2).astype(jnp.float32)
    base_freq = 500000.0 ** (-2.0 * pair_index / head_size)
    wavelen = 2.0 * jnp.pi / base_freq
    smooth = (8192.0 / wavelen - 1.0) / 3.0
    blended = (1.0 - smooth) * base_freq / 32.0 + smooth * base_freq
    return jnp.where(
        wavelen < 2048.0, base_freq, jnp.where(wavelen > 8192.0, base_freq / 32.0, blended)
    )


LONG = 60e9


def wide(out_ref, value):
    for k in range(4):
        out_ref[k] = value


def arrived_sum(ref):
    return fl(ref[0]) + fl(ref[1]) + fl(ref[2]) + fl(ref[3])


def mlp_norm(inputs, arrived, gain):
    def kernel(x_ref, a_ref, gain_ref, residual_ref, out_ref):
        residual = fl(x_ref[...]) + arrived_sum(a_ref)
        residual_ref[...] = residual
        inverse = lax.rsqrt(jnp.mean(residual * residual, axis=1, keepdims=True) + eps)
        wide(out_ref, bf(residual * inverse * gain_ref[...]))

    outs = [sds((128, D), jnp.float32), sds((4, 128, D))]
    return call(kernel, "mlp_norm", outs, [inputs, arrived, gain], LONG)


def norm_grad(grad, values, gain):
    inverse = lax.rsqrt(jnp.mean(values * values, axis=1, keepdims=True) + eps)
    unit = values * inverse
    scaled = grad * gain
    return inverse * (scaled - unit * jnp.mean(scaled * unit, axis=1, keepdims=True))


def mlp_norm_backward(upstream, arrived, residual, gain):
    def kernel(g_ref, a_ref, r_ref, gain_ref, grad_ref, out_ref):
        grad = fl(g_ref[...]) + norm_grad(arrived_sum(a_ref), r_ref[...], gain_ref[...])
        grad_ref[...] = grad
        wide(out_ref, bf(grad))

    outs = [sds((128, D), jnp.float32), sds((4, 128, D))]
    return call(kernel, "mlp_norm_backward", outs, [upstream, arrived, residual, gain], LONG)


def attn_norm_backward(grad_residual, arrived, inputs, gain):
    def kernel(g_ref, a_ref, x_ref, gain_ref, out_ref):
        out_ref[...] = bf(g_ref[...] + norm_grad(arrived_sum(a_ref), fl(x_ref[...]), gain_ref[...]))

    return call(kernel, "attn_norm_backward", [sds((128, D))], [grad_residual, arrived, inputs, gain], LONG)[0]


def layer_output(residual, arrived):
    def kernel(r_ref, a_ref, out_ref):
        out_ref[...] = bf(r_ref[...] + arrived_sum(a_ref))

    return call(kernel, "layer_output", [sds((128, D))], [residual, arrived], 1)[0]


def on_device(
    tokens, positions, w_query, w_key, w_value, w_out, attn_gain, w_gate, w_up, w_down, mlp_gain, cotangent
):
    me = Place()
    inputs_b = swapped(tokens)
    places = jnp.concatenate([(positions // 256).reshape(128, 8), (positions % 256).reshape(128, 8)], axis=1)
    extra = jnp.concatenate([attn_gain[:, None], mlp_gain[:, None], bf(places)], axis=1)
    extra = jnp.pad(extra, ((0, 0), (0, 110)))
    part_attn = swapped(jnp.concatenate([w_query, w_key, w_value, extra, w_out.T], axis=1))
    part_attn, inputs_b = lax.optimization_barrier((part_attn, inputs_b))

    blocks_in = send_z(inputs_b)
    w_qkv = gather_plane(part_attn[:, :512])
    w_gate, w_up, w_down, cotangent = after((w_gate, w_up, w_down, cotangent), inputs_b)
    upstream = swapped(cotangent)
    down_rows = w_down.T
    part_ab = swapped(jnp.concatenate([w_gate, down_rows[:, :512], w_up, down_rows[:, 512:]], axis=1))

    place = fl(part_attn[:, 386:402])
    seq_positions = (256.0 * place[:, :8] + place[:, 8:]).reshape(SEQ_LEN)
    freq = jnp.tile(frequencies(DH), 4)
    angles = seq_positions[:, None] * freq[None, :]
    sign = jnp.where(jnp.arange(128) % DH < DH // 2, -1.0, 1.0)
    tables = (jnp.cos(angles), jnp.sin(angles) * sign[None, :])
    pick = bf(jnp.arange(128)[None, :] == jnp.arange(8)[:, None])
    gain_rows = dot(pick, w_qkv[:, 384:], 1, 1)
    gain_attn, gain_mlp = gain_rows[:1], gain_rows[1:2]

    blocks_in = after(blocks_in, *tables, upstream, part_ab)
    own_normed = norm_tokens(blocks_in, gain_attn, me)
    normed_attn = [own_normed, sibling(own_normed)]
    own_qkv = project_qkv(0, normed_attn[0], w_qkv, tables, me.halves)
    projected = [own_qkv, project_qkv(1, normed_attn[1], w_qkv, tables, me.halves)]

    (own_up,) = after((upstream,), own_normed)
    blocks_up = send_z(own_up)
    (part_out,) = after((part_attn[:, 512:],), own_qkv)
    w_out_t = gather_plane(part_out)

    projected = after(projected, *blocks_up[1:3])
    attended, other_attended, qkv, lse = attend(projected, me.halves)
    (w_out_t,) = after((w_out_t,), attended, blocks_up[3])
    out_sums = chip_product(attended, other_attended, w_out_t, sibling(w_out_t))
    (out_sums,) = after((out_sums,), *blocks_up)

    (part_ab,) = after((part_ab,), own_normed)
    part_a, part_b = part_ab[:, :1536], part_ab[:, 1536:]
    holds = (projected[1], attended, out_sums)
    stage_a, stage_b = (jnp.concatenate(chain(p, axis, holds), axis=0) for p, axis in ((part_a, "x"), (part_b, "y")))

    own_up = place_tokens(blocks_up, me)
    rows_up = [own_up, sibling(own_up)]
    arrived = arrive_z(out_sums)

    parts_a, parts_b = chain(stage_a, "y", (None, None, None)), chain(stage_b, "x", (None, None, None))
    full_gate, down_a = place_rows(parts_a, me.blocks["x"], (1024, 512))
    full_up, down_b = place_rows(parts_b, me.blocks["y"], (1024, 512))
    full_down = [down_a, down_b]

    (arrived,) = after((arrived,), parts_a[2], parts_b[2], *rows_up)
    residual, normed_mlp = mlp_norm(inputs_b, arrived, gain_mlp)
    own_mlp = gather_z(normed_mlp)
    up_held = after(rows_up, normed_mlp)
    grad_act = [project(r, [pinned(w) for w in full_down], jnp.bfloat16) for r in up_held]
    (own_mlp,) = after((own_mlp,), full_gate, full_up, grad_act[0])
    rows_mlp = [own_mlp, sibling(own_mlp)]
    steps = [mlp_step(r, full_gate, full_up, g) for r, g in zip(rows_mlp, grad_act)]
    activated, grad_gate_pre, grad_up_pre = zip(*steps)

    gate_up = list(zip(grad_gate_pre, grad_up_pre))
    mlp_sums = chip_sums(gate_up[0], gate_up[1], [full_gate, full_up])
    arrived = arrive_z(mlp_sums)

    gg, gu = after((grad_gate_pre, grad_up_pre), mlp_sums)
    made_a = weight_product([(rows_mlp, gg, 0, 1024), (rows_up, activated, 0, 512)], "x", me, 2)
    made_b = weight_product([(rows_mlp, gu, 0, 1024), (rows_up, activated, 512, 1024)], "y", me, 2)
    sums = [made_a[0], made_b[0]]
    rings = [ring_cuts(total, axis) for total, axis in zip(sums, "xy")]
    (arrived,) = after((arrived,), made_a[-1][0], made_b[-1][0])
    grad_residual, grad_residual_b = mlp_norm_backward(upstream, arrived, residual, gain_mlp)

    own_gr = gather_z(grad_residual_b)
    rings = [after(cuts, grad_residual_b) for cuts in rings]
    sums = [add(received, made[1]) for received, made in zip(rings, (made_a, made_b))]
    rings = [ring_cuts(total, axis) for total, axis in zip(sums, "xy")]
    acts = after(activated, *sums[0], *sums[1])
    down_other = down_products(acts[1], full_down)
    down_own = down_products(acts[0], full_down)
    down_arrived = [sibling(half) for half in down_other]
    (own_gr,) = after((own_gr,), *down_own, *down_arrived, *rings[0], *rings[1])
    rows_gr = [own_gr, sibling(own_gr)]
    rings = [after(cuts, own_gr) for cuts in rings]
    sums = [add(received, made[2]) for received, made in zip(rings, (made_a, made_b))]
    rings = [ring_cuts(total, axis) for total, axis in zip(sums, "xy")]
    down_sums = join_sums(after(down_own, sums[0][0], sums[1][0]), down_arrived)
    arrived = arrive_z(down_sums)
    grad_attended = [project(r, [w_out_t], jnp.bfloat16) for r in after(rows_gr, sums[0][0], sums[1][0])]
    grad_qkv, other_grad_qkv = attend_backward(qkv, lse, grad_attended, tables, me.halves)
    blocks_a = second_blocks([after(rings[0], grad_qkv), made_a[3]], "x", me)
    parts_a = second_stage(blocks_a, "x")
    attn_sums = chip_product(grad_qkv, other_grad_qkv, w_qkv, sibling(w_qkv))
    (attn_sums,) = after((attn_sums,), arrived, blocks_a[0])
    grad_arrived = arrive_z(attn_sums)

    d_qkv = after((grad_qkv, other_grad_qkv), attn_sums)
    made_in = weight_product([(normed_attn, d_qkv, 0, 384)], "x", me)
    sent_in = send_pieces([cut for (cut,) in made_in], "x")
    att = after((attended, other_attended), *made_in[-1])
    made_out = weight_product([(rows_gr, att, 0, 256)], "y", me)
    blocks_b = second_blocks([after(rings[1], *made_out[-1]), made_b[3]], "y", me)
    (arrived,) = after((arrived,), blocks_b[0])
    layer_out = layer_output(residual, arrived)
    share_a = summed(parts_a, layer_out)
    sent_out = send_pieces([cut for (cut,) in made_out], "y")
    (grad_arrived,) = after((grad_arrived,), share_a)
    grad_tokens = attn_norm_backward(grad_residual, grad_arrived, inputs_b, gain_attn)
    (layer_out,) = after((layer_out,), grad_tokens)
    blocks_in = second_blocks([[part] for part in after(sent_in, grad_tokens)], "x", me)
    share_in = summed(second_stage(blocks_in, "x"), grad_tokens)
    parts_b = second_stage(after(blocks_b, grad_tokens), "y")
    share_b = fl(swapped(bf(summed(parts_b, grad_tokens))))
    blocks_out = second_blocks([[part] for part in after(sent_out, grad_tokens)], "y", me)
    share_out = fl(swapped(bf(summed(second_stage(blocks_out, "y"), grad_tokens))))

    def gain_sum(*terms):
        return sum(jnp.sum(fl(w) * g, axis=1) for w, g in terms)

    gain_sums = jnp.stack(
        [
            gain_sum((jnp.concatenate([w_query, w_key, w_value], axis=1), share_in)),
            gain_sum((w_gate, share_a[:, :1024]), (w_up, share_b[:, :1024])),
        ]
    )
    gain_sums = gain_sums / fl(jnp.stack([attn_gain, mlp_gain]))
    gain_sums = gain_sums + z_moved(gain_sums, 1) + z_moved(gain_sums, 2) + z_moved(gain_sums, 3)
    gain_sums = gain_sums + h_flipped(gain_sums)
    return (
        swapped(layer_out),
        swapped(grad_tokens),
        share_in[:, :256],
        share_in[:, 256:320],
        share_in[:, 320:384],
        share_out.T,
        gain_sums[0],
        share_a[:, :1024],
        share_b[:, :1024],
        jnp.concatenate([share_a[:, 1024:], share_b[:, 1024:]], axis=1).T,
        gain_sums[1],
    )


def solution(mesh):
    split = Mesh(mesh.devices.reshape(4, 2, 2, 2, 4), AXES)
    dp, tensor = ("x", "l", "c"), ("h", "z")
    both = P(AXES, None)
    weight, turned, vector = P(dp, tensor), P(tensor, dp), P(dp)
    in_specs = (
        both, vector, weight, weight, weight, turned, vector, weight, weight, turned, vector, both,
    )
    out_specs = (
        both, both, weight, weight, weight, turned, vector, weight, weight, turned, vector,
    )
    return jax.shard_map(on_device, mesh=split, in_specs=in_specs, out_specs=out_specs, check_vma=False)
```

```python
import functools
import itertools
import math

import jax
import jax.numpy as jnp
from jax import lax
from jax.experimental import pallas as pl
from jax.experimental.pallas import tpu as pltpu
from jax.sharding import Mesh, PartitionSpec as P

H = 32
KV = 8
DH = 64
SEQ_LEN = 1024
D = 2048
eps = 1e-05

SIZES = dict(x=4, l=2, c=2, h=2, z=4)
AXES = ("x", "l", "c", "h", "z")

SCALE = DH ** (-0.5)
SCALE2 = SCALE * math.log2(math.e)
VMEM_LIMIT = 12 * 1024 * 1024


def pairs(axes, move):
    def place(index):
        at = 0
        for a in axes:
            at = at * SIZES[a] + index[a]
        return at

    out = []
    for index in itertools.product(*[range(SIZES[a]) for a in axes]):
        here = dict(zip(axes, index))
        out.append((place(here), place(move(dict(here)))))
    return out


def to_swapped(d):
    d["c"], d["h"] = d["h"], d["c"]
    return d


def to_sibling(d):
    d["c"] = 1 - d["c"]
    return d


def along(axis):
    def move(d):
        step = 1 - 2 * d["c"]
        if axis == "y":
            y = (2 * d["h"] + d["l"] + step) % 4
            d["h"], d["l"] = y // 2, y % 2
        else:
            d[axis] = (d[axis] + step) % 4
        return d

    return move


RING_AXES = dict(x=("x", "c"), y=("l", "c", "h"))
Z_STEPS = (0, 1, 3, 2)
PIECES = (1, 2, 3, 0)


def ring(value, axis):
    axes = RING_AXES[axis]
    return lax.ppermute(value, axes, pairs(axes, along(axis)))


def swapped(value):
    return lax.ppermute(value, ("c", "h"), pairs(("c", "h"), to_swapped))


def sibling(value):
    return lax.ppermute(value, ("c",), pairs(("c",), to_sibling))


def z_moved(value, step):
    def move(d):
        d["z"] = (d["z"] + step) % 4
        return d

    return lax.ppermute(value, ("z",), pairs(("z",), move))


def h_flipped(value):
    def move(d):
        d["h"] = 1 - d["h"]
        return d

    return lax.ppermute(value, ("h",), pairs(("h",), move))


def after(values, *earlier):
    held = lax.optimization_barrier((tuple(values), tuple(earlier)))
    return held[0]


def dot(a, b, ca, cb):
    return lax.dot_general(a, b, (((ca,), (cb,)), ((), ())), preferred_element_type=jnp.float32)


def bf(v):
    return v.astype(jnp.bfloat16)


def fl(v):
    return v.astype(jnp.float32)


def sds(shape, dtype=jnp.bfloat16):
    return jax.ShapeDtypeStruct(shape, dtype)


def cost(flops):
    return pl.CostEstimate(flops=int(flops), bytes_accessed=1, transcendentals=0)


PARAMS = pltpu.CompilerParams(vmem_limit_bytes=VMEM_LIMIT)
ANY = pl.BlockSpec(memory_space=pl.ANY)
WHOLE = pl.BlockSpec(memory_space=pltpu.VMEM)


class Place:
    def __init__(self):
        self.c = lax.axis_index("c")
        self.x = lax.axis_index("x")
        self.h = lax.axis_index("h")
        self.y = 2 * self.h + lax.axis_index("l")
        self.step = 1 - 2 * self.c
        self.halves = jnp.stack([512 * self.c, 512 * (1 - self.c)]).astype(jnp.int32)
        z = lax.axis_index("z")
        self.z_order = jnp.stack([lax.rem(z - step + 4, 4) for step in Z_STEPS]).astype(jnp.int32)
        self.blocks = {}
        for first, second in (("x", "y"), ("y", "x")):
            out = []
            for k2 in range(4):
                for k1 in range(4):
                    a, b = self.source(first, k1), self.source(second, k2)
                    out.append(4 * a + b if first == "x" else 4 * b + a)
            self.blocks[first] = jnp.stack(out).astype(jnp.int32)

    def source(self, axis, k):
        at = lax.rem(dict(x=self.x, y=self.y)[axis] - self.step * k + 4, 4)
        if axis == "y":
            at = 2 * lax.rem(at, 2) + lax.div(at, 2)
        return at


SMEM = pl.BlockSpec(memory_space=pltpu.SMEM)


def pinned(value):
    return pltpu.with_memory_space_constraint(value, pltpu.VMEM)


def place_rows(parts, blocks, widths):
    def kernel(blocks_ref, p0, p1, p2, p3, *rest):
        sems = rest[-1]
        copies = []
        for k2, part in enumerate((p0, p1, p2, p3)):
            for k1 in range(4):
                at = pl.multiple_of(blocks_ref[4 * k2 + k1] * 128, 128)
                low = 0
                for i, width in enumerate(widths):
                    copies.append(
                        pltpu.make_async_copy(
                            part.at[pl.ds(128 * k1, 128), pl.ds(low, width)],
                            rest[i].at[pl.ds(at, 128)],
                            sems.at[len(widths) * (4 * k2 + k1) + i],
                        )
                    )
                    low += width
        for copy in copies:
            copy.start()
        for copy in copies:
            copy.wait()

    return pl.pallas_call(
        kernel,
        out_shape=[pltpu.VMEM((D, width), jnp.bfloat16) for width in widths],
        in_specs=[SMEM] + [ANY] * 4,
        out_specs=[WHOLE] * len(widths),
        scratch_shapes=[pltpu.SemaphoreType.DMA((16 * len(widths),))],
        compiler_params=PARAMS,
        cost_estimate=cost(1),
        name="place_rows",
    )(blocks, *parts)


def stepped(value, axis, steps):
    def move(d):
        for _ in range(steps):
            d = along(axis)(d)
        return d

    axes = RING_AXES[axis]
    return lax.ppermute(value, axes, pairs(axes, move))


def chain(block, axis, holds):
    parts = [block]
    for hold in holds:
        part = ring(parts[-1], axis)
        parts.append(part if hold is None else after((part,), hold)[0])
    return parts


def gather_plane(block):
    wide = jnp.broadcast_to(block[None], (16,) + block.shape)
    return lax.all_to_all(wide, ("x", "l", "h"), split_axis=0, concat_axis=0, tiled=True).reshape(D, block.shape[1])


def call(kernel, name, outs, args, flops, scratch=(), limit=VMEM_LIMIT):
    return pl.pallas_call(
        kernel,
        out_shape=outs,
        in_specs=[SMEM if a.dtype == jnp.int32 else WHOLE for a in args],
        out_specs=[WHOLE] * len(outs),
        scratch_shapes=list(scratch),
        compiler_params=pltpu.CompilerParams(vmem_limit_bytes=limit),
        cost_estimate=cost(flops),
        name=name,
    )(*args)


def weight_product(terms, first, me, cuts=1):
    order = jnp.stack([me.source(first, k) for k in PIECES]).astype(jnp.int32)
    n = sum(high - low for _, _, low, high in terms) // cuts
    args = [order]
    for rows, right, _, _ in terms:
        args += [*rows, *right]

    def kernel(order_ref, *refs):
        for p in range(4):
            at = 0
            for t, (_, _, low, high) in enumerate(terms):
                rows, right = refs[4 * t : 4 * t + 2], refs[4 * t + 2 : 4 * t + 4]
                left = []
                for r in rows:
                    lanes = []
                    for j in range(4):
                        block = 4 * order_ref[p] + j if first == "x" else 4 * j + order_ref[p]
                        lanes.append(r[:, pl.ds(pl.multiple_of(block * 128, 128), 128)])
                    left.append(jnp.concatenate(lanes, axis=1))
                for j in range(low, high, 256):
                    end = min(j + 256, high)
                    total = dot(left[0], right[0][:, j:end], 0, 0) + dot(left[1], right[1][:, j:end], 0, 0)
                    out_ref = refs[4 * len(terms) + cuts * p + at // n]
                    out_ref[:, at % n : at % n + end - j] = bf(total)
                    at += end - j

    outs = [pltpu.HBM((512, n), jnp.bfloat16)] * (4 * cuts)
    made = call(kernel, "weight_product", outs, args, 2 * D * SEQ_LEN * n * cuts, limit=24 * 1024 * 1024)
    return [made[cuts * p : cuts * p + cuts] for p in range(4)]


def sum_blocks(parts, order):
    n = sum(cut.shape[1] for cut in parts[0])
    width = min(cut.shape[1] for part in parts for cut in part)

    def kernel(order_ref, *refs):
        for k in range(4):
            at = pl.ds(pl.multiple_of(order_ref[k] * 128, 128), 128)
            for low in range(0, n, width):
                total, first = None, 0
                for part in parts:
                    cut = part[0].shape[1]
                    value = fl(refs[first + low // cut][at, low % cut : low % cut + width])
                    total = value if total is None else total + value
                    first += len(part)
                refs[first + k][:, low : low + width] = bf(total)

    args = [order, *[cut for part in parts for cut in part]]
    return call(kernel, "sum_blocks", [sds((128, n))] * 4, args, 1)


def send_pieces(made, first):
    return [stepped(piece, first, 4 - k) if k else piece for k, piece in zip(PIECES, made)]


def homeward(value, k):
    def move(d):
        y = (2 * d["h"] + d["l"] - k * (1 - 2 * d["c"])) % 4
        d["l"], d["h"], d["c"] = y % 2, d["c"], y // 2
        return d

    axes = ("l", "c", "h")
    return lax.ppermute(value, axes, pairs(axes, move))


def add(one, other, join=False):
    count = len(one)
    n = one[0].shape[1]

    def kernel(*refs):
        for i in range(count):
            total = bf(fl(refs[i][...]) + fl(refs[count + i][...]))
            if join:
                refs[2 * count][:, n * i : n * i + n] = total
            else:
                refs[2 * count + i][...] = total

    outs = [sds((512, n * count))] if join else [sds(a.shape) for a in one]
    return call(kernel, "add", outs, [*one, *other], 1)


def ring_cuts(cuts, axis):
    return [ring(cut, axis) for cut in cuts]


def second_blocks(parts, first, me):
    second = "y" if first == "x" else "x"
    return sum_blocks(parts, jnp.stack([me.source(second, k) for k in PIECES]).astype(jnp.int32))


def second_stage(blocks, first):
    if first == "x":
        return [homeward(block, k) for k, block in zip(PIECES, blocks)]
    return send_pieces(blocks, "x")


def summed(parts, hold):
    return sum(fl(part) for part in after(parts, hold))


def send_z(block):
    return [z_moved(block, step) if step else block for step in Z_STEPS]


def place_tokens(blocks, me):
    def kernel(order_ref, b0, b1, b2, b3, out_ref):
        for k, ref in enumerate((b0, b1, b2, b3)):
            out_ref[pl.ds(pl.multiple_of(order_ref[k] * 128, 128), 128), :] = ref[...]

    return call(kernel, "place_tokens", [sds((512, D))], [me.z_order, *blocks], 1)[0]


def norm_tokens(blocks, gain, me):
    def kernel(order_ref, b0, b1, b2, b3, gain_ref, out_ref):
        for k, ref in enumerate((b0, b1, b2, b3)):
            x = fl(ref[...])
            inverse = lax.rsqrt(jnp.mean(x * x, axis=1, keepdims=True) + eps)
            out_ref[pl.ds(pl.multiple_of(order_ref[k] * 128, 128), 128), :] = bf(x * inverse * gain_ref[...])

    return call(kernel, "norm_tokens", [sds((512, D))], [me.z_order, *blocks, gain], 1)[0]


def gather_z(wide_block):
    whole = lax.all_to_all(wide_block, "z", split_axis=0, concat_axis=0, tiled=True)
    return whole.reshape(512, whole.shape[2])


def arrive_z(sums):
    parts = sums.reshape(4, 128, sums.shape[1])
    return lax.all_to_all(parts, "z", split_axis=0, concat_axis=0, tiled=True)


def partial_sums(pieces, weights):
    count = len(pieces)

    def kernel(*refs):
        for j in range(0, D, 512):
            total = None
            for i in range(count):
                one = dot(refs[i][...], refs[count + i][j : j + 512, :], 1, 1)
                total = one if total is None else total + one
            refs[-1][:, j : j + 512] = bf(total)

    depth = sum(p.shape[1] for p in pieces)
    return call(kernel, "partial_sums", [sds((512, D))], [*pieces, *map(pinned, weights)], 2 * 512 * depth * D)[0]


def chip_sums(own, other, weights):
    received = sibling(partial_sums(other, weights))
    return bf(fl(partial_sums(own, weights)) + fl(received))


def chip_product(own, other, weight, sibling_weight):
    received = sibling(other)
    m = own.shape[1]

    def kernel(a_ref, b_ref, v_ref, w_ref, out_ref):
        for j in range(0, D, 512):
            here = slice(j, j + 512)
            total = dot(a_ref[...], v_ref[here, :m], 1, 1) + dot(b_ref[...], w_ref[here, :m], 1, 1)
            out_ref[:, here] = bf(total)

    args = [own, received, weight, sibling_weight]
    return call(kernel, "chip_product", [sds((512, D))], args, 4 * 512 * m * D)[0]


def project(rows, weights, dtype, width=None):
    width = width or weights[0].shape[1]
    n = width * len(weights)

    def kernel(rows_ref, *refs):
        for i, w_ref in enumerate(refs[:-1]):
            for j in range(0, width, 256):
                product = dot(rows_ref[...], w_ref[:, j : j + 256], 1, 0)
                refs[-1][:, i * width + j : i * width + j + 256] = product.astype(dtype)

    return call(kernel, "project", [sds((512, n), dtype)], [rows, *weights], 2 * 512 * D * n)[0]


def down_products(rows, weights):
    def kernel(rows_ref, w0, w1, *out_refs):
        for j in range(0, D, 512):
            here = slice(j, j + 512)
            total = dot(rows_ref[:, :512], w0[here, :], 1, 1) + dot(rows_ref[:, 512:], w1[here, :], 1, 1)
            out_refs[j // 1024][:, j % 1024 : j % 1024 + 512] = bf(total)

    args = [rows, *map(pinned, weights)]
    return call(kernel, "down_products", [sds((512, D // 2))] * 2, args, 2 * 512 * 1024 * D)


def join_sums(one, other):
    def kernel(a0, a1, b0, b1, out_ref):
        out_ref[:, :1024] = bf(fl(a0[...]) + fl(b0[...]))
        out_ref[:, 1024:] = bf(fl(a1[...]) + fl(b1[...]))

    return call(kernel, "join_sums", [sds((512, D))], [*one, *other], 1)[0]


def rope(u, cosine, sine):
    lane = lax.broadcasted_iota(jnp.int32, u.shape, 1)
    turned = jnp.where(lane % DH < DH // 2, pltpu.roll(u, 96, 1), pltpu.roll(u, 32, 1))
    return u * cosine + turned * sine


def rope_three(u, cosine, sine):
    lane = lax.broadcasted_iota(jnp.int32, cosine.shape, 1)
    last = u[:, 256:]
    return jnp.concatenate(
        [
            rope(u[:, :128], cosine, sine),
            rope(u[:, 128:256], cosine, sine),
            jnp.where(lane < DH, rope(last, cosine, sine), last),
        ],
        axis=1,
    )


def half_at(halves_ref, i):
    return pl.ds(pl.multiple_of(halves_ref[i], 512), 512)


def project_qkv(i, rows, weight, tables, halves):
    def kernel(halves_ref, rows_ref, w_ref, cos_ref, sin_ref, out_ref):
        here = half_at(halves_ref, i)
        product = dot(rows_ref[...], w_ref[:, :384], 1, 0)
        out_ref[...] = bf(rope_three(product, cos_ref[here, :], sin_ref[here, :]))

    args = [halves, rows, weight, *tables]
    return call(kernel, "project_qkv", [sds((512, 384))], args, 2 * 512 * D * 384)[0]


def scores_t(keys, query, q_at):
    s = dot(keys, query, 1, 1)
    key = lax.broadcasted_iota(jnp.int32, (256, 256), 0)
    column = lax.broadcasted_iota(jnp.int32, (256, 256), 1)
    diagonal = jnp.where(key <= column, s[q_at:], -1e30)
    return diagonal if q_at == 0 else jnp.concatenate([s[:q_at], diagonal], axis=0)


def attend(qkv, halves):
    def kernel(halves_ref, q0, q1, own_ref, other_ref, nat_ref, lse_ref, att_ref):
        nat_ref[half_at(halves_ref, 0), :] = q0[...]
        nat_ref[half_at(halves_ref, 1), :] = q1[...]
        kv = nat_ref[:, 256:]
        keys = kv[:, :DH]
        values_t = kv.T[DH:]
        lse_ref[...] = jnp.zeros_like(lse_ref)
        for q_at in range(0, SEQ_LEN, 256):
            end = q_at + 256
            for pair in range(2):
                two = nat_ref[q_at:end, 128 * pair : 128 * pair + 128]
                outs = []
                for i in range(2):
                    s = scores_t(keys[:end], two[:, DH * i : DH * i + DH], q_at)
                    top = jnp.max(s, axis=0, keepdims=True)
                    p = jnp.exp2((s - top) * SCALE2)
                    total = jnp.sum(p, axis=0, keepdims=True)
                    outs.append(dot(values_t[:, :end], bf(p), 1, 0) / total)
                    g = 2 * pair + i
                    lse_ref[g : g + 1, q_at:end] = top * SCALE2 + jnp.log2(total)
                att_ref[q_at:end, 128 * pair : 128 * pair + 128] = bf(jnp.concatenate(outs, axis=0).T)
        own_ref[...] = att_ref[half_at(halves_ref, 0), :]
        other_ref[...] = att_ref[half_at(halves_ref, 1), :]

    outs = [sds((512, 256)), sds((512, 256)), sds((SEQ_LEN, 384)), sds((8, SEQ_LEN), jnp.float32)]
    scratch = [pltpu.VMEM((SEQ_LEN, 256), jnp.bfloat16)]
    return call(kernel, "attend", outs, [halves, *qkv], 20e9, scratch)


def attend_backward(qkv, lse, grad_out, tables, halves):
    def kernel(halves_ref, nat_ref, lse_ref, g0, g1, cos_ref, sin_ref, own_ref, other_ref, go_nat, kv_sum, d_nat):
        go_nat[half_at(halves_ref, 0), :] = g0[...]
        go_nat[half_at(halves_ref, 1), :] = g1[...]
        kv = nat_ref[:, 256:]
        keys = kv[:, :DH]
        values = kv[:, DH:]
        keys_t = kv.T[:DH]
        kv_sum[...] = jnp.zeros_like(kv_sum)
        for q_at in range(0, SEQ_LEN, 256):
            end = q_at + 256
            cosine = cos_ref[q_at:end, :]
            sine = -sin_ref[q_at:end, :]
            for pair in range(2):
                lanes = slice(128 * pair, 128 * pair + 128)
                two = nat_ref[q_at:end, lanes]
                two_grad = go_nat[q_at:end, lanes]
                outs = []
                for i in range(2):
                    query = two[:, DH * i : DH * i + DH]
                    grad = two_grad[:, DH * i : DH * i + DH]
                    g = 2 * pair + i
                    s = scores_t(keys[:end], query, q_at)
                    p = jnp.exp2(s * SCALE2 - lse_ref[g : g + 1, q_at:end])
                    dp = dot(values[:end], grad, 1, 1)
                    delta = jnp.sum(dp * p, axis=0, keepdims=True)
                    ds = bf(p * (dp - delta))
                    kv_sum[:end, :] += jnp.concatenate(
                        [dot(ds, query, 1, 0), dot(bf(p), grad, 1, 0)], axis=1
                    )
                    outs.append(dot(keys_t[:, :end], ds, 1, 0))
                d_query = jnp.concatenate(outs, axis=0).T * SCALE
                d_nat[q_at:end, lanes] = bf(rope(d_query, cosine, sine))
        lane = lax.broadcasted_iota(jnp.int32, (SEQ_LEN, 128), 1)
        total = kv_sum[...]
        turned = rope(total * SCALE, cos_ref[...], -sin_ref[...])
        d_nat[:, 256:] = bf(jnp.where(lane < DH, turned, total))
        own_ref[...] = d_nat[half_at(halves_ref, 0), :]
        other_ref[...] = d_nat[half_at(halves_ref, 1), :]

    scratch = [
        pltpu.VMEM((SEQ_LEN, 256), jnp.bfloat16),
        pltpu.VMEM((SEQ_LEN, 128), jnp.float32),
        pltpu.VMEM((SEQ_LEN, 384), jnp.bfloat16),
    ]
    args = [halves, qkv, lse, *grad_out, *tables]
    return call(kernel, "attend_backward", [sds((512, 384))] * 2, args, 30e9, scratch)


def mlp_step(rows, w_gate, w_up, grad_act):
    width = w_gate.shape[1]

    def kernel(rows_ref, g_ref, u_ref, ga_ref, act_ref, gg_ref, gu_ref):
        for j in range(0, width, 256):
            here = slice(j, j + 256)
            gate = dot(rows_ref[...], g_ref[:, here], 1, 0)
            up = dot(rows_ref[...], u_ref[:, here], 1, 0)
            sig = jax.nn.sigmoid(gate)
            silu = gate * sig
            ga = fl(ga_ref[:, here])
            act_ref[:, here] = bf(silu * up)
            gg_ref[:, here] = bf(ga * up * sig * (1.0 + gate * (1.0 - sig)))
            gu_ref[:, here] = bf(ga * silu)

    args = [rows, pinned(w_gate), pinned(w_up), grad_act]
    return call(kernel, "mlp_step", [sds((512, width))] * 3, args, 4 * 512 * D * width)


def frequencies(head_size):
    pair_index = jnp.arange(head_size // 2).astype(jnp.float32)
    base_freq = 500000.0 ** (-2.0 * pair_index / head_size)
    wavelen = 2.0 * jnp.pi / base_freq
    smooth = (8192.0 / wavelen - 1.0) / 3.0
    blended = (1.0 - smooth) * base_freq / 32.0 + smooth * base_freq
    return jnp.where(
        wavelen < 2048.0, base_freq, jnp.where(wavelen > 8192.0, base_freq / 32.0, blended)
    )


LONG = 60e9


def wide(out_ref, value):
    for k in range(4):
        out_ref[k] = value


def arrived_sum(ref):
    return fl(ref[0]) + fl(ref[1]) + fl(ref[2]) + fl(ref[3])


def mlp_norm(inputs, arrived, gain):
    def kernel(x_ref, a_ref, gain_ref, residual_ref, out_ref):
        residual = fl(x_ref[...]) + arrived_sum(a_ref)
        residual_ref[...] = residual
        inverse = lax.rsqrt(jnp.mean(residual * residual, axis=1, keepdims=True) + eps)
        wide(out_ref, bf(residual * inverse * gain_ref[...]))

    outs = [sds((128, D), jnp.float32), sds((4, 128, D))]
    return call(kernel, "mlp_norm", outs, [inputs, arrived, gain], LONG)


def norm_grad(grad, values, gain):
    inverse = lax.rsqrt(jnp.mean(values * values, axis=1, keepdims=True) + eps)
    unit = values * inverse
    scaled = grad * gain
    return inverse * (scaled - unit * jnp.mean(scaled * unit, axis=1, keepdims=True))


def mlp_norm_backward(upstream, arrived, residual, gain):
    def kernel(g_ref, a_ref, r_ref, gain_ref, grad_ref, out_ref):
        grad = fl(g_ref[...]) + norm_grad(arrived_sum(a_ref), r_ref[...], gain_ref[...])
        grad_ref[...] = grad
        wide(out_ref, bf(grad))

    outs = [sds((128, D), jnp.float32), sds((4, 128, D))]
    return call(kernel, "mlp_norm_backward", outs, [upstream, arrived, residual, gain], LONG)


def attn_norm_backward(grad_residual, arrived, inputs, gain):
    def kernel(g_ref, a_ref, x_ref, gain_ref, out_ref):
        out_ref[...] = bf(g_ref[...] + norm_grad(arrived_sum(a_ref), fl(x_ref[...]), gain_ref[...]))

    return call(kernel, "attn_norm_backward", [sds((128, D))], [grad_residual, arrived, inputs, gain], LONG)[0]


def layer_output(residual, arrived):
    def kernel(r_ref, a_ref, out_ref):
        out_ref[...] = bf(r_ref[...] + arrived_sum(a_ref))

    return call(kernel, "layer_output", [sds((128, D))], [residual, arrived], 1)[0]


def on_device(
    tokens, positions, w_query, w_key, w_value, w_out, attn_gain, w_gate, w_up, w_down, mlp_gain, cotangent
):
    me = Place()
    inputs_b = swapped(tokens)
    places = jnp.concatenate([(positions // 256).reshape(128, 8), (positions % 256).reshape(128, 8)], axis=1)
    extra = jnp.concatenate([attn_gain[:, None], mlp_gain[:, None], bf(places)], axis=1)
    extra = jnp.pad(extra, ((0, 0), (0, 110)))
    part_attn = swapped(jnp.concatenate([w_query, w_key, w_value, extra, w_out.T], axis=1))
    part_attn, inputs_b = lax.optimization_barrier((part_attn, inputs_b))

    blocks_in = send_z(inputs_b)
    w_qkv = gather_plane(part_attn[:, :512])
    w_gate, w_up, w_down, cotangent = after((w_gate, w_up, w_down, cotangent), inputs_b)
    upstream = swapped(cotangent)
    down_rows = w_down.T
    part_ab = swapped(jnp.concatenate([w_gate, down_rows[:, :512], w_up, down_rows[:, 512:]], axis=1))

    place = fl(part_attn[:, 386:402])
    seq_positions = (256.0 * place[:, :8] + place[:, 8:]).reshape(SEQ_LEN)
    freq = jnp.tile(frequencies(DH), 4)
    angles = seq_positions[:, None] * freq[None, :]
    sign = jnp.where(jnp.arange(128) % DH < DH // 2, -1.0, 1.0)
    tables = (jnp.cos(angles), jnp.sin(angles) * sign[None, :])
    pick = bf(jnp.arange(128)[None, :] == jnp.arange(8)[:, None])
    gain_rows = dot(pick, w_qkv[:, 384:], 1, 1)
    gain_attn, gain_mlp = gain_rows[:1], gain_rows[1:2]

    blocks_in = after(blocks_in, *tables, upstream, part_ab)
    own_normed = norm_tokens(blocks_in, gain_attn, me)
    normed_attn = [own_normed, sibling(own_normed)]
    own_qkv = project_qkv(0, normed_attn[0], w_qkv, tables, me.halves)
    projected = [own_qkv, project_qkv(1, normed_attn[1], w_qkv, tables, me.halves)]

    (own_up,) = after((upstream,), own_normed)
    blocks_up = send_z(own_up)
    (part_out,) = after((part_attn[:, 512:],), own_qkv)
    w_out_t = gather_plane(part_out)

    projected = after(projected, *blocks_up[1:3])
    attended, other_attended, qkv, lse = attend(projected, me.halves)
    (w_out_t,) = after((w_out_t,), attended, blocks_up[3])
    out_sums = chip_product(attended, other_attended, w_out_t, sibling(w_out_t))
    (out_sums,) = after((out_sums,), *blocks_up)

    (part_ab,) = after((part_ab,), own_normed)
    part_a, part_b = part_ab[:, :1536], part_ab[:, 1536:]
    holds = (projected[1], attended, out_sums)
    stage_a, stage_b = (jnp.concatenate(chain(p, axis, holds), axis=0) for p, axis in ((part_a, "x"), (part_b, "y")))

    own_up = place_tokens(blocks_up, me)
    rows_up = [own_up, sibling(own_up)]
    arrived = arrive_z(out_sums)

    parts_a, parts_b = chain(stage_a, "y", (None, None, None)), chain(stage_b, "x", (None, None, None))
    full_gate, down_a = place_rows(parts_a, me.blocks["x"], (1024, 512))
    full_up, down_b = place_rows(parts_b, me.blocks["y"], (1024, 512))
    full_down = [down_a, down_b]

    (arrived,) = after((arrived,), parts_a[2], parts_b[2], *rows_up)
    residual, normed_mlp = mlp_norm(inputs_b, arrived, gain_mlp)
    own_mlp = gather_z(normed_mlp)
    up_held = after(rows_up, normed_mlp)
    grad_act = [project(r, [pinned(w) for w in full_down], jnp.bfloat16) for r in up_held]
    (own_mlp,) = after((own_mlp,), full_gate, full_up, grad_act[0])
    rows_mlp = [own_mlp, sibling(own_mlp)]
    steps = [mlp_step(r, full_gate, full_up, g) for r, g in zip(rows_mlp, grad_act)]
    activated, grad_gate_pre, grad_up_pre = zip(*steps)

    gate_up = list(zip(grad_gate_pre, grad_up_pre))
    mlp_sums = chip_sums(gate_up[0], gate_up[1], [full_gate, full_up])
    arrived = arrive_z(mlp_sums)

    gg, gu = after((grad_gate_pre, grad_up_pre), mlp_sums)
    made_a = weight_product([(rows_mlp, gg, 0, 1024), (rows_up, activated, 0, 512)], "x", me, 2)
    made_b = weight_product([(rows_mlp, gu, 0, 1024), (rows_up, activated, 512, 1024)], "y", me, 2)
    sums = [made_a[0], made_b[0]]
    rings = [ring_cuts(total, axis) for total, axis in zip(sums, "xy")]
    (arrived,) = after((arrived,), made_a[-1][0], made_b[-1][0])
    grad_residual, grad_residual_b = mlp_norm_backward(upstream, arrived, residual, gain_mlp)

    own_gr = gather_z(grad_residual_b)
    rings = [after(cuts, grad_residual_b) for cuts in rings]
    sums = [add(received, made[1]) for received, made in zip(rings, (made_a, made_b))]
    rings = [ring_cuts(total, axis) for total, axis in zip(sums, "xy")]
    acts = after(activated, *sums[0], *sums[1])
    down_other = down_products(acts[1], full_down)
    down_own = down_products(acts[0], full_down)
    down_arrived = [sibling(half) for half in down_other]
    (own_gr,) = after((own_gr,), *down_own, *down_arrived, *rings[0], *rings[1])
    rows_gr = [own_gr, sibling(own_gr)]
    rings = [after(cuts, own_gr) for cuts in rings]
    sums = [add(received, made[2], True) for received, made in zip(rings, (made_a, made_b))]
    rings = [ring_cuts(total, axis) for total, axis in zip(sums, "xy")]
    down_sums = join_sums(after(down_own, sums[0][0], sums[1][0]), down_arrived)
    arrived = arrive_z(down_sums)
    grad_attended = [project(r, [w_out_t], jnp.bfloat16) for r in after(rows_gr, sums[0][0], sums[1][0])]
    grad_qkv, other_grad_qkv = attend_backward(qkv, lse, grad_attended, tables, me.halves)
    blocks_a = second_blocks([after(rings[0], grad_qkv), made_a[3]], "x", me)
    parts_a = second_stage(blocks_a, "x")
    attn_sums = chip_product(grad_qkv, other_grad_qkv, w_qkv, sibling(w_qkv))
    (attn_sums,) = after((attn_sums,), arrived, blocks_a[0])
    grad_arrived = arrive_z(attn_sums)

    d_qkv = after((grad_qkv, other_grad_qkv), attn_sums)
    terms = [(normed_attn, d_qkv, 0, 384), (rows_gr, (attended, other_attended), 0, 256)]
    made_attn = [cut for (cut,) in weight_product(terms, "y", me)]
    sent_attn = send_pieces(made_attn, "y")
    blocks_b = second_blocks([after(rings[1], made_attn[-1]), made_b[3]], "y", me)
    (arrived,) = after((arrived,), blocks_b[0])
    layer_out = layer_output(residual, arrived)
    share_a = summed(parts_a, layer_out)
    (grad_arrived,) = after((grad_arrived,), share_a)
    grad_tokens = attn_norm_backward(grad_residual, grad_arrived, inputs_b, gain_attn)
    (layer_out,) = after((layer_out,), grad_tokens)
    blocks_b = list(after(blocks_b, share_a))
    blocks_b[2:3] = after(blocks_b[2:3], grad_tokens)
    parts_b = second_stage(blocks_b, "y")
    share_b = fl(swapped(bf(summed(parts_b, grad_tokens))))
    blocks_attn = second_blocks([[part] for part in after(sent_attn, grad_tokens)], "y", me)
    share_attn = fl(swapped(bf(summed(second_stage(blocks_attn, "y"), grad_tokens))))

    def gain_sum(*terms):
        return sum(jnp.sum(fl(w) * g, axis=1) for w, g in terms)

    gain_sums = jnp.stack(
        [
            gain_sum((jnp.concatenate([w_query, w_key, w_value], axis=1), share_attn[:, :384])),
            gain_sum((w_gate, share_a[:, :1024]), (w_up, share_b[:, :1024])),
        ]
    )
    gain_sums = gain_sums / fl(jnp.stack([attn_gain, mlp_gain]))
    gain_sums = gain_sums + z_moved(gain_sums, 1) + z_moved(gain_sums, 2) + z_moved(gain_sums, 3)
    gain_sums = gain_sums + h_flipped(gain_sums)
    return (
        swapped(layer_out),
        swapped(grad_tokens),
        share_attn[:, :256],
        share_attn[:, 256:320],
        share_attn[:, 320:384],
        share_attn[:, 384:].T,
        gain_sums[0],
        share_a[:, :1024],
        share_b[:, :1024],
        jnp.concatenate([share_a[:, 1024:], share_b[:, 1024:]], axis=1).T,
        gain_sums[1],
    )


def solution(mesh):
    split = Mesh(mesh.devices.reshape(4, 2, 2, 2, 4), AXES)
    dp, tensor = ("x", "l", "c"), ("h", "z")
    both = P(AXES, None)
    weight, turned, vector = P(dp, tensor), P(tensor, dp), P(dp)
    in_specs = (
        both, vector, weight, weight, weight, turned, vector, weight, weight, turned, vector, both,
    )
    out_specs = (
        both, both, weight, weight, weight, turned, vector, weight, weight, turned, vector,
    )
    return jax.shard_map(on_device, mesh=split, in_specs=in_specs, out_specs=out_specs, check_vma=False)
```

```python
import functools
import itertools
import math

import jax
import jax.numpy as jnp
from jax import lax
from jax.experimental import pallas as pl
from jax.experimental.pallas import tpu as pltpu
from jax.sharding import Mesh, PartitionSpec as P

H = 32
KV = 8
DH = 64
SEQ_LEN = 1024
D = 2048
eps = 1e-05

SIZES = dict(x=4, l=2, c=2, h=2, z=4)
AXES = ("x", "l", "c", "h", "z")

SCALE = DH ** (-0.5)
SCALE2 = SCALE * math.log2(math.e)
VMEM_LIMIT = 12 * 1024 * 1024


def pairs(axes, move):
    def place(index):
        at = 0
        for a in axes:
            at = at * SIZES[a] + index[a]
        return at

    out = []
    for index in itertools.product(*[range(SIZES[a]) for a in axes]):
        here = dict(zip(axes, index))
        out.append((place(here), place(move(dict(here)))))
    return out


def to_swapped(d):
    d["c"], d["h"] = d["h"], d["c"]
    return d


def to_sibling(d):
    d["c"] = 1 - d["c"]
    return d


def along(axis):
    def move(d):
        step = 1 - 2 * d["c"]
        if axis == "y":
            y = (2 * d["h"] + d["l"] + step) % 4
            d["h"], d["l"] = y // 2, y % 2
        else:
            d[axis] = (d[axis] + step) % 4
        return d

    return move


RING_AXES = dict(x=("x", "c"), y=("l", "c", "h"))
Z_STEPS = (0, 1, 3, 2)
PIECES = (1, 2, 3, 0)


def ring(value, axis):
    axes = RING_AXES[axis]
    return lax.ppermute(value, axes, pairs(axes, along(axis)))


def swapped(value):
    return lax.ppermute(value, ("c", "h"), pairs(("c", "h"), to_swapped))


def sibling(value):
    return lax.ppermute(value, ("c",), pairs(("c",), to_sibling))


def z_moved(value, step):
    def move(d):
        d["z"] = (d["z"] + step) % 4
        return d

    return lax.ppermute(value, ("z",), pairs(("z",), move))


def h_flipped(value):
    def move(d):
        d["h"] = 1 - d["h"]
        return d

    return lax.ppermute(value, ("h",), pairs(("h",), move))


def after(values, *earlier):
    held = lax.optimization_barrier((tuple(values), tuple(earlier)))
    return held[0]


def dot(a, b, ca, cb):
    return lax.dot_general(a, b, (((ca,), (cb,)), ((), ())), preferred_element_type=jnp.float32)


def bf(v):
    return v.astype(jnp.bfloat16)


def fl(v):
    return v.astype(jnp.float32)


def sds(shape, dtype=jnp.bfloat16):
    return jax.ShapeDtypeStruct(shape, dtype)


def cost(flops):
    return pl.CostEstimate(flops=int(flops), bytes_accessed=1, transcendentals=0)


PARAMS = pltpu.CompilerParams(vmem_limit_bytes=VMEM_LIMIT)
ANY = pl.BlockSpec(memory_space=pl.ANY)
WHOLE = pl.BlockSpec(memory_space=pltpu.VMEM)


class Place:
    def __init__(self):
        self.c = lax.axis_index("c")
        self.x = lax.axis_index("x")
        self.h = lax.axis_index("h")
        self.y = 2 * self.h + lax.axis_index("l")
        self.step = 1 - 2 * self.c
        self.halves = jnp.stack([512 * self.c, 512 * (1 - self.c)]).astype(jnp.int32)
        z = lax.axis_index("z")
        self.z_order = jnp.stack([lax.rem(z - step + 4, 4) for step in Z_STEPS]).astype(jnp.int32)
        self.blocks = {}
        for first, second in (("x", "y"), ("y", "x")):
            out = []
            for k2 in range(4):
                for k1 in range(4):
                    a, b = self.source(first, k1), self.source(second, k2)
                    out.append(4 * a + b if first == "x" else 4 * b + a)
            self.blocks[first] = jnp.stack(out).astype(jnp.int32)

    def source(self, axis, k):
        at = lax.rem(dict(x=self.x, y=self.y)[axis] - self.step * k + 4, 4)
        if axis == "y":
            at = 2 * lax.rem(at, 2) + lax.div(at, 2)
        return at


SMEM = pl.BlockSpec(memory_space=pltpu.SMEM)


def pinned(value):
    return pltpu.with_memory_space_constraint(value, pltpu.VMEM)


def place_rows(halves, blocks, widths):
    m = halves[0][0].shape[1]
    runs = []
    low = 0
    for i, width in enumerate(widths):
        at = low
        while at < low + width:
            end = min(low + width, (at // m + 1) * m)
            runs.append((at // m, at % m, i, at - low, end - at))
            at = end
        low += width

    def kernel(blocks_ref, *rest):
        sems = rest[-1]
        copies = []
        for k2 in range(4):
            for k1 in range(4):
                at = pl.multiple_of(blocks_ref[4 * k2 + k1] * 128, 128)
                for half, source, i, target, width in runs:
                    copies.append(
                        pltpu.make_async_copy(
                            rest[4 * half + k2].at[pl.ds(128 * k1, 128), pl.ds(source, width)],
                            rest[8 + i].at[pl.ds(at, 128), pl.ds(target, width)],
                            sems.at[len(copies)],
                        )
                    )
        for copy in copies:
            copy.start()
        for copy in copies:
            copy.wait()

    return pl.pallas_call(
        kernel,
        out_shape=[pltpu.VMEM((D, width), jnp.bfloat16) for width in widths],
        in_specs=[SMEM] + [ANY] * 8,
        out_specs=[WHOLE] * len(widths),
        scratch_shapes=[pltpu.SemaphoreType.DMA((16 * len(runs),))],
        compiler_params=PARAMS,
        cost_estimate=cost(1),
        name="place_rows",
    )(blocks, *halves[0], *halves[1])


def stepped(value, axis, steps):
    def move(d):
        for _ in range(steps):
            d = along(axis)(d)
        return d

    axes = RING_AXES[axis]
    return lax.ppermute(value, axes, pairs(axes, move))


def chain(block, axis, holds):
    parts = [block]
    for hold in holds:
        part = ring(parts[-1], axis)
        parts.append(part if hold is None else after((part,), hold)[0])
    return parts


def gather_plane(block):
    wide = jnp.broadcast_to(block[None], (16,) + block.shape)
    return lax.all_to_all(wide, ("x", "l", "h"), split_axis=0, concat_axis=0, tiled=True).reshape(D, block.shape[1])


def call(kernel, name, outs, args, flops, scratch=(), limit=VMEM_LIMIT):
    return pl.pallas_call(
        kernel,
        out_shape=outs,
        in_specs=[SMEM if a.dtype == jnp.int32 else WHOLE for a in args],
        out_specs=[WHOLE] * len(outs),
        scratch_shapes=list(scratch),
        compiler_params=pltpu.CompilerParams(vmem_limit_bytes=limit),
        cost_estimate=cost(flops),
        name=name,
    )(*args)


def weight_product(terms, first, me, cuts=1):
    order = jnp.stack([me.source(first, k) for k in PIECES]).astype(jnp.int32)
    n = sum(high - low for _, _, low, high in terms) // cuts
    args = [order]
    for rows, right, _, _ in terms:
        args += [*rows, *right]

    def kernel(order_ref, *refs):
        for p in range(4):
            at = 0
            for t, (_, _, low, high) in enumerate(terms):
                rows, right = refs[4 * t : 4 * t + 2], refs[4 * t + 2 : 4 * t + 4]
                left = []
                for r in rows:
                    lanes = []
                    for j in range(4):
                        block = 4 * order_ref[p] + j if first == "x" else 4 * j + order_ref[p]
                        lanes.append(r[:, pl.ds(pl.multiple_of(block * 128, 128), 128)])
                    left.append(jnp.concatenate(lanes, axis=1))
                for j in range(low, high, 256):
                    end = min(j + 256, high)
                    total = dot(left[0], right[0][:, j:end], 0, 0) + dot(left[1], right[1][:, j:end], 0, 0)
                    out_ref = refs[4 * len(terms) + cuts * p + at // n]
                    out_ref[:, at % n : at % n + end - j] = bf(total)
                    at += end - j

    outs = [pltpu.HBM((512, n), jnp.bfloat16)] * (4 * cuts)
    made = call(kernel, "weight_product", outs, args, 2 * D * SEQ_LEN * n * cuts, limit=24 * 1024 * 1024)
    return [made[cuts * p : cuts * p + cuts] for p in range(4)]


def sum_blocks(parts, order):
    n = sum(cut.shape[1] for cut in parts[0])
    width = min(cut.shape[1] for part in parts for cut in part)

    def kernel(order_ref, *refs):
        for k in range(4):
            at = pl.ds(pl.multiple_of(order_ref[k] * 128, 128), 128)
            for low in range(0, n, width):
                total, first = None, 0
                for part in parts:
                    cut = part[0].shape[1]
                    value = fl(refs[first + low // cut][at, low % cut : low % cut + width])
                    total = value if total is None else total + value
                    first += len(part)
                refs[first + k][:, low : low + width] = bf(total)

    args = [order, *[cut for part in parts for cut in part]]
    return call(kernel, "sum_blocks", [sds((128, n))] * 4, args, 1)


def send_pieces(made, first):
    return [stepped(piece, first, 4 - k) if k else piece for k, piece in zip(PIECES, made)]


def homeward(value, k):
    def move(d):
        y = (2 * d["h"] + d["l"] - k * (1 - 2 * d["c"])) % 4
        d["l"], d["h"], d["c"] = y % 2, d["c"], y // 2
        return d

    axes = ("l", "c", "h")
    return lax.ppermute(value, axes, pairs(axes, move))


def add(one, other, join=False):
    count = len(one)
    n = one[0].shape[1]

    def kernel(*refs):
        for i in range(count):
            total = bf(fl(refs[i][...]) + fl(refs[count + i][...]))
            if join:
                refs[2 * count][:, n * i : n * i + n] = total
            else:
                refs[2 * count + i][...] = total

    outs = [sds((512, n * count))] if join else [sds(a.shape) for a in one]
    return call(kernel, "add", outs, [*one, *other], 1)


def ring_cuts(cuts, axis):
    return [ring(cut, axis) for cut in cuts]


def second_blocks(parts, first, me):
    second = "y" if first == "x" else "x"
    return sum_blocks(parts, jnp.stack([me.source(second, k) for k in PIECES]).astype(jnp.int32))


def second_stage(blocks, first):
    if first == "x":
        return [homeward(block, k) for k, block in zip(PIECES, blocks)]
    return send_pieces(blocks, "x")


def summed(parts, hold):
    return sum(fl(part) for part in after(parts, hold))


def send_z(block):
    return [z_moved(block, step) if step else block for step in Z_STEPS]


def place_tokens(blocks, me):
    def kernel(order_ref, b0, b1, b2, b3, out_ref):
        for k, ref in enumerate((b0, b1, b2, b3)):
            out_ref[pl.ds(pl.multiple_of(order_ref[k] * 128, 128), 128), :] = ref[...]

    return call(kernel, "place_tokens", [sds((512, D))], [me.z_order, *blocks], 1)[0]


def norm_tokens(blocks, gain, me):
    def kernel(order_ref, b0, b1, b2, b3, gain_ref, out_ref):
        for k, ref in enumerate((b0, b1, b2, b3)):
            x = fl(ref[...])
            inverse = lax.rsqrt(jnp.mean(x * x, axis=1, keepdims=True) + eps)
            out_ref[pl.ds(pl.multiple_of(order_ref[k] * 128, 128), 128), :] = bf(x * inverse * gain_ref[...])

    return call(kernel, "norm_tokens", [sds((512, D))], [me.z_order, *blocks, gain], 1)[0]


def gather_z(wide_block):
    whole = lax.all_to_all(wide_block, "z", split_axis=0, concat_axis=0, tiled=True)
    return whole.reshape(512, whole.shape[2])


def arrive_z(sums):
    parts = sums.reshape(4, 128, sums.shape[1])
    return lax.all_to_all(parts, "z", split_axis=0, concat_axis=0, tiled=True)


def partial_sums(pieces, weights):
    count = len(pieces)

    def kernel(*refs):
        for j in range(0, D, 512):
            total = None
            for i in range(count):
                one = dot(refs[i][...], refs[count + i][j : j + 512, :], 1, 1)
                total = one if total is None else total + one
            refs[-1][:, j : j + 512] = bf(total)

    depth = sum(p.shape[1] for p in pieces)
    return call(kernel, "partial_sums", [sds((512, D))], [*pieces, *map(pinned, weights)], 2 * 512 * depth * D)[0]


def chip_sums(own, other, weights):
    received = sibling(partial_sums(other, weights))
    return bf(fl(partial_sums(own, weights)) + fl(received))


def chip_product(own, other, weight, sibling_weight):
    received = sibling(other)
    m = own.shape[1]

    def kernel(a_ref, b_ref, v_ref, w_ref, out_ref):
        for j in range(0, D, 512):
            here = slice(j, j + 512)
            total = dot(a_ref[...], v_ref[here, :m], 1, 1) + dot(b_ref[...], w_ref[here, :m], 1, 1)
            out_ref[:, here] = bf(total)

    args = [own, received, weight, sibling_weight]
    return call(kernel, "chip_product", [sds((512, D))], args, 4 * 512 * m * D)[0]


def project(rows, weights, dtype, width=None):
    width = width or weights[0].shape[1]
    n = width * len(weights)

    def kernel(rows_ref, *refs):
        for i, w_ref in enumerate(refs[:-1]):
            for j in range(0, width, 256):
                product = dot(rows_ref[...], w_ref[:, j : j + 256], 1, 0)
                refs[-1][:, i * width + j : i * width + j + 256] = product.astype(dtype)

    return call(kernel, "project", [sds((512, n), dtype)], [rows, *weights], 2 * 512 * D * n)[0]


def down_products(rows, weights):
    def kernel(rows_ref, w0, w1, *out_refs):
        for j in range(0, D, 512):
            here = slice(j, j + 512)
            total = dot(rows_ref[:, :512], w0[here, :], 1, 1) + dot(rows_ref[:, 512:], w1[here, :], 1, 1)
            out_refs[j // 1024][:, j % 1024 : j % 1024 + 512] = bf(total)

    args = [rows, *map(pinned, weights)]
    return call(kernel, "down_products", [sds((512, D // 2))] * 2, args, 2 * 512 * 1024 * D)


def join_sums(one, other):
    def kernel(a0, a1, b0, b1, out_ref):
        out_ref[:, :1024] = bf(fl(a0[...]) + fl(b0[...]))
        out_ref[:, 1024:] = bf(fl(a1[...]) + fl(b1[...]))

    return call(kernel, "join_sums", [sds((512, D))], [*one, *other], 1)[0]


def rope(u, cosine, sine):
    lane = lax.broadcasted_iota(jnp.int32, u.shape, 1)
    turned = jnp.where(lane % DH < DH // 2, pltpu.roll(u, 96, 1), pltpu.roll(u, 32, 1))
    return u * cosine + turned * sine


def rope_three(u, cosine, sine):
    lane = lax.broadcasted_iota(jnp.int32, cosine.shape, 1)
    last = u[:, 256:]
    return jnp.concatenate(
        [
            rope(u[:, :128], cosine, sine),
            rope(u[:, 128:256], cosine, sine),
            jnp.where(lane < DH, rope(last, cosine, sine), last),
        ],
        axis=1,
    )


def half_at(halves_ref, i):
    return pl.ds(pl.multiple_of(halves_ref[i], 512), 512)


def project_qkv(i, rows, weight, tables, halves):
    def kernel(halves_ref, rows_ref, w_ref, cos_ref, sin_ref, out_ref):
        here = half_at(halves_ref, i)
        product = dot(rows_ref[...], w_ref[:, :384], 1, 0)
        out_ref[...] = bf(rope_three(product, cos_ref[here, :], sin_ref[here, :]))

    args = [halves, rows, weight, *tables]
    return call(kernel, "project_qkv", [sds((512, 384))], args, 2 * 512 * D * 384)[0]


def scores_t(keys, query, q_at):
    s = dot(keys, query, 1, 1)
    key = lax.broadcasted_iota(jnp.int32, (256, 256), 0)
    column = lax.broadcasted_iota(jnp.int32, (256, 256), 1)
    diagonal = jnp.where(key <= column, s[q_at:], -1e30)
    return diagonal if q_at == 0 else jnp.concatenate([s[:q_at], diagonal], axis=0)


def attend(qkv, halves):
    def kernel(halves_ref, q0, q1, own_ref, other_ref, nat_ref, lse_ref, att_ref):
        nat_ref[half_at(halves_ref, 0), :] = q0[...]
        nat_ref[half_at(halves_ref, 1), :] = q1[...]
        kv = nat_ref[:, 256:]
        keys = kv[:, :DH]
        values_t = kv.T[DH:]
        lse_ref[...] = jnp.zeros_like(lse_ref)
        for q_at in range(0, SEQ_LEN, 256):
            end = q_at + 256
            for pair in range(2):
                two = nat_ref[q_at:end, 128 * pair : 128 * pair + 128]
                outs = []
                for i in range(2):
                    s = scores_t(keys[:end], two[:, DH * i : DH * i + DH], q_at)
                    top = jnp.max(s, axis=0, keepdims=True)
                    p = jnp.exp2((s - top) * SCALE2)
                    total = jnp.sum(p, axis=0, keepdims=True)
                    outs.append(dot(values_t[:, :end], bf(p), 1, 0) / total)
                    g = 2 * pair + i
                    lse_ref[g : g + 1, q_at:end] = top * SCALE2 + jnp.log2(total)
                att_ref[q_at:end, 128 * pair : 128 * pair + 128] = bf(jnp.concatenate(outs, axis=0).T)
        own_ref[...] = att_ref[half_at(halves_ref, 0), :]
        other_ref[...] = att_ref[half_at(halves_ref, 1), :]

    outs = [sds((512, 256)), sds((512, 256)), sds((SEQ_LEN, 384)), sds((8, SEQ_LEN), jnp.float32)]
    scratch = [pltpu.VMEM((SEQ_LEN, 256), jnp.bfloat16)]
    return call(kernel, "attend", outs, [halves, *qkv], 20e9, scratch)


def attend_backward(qkv, lse, grad_out, tables, halves):
    def kernel(halves_ref, nat_ref, lse_ref, g0, g1, cos_ref, sin_ref, own_ref, other_ref, go_nat, kv_sum, d_nat):
        go_nat[half_at(halves_ref, 0), :] = g0[...]
        go_nat[half_at(halves_ref, 1), :] = g1[...]
        kv = nat_ref[:, 256:]
        keys = kv[:, :DH]
        values = kv[:, DH:]
        keys_t = kv.T[:DH]
        kv_sum[...] = jnp.zeros_like(kv_sum)
        for q_at in range(0, SEQ_LEN, 256):
            end = q_at + 256
            cosine = cos_ref[q_at:end, :]
            sine = -sin_ref[q_at:end, :]
            for pair in range(2):
                lanes = slice(128 * pair, 128 * pair + 128)
                two = nat_ref[q_at:end, lanes]
                two_grad = go_nat[q_at:end, lanes]
                outs = []
                for i in range(2):
                    query = two[:, DH * i : DH * i + DH]
                    grad = two_grad[:, DH * i : DH * i + DH]
                    g = 2 * pair + i
                    s = scores_t(keys[:end], query, q_at)
                    p = jnp.exp2(s * SCALE2 - lse_ref[g : g + 1, q_at:end])
                    dp = dot(values[:end], grad, 1, 1)
                    delta = jnp.sum(dp * p, axis=0, keepdims=True)
                    ds = bf(p * (dp - delta))
                    kv_sum[:end, :] += jnp.concatenate(
                        [dot(ds, query, 1, 0), dot(bf(p), grad, 1, 0)], axis=1
                    )
                    outs.append(dot(keys_t[:, :end], ds, 1, 0))
                d_query = jnp.concatenate(outs, axis=0).T * SCALE
                d_nat[q_at:end, lanes] = bf(rope(d_query, cosine, sine))
        lane = lax.broadcasted_iota(jnp.int32, (SEQ_LEN, 128), 1)
        total = kv_sum[...]
        turned = rope(total * SCALE, cos_ref[...], -sin_ref[...])
        d_nat[:, 256:] = bf(jnp.where(lane < DH, turned, total))
        own_ref[...] = d_nat[half_at(halves_ref, 0), :]
        other_ref[...] = d_nat[half_at(halves_ref, 1), :]

    scratch = [
        pltpu.VMEM((SEQ_LEN, 256), jnp.bfloat16),
        pltpu.VMEM((SEQ_LEN, 128), jnp.float32),
        pltpu.VMEM((SEQ_LEN, 384), jnp.bfloat16),
    ]
    args = [halves, qkv, lse, *grad_out, *tables]
    return call(kernel, "attend_backward", [sds((512, 384))] * 2, args, 30e9, scratch)


def mlp_step(rows, w_gate, w_up, grad_act):
    width = w_gate.shape[1]

    def kernel(rows_ref, g_ref, u_ref, ga_ref, act_ref, gg_ref, gu_ref):
        for j in range(0, width, 256):
            here = slice(j, j + 256)
            gate = dot(rows_ref[...], g_ref[:, here], 1, 0)
            up = dot(rows_ref[...], u_ref[:, here], 1, 0)
            sig = jax.nn.sigmoid(gate)
            silu = gate * sig
            ga = fl(ga_ref[:, here])
            act_ref[:, here] = bf(silu * up)
            gg_ref[:, here] = bf(ga * up * sig * (1.0 + gate * (1.0 - sig)))
            gu_ref[:, here] = bf(ga * silu)

    args = [rows, pinned(w_gate), pinned(w_up), grad_act]
    return call(kernel, "mlp_step", [sds((512, width))] * 3, args, 4 * 512 * D * width)


def frequencies(head_size):
    pair_index = jnp.arange(head_size // 2).astype(jnp.float32)
    base_freq = 500000.0 ** (-2.0 * pair_index / head_size)
    wavelen = 2.0 * jnp.pi / base_freq
    smooth = (8192.0 / wavelen - 1.0) / 3.0
    blended = (1.0 - smooth) * base_freq / 32.0 + smooth * base_freq
    return jnp.where(
        wavelen < 2048.0, base_freq, jnp.where(wavelen > 8192.0, base_freq / 32.0, blended)
    )


LONG = 60e9


def wide(out_ref, value):
    for k in range(4):
        out_ref[k] = value


def arrived_sum(ref):
    return fl(ref[0]) + fl(ref[1]) + fl(ref[2]) + fl(ref[3])


def mlp_norm(inputs, arrived, gain):
    def kernel(x_ref, a_ref, gain_ref, residual_ref, out_ref):
        residual = fl(x_ref[...]) + arrived_sum(a_ref)
        residual_ref[...] = residual
        inverse = lax.rsqrt(jnp.mean(residual * residual, axis=1, keepdims=True) + eps)
        wide(out_ref, bf(residual * inverse * gain_ref[...]))

    outs = [sds((128, D), jnp.float32), sds((4, 128, D))]
    return call(kernel, "mlp_norm", outs, [inputs, arrived, gain], LONG)


def norm_grad(grad, values, gain):
    inverse = lax.rsqrt(jnp.mean(values * values, axis=1, keepdims=True) + eps)
    unit = values * inverse
    scaled = grad * gain
    return inverse * (scaled - unit * jnp.mean(scaled * unit, axis=1, keepdims=True))


def mlp_norm_backward(upstream, arrived, residual, gain):
    def kernel(g_ref, a_ref, r_ref, gain_ref, grad_ref, out_ref):
        grad = fl(g_ref[...]) + norm_grad(arrived_sum(a_ref), r_ref[...], gain_ref[...])
        grad_ref[...] = grad
        wide(out_ref, bf(grad))

    outs = [sds((128, D), jnp.float32), sds((4, 128, D))]
    return call(kernel, "mlp_norm_backward", outs, [upstream, arrived, residual, gain], LONG)


def attn_norm_backward(grad_residual, arrived, inputs, gain):
    def kernel(g_ref, a_ref, x_ref, gain_ref, out_ref):
        out_ref[...] = bf(g_ref[...] + norm_grad(arrived_sum(a_ref), fl(x_ref[...]), gain_ref[...]))

    return call(kernel, "attn_norm_backward", [sds((128, D))], [grad_residual, arrived, inputs, gain], LONG)[0]


def layer_output(residual, arrived):
    def kernel(r_ref, a_ref, out_ref):
        out_ref[...] = bf(r_ref[...] + arrived_sum(a_ref))

    return call(kernel, "layer_output", [sds((128, D))], [residual, arrived], 1)[0]


def on_device(
    tokens, positions, w_query, w_key, w_value, w_out, attn_gain, w_gate, w_up, w_down, mlp_gain, cotangent
):
    me = Place()
    inputs_b = swapped(tokens)
    places = jnp.concatenate([(positions // 256).reshape(128, 8), (positions % 256).reshape(128, 8)], axis=1)
    extra = jnp.concatenate([attn_gain[:, None], mlp_gain[:, None], bf(places)], axis=1)
    extra = jnp.pad(extra, ((0, 0), (0, 110)))
    part_attn = swapped(jnp.concatenate([w_query, w_key, w_value, extra, w_out.T], axis=1))
    part_attn, inputs_b = lax.optimization_barrier((part_attn, inputs_b))

    blocks_in = send_z(inputs_b)
    w_qkv = gather_plane(part_attn[:, :512])
    w_gate, w_up, w_down, cotangent = after((w_gate, w_up, w_down, cotangent), inputs_b)
    upstream = swapped(cotangent)
    down_rows = w_down.T
    part_ab = swapped(jnp.concatenate([w_gate, down_rows[:, :512], w_up, down_rows[:, 512:]], axis=1))

    place = fl(part_attn[:, 386:402])
    seq_positions = (256.0 * place[:, :8] + place[:, 8:]).reshape(SEQ_LEN)
    freq = jnp.tile(frequencies(DH), 4)
    angles = seq_positions[:, None] * freq[None, :]
    sign = jnp.where(jnp.arange(128) % DH < DH // 2, -1.0, 1.0)
    tables = (jnp.cos(angles), jnp.sin(angles) * sign[None, :])
    pick = bf(jnp.arange(128)[None, :] == jnp.arange(8)[:, None])
    gain_rows = dot(pick, w_qkv[:, 384:], 1, 1)
    gain_attn, gain_mlp = gain_rows[:1], gain_rows[1:2]

    blocks_in = after(blocks_in, *tables, upstream, part_ab)
    own_normed = norm_tokens(blocks_in, gain_attn, me)
    normed_attn = [own_normed, sibling(own_normed)]
    own_qkv = project_qkv(0, normed_attn[0], w_qkv, tables, me.halves)
    projected = [own_qkv, project_qkv(1, normed_attn[1], w_qkv, tables, me.halves)]

    (own_up,) = after((upstream,), own_normed)
    blocks_up = send_z(own_up)
    (part_out,) = after((part_attn[:, 512:],), own_qkv)
    w_out_t = gather_plane(part_out)

    projected = after(projected, *blocks_up[1:3])
    attended, other_attended, qkv, lse = attend(projected, me.halves)
    (w_out_t,) = after((w_out_t,), attended, blocks_up[3])
    out_sums = chip_product(attended, other_attended, w_out_t, sibling(w_out_t))
    (out_sums,) = after((out_sums,), *blocks_up)

    (part_ab,) = after((part_ab,), own_normed)
    part_a, part_b = part_ab[:, :1536], part_ab[:, 1536:]
    holds = (projected[1], attended, out_sums)
    stages_a, stages_b = (
        [jnp.concatenate([part[:, low : low + 768] for part in chain(p, axis, holds)], axis=0) for low in (0, 768)]
        for p, axis in ((part_a, "x"), (part_b, "y"))
    )

    own_up = place_tokens(blocks_up, me)
    rows_up = [own_up, sibling(own_up)]
    arrived = arrive_z(out_sums)

    parts_a = [chain(stage, "y", (None, None, None)) for stage in stages_a]
    parts_b = [chain(stage, "x", (None, None, None)) for stage in stages_b]
    full_gate, down_a = place_rows(parts_a, me.blocks["x"], (1024, 512))
    full_up, down_b = place_rows(parts_b, me.blocks["y"], (1024, 512))
    full_down = [down_a, down_b]

    (arrived,) = after((arrived,), *[parts[2] for parts in (*parts_a, *parts_b)], *rows_up)
    residual, normed_mlp = mlp_norm(inputs_b, arrived, gain_mlp)
    own_mlp = gather_z(normed_mlp)
    up_held = after(rows_up, normed_mlp)
    grad_act = [project(r, [pinned(w) for w in full_down], jnp.bfloat16) for r in up_held]
    (own_mlp,) = after((own_mlp,), full_gate, full_up, grad_act[0])
    rows_mlp = [own_mlp, sibling(own_mlp)]
    steps = [mlp_step(r, full_gate, full_up, g) for r, g in zip(rows_mlp, grad_act)]
    activated, grad_gate_pre, grad_up_pre = zip(*steps)

    gate_up = list(zip(grad_gate_pre, grad_up_pre))
    mlp_sums = chip_sums(gate_up[0], gate_up[1], [full_gate, full_up])
    arrived = arrive_z(mlp_sums)

    gg, gu = after((grad_gate_pre, grad_up_pre), mlp_sums)
    made_a = weight_product([(rows_mlp, gg, 0, 1024), (rows_up, activated, 0, 512)], "x", me, 2)
    made_b = weight_product([(rows_mlp, gu, 0, 1024), (rows_up, activated, 512, 1024)], "y", me, 2)
    sums = [made_a[0], made_b[0]]
    rings = [ring_cuts(total, axis) for total, axis in zip(sums, "xy")]
    (arrived,) = after((arrived,), made_a[-1][0], made_b[-1][0])
    grad_residual, grad_residual_b = mlp_norm_backward(upstream, arrived, residual, gain_mlp)

    own_gr = gather_z(grad_residual_b)
    rings = [after(cuts, grad_residual_b) for cuts in rings]
    sums = [add(received, made[1]) for received, made in zip(rings, (made_a, made_b))]
    rings = [ring_cuts(total, axis) for total, axis in zip(sums, "xy")]
    acts = after(activated, *sums[0], *sums[1])
    down_other = down_products(acts[1], full_down)
    down_own = down_products(acts[0], full_down)
    down_arrived = [sibling(half) for half in down_other]
    (own_gr,) = after((own_gr,), *down_own, *down_arrived, *rings[0], *rings[1])
    rows_gr = [own_gr, sibling(own_gr)]
    rings = [after(cuts, own_gr) for cuts in rings]
    sums = [add(received, made[2], True) for received, made in zip(rings, (made_a, made_b))]
    rings = [ring_cuts(total, axis) for total, axis in zip(sums, "xy")]
    down_sums = join_sums(after(down_own, sums[0][0], sums[1][0]), down_arrived)
    arrived = arrive_z(down_sums)
    grad_attended = [project(r, [w_out_t], jnp.bfloat16) for r in after(rows_gr, sums[0][0], sums[1][0])]
    grad_qkv, other_grad_qkv = attend_backward(qkv, lse, grad_attended, tables, me.halves)
    blocks_a = second_blocks([after(rings[0], grad_qkv), made_a[3]], "x", me)
    parts_a = second_stage(blocks_a, "x")
    attn_sums = chip_product(grad_qkv, other_grad_qkv, w_qkv, sibling(w_qkv))
    (attn_sums,) = after((attn_sums,), arrived, blocks_a[0])
    grad_arrived = arrive_z(attn_sums)

    d_qkv = after((grad_qkv, other_grad_qkv), attn_sums)
    terms = [(normed_attn, d_qkv, 0, 384), (rows_gr, (attended, other_attended), 0, 256)]
    made_attn = [cut for (cut,) in weight_product(terms, "y", me)]
    sent_attn = send_pieces(made_attn, "y")
    blocks_b = second_blocks([after(rings[1], made_attn[-1]), made_b[3]], "y", me)
    (arrived,) = after((arrived,), blocks_b[0])
    layer_out = layer_output(residual, arrived)
    share_a = summed(parts_a, layer_out)
    (grad_arrived,) = after((grad_arrived,), share_a)
    grad_tokens = attn_norm_backward(grad_residual, grad_arrived, inputs_b, gain_attn)
    (layer_out,) = after((layer_out,), grad_tokens)
    blocks_b = list(after(blocks_b, share_a))
    blocks_b[2:3] = after(blocks_b[2:3], grad_tokens)
    parts_b = second_stage(blocks_b, "y")
    tokens_out = swapped(grad_tokens)
    *sent_attn, parts_b[0], parts_b[1] = after([*sent_attn, *parts_b[:2]], grad_tokens)
    blocks_attn = second_blocks([[part] for part in sent_attn], "y", me)
    share_b = fl(swapped(bf(summed(parts_b, blocks_attn[0]))))
    share_attn = fl(swapped(bf(summed(second_stage(blocks_attn, "y"), tokens_out))))

    def gain_sum(*terms):
        return sum(jnp.sum(fl(w) * g, axis=1) for w, g in terms)

    gain_sums = jnp.stack(
        [
            gain_sum((jnp.concatenate([w_query, w_key, w_value], axis=1), share_attn[:, :384])),
            gain_sum((w_gate, share_a[:, :1024]), (w_up, share_b[:, :1024])),
        ]
    )
    gain_sums = gain_sums / fl(jnp.stack([attn_gain, mlp_gain]))
    gain_sums = gain_sums + z_moved(gain_sums, 1) + z_moved(gain_sums, 2) + z_moved(gain_sums, 3)
    gain_sums = gain_sums + h_flipped(gain_sums)
    return (
        swapped(layer_out),
        tokens_out,
        share_attn[:, :256],
        share_attn[:, 256:320],
        share_attn[:, 320:384],
        share_attn[:, 384:].T,
        gain_sums[0],
        share_a[:, :1024],
        share_b[:, :1024],
        jnp.concatenate([share_a[:, 1024:], share_b[:, 1024:]], axis=1).T,
        gain_sums[1],
    )


def solution(mesh):
    split = Mesh(mesh.devices.reshape(4, 2, 2, 2, 4), AXES)
    dp, tensor = ("x", "l", "c"), ("h", "z")
    both = P(AXES, None)
    weight, turned, vector = P(dp, tensor), P(tensor, dp), P(dp)
    in_specs = (
        both, vector, weight, weight, weight, turned, vector, weight, weight, turned, vector, both,
    )
    out_specs = (
        both, both, weight, weight, weight, turned, vector, weight, weight, turned, vector,
    )
    return jax.shard_map(on_device, mesh=split, in_specs=in_specs, out_specs=out_specs, check_vma=False)
```

```python
import functools
import itertools
import math

import jax
import jax.numpy as jnp
from jax import lax
from jax.experimental import pallas as pl
from jax.experimental.pallas import tpu as pltpu
from jax.sharding import Mesh, PartitionSpec as P

H = 32
KV = 8
DH = 64
SEQ_LEN = 1024
D = 2048
eps = 1e-05

SIZES = dict(x=4, l=2, c=2, h=2, z=4)
AXES = ("x", "l", "c", "h", "z")

SCALE = DH ** (-0.5)
SCALE2 = SCALE * math.log2(math.e)
VMEM_LIMIT = 12 * 1024 * 1024


def pairs(axes, move):
    def place(index):
        at = 0
        for a in axes:
            at = at * SIZES[a] + index[a]
        return at

    out = []
    for index in itertools.product(*[range(SIZES[a]) for a in axes]):
        here = dict(zip(axes, index))
        out.append((place(here), place(move(dict(here)))))
    return out


def to_swapped(d):
    d["c"], d["h"] = d["h"], d["c"]
    return d


def to_sibling(d):
    d["c"] = 1 - d["c"]
    return d


def along(axis):
    def move(d):
        step = 1 - 2 * d["c"]
        if axis == "y":
            y = (2 * d["h"] + d["l"] + step) % 4
            d["h"], d["l"] = y // 2, y % 2
        else:
            d[axis] = (d[axis] + step) % 4
        return d

    return move


RING_AXES = dict(x=("x", "c"), y=("l", "c", "h"))
Z_STEPS = (0, 1, 3, 2)
PIECES = (1, 2, 3, 0)


def ring(value, axis):
    axes = RING_AXES[axis]
    return lax.ppermute(value, axes, pairs(axes, along(axis)))


def swapped(value):
    return lax.ppermute(value, ("c", "h"), pairs(("c", "h"), to_swapped))


def sibling(value):
    return lax.ppermute(value, ("c",), pairs(("c",), to_sibling))


def z_moved(value, step):
    def move(d):
        d["z"] = (d["z"] + step) % 4
        return d

    return lax.ppermute(value, ("z",), pairs(("z",), move))


def h_flipped(value):
    def move(d):
        d["h"] = 1 - d["h"]
        return d

    return lax.ppermute(value, ("h",), pairs(("h",), move))


def after(values, *earlier):
    held = lax.optimization_barrier((tuple(values), tuple(earlier)))
    return held[0]


def dot(a, b, ca, cb):
    return lax.dot_general(a, b, (((ca,), (cb,)), ((), ())), preferred_element_type=jnp.float32)


def bf(v):
    return v.astype(jnp.bfloat16)


def fl(v):
    return v.astype(jnp.float32)


def sds(shape, dtype=jnp.bfloat16):
    return jax.ShapeDtypeStruct(shape, dtype)


def cost(flops):
    return pl.CostEstimate(flops=int(flops), bytes_accessed=1, transcendentals=0)


PARAMS = pltpu.CompilerParams(vmem_limit_bytes=VMEM_LIMIT)
ANY = pl.BlockSpec(memory_space=pl.ANY)
WHOLE = pl.BlockSpec(memory_space=pltpu.VMEM)


class Place:
    def __init__(self):
        self.c = lax.axis_index("c")
        self.x = lax.axis_index("x")
        self.h = lax.axis_index("h")
        self.y = 2 * self.h + lax.axis_index("l")
        self.step = 1 - 2 * self.c
        self.halves = jnp.stack([512 * self.c, 512 * (1 - self.c)]).astype(jnp.int32)
        z = lax.axis_index("z")
        self.z_order = jnp.stack([lax.rem(z - step + 4, 4) for step in Z_STEPS]).astype(jnp.int32)
        self.blocks = {}
        for first, second in (("x", "y"), ("y", "x")):
            out = []
            for k2 in range(4):
                for k1 in range(4):
                    a, b = self.source(first, k1), self.source(second, k2)
                    out.append(4 * a + b if first == "x" else 4 * b + a)
            self.blocks[first] = jnp.stack(out).astype(jnp.int32)

    def source(self, axis, k):
        at = lax.rem(dict(x=self.x, y=self.y)[axis] - self.step * k + 4, 4)
        if axis == "y":
            at = 2 * lax.rem(at, 2) + lax.div(at, 2)
        return at


SMEM = pl.BlockSpec(memory_space=pltpu.SMEM)


def pinned(value):
    return pltpu.with_memory_space_constraint(value, pltpu.VMEM)


def place_rows(parts, blocks, widths):
    def kernel(blocks_ref, p0, p1, p2, p3, *rest):
        sems = rest[-1]
        copies = []
        for k2, part in enumerate((p0, p1, p2, p3)):
            for k1 in range(4):
                at = pl.multiple_of(blocks_ref[4 * k2 + k1] * 128, 128)
                low = 0
                for i, width in enumerate(widths):
                    copies.append(
                        pltpu.make_async_copy(
                            part.at[pl.ds(128 * k1, 128), pl.ds(low, width)],
                            rest[i].at[pl.ds(at, 128)],
                            sems.at[len(widths) * (4 * k2 + k1) + i],
                        )
                    )
                    low += width
        for copy in copies:
            copy.start()
        for copy in copies:
            copy.wait()

    return pl.pallas_call(
        kernel,
        out_shape=[pltpu.VMEM((D, width), jnp.bfloat16) for width in widths],
        in_specs=[SMEM] + [ANY] * 4,
        out_specs=[WHOLE] * len(widths),
        scratch_shapes=[pltpu.SemaphoreType.DMA((16 * len(widths),))],
        compiler_params=PARAMS,
        cost_estimate=cost(1),
        name="place_rows",
    )(blocks, *parts)


def stepped(value, axis, steps):
    def move(d):
        for _ in range(steps):
            d = along(axis)(d)
        return d

    axes = RING_AXES[axis]
    return lax.ppermute(value, axes, pairs(axes, move))


def chain(block, axis, holds):
    parts = [block]
    for hold in holds:
        part = ring(parts[-1], axis)
        parts.append(part if hold is None else after((part,), hold)[0])
    return parts


def gather_plane(block):
    wide = jnp.broadcast_to(block[None], (16,) + block.shape)
    return lax.all_to_all(wide, ("x", "l", "h"), split_axis=0, concat_axis=0, tiled=True).reshape(D, block.shape[1])


def call(kernel, name, outs, args, flops, scratch=(), limit=VMEM_LIMIT):
    return pl.pallas_call(
        kernel,
        out_shape=outs,
        in_specs=[SMEM if a.dtype == jnp.int32 else WHOLE for a in args],
        out_specs=[WHOLE] * len(outs),
        scratch_shapes=list(scratch),
        compiler_params=pltpu.CompilerParams(vmem_limit_bytes=limit),
        cost_estimate=cost(flops),
        name=name,
    )(*args)


def weight_product(terms, first, me, cuts=1):
    order = jnp.stack([me.source(first, k) for k in PIECES]).astype(jnp.int32)
    n = sum(high - low for _, _, low, high in terms) // cuts
    args = [order]
    for rows, right, _, _ in terms:
        args += [*rows, *right]

    def kernel(order_ref, *refs):
        for p in range(4):
            at = 0
            for t, (_, _, low, high) in enumerate(terms):
                rows, right = refs[4 * t : 4 * t + 2], refs[4 * t + 2 : 4 * t + 4]
                left = []
                for r in rows:
                    lanes = []
                    for j in range(4):
                        block = 4 * order_ref[p] + j if first == "x" else 4 * j + order_ref[p]
                        lanes.append(r[:, pl.ds(pl.multiple_of(block * 128, 128), 128)])
                    left.append(jnp.concatenate(lanes, axis=1))
                for j in range(low, high, 256):
                    end = min(j + 256, high)
                    total = dot(left[0], right[0][:, j:end], 0, 0) + dot(left[1], right[1][:, j:end], 0, 0)
                    out_ref = refs[4 * len(terms) + cuts * p + at // n]
                    out_ref[:, at % n : at % n + end - j] = bf(total)
                    at += end - j

    outs = [pltpu.HBM((512, n), jnp.bfloat16)] * (4 * cuts)
    made = call(kernel, "weight_product", outs, args, 2 * D * SEQ_LEN * n * cuts, limit=24 * 1024 * 1024)
    return [made[cuts * p : cuts * p + cuts] for p in range(4)]


def sum_blocks(parts, order):
    n = sum(cut.shape[1] for cut in parts[0])
    width = min(cut.shape[1] for part in parts for cut in part)

    def kernel(order_ref, *refs):
        for k in range(4):
            at = pl.ds(pl.multiple_of(order_ref[k] * 128, 128), 128)
            for low in range(0, n, width):
                total, first = None, 0
                for part in parts:
                    cut = part[0].shape[1]
                    value = fl(refs[first + low // cut][at, low % cut : low % cut + width])
                    total = value if total is None else total + value
                    first += len(part)
                refs[first + k][:, low : low + width] = bf(total)

    args = [order, *[cut for part in parts for cut in part]]
    return call(kernel, "sum_blocks", [sds((128, n))] * 4, args, 1)


def send_pieces(made, first):
    return [stepped(piece, first, 4 - k) if k else piece for k, piece in zip(PIECES, made)]


def homeward(value, k):
    def move(d):
        y = (2 * d["h"] + d["l"] - k * (1 - 2 * d["c"])) % 4
        d["l"], d["h"], d["c"] = y % 2, d["c"], y // 2
        return d

    axes = ("l", "c", "h")
    return lax.ppermute(value, axes, pairs(axes, move))


def add(one, other, join=False):
    count = len(one)
    n = one[0].shape[1]

    def kernel(*refs):
        for i in range(count):
            total = bf(fl(refs[i][...]) + fl(refs[count + i][...]))
            if join:
                refs[2 * count][:, n * i : n * i + n] = total
            else:
                refs[2 * count + i][...] = total

    outs = [sds((512, n * count))] if join else [sds(a.shape) for a in one]
    return call(kernel, "add", outs, [*one, *other], 1)


def ring_cuts(cuts, axis):
    return [ring(cut, axis) for cut in cuts]


def second_blocks(parts, first, me):
    second = "y" if first == "x" else "x"
    return sum_blocks(parts, jnp.stack([me.source(second, k) for k in PIECES]).astype(jnp.int32))


def second_stage(blocks, first):
    if first == "x":
        return [homeward(block, k) for k, block in zip(PIECES, blocks)]
    return send_pieces(blocks, "x")


def summed(parts, hold):
    return sum(fl(part) for part in after(parts, hold))


def send_z(block):
    return [z_moved(block, step) if step else block for step in Z_STEPS]


def place_tokens(blocks, me):
    def kernel(order_ref, b0, b1, b2, b3, out_ref):
        for k, ref in enumerate((b0, b1, b2, b3)):
            out_ref[pl.ds(pl.multiple_of(order_ref[k] * 128, 128), 128), :] = ref[...]

    return call(kernel, "place_tokens", [sds((512, D))], [me.z_order, *blocks], 1)[0]


def norm_tokens(blocks, gain, me):
    def kernel(order_ref, b0, b1, b2, b3, gain_ref, out_ref):
        for k, ref in enumerate((b0, b1, b2, b3)):
            x = fl(ref[...])
            inverse = lax.rsqrt(jnp.mean(x * x, axis=1, keepdims=True) + eps)
            out_ref[pl.ds(pl.multiple_of(order_ref[k] * 128, 128), 128), :] = bf(x * inverse * gain_ref[...])

    return call(kernel, "norm_tokens", [sds((512, D))], [me.z_order, *blocks, gain], 1)[0]


def gather_z(wide_block):
    whole = lax.all_to_all(wide_block, "z", split_axis=0, concat_axis=0, tiled=True)
    return whole.reshape(512, whole.shape[2])


def arrive_z(sums):
    parts = sums.reshape(4, 128, sums.shape[1])
    return lax.all_to_all(parts, "z", split_axis=0, concat_axis=0, tiled=True)


def partial_sums(pieces, weights):
    count = len(pieces)

    def kernel(*refs):
        for j in range(0, D, 512):
            total = None
            for i in range(count):
                one = dot(refs[i][...], refs[count + i][j : j + 512, :], 1, 1)
                total = one if total is None else total + one
            refs[-1][:, j : j + 512] = bf(total)

    depth = sum(p.shape[1] for p in pieces)
    return call(kernel, "partial_sums", [sds((512, D))], [*pieces, *map(pinned, weights)], 2 * 512 * depth * D)[0]


def chip_sums(own, other, weights):
    received = sibling(partial_sums(other, weights))
    return bf(fl(partial_sums(own, weights)) + fl(received))


def chip_product(own, other, weight, sibling_weight):
    received = sibling(other)
    m = own.shape[1]

    def kernel(a_ref, b_ref, v_ref, w_ref, out_ref):
        for j in range(0, D, 512):
            here = slice(j, j + 512)
            total = dot(a_ref[...], v_ref[here, :m], 1, 1) + dot(b_ref[...], w_ref[here, :m], 1, 1)
            out_ref[:, here] = bf(total)

    args = [own, received, weight, sibling_weight]
    return call(kernel, "chip_product", [sds((512, D))], args, 4 * 512 * m * D)[0]


def project(rows, weights, dtype, width=None):
    width = width or weights[0].shape[1]
    n = width * len(weights)

    def kernel(rows_ref, *refs):
        for i, w_ref in enumerate(refs[:-1]):
            for j in range(0, width, 256):
                product = dot(rows_ref[...], w_ref[:, j : j + 256], 1, 0)
                refs[-1][:, i * width + j : i * width + j + 256] = product.astype(dtype)

    return call(kernel, "project", [sds((512, n), dtype)], [rows, *weights], 2 * 512 * D * n)[0]


def down_products(rows, weights):
    def kernel(rows_ref, w0, w1, *out_refs):
        for j in range(0, D, 512):
            here = slice(j, j + 512)
            total = dot(rows_ref[:, :512], w0[here, :], 1, 1) + dot(rows_ref[:, 512:], w1[here, :], 1, 1)
            out_refs[j // 1024][:, j % 1024 : j % 1024 + 512] = bf(total)

    args = [rows, *map(pinned, weights)]
    return call(kernel, "down_products", [sds((512, D // 2))] * 2, args, 2 * 512 * 1024 * D)


def join_sums(one, other):
    def kernel(a0, a1, b0, b1, out_ref):
        out_ref[:, :1024] = bf(fl(a0[...]) + fl(b0[...]))
        out_ref[:, 1024:] = bf(fl(a1[...]) + fl(b1[...]))

    return call(kernel, "join_sums", [sds((512, D))], [*one, *other], 1)[0]


def rope(u, cosine, sine):
    lane = lax.broadcasted_iota(jnp.int32, u.shape, 1)
    turned = jnp.where(lane % DH < DH // 2, pltpu.roll(u, 96, 1), pltpu.roll(u, 32, 1))
    return u * cosine + turned * sine


def rope_three(u, cosine, sine):
    lane = lax.broadcasted_iota(jnp.int32, cosine.shape, 1)
    last = u[:, 256:]
    return jnp.concatenate(
        [
            rope(u[:, :128], cosine, sine),
            rope(u[:, 128:256], cosine, sine),
            jnp.where(lane < DH, rope(last, cosine, sine), last),
        ],
        axis=1,
    )


def half_at(halves_ref, i):
    return pl.ds(pl.multiple_of(halves_ref[i], 512), 512)


def project_qkv(i, rows, weight, tables, halves):
    def kernel(halves_ref, rows_ref, w_ref, cos_ref, sin_ref, out_ref):
        here = half_at(halves_ref, i)
        product = dot(rows_ref[...], w_ref[:, :384], 1, 0)
        out_ref[...] = bf(rope_three(product, cos_ref[here, :], sin_ref[here, :]))

    args = [halves, rows, weight, *tables]
    return call(kernel, "project_qkv", [sds((512, 384))], args, 2 * 512 * D * 384)[0]


def scores_t(keys, query, q_at):
    s = dot(keys, query, 1, 1)
    key = lax.broadcasted_iota(jnp.int32, (256, 256), 0)
    column = lax.broadcasted_iota(jnp.int32, (256, 256), 1)
    diagonal = jnp.where(key <= column, s[q_at:], -1e30)
    return diagonal if q_at == 0 else jnp.concatenate([s[:q_at], diagonal], axis=0)


def attend(qkv, halves):
    def kernel(halves_ref, q0, q1, own_ref, other_ref, nat_ref, lse_ref, att_ref):
        nat_ref[half_at(halves_ref, 0), :] = q0[...]
        nat_ref[half_at(halves_ref, 1), :] = q1[...]
        kv = nat_ref[:, 256:]
        keys = kv[:, :DH]
        values_t = kv.T[DH:]
        lse_ref[...] = jnp.zeros_like(lse_ref)
        for q_at in range(0, SEQ_LEN, 256):
            end = q_at + 256
            for pair in range(2):
                two = nat_ref[q_at:end, 128 * pair : 128 * pair + 128]
                outs = []
                for i in range(2):
                    s = scores_t(keys[:end], two[:, DH * i : DH * i + DH], q_at)
                    top = jnp.max(s, axis=0, keepdims=True)
                    p = jnp.exp2((s - top) * SCALE2)
                    total = jnp.sum(p, axis=0, keepdims=True)
                    outs.append(dot(values_t[:, :end], bf(p), 1, 0) / total)
                    g = 2 * pair + i
                    lse_ref[g : g + 1, q_at:end] = top * SCALE2 + jnp.log2(total)
                att_ref[q_at:end, 128 * pair : 128 * pair + 128] = bf(jnp.concatenate(outs, axis=0).T)
        own_ref[...] = att_ref[half_at(halves_ref, 0), :]
        other_ref[...] = att_ref[half_at(halves_ref, 1), :]

    outs = [sds((512, 256)), sds((512, 256)), sds((SEQ_LEN, 384)), sds((8, SEQ_LEN), jnp.float32)]
    scratch = [pltpu.VMEM((SEQ_LEN, 256), jnp.bfloat16)]
    return call(kernel, "attend", outs, [halves, *qkv], 20e9, scratch)


def attend_backward(qkv, lse, grad_out, tables, halves):
    def kernel(halves_ref, nat_ref, lse_ref, g0, g1, cos_ref, sin_ref, own_ref, other_ref, go_nat, kv_sum, d_nat):
        go_nat[half_at(halves_ref, 0), :] = g0[...]
        go_nat[half_at(halves_ref, 1), :] = g1[...]
        kv = nat_ref[:, 256:]
        keys = kv[:, :DH]
        values = kv[:, DH:]
        keys_t = kv.T[:DH]
        kv_sum[...] = jnp.zeros_like(kv_sum)
        for q_at in range(0, SEQ_LEN, 256):
            end = q_at + 256
            cosine = cos_ref[q_at:end, :]
            sine = -sin_ref[q_at:end, :]
            for pair in range(2):
                lanes = slice(128 * pair, 128 * pair + 128)
                two = nat_ref[q_at:end, lanes]
                two_grad = go_nat[q_at:end, lanes]
                outs = []
                for i in range(2):
                    query = two[:, DH * i : DH * i + DH]
                    grad = two_grad[:, DH * i : DH * i + DH]
                    g = 2 * pair + i
                    s = scores_t(keys[:end], query, q_at)
                    p = jnp.exp2(s * SCALE2 - lse_ref[g : g + 1, q_at:end])
                    dp = dot(values[:end], grad, 1, 1)
                    delta = jnp.sum(dp * p, axis=0, keepdims=True)
                    ds = bf(p * (dp - delta))
                    kv_sum[:end, :] += jnp.concatenate(
                        [dot(ds, query, 1, 0), dot(bf(p), grad, 1, 0)], axis=1
                    )
                    outs.append(dot(keys_t[:, :end], ds, 1, 0))
                d_query = jnp.concatenate(outs, axis=0).T * SCALE
                d_nat[q_at:end, lanes] = bf(rope(d_query, cosine, sine))
        lane = lax.broadcasted_iota(jnp.int32, (SEQ_LEN, 128), 1)
        total = kv_sum[...]
        turned = rope(total * SCALE, cos_ref[...], -sin_ref[...])
        d_nat[:, 256:] = bf(jnp.where(lane < DH, turned, total))
        own_ref[...] = d_nat[half_at(halves_ref, 0), :]
        other_ref[...] = d_nat[half_at(halves_ref, 1), :]

    scratch = [
        pltpu.VMEM((SEQ_LEN, 256), jnp.bfloat16),
        pltpu.VMEM((SEQ_LEN, 128), jnp.float32),
        pltpu.VMEM((SEQ_LEN, 384), jnp.bfloat16),
    ]
    args = [halves, qkv, lse, *grad_out, *tables]
    return call(kernel, "attend_backward", [sds((512, 384))] * 2, args, 30e9, scratch)


def mlp_step(rows, w_gate, w_up, grad_act):
    width = w_gate.shape[1]

    def kernel(rows_ref, g_ref, u_ref, ga_ref, act_ref, gg_ref, gu_ref):
        for j in range(0, width, 256):
            here = slice(j, j + 256)
            gate = dot(rows_ref[...], g_ref[:, here], 1, 0)
            up = dot(rows_ref[...], u_ref[:, here], 1, 0)
            sig = jax.nn.sigmoid(gate)
            silu = gate * sig
            ga = fl(ga_ref[:, here])
            act_ref[:, here] = bf(silu * up)
            gg_ref[:, here] = bf(ga * up * sig * (1.0 + gate * (1.0 - sig)))
            gu_ref[:, here] = bf(ga * silu)

    args = [rows, pinned(w_gate), pinned(w_up), grad_act]
    return call(kernel, "mlp_step", [sds((512, width))] * 3, args, 4 * 512 * D * width)


def frequencies(head_size):
    pair_index = jnp.arange(head_size // 2).astype(jnp.float32)
    base_freq = 500000.0 ** (-2.0 * pair_index / head_size)
    wavelen = 2.0 * jnp.pi / base_freq
    smooth = (8192.0 / wavelen - 1.0) / 3.0
    blended = (1.0 - smooth) * base_freq / 32.0 + smooth * base_freq
    return jnp.where(
        wavelen < 2048.0, base_freq, jnp.where(wavelen > 8192.0, base_freq / 32.0, blended)
    )


LONG = 60e9


def wide(out_ref, value):
    for k in range(4):
        out_ref[k] = value


def arrived_sum(ref):
    return fl(ref[0]) + fl(ref[1]) + fl(ref[2]) + fl(ref[3])


def mlp_norm(inputs, arrived, gain):
    def kernel(x_ref, a_ref, gain_ref, residual_ref, out_ref):
        residual = fl(x_ref[...]) + arrived_sum(a_ref)
        residual_ref[...] = residual
        inverse = lax.rsqrt(jnp.mean(residual * residual, axis=1, keepdims=True) + eps)
        wide(out_ref, bf(residual * inverse * gain_ref[...]))

    outs = [sds((128, D), jnp.float32), sds((4, 128, D))]
    return call(kernel, "mlp_norm", outs, [inputs, arrived, gain], LONG)


def norm_grad(grad, values, gain):
    inverse = lax.rsqrt(jnp.mean(values * values, axis=1, keepdims=True) + eps)
    unit = values * inverse
    scaled = grad * gain
    return inverse * (scaled - unit * jnp.mean(scaled * unit, axis=1, keepdims=True))


def mlp_norm_backward(upstream, arrived, residual, gain):
    def kernel(g_ref, a_ref, r_ref, gain_ref, grad_ref, out_ref):
        grad = fl(g_ref[...]) + norm_grad(arrived_sum(a_ref), r_ref[...], gain_ref[...])
        grad_ref[...] = grad
        wide(out_ref, bf(grad))

    outs = [sds((128, D), jnp.float32), sds((4, 128, D))]
    return call(kernel, "mlp_norm_backward", outs, [upstream, arrived, residual, gain], LONG)


def attn_norm_backward(grad_residual, arrived, inputs, gain):
    def kernel(g_ref, a_ref, x_ref, gain_ref, out_ref):
        out_ref[...] = bf(g_ref[...] + norm_grad(arrived_sum(a_ref), fl(x_ref[...]), gain_ref[...]))

    return call(kernel, "attn_norm_backward", [sds((128, D))], [grad_residual, arrived, inputs, gain], LONG)[0]


def layer_output(residual, arrived):
    def kernel(r_ref, a_ref, out_ref):
        out_ref[...] = bf(r_ref[...] + arrived_sum(a_ref))

    return call(kernel, "layer_output", [sds((128, D))], [residual, arrived], 1)[0]


def on_device(
    tokens, positions, w_query, w_key, w_value, w_out, attn_gain, w_gate, w_up, w_down, mlp_gain, cotangent
):
    me = Place()
    inputs_b = swapped(tokens)
    places = jnp.concatenate([(positions // 256).reshape(128, 8), (positions % 256).reshape(128, 8)], axis=1)
    extra = jnp.concatenate([attn_gain[:, None], mlp_gain[:, None], bf(places)], axis=1)
    extra = jnp.pad(extra, ((0, 0), (0, 110)))
    part_attn = swapped(jnp.concatenate([w_query, w_key, w_value, extra, w_out.T], axis=1))
    part_attn, inputs_b = lax.optimization_barrier((part_attn, inputs_b))

    blocks_in = send_z(inputs_b)
    w_qkv = gather_plane(part_attn[:, :512])
    w_gate, w_up, w_down, cotangent = after((w_gate, w_up, w_down, cotangent), inputs_b)
    upstream = swapped(cotangent)
    down_rows = w_down.T
    part_ab = swapped(jnp.concatenate([w_gate, down_rows[:, :512], w_up, down_rows[:, 512:]], axis=1))

    place = fl(part_attn[:, 386:402])
    seq_positions = (256.0 * place[:, :8] + place[:, 8:]).reshape(SEQ_LEN)
    freq = jnp.tile(frequencies(DH), 4)
    angles = seq_positions[:, None] * freq[None, :]
    sign = jnp.where(jnp.arange(128) % DH < DH // 2, -1.0, 1.0)
    tables = (jnp.cos(angles), jnp.sin(angles) * sign[None, :])
    pick = bf(jnp.arange(128)[None, :] == jnp.arange(8)[:, None])
    gain_rows = dot(pick, w_qkv[:, 384:], 1, 1)
    gain_attn, gain_mlp = gain_rows[:1], gain_rows[1:2]

    blocks_in = after(blocks_in, *tables, upstream, part_ab)
    own_normed = norm_tokens(blocks_in, gain_attn, me)
    normed_attn = [own_normed, sibling(own_normed)]
    own_qkv = project_qkv(0, normed_attn[0], w_qkv, tables, me.halves)
    projected = [own_qkv, project_qkv(1, normed_attn[1], w_qkv, tables, me.halves)]

    (own_up,) = after((upstream,), own_normed)
    blocks_up = send_z(own_up)
    (part_out,) = after((part_attn[:, 512:],), own_qkv)
    w_out_t = gather_plane(part_out)

    projected = after(projected, *blocks_up[1:3])
    attended, other_attended, qkv, lse = attend(projected, me.halves)
    (w_out_t,) = after((w_out_t,), attended, blocks_up[3])
    out_sums = chip_product(attended, other_attended, w_out_t, sibling(w_out_t))
    (out_sums,) = after((out_sums,), *blocks_up)

    (part_ab,) = after((part_ab,), own_normed)
    part_a, part_b = part_ab[:, :1536], part_ab[:, 1536:]
    holds = (projected[1], attended, out_sums)
    stage_a, stage_b = (jnp.concatenate(chain(p, axis, holds), axis=0) for p, axis in ((part_a, "x"), (part_b, "y")))

    own_up = place_tokens(blocks_up, me)
    rows_up = [own_up, sibling(own_up)]
    arrived = arrive_z(out_sums)

    parts_a, parts_b = chain(stage_a, "y", (None, None, None)), chain(stage_b, "x", (None, None, None))
    full_gate, down_a = place_rows(parts_a, me.blocks["x"], (1024, 512))
    full_up, down_b = place_rows(parts_b, me.blocks["y"], (1024, 512))
    full_down = [down_a, down_b]

    (arrived,) = after((arrived,), parts_a[2], parts_b[2], *rows_up)
    residual, normed_mlp = mlp_norm(inputs_b, arrived, gain_mlp)
    own_mlp = gather_z(normed_mlp)
    up_held = after(rows_up, normed_mlp)
    grad_act = [project(r, [pinned(w) for w in full_down], jnp.bfloat16) for r in up_held]
    (own_mlp,) = after((own_mlp,), full_gate, full_up, grad_act[0])
    rows_mlp = [own_mlp, sibling(own_mlp)]
    steps = [mlp_step(r, full_gate, full_up, g) for r, g in zip(rows_mlp, grad_act)]
    activated, grad_gate_pre, grad_up_pre = zip(*steps)

    gate_up = list(zip(grad_gate_pre, grad_up_pre))
    mlp_sums = chip_sums(gate_up[0], gate_up[1], [full_gate, full_up])
    arrived = arrive_z(mlp_sums)

    gg, gu = after((grad_gate_pre, grad_up_pre), mlp_sums)
    made_a = weight_product([(rows_mlp, gg, 0, 1024), (rows_up, activated, 0, 512)], "x", me, 2)
    made_b = weight_product([(rows_mlp, gu, 0, 1024), (rows_up, activated, 512, 1024)], "y", me, 2)
    sums = [made_a[0], made_b[0]]
    rings = [ring_cuts(total, axis) for total, axis in zip(sums, "xy")]
    (arrived,) = after((arrived,), made_a[-1][0], made_b[-1][0])
    grad_residual, grad_residual_b = mlp_norm_backward(upstream, arrived, residual, gain_mlp)

    own_gr = gather_z(grad_residual_b)
    rings = [after(cuts, grad_residual_b) for cuts in rings]
    sums = [add(received, made[1]) for received, made in zip(rings, (made_a, made_b))]
    rings = [ring_cuts(total, axis) for total, axis in zip(sums, "xy")]
    acts = after(activated, *sums[0], *sums[1])
    down_other = down_products(acts[1], full_down)
    down_own = down_products(acts[0], full_down)
    down_arrived = [sibling(half) for half in down_other]
    (own_gr,) = after((own_gr,), *down_own, *down_arrived, *rings[0], *rings[1])
    rows_gr = [own_gr, sibling(own_gr)]
    arrived = arrive_z(join_sums(after(down_own, own_gr), down_arrived))
    grad_attended = [project(r, [w_out_t], jnp.bfloat16) for r in rows_gr]
    grad_qkv, other_grad_qkv = attend_backward(qkv, lse, grad_attended, tables, me.halves)
    attn_sums = chip_product(grad_qkv, other_grad_qkv, w_qkv, sibling(w_qkv))
    (attn_sums,) = after((attn_sums,), arrived)
    grad_arrived = arrive_z(attn_sums)

    d_qkv = after((grad_qkv, other_grad_qkv), attn_sums)
    terms = [(normed_attn, d_qkv, 0, 384), (rows_gr, (attended, other_attended), 0, 256)]
    made_attn = [cut for (cut,) in weight_product(terms, "x", me)]
    sent_attn = send_pieces(made_attn, "x")
    rings = [after(cuts, made_attn[-1]) for cuts in rings]
    sums = [add(received, made[2], True) for received, made in zip(rings, (made_a, made_b))]
    rings = [ring_cuts(total, axis) for total, axis in zip(sums, "xy")]
    (arrived,) = after((arrived,), sums[0][0], sums[1][0])
    layer_out = layer_output(residual, arrived)
    (grad_arrived,) = after((grad_arrived,), layer_out)
    grad_tokens = attn_norm_backward(grad_residual, grad_arrived, inputs_b, gain_attn)

    (layer_out,) = after((layer_out,), grad_tokens)
    blocks_a, blocks_b = (
        second_blocks([after(cuts, grad_tokens), made[3]], first, me)
        for cuts, made, first in zip(rings, (made_a, made_b), "xy")
    )
    blocks_attn = second_blocks([[part] for part in after(sent_attn, grad_tokens)], "x", me)
    parts_b, parts_attn, parts_a = (
        second_stage(blocks, first) for blocks, first in ((blocks_b, "y"), (blocks_attn, "x"), (blocks_a, "x"))
    )
    share_b = fl(swapped(bf(summed(parts_b, blocks_attn[0]))))
    share_attn = summed(parts_attn, blocks_attn[0])
    share_a = summed(parts_a, blocks_attn[0])

    def gain_sum(*terms):
        return sum(jnp.sum(fl(w) * g, axis=1) for w, g in terms)

    gain_sums = jnp.stack(
        [
            gain_sum((jnp.concatenate([w_query, w_key, w_value], axis=1), share_attn[:, :384])),
            gain_sum((w_gate, share_a[:, :1024]), (w_up, share_b[:, :1024])),
        ]
    )
    gain_sums = gain_sums / fl(jnp.stack([attn_gain, mlp_gain]))
    gain_sums = gain_sums + z_moved(gain_sums, 1) + z_moved(gain_sums, 2) + z_moved(gain_sums, 3)
    gain_sums = gain_sums + h_flipped(gain_sums)
    return (
        swapped(layer_out),
        swapped(grad_tokens),
        share_attn[:, :256],
        share_attn[:, 256:320],
        share_attn[:, 320:384],
        share_attn[:, 384:].T,
        gain_sums[0],
        share_a[:, :1024],
        share_b[:, :1024],
        jnp.concatenate([share_a[:, 1024:], share_b[:, 1024:]], axis=1).T,
        gain_sums[1],
    )


def solution(mesh):
    split = Mesh(mesh.devices.reshape(4, 2, 2, 2, 4), AXES)
    dp, tensor = ("x", "l", "c"), ("h", "z")
    both = P(AXES, None)
    weight, turned, vector = P(dp, tensor), P(tensor, dp), P(dp)
    in_specs = (
        both, vector, weight, weight, weight, turned, vector, weight, weight, turned, vector, both,
    )
    out_specs = (
        both, both, weight, weight, weight, turned, vector, weight, weight, turned, vector,
    )
    return jax.shard_map(on_device, mesh=split, in_specs=in_specs, out_specs=out_specs, check_vma=False)
```

```python
import functools
import itertools
import math

import jax
import jax.numpy as jnp
from jax import lax
from jax.experimental import pallas as pl
from jax.experimental.pallas import tpu as pltpu
from jax.sharding import Mesh, PartitionSpec as P

H = 32
KV = 8
DH = 64
SEQ_LEN = 1024
D = 2048
eps = 1e-05

SIZES = dict(x=4, l=2, c=2, h=2, z=4)
AXES = ("x", "l", "c", "h", "z")

SCALE = DH ** (-0.5)
SCALE2 = SCALE * math.log2(math.e)
VMEM_LIMIT = 12 * 1024 * 1024


def pairs(axes, move):
    def place(index):
        at = 0
        for a in axes:
            at = at * SIZES[a] + index[a]
        return at

    out = []
    for index in itertools.product(*[range(SIZES[a]) for a in axes]):
        here = dict(zip(axes, index))
        out.append((place(here), place(move(dict(here)))))
    return out


def to_swapped(d):
    d["c"], d["h"] = d["h"], d["c"]
    return d


def to_sibling(d):
    d["c"] = 1 - d["c"]
    return d


def along(axis):
    def move(d):
        step = 1 - 2 * d["c"]
        if axis == "y":
            y = (2 * d["h"] + d["l"] + step) % 4
            d["h"], d["l"] = y // 2, y % 2
        else:
            d[axis] = (d[axis] + step) % 4
        return d

    return move


RING_AXES = dict(x=("x", "c"), y=("l", "c", "h"))
Z_STEPS = (0, 1, 3, 2)
PIECES = (1, 2, 3, 0)


def ring(value, axis):
    axes = RING_AXES[axis]
    return lax.ppermute(value, axes, pairs(axes, along(axis)))


def swapped(value):
    return lax.ppermute(value, ("c", "h"), pairs(("c", "h"), to_swapped))


def sibling(value):
    return lax.ppermute(value, ("c",), pairs(("c",), to_sibling))


def z_moved(value, step):
    def move(d):
        d["z"] = (d["z"] + step) % 4
        return d

    return lax.ppermute(value, ("z",), pairs(("z",), move))


def h_flipped(value):
    def move(d):
        d["h"] = 1 - d["h"]
        return d

    return lax.ppermute(value, ("h",), pairs(("h",), move))


def after(values, *earlier):
    held = lax.optimization_barrier((tuple(values), tuple(earlier)))
    return held[0]


def dot(a, b, ca, cb):
    return lax.dot_general(a, b, (((ca,), (cb,)), ((), ())), preferred_element_type=jnp.float32)


def bf(v):
    return v.astype(jnp.bfloat16)


def fl(v):
    return v.astype(jnp.float32)


def sds(shape, dtype=jnp.bfloat16):
    return jax.ShapeDtypeStruct(shape, dtype)


def cost(flops):
    return pl.CostEstimate(flops=int(flops), bytes_accessed=1, transcendentals=0)


PARAMS = pltpu.CompilerParams(vmem_limit_bytes=VMEM_LIMIT)
ANY = pl.BlockSpec(memory_space=pl.ANY)
WHOLE = pl.BlockSpec(memory_space=pltpu.VMEM)


class Place:
    def __init__(self):
        self.c = lax.axis_index("c")
        self.x = lax.axis_index("x")
        self.h = lax.axis_index("h")
        self.y = 2 * self.h + lax.axis_index("l")
        self.step = 1 - 2 * self.c
        self.halves = jnp.stack([512 * self.c, 512 * (1 - self.c)]).astype(jnp.int32)
        z = lax.axis_index("z")
        self.z_order = jnp.stack([lax.rem(z - step + 4, 4) for step in Z_STEPS]).astype(jnp.int32)
        self.blocks = {}
        for first, second in (("x", "y"), ("y", "x")):
            out = []
            for k2 in range(4):
                for k1 in range(4):
                    a, b = self.source(first, k1), self.source(second, k2)
                    out.append(4 * a + b if first == "x" else 4 * b + a)
            self.blocks[first] = jnp.stack(out).astype(jnp.int32)

    def source(self, axis, k):
        at = lax.rem(dict(x=self.x, y=self.y)[axis] - self.step * k + 4, 4)
        if axis == "y":
            at = 2 * lax.rem(at, 2) + lax.div(at, 2)
        return at


SMEM = pl.BlockSpec(memory_space=pltpu.SMEM)


def pinned(value):
    return pltpu.with_memory_space_constraint(value, pltpu.VMEM)


def place_rows(parts, blocks, widths):
    def kernel(blocks_ref, p0, p1, p2, p3, *rest):
        sems = rest[-1]
        copies = []
        for k2, part in enumerate((p0, p1, p2, p3)):
            for k1 in range(4):
                at = pl.multiple_of(blocks_ref[4 * k2 + k1] * 128, 128)
                low = 0
                for i, width in enumerate(widths):
                    copies.append(
                        pltpu.make_async_copy(
                            part.at[pl.ds(128 * k1, 128), pl.ds(low, width)],
                            rest[i].at[pl.ds(at, 128)],
                            sems.at[len(widths) * (4 * k2 + k1) + i],
                        )
                    )
                    low += width
        for copy in copies:
            copy.start()
        for copy in copies:
            copy.wait()

    return pl.pallas_call(
        kernel,
        out_shape=[pltpu.VMEM((D, width), jnp.bfloat16) for width in widths],
        in_specs=[SMEM] + [ANY] * 4,
        out_specs=[WHOLE] * len(widths),
        scratch_shapes=[pltpu.SemaphoreType.DMA((16 * len(widths),))],
        compiler_params=PARAMS,
        cost_estimate=cost(1),
        name="place_rows",
    )(blocks, *parts)


def stepped(value, axis, steps):
    def move(d):
        for _ in range(steps):
            d = along(axis)(d)
        return d

    axes = RING_AXES[axis]
    return lax.ppermute(value, axes, pairs(axes, move))


def chain(block, axis, holds):
    parts = [block]
    for hold in holds:
        part = ring(parts[-1], axis)
        parts.append(part if hold is None else after((part,), hold)[0])
    return parts


def gather_plane(block):
    wide = jnp.broadcast_to(block[None], (16,) + block.shape)
    return lax.all_to_all(wide, ("x", "l", "h"), split_axis=0, concat_axis=0, tiled=True).reshape(D, block.shape[1])


def call(kernel, name, outs, args, flops, scratch=(), limit=VMEM_LIMIT):
    return pl.pallas_call(
        kernel,
        out_shape=outs,
        in_specs=[SMEM if a.dtype == jnp.int32 else WHOLE for a in args],
        out_specs=[WHOLE] * len(outs),
        scratch_shapes=list(scratch),
        compiler_params=pltpu.CompilerParams(vmem_limit_bytes=limit),
        cost_estimate=cost(flops),
        name=name,
    )(*args)


def weight_product(terms, first, me, cuts=1):
    order = jnp.stack([me.source(first, k) for k in PIECES]).astype(jnp.int32)
    n = sum(high - low for _, _, low, high in terms) // cuts
    args = [order]
    for rows, right, _, _ in terms:
        args += [*rows, *right]

    def kernel(order_ref, *refs):
        for p in range(4):
            at = 0
            for t, (_, _, low, high) in enumerate(terms):
                rows, right = refs[4 * t : 4 * t + 2], refs[4 * t + 2 : 4 * t + 4]
                left = []
                for r in rows:
                    lanes = []
                    for j in range(4):
                        block = 4 * order_ref[p] + j if first == "x" else 4 * j + order_ref[p]
                        lanes.append(r[:, pl.ds(pl.multiple_of(block * 128, 128), 128)])
                    left.append(jnp.concatenate(lanes, axis=1))
                for j in range(low, high, 256):
                    end = min(j + 256, high)
                    total = dot(left[0], right[0][:, j:end], 0, 0) + dot(left[1], right[1][:, j:end], 0, 0)
                    out_ref = refs[4 * len(terms) + cuts * p + at // n]
                    out_ref[:, at % n : at % n + end - j] = bf(total)
                    at += end - j

    outs = [pltpu.HBM((512, n), jnp.bfloat16)] * (4 * cuts)
    made = call(kernel, "weight_product", outs, args, 2 * D * SEQ_LEN * n * cuts, limit=24 * 1024 * 1024)
    return [made[cuts * p : cuts * p + cuts] for p in range(4)]


def sum_blocks(parts, order):
    n = sum(cut.shape[1] for cut in parts[0])
    width = min(cut.shape[1] for part in parts for cut in part)

    def kernel(order_ref, *refs):
        for k in range(4):
            at = pl.ds(pl.multiple_of(order_ref[k] * 128, 128), 128)
            for low in range(0, n, width):
                total, first = None, 0
                for part in parts:
                    cut = part[0].shape[1]
                    value = fl(refs[first + low // cut][at, low % cut : low % cut + width])
                    total = value if total is None else total + value
                    first += len(part)
                refs[first + k][:, low : low + width] = bf(total)

    args = [order, *[cut for part in parts for cut in part]]
    return call(kernel, "sum_blocks", [sds((128, n))] * 4, args, 1)


def send_pieces(made, first):
    return [stepped(piece, first, 4 - k) if k else piece for k, piece in zip(PIECES, made)]


def homeward(value, k):
    def move(d):
        y = (2 * d["h"] + d["l"] - k * (1 - 2 * d["c"])) % 4
        d["l"], d["h"], d["c"] = y % 2, d["c"], y // 2
        return d

    axes = ("l", "c", "h")
    return lax.ppermute(value, axes, pairs(axes, move))


def add(one, other, join=False):
    count = len(one)
    n = one[0].shape[1]

    def kernel(*refs):
        for i in range(count):
            total = bf(fl(refs[i][...]) + fl(refs[count + i][...]))
            if join:
                refs[2 * count][:, n * i : n * i + n] = total
            else:
                refs[2 * count + i][...] = total

    outs = [sds((512, n * count))] if join else [sds(a.shape) for a in one]
    return call(kernel, "add", outs, [*one, *other], 1)


def ring_cuts(cuts, axis):
    return [ring(cut, axis) for cut in cuts]


def second_blocks(parts, first, me):
    second = "y" if first == "x" else "x"
    return sum_blocks(parts, jnp.stack([me.source(second, k) for k in PIECES]).astype(jnp.int32))


def second_stage(blocks, first):
    if first == "x":
        return [homeward(block, k) for k, block in zip(PIECES, blocks)]
    return send_pieces(blocks, "x")


def summed(parts, hold):
    return sum(fl(part) for part in after(parts, hold))


def send_z(block):
    return [z_moved(block, step) if step else block for step in Z_STEPS]


def place_tokens(blocks, me):
    def kernel(order_ref, b0, b1, b2, b3, out_ref):
        for k, ref in enumerate((b0, b1, b2, b3)):
            out_ref[pl.ds(pl.multiple_of(order_ref[k] * 128, 128), 128), :] = ref[...]

    return call(kernel, "place_tokens", [sds((512, D))], [me.z_order, *blocks], 1)[0]


def norm_tokens(blocks, gain, me):
    def kernel(order_ref, b0, b1, b2, b3, gain_ref, out_ref):
        for k, ref in enumerate((b0, b1, b2, b3)):
            x = fl(ref[...])
            inverse = lax.rsqrt(jnp.mean(x * x, axis=1, keepdims=True) + eps)
            out_ref[pl.ds(pl.multiple_of(order_ref[k] * 128, 128), 128), :] = bf(x * inverse * gain_ref[...])

    return call(kernel, "norm_tokens", [sds((512, D))], [me.z_order, *blocks, gain], 1)[0]


def gather_z(wide_block):
    whole = lax.all_to_all(wide_block, "z", split_axis=0, concat_axis=0, tiled=True)
    return whole.reshape(512, whole.shape[2])


def arrive_z(sums):
    parts = sums.reshape(4, 128, sums.shape[1])
    return lax.all_to_all(parts, "z", split_axis=0, concat_axis=0, tiled=True)


def partial_sums(pieces, weights):
    count = len(pieces)

    def kernel(*refs):
        for j in range(0, D, 512):
            total = None
            for i in range(count):
                one = dot(refs[i][...], refs[count + i][j : j + 512, :], 1, 1)
                total = one if total is None else total + one
            refs[-1][:, j : j + 512] = bf(total)

    depth = sum(p.shape[1] for p in pieces)
    return call(kernel, "partial_sums", [sds((512, D))], [*pieces, *map(pinned, weights)], 2 * 512 * depth * D)[0]


def chip_sums(own, other, weights):
    received = sibling(partial_sums(other, weights))
    return bf(fl(partial_sums(own, weights)) + fl(received))


def chip_product(own, other, weight, sibling_weight):
    received = sibling(other)
    m = own.shape[1]

    def kernel(a_ref, b_ref, v_ref, w_ref, out_ref):
        for j in range(0, D, 512):
            here = slice(j, j + 512)
            total = dot(a_ref[...], v_ref[here, :m], 1, 1) + dot(b_ref[...], w_ref[here, :m], 1, 1)
            out_ref[:, here] = bf(total)

    args = [own, received, weight, sibling_weight]
    return call(kernel, "chip_product", [sds((512, D))], args, 4 * 512 * m * D)[0]


def project(rows, weights, dtype, width=None):
    width = width or weights[0].shape[1]
    n = width * len(weights)

    def kernel(rows_ref, *refs):
        for i, w_ref in enumerate(refs[:-1]):
            for j in range(0, width, 256):
                product = dot(rows_ref[...], w_ref[:, j : j + 256], 1, 0)
                refs[-1][:, i * width + j : i * width + j + 256] = product.astype(dtype)

    return call(kernel, "project", [sds((512, n), dtype)], [rows, *weights], 2 * 512 * D * n)[0]


def down_products(rows, weights):
    def kernel(rows_ref, w0, w1, *out_refs):
        for j in range(0, D, 512):
            here = slice(j, j + 512)
            total = dot(rows_ref[:, :512], w0[here, :], 1, 1) + dot(rows_ref[:, 512:], w1[here, :], 1, 1)
            out_refs[j // 1024][:, j % 1024 : j % 1024 + 512] = bf(total)

    args = [rows, *map(pinned, weights)]
    return call(kernel, "down_products", [sds((512, D // 2))] * 2, args, 2 * 512 * 1024 * D)


def join_sums(one, other):
    def kernel(a0, a1, b0, b1, out_ref):
        out_ref[:, :1024] = bf(fl(a0[...]) + fl(b0[...]))
        out_ref[:, 1024:] = bf(fl(a1[...]) + fl(b1[...]))

    return call(kernel, "join_sums", [sds((512, D))], [*one, *other], 1)[0]


def rope(u, cosine, sine):
    lane = lax.broadcasted_iota(jnp.int32, u.shape, 1)
    turned = jnp.where(lane % DH < DH // 2, pltpu.roll(u, 96, 1), pltpu.roll(u, 32, 1))
    return u * cosine + turned * sine


def rope_three(u, cosine, sine):
    lane = lax.broadcasted_iota(jnp.int32, cosine.shape, 1)
    last = u[:, 256:]
    return jnp.concatenate(
        [
            rope(u[:, :128], cosine, sine),
            rope(u[:, 128:256], cosine, sine),
            jnp.where(lane < DH, rope(last, cosine, sine), last),
        ],
        axis=1,
    )


def half_at(halves_ref, i):
    return pl.ds(pl.multiple_of(halves_ref[i], 512), 512)


def project_qkv(i, rows, weight, tables, halves):
    def kernel(halves_ref, rows_ref, w_ref, cos_ref, sin_ref, out_ref):
        here = half_at(halves_ref, i)
        product = dot(rows_ref[...], w_ref[:, :384], 1, 0)
        out_ref[...] = bf(rope_three(product, cos_ref[here, :], sin_ref[here, :]))

    args = [halves, rows, weight, *tables]
    return call(kernel, "project_qkv", [sds((512, 384))], args, 2 * 512 * D * 384)[0]


def scores_t(keys, query, q_at):
    s = dot(keys, query, 1, 1)
    key = lax.broadcasted_iota(jnp.int32, (256, 256), 0)
    column = lax.broadcasted_iota(jnp.int32, (256, 256), 1)
    diagonal = jnp.where(key <= column, s[q_at:], -1e30)
    return diagonal if q_at == 0 else jnp.concatenate([s[:q_at], diagonal], axis=0)


def attend(qkv, halves):
    def kernel(halves_ref, q0, q1, own_ref, other_ref, nat_ref, lse_ref, att_ref):
        nat_ref[half_at(halves_ref, 0), :] = q0[...]
        nat_ref[half_at(halves_ref, 1), :] = q1[...]
        kv = nat_ref[:, 256:]
        keys = kv[:, :DH]
        values_t = kv.T[DH:]
        lse_ref[...] = jnp.zeros_like(lse_ref)
        for q_at in range(0, SEQ_LEN, 256):
            end = q_at + 256
            for pair in range(2):
                two = nat_ref[q_at:end, 128 * pair : 128 * pair + 128]
                outs = []
                for i in range(2):
                    s = scores_t(keys[:end], two[:, DH * i : DH * i + DH], q_at)
                    top = jnp.max(s, axis=0, keepdims=True)
                    p = jnp.exp2((s - top) * SCALE2)
                    total = jnp.sum(p, axis=0, keepdims=True)
                    outs.append(dot(values_t[:, :end], bf(p), 1, 0) / total)
                    g = 2 * pair + i
                    lse_ref[g : g + 1, q_at:end] = top * SCALE2 + jnp.log2(total)
                att_ref[q_at:end, 128 * pair : 128 * pair + 128] = bf(jnp.concatenate(outs, axis=0).T)
        own_ref[...] = att_ref[half_at(halves_ref, 0), :]
        other_ref[...] = att_ref[half_at(halves_ref, 1), :]

    outs = [sds((512, 256)), sds((512, 256)), sds((SEQ_LEN, 384)), sds((8, SEQ_LEN), jnp.float32)]
    scratch = [pltpu.VMEM((SEQ_LEN, 256), jnp.bfloat16)]
    return call(kernel, "attend", outs, [halves, *qkv], 20e9, scratch)


def attend_backward(qkv, lse, grad_out, tables, halves):
    def kernel(halves_ref, nat_ref, lse_ref, g0, g1, cos_ref, sin_ref, own_ref, other_ref, go_nat, kv_sum, d_nat):
        go_nat[half_at(halves_ref, 0), :] = g0[...]
        go_nat[half_at(halves_ref, 1), :] = g1[...]
        kv = nat_ref[:, 256:]
        keys = kv[:, :DH]
        values = kv[:, DH:]
        keys_t = kv.T[:DH]
        kv_sum[...] = jnp.zeros_like(kv_sum)
        for q_at in range(0, SEQ_LEN, 256):
            end = q_at + 256
            cosine = cos_ref[q_at:end, :]
            sine = -sin_ref[q_at:end, :]
            for pair in range(2):
                lanes = slice(128 * pair, 128 * pair + 128)
                two = nat_ref[q_at:end, lanes]
                two_grad = go_nat[q_at:end, lanes]
                outs = []
                for i in range(2):
                    query = two[:, DH * i : DH * i + DH]
                    grad = two_grad[:, DH * i : DH * i + DH]
                    g = 2 * pair + i
                    s = scores_t(keys[:end], query, q_at)
                    p = jnp.exp2(s * SCALE2 - lse_ref[g : g + 1, q_at:end])
                    dp = dot(values[:end], grad, 1, 1)
                    delta = jnp.sum(dp * p, axis=0, keepdims=True)
                    ds = bf(p * (dp - delta))
                    kv_sum[:end, :] += jnp.concatenate(
                        [dot(ds, query, 1, 0), dot(bf(p), grad, 1, 0)], axis=1
                    )
                    outs.append(dot(keys_t[:, :end], ds, 1, 0))
                d_query = jnp.concatenate(outs, axis=0).T * SCALE
                d_nat[q_at:end, lanes] = bf(rope(d_query, cosine, sine))
        lane = lax.broadcasted_iota(jnp.int32, (SEQ_LEN, 128), 1)
        total = kv_sum[...]
        turned = rope(total * SCALE, cos_ref[...], -sin_ref[...])
        d_nat[:, 256:] = bf(jnp.where(lane < DH, turned, total))
        own_ref[...] = d_nat[half_at(halves_ref, 0), :]
        other_ref[...] = d_nat[half_at(halves_ref, 1), :]

    scratch = [
        pltpu.VMEM((SEQ_LEN, 256), jnp.bfloat16),
        pltpu.VMEM((SEQ_LEN, 128), jnp.float32),
        pltpu.VMEM((SEQ_LEN, 384), jnp.bfloat16),
    ]
    args = [halves, qkv, lse, *grad_out, *tables]
    return call(kernel, "attend_backward", [sds((512, 384))] * 2, args, 30e9, scratch)


def mlp_step(rows, w_gate, w_up, grad_act):
    width = w_gate.shape[1]

    def kernel(rows_ref, g_ref, u_ref, ga_ref, act_ref, gg_ref, gu_ref):
        for j in range(0, width, 256):
            here = slice(j, j + 256)
            gate = dot(rows_ref[...], g_ref[:, here], 1, 0)
            up = dot(rows_ref[...], u_ref[:, here], 1, 0)
            sig = jax.nn.sigmoid(gate)
            silu = gate * sig
            ga = fl(ga_ref[:, here])
            act_ref[:, here] = bf(silu * up)
            gg_ref[:, here] = bf(ga * up * sig * (1.0 + gate * (1.0 - sig)))
            gu_ref[:, here] = bf(ga * silu)

    args = [rows, pinned(w_gate), pinned(w_up), grad_act]
    return call(kernel, "mlp_step", [sds((512, width))] * 3, args, 4 * 512 * D * width)


def frequencies(head_size):
    pair_index = jnp.arange(head_size // 2).astype(jnp.float32)
    base_freq = 500000.0 ** (-2.0 * pair_index / head_size)
    wavelen = 2.0 * jnp.pi / base_freq
    smooth = (8192.0 / wavelen - 1.0) / 3.0
    blended = (1.0 - smooth) * base_freq / 32.0 + smooth * base_freq
    return jnp.where(
        wavelen < 2048.0, base_freq, jnp.where(wavelen > 8192.0, base_freq / 32.0, blended)
    )


LONG = 60e9


def wide(out_ref, value):
    for k in range(4):
        out_ref[k] = value


def arrived_sum(ref):
    return fl(ref[0]) + fl(ref[1]) + fl(ref[2]) + fl(ref[3])


def mlp_norm(inputs, arrived, gain):
    def kernel(x_ref, a_ref, gain_ref, residual_ref, out_ref):
        residual = fl(x_ref[...]) + arrived_sum(a_ref)
        residual_ref[...] = residual
        inverse = lax.rsqrt(jnp.mean(residual * residual, axis=1, keepdims=True) + eps)
        wide(out_ref, bf(residual * inverse * gain_ref[...]))

    outs = [sds((128, D), jnp.float32), sds((4, 128, D))]
    return call(kernel, "mlp_norm", outs, [inputs, arrived, gain], LONG)


def norm_grad(grad, values, gain):
    inverse = lax.rsqrt(jnp.mean(values * values, axis=1, keepdims=True) + eps)
    unit = values * inverse
    scaled = grad * gain
    return inverse * (scaled - unit * jnp.mean(scaled * unit, axis=1, keepdims=True))


def mlp_norm_backward(upstream, arrived, residual, gain):
    def kernel(g_ref, a_ref, r_ref, gain_ref, grad_ref, out_ref):
        grad = fl(g_ref[...]) + norm_grad(arrived_sum(a_ref), r_ref[...], gain_ref[...])
        grad_ref[...] = grad
        wide(out_ref, bf(grad))

    outs = [sds((128, D), jnp.float32), sds((4, 128, D))]
    return call(kernel, "mlp_norm_backward", outs, [upstream, arrived, residual, gain], LONG)


def attn_norm_backward(grad_residual, arrived, inputs, gain):
    def kernel(g_ref, a_ref, x_ref, gain_ref, out_ref):
        out_ref[...] = bf(g_ref[...] + norm_grad(arrived_sum(a_ref), fl(x_ref[...]), gain_ref[...]))

    return call(kernel, "attn_norm_backward", [sds((128, D))], [grad_residual, arrived, inputs, gain], LONG)[0]


def layer_output(residual, arrived):
    def kernel(r_ref, a_ref, out_ref):
        out_ref[...] = bf(r_ref[...] + arrived_sum(a_ref))

    return call(kernel, "layer_output", [sds((128, D))], [residual, arrived], 1)[0]


def on_device(
    tokens, positions, w_query, w_key, w_value, w_out, attn_gain, w_gate, w_up, w_down, mlp_gain, cotangent
):
    me = Place()
    inputs_b = swapped(tokens)
    places = jnp.concatenate([(positions // 256).reshape(128, 8), (positions % 256).reshape(128, 8)], axis=1)
    extra = jnp.concatenate([attn_gain[:, None], mlp_gain[:, None], bf(places)], axis=1)
    extra = jnp.pad(extra, ((0, 0), (0, 110)))
    part_attn = swapped(jnp.concatenate([w_query, w_key, w_value, extra, w_out.T], axis=1))
    part_attn, inputs_b = lax.optimization_barrier((part_attn, inputs_b))

    blocks_in = send_z(inputs_b)
    w_qkv = gather_plane(part_attn[:, :512])
    w_gate, w_up, w_down, cotangent = after((w_gate, w_up, w_down, cotangent), inputs_b)
    upstream = swapped(cotangent)
    down_rows = w_down.T
    part_ab = swapped(jnp.concatenate([w_gate, down_rows[:, :512], w_up, down_rows[:, 512:]], axis=1))

    place = fl(part_attn[:, 386:402])
    seq_positions = (256.0 * place[:, :8] + place[:, 8:]).reshape(SEQ_LEN)
    freq = jnp.tile(frequencies(DH), 4)
    angles = seq_positions[:, None] * freq[None, :]
    sign = jnp.where(jnp.arange(128) % DH < DH // 2, -1.0, 1.0)
    tables = (jnp.cos(angles), jnp.sin(angles) * sign[None, :])
    pick = bf(jnp.arange(128)[None, :] == jnp.arange(8)[:, None])
    gain_rows = dot(pick, w_qkv[:, 384:], 1, 1)
    gain_attn, gain_mlp = gain_rows[:1], gain_rows[1:2]

    blocks_in = after(blocks_in, *tables, upstream, part_ab)
    own_normed = norm_tokens(blocks_in, gain_attn, me)
    normed_attn = [own_normed, sibling(own_normed)]
    own_qkv = project_qkv(0, normed_attn[0], w_qkv, tables, me.halves)
    projected = [own_qkv, project_qkv(1, normed_attn[1], w_qkv, tables, me.halves)]

    (own_up,) = after((upstream,), own_normed)
    blocks_up = send_z(own_up)
    (part_out,) = after((part_attn[:, 512:],), own_qkv)
    w_out_t = gather_plane(part_out)

    projected = after(projected, *blocks_up[1:3])
    attended, other_attended, qkv, lse = attend(projected, me.halves)
    (w_out_t,) = after((w_out_t,), attended, blocks_up[3])
    out_sums = chip_product(attended, other_attended, w_out_t, sibling(w_out_t))
    (out_sums,) = after((out_sums,), *blocks_up)

    (part_ab,) = after((part_ab,), own_normed)
    part_a, part_b = part_ab[:, :1536], part_ab[:, 1536:]
    holds = (projected[1], attended, out_sums)
    stage_a, stage_b = (jnp.concatenate(chain(p, axis, holds), axis=0) for p, axis in ((part_a, "x"), (part_b, "y")))

    own_up = place_tokens(blocks_up, me)
    rows_up = [own_up, sibling(own_up)]
    arrived = arrive_z(out_sums)

    parts_a, parts_b = chain(stage_a, "y", (None, None, None)), chain(stage_b, "x", (None, None, None))
    full_gate, down_a = place_rows(parts_a, me.blocks["x"], (1024, 512))
    full_up, down_b = place_rows(parts_b, me.blocks["y"], (1024, 512))
    full_down = [down_a, down_b]

    (arrived,) = after((arrived,), parts_a[2], parts_b[2], *rows_up)
    residual, normed_mlp = mlp_norm(inputs_b, arrived, gain_mlp)
    own_mlp = gather_z(normed_mlp)
    up_held = after(rows_up, normed_mlp)
    grad_act = [project(r, [pinned(w) for w in full_down], jnp.bfloat16) for r in up_held]
    (own_mlp,) = after((own_mlp,), full_gate, full_up, grad_act[0])
    rows_mlp = [own_mlp, sibling(own_mlp)]
    steps = [mlp_step(r, full_gate, full_up, g) for r, g in zip(rows_mlp, grad_act)]
    activated, grad_gate_pre, grad_up_pre = zip(*steps)

    gate_up = list(zip(grad_gate_pre, grad_up_pre))
    mlp_sums = chip_sums(gate_up[0], gate_up[1], [full_gate, full_up])
    arrived = arrive_z(mlp_sums)

    gg, gu = after((grad_gate_pre, grad_up_pre), mlp_sums)
    made_a = weight_product([(rows_mlp, gg, 0, 1024), (rows_up, activated, 0, 512)], "x", me, 2)
    made_b = weight_product([(rows_mlp, gu, 0, 1024), (rows_up, activated, 512, 1024)], "y", me, 2)
    sums = [made_a[0], made_b[0]]
    rings = [ring_cuts(total, axis) for total, axis in zip(sums, "xy")]
    (arrived,) = after((arrived,), made_a[-1][0], made_b[-1][0])
    grad_residual, grad_residual_b = mlp_norm_backward(upstream, arrived, residual, gain_mlp)

    own_gr = gather_z(grad_residual_b)
    rings = [after(cuts, grad_residual_b) for cuts in rings]
    sums = [add(received, made[1]) for received, made in zip(rings, (made_a, made_b))]
    rings = [ring_cuts(total, axis) for total, axis in zip(sums, "xy")]
    acts = after(activated, *sums[0], *sums[1])
    down_other = down_products(acts[1], full_down)
    down_own = down_products(acts[0], full_down)
    down_arrived = [sibling(half) for half in down_other]
    (own_gr,) = after((own_gr,), *down_own, *down_arrived, *rings[0], *rings[1])
    rows_gr = [own_gr, sibling(own_gr)]
    rings = [after(cuts, own_gr) for cuts in rings]
    sums = [add(received, made[2], True) for received, made in zip(rings, (made_a, made_b))]
    rings = [ring_cuts(total, axis) for total, axis in zip(sums, "xy")]
    down_sums = join_sums(after(down_own, sums[0][0], sums[1][0]), down_arrived)
    arrived = arrive_z(down_sums)
    grad_attended = [project(r, [w_out_t], jnp.bfloat16) for r in after(rows_gr, sums[0][0], sums[1][0])]
    grad_qkv, other_grad_qkv = attend_backward(qkv, lse, grad_attended, tables, me.halves)
    blocks_a = second_blocks([after(rings[0], grad_qkv), made_a[3]], "x", me)
    attn_sums = chip_product(grad_qkv, other_grad_qkv, w_qkv, sibling(w_qkv))
    (attn_sums,) = after((attn_sums,), arrived, blocks_a[0])
    grad_arrived = arrive_z(attn_sums)

    d_qkv = after((grad_qkv, other_grad_qkv), attn_sums)
    terms = [(normed_attn, d_qkv, 0, 384), (rows_gr, (attended, other_attended), 0, 256)]
    made_attn = [cut for (cut,) in weight_product(terms, "x", me)]
    sent_attn = send_pieces(made_attn, "x")
    blocks_b = second_blocks([after(rings[1], made_attn[-1]), made_b[3]], "y", me)
    (arrived,) = after((arrived,), blocks_b[0])
    layer_out = layer_output(residual, arrived)
    (grad_arrived,) = after((grad_arrived,), layer_out)
    grad_tokens = attn_norm_backward(grad_residual, grad_arrived, inputs_b, gain_attn)
    (layer_out,) = after((layer_out,), grad_tokens)
    blocks_a = list(after(blocks_a, made_attn[-1]))
    blocks_a[2:] = after(blocks_a[2:], grad_tokens)
    parts_a = second_stage(blocks_a, "x")
    parts_b = second_stage(after(blocks_b, grad_tokens), "y")
    *sent_attn, parts_a[0], parts_a[1] = after([*sent_attn, *parts_a[:2]], grad_tokens)
    blocks_attn = second_blocks([[part] for part in sent_attn], "x", me)
    share_b = fl(swapped(bf(summed(parts_b, blocks_attn[0]))))
    share_attn = summed(second_stage(blocks_attn, "x"), grad_tokens)
    share_a = summed(parts_a, grad_tokens)

    def gain_sum(*terms):
        return sum(jnp.sum(fl(w) * g, axis=1) for w, g in terms)

    gain_sums = jnp.stack(
        [
            gain_sum((jnp.concatenate([w_query, w_key, w_value], axis=1), share_attn[:, :384])),
            gain_sum((w_gate, share_a[:, :1024]), (w_up, share_b[:, :1024])),
        ]
    )
    gain_sums = gain_sums / fl(jnp.stack([attn_gain, mlp_gain]))
    gain_sums = gain_sums + z_moved(gain_sums, 1) + z_moved(gain_sums, 2) + z_moved(gain_sums, 3)
    gain_sums = gain_sums + h_flipped(gain_sums)
    return (
        swapped(layer_out),
        swapped(grad_tokens),
        share_attn[:, :256],
        share_attn[:, 256:320],
        share_attn[:, 320:384],
        share_attn[:, 384:].T,
        gain_sums[0],
        share_a[:, :1024],
        share_b[:, :1024],
        jnp.concatenate([share_a[:, 1024:], share_b[:, 1024:]], axis=1).T,
        gain_sums[1],
    )


def solution(mesh):
    split = Mesh(mesh.devices.reshape(4, 2, 2, 2, 4), AXES)
    dp, tensor = ("x", "l", "c"), ("h", "z")
    both = P(AXES, None)
    weight, turned, vector = P(dp, tensor), P(tensor, dp), P(dp)
    in_specs = (
        both, vector, weight, weight, weight, turned, vector, weight, weight, turned, vector, both,
    )
    out_specs = (
        both, both, weight, weight, weight, turned, vector, weight, weight, turned, vector,
    )
    return jax.shard_map(on_device, mesh=split, in_specs=in_specs, out_specs=out_specs, check_vma=False)
```

```python
import functools
import itertools
import math

import jax
import jax.numpy as jnp
from jax import lax
from jax.experimental import pallas as pl
from jax.experimental.pallas import tpu as pltpu
from jax.sharding import Mesh, PartitionSpec as P

H = 32
KV = 8
DH = 64
SEQ_LEN = 1024
D = 2048
eps = 1e-05

SIZES = dict(x=4, l=2, c=2, h=2, z=4)
AXES = ("x", "l", "c", "h", "z")

SCALE = DH ** (-0.5)
SCALE2 = SCALE * math.log2(math.e)
VMEM_LIMIT = 12 * 1024 * 1024


def pairs(axes, move):
    def place(index):
        at = 0
        for a in axes:
            at = at * SIZES[a] + index[a]
        return at

    out = []
    for index in itertools.product(*[range(SIZES[a]) for a in axes]):
        here = dict(zip(axes, index))
        out.append((place(here), place(move(dict(here)))))
    return out


def to_swapped(d):
    d["c"], d["h"] = d["h"], d["c"]
    return d


def to_sibling(d):
    d["c"] = 1 - d["c"]
    return d


def along(axis):
    def move(d):
        step = 1 - 2 * d["c"]
        if axis == "y":
            y = (2 * d["h"] + d["l"] + step) % 4
            d["h"], d["l"] = y // 2, y % 2
        else:
            d[axis] = (d[axis] + step) % 4
        return d

    return move


RING_AXES = dict(x=("x", "c"), y=("l", "c", "h"))
Z_STEPS = (0, 1, 3, 2)
PIECES = (1, 2, 3, 0)


def ring(value, axis):
    axes = RING_AXES[axis]
    return lax.ppermute(value, axes, pairs(axes, along(axis)))


def swapped(value):
    return lax.ppermute(value, ("c", "h"), pairs(("c", "h"), to_swapped))


def sibling(value):
    return lax.ppermute(value, ("c",), pairs(("c",), to_sibling))


def z_moved(value, step):
    def move(d):
        d["z"] = (d["z"] + step) % 4
        return d

    return lax.ppermute(value, ("z",), pairs(("z",), move))


def h_flipped(value):
    def move(d):
        d["h"] = 1 - d["h"]
        return d

    return lax.ppermute(value, ("h",), pairs(("h",), move))


def after(values, *earlier):
    held = lax.optimization_barrier((tuple(values), tuple(earlier)))
    return held[0]


def dot(a, b, ca, cb):
    return lax.dot_general(a, b, (((ca,), (cb,)), ((), ())), preferred_element_type=jnp.float32)


def bf(v):
    return v.astype(jnp.bfloat16)


def fl(v):
    return v.astype(jnp.float32)


def sds(shape, dtype=jnp.bfloat16):
    return jax.ShapeDtypeStruct(shape, dtype)


def cost(flops):
    return pl.CostEstimate(flops=int(flops), bytes_accessed=1, transcendentals=0)


PARAMS = pltpu.CompilerParams(vmem_limit_bytes=VMEM_LIMIT)
ANY = pl.BlockSpec(memory_space=pl.ANY)
WHOLE = pl.BlockSpec(memory_space=pltpu.VMEM)


class Place:
    def __init__(self):
        self.c = lax.axis_index("c")
        self.x = lax.axis_index("x")
        self.h = lax.axis_index("h")
        self.y = 2 * self.h + lax.axis_index("l")
        self.step = 1 - 2 * self.c
        self.halves = jnp.stack([512 * self.c, 512 * (1 - self.c)]).astype(jnp.int32)
        z = lax.axis_index("z")
        self.z_order = jnp.stack([lax.rem(z - step + 4, 4) for step in Z_STEPS]).astype(jnp.int32)
        self.blocks = {}
        for first, second in (("x", "y"), ("y", "x")):
            out = []
            for k2 in range(4):
                for k1 in range(4):
                    a, b = self.source(first, k1), self.source(second, k2)
                    out.append(4 * a + b if first == "x" else 4 * b + a)
            self.blocks[first] = jnp.stack(out).astype(jnp.int32)

    def source(self, axis, k):
        at = lax.rem(dict(x=self.x, y=self.y)[axis] - self.step * k + 4, 4)
        if axis == "y":
            at = 2 * lax.rem(at, 2) + lax.div(at, 2)
        return at


SMEM = pl.BlockSpec(memory_space=pltpu.SMEM)


def pinned(value):
    return pltpu.with_memory_space_constraint(value, pltpu.VMEM)


def place_rows(parts, blocks, widths):
    def kernel(blocks_ref, p0, p1, p2, p3, *rest):
        sems = rest[-1]
        copies = []
        for k2, part in enumerate((p0, p1, p2, p3)):
            for k1 in range(4):
                at = pl.multiple_of(blocks_ref[4 * k2 + k1] * 128, 128)
                low = 0
                for i, width in enumerate(widths):
                    copies.append(
                        pltpu.make_async_copy(
                            part.at[pl.ds(128 * k1, 128), pl.ds(low, width)],
                            rest[i].at[pl.ds(at, 128)],
                            sems.at[len(widths) * (4 * k2 + k1) + i],
                        )
                    )
                    low += width
        for copy in copies:
            copy.start()
        for copy in copies:
            copy.wait()

    return pl.pallas_call(
        kernel,
        out_shape=[pltpu.VMEM((D, width), jnp.bfloat16) for width in widths],
        in_specs=[SMEM] + [ANY] * 4,
        out_specs=[WHOLE] * len(widths),
        scratch_shapes=[pltpu.SemaphoreType.DMA((16 * len(widths),))],
        compiler_params=PARAMS,
        cost_estimate=cost(1),
        name="place_rows",
    )(blocks, *parts)


def stepped(value, axis, steps):
    def move(d):
        for _ in range(steps):
            d = along(axis)(d)
        return d

    axes = RING_AXES[axis]
    return lax.ppermute(value, axes, pairs(axes, move))


def chain(block, axis, holds):
    parts = [block]
    for hold in holds:
        part = ring(parts[-1], axis)
        parts.append(part if hold is None else after((part,), hold)[0])
    return parts


def gather_plane(block):
    wide = jnp.broadcast_to(block[None], (16,) + block.shape)
    return lax.all_to_all(wide, ("x", "l", "h"), split_axis=0, concat_axis=0, tiled=True).reshape(D, block.shape[1])


def call(kernel, name, outs, args, flops, scratch=(), limit=VMEM_LIMIT):
    return pl.pallas_call(
        kernel,
        out_shape=outs,
        in_specs=[SMEM if a.dtype == jnp.int32 else WHOLE for a in args],
        out_specs=[WHOLE] * len(outs),
        scratch_shapes=list(scratch),
        compiler_params=pltpu.CompilerParams(vmem_limit_bytes=limit),
        cost_estimate=cost(flops),
        name=name,
    )(*args)


def weight_product(terms, first, me, cuts=1):
    order = jnp.stack([me.source(first, k) for k in PIECES]).astype(jnp.int32)
    n = sum(high - low for _, _, low, high in terms) // cuts
    args = [order]
    for rows, right, _, _ in terms:
        args += [*rows, *right]

    def kernel(order_ref, *refs):
        for p in range(4):
            at = 0
            for t, (_, _, low, high) in enumerate(terms):
                rows, right = refs[4 * t : 4 * t + 2], refs[4 * t + 2 : 4 * t + 4]
                left = []
                for r in rows:
                    lanes = []
                    for j in range(4):
                        block = 4 * order_ref[p] + j if first == "x" else 4 * j + order_ref[p]
                        lanes.append(r[:, pl.ds(pl.multiple_of(block * 128, 128), 128)])
                    left.append(jnp.concatenate(lanes, axis=1))
                for j in range(low, high, 256):
                    end = min(j + 256, high)
                    total = dot(left[0], right[0][:, j:end], 0, 0) + dot(left[1], right[1][:, j:end], 0, 0)
                    out_ref = refs[4 * len(terms) + cuts * p + at // n]
                    out_ref[:, at % n : at % n + end - j] = bf(total)
                    at += end - j

    outs = [pltpu.HBM((512, n), jnp.bfloat16)] * (4 * cuts)
    made = call(kernel, "weight_product", outs, args, 2 * D * SEQ_LEN * n * cuts, limit=24 * 1024 * 1024)
    return [made[cuts * p : cuts * p + cuts] for p in range(4)]


def sum_blocks(parts, order):
    n = sum(cut.shape[1] for cut in parts[0])
    width = min(cut.shape[1] for part in parts for cut in part)

    def kernel(order_ref, *refs):
        for k in range(4):
            at = pl.ds(pl.multiple_of(order_ref[k] * 128, 128), 128)
            for low in range(0, n, width):
                total, first = None, 0
                for part in parts:
                    cut = part[0].shape[1]
                    value = fl(refs[first + low // cut][at, low % cut : low % cut + width])
                    total = value if total is None else total + value
                    first += len(part)
                refs[first + k][:, low : low + width] = bf(total)

    args = [order, *[cut for part in parts for cut in part]]
    return call(kernel, "sum_blocks", [sds((128, n))] * 4, args, 1)


def send_pieces(made, first):
    return [stepped(piece, first, 4 - k) if k else piece for k, piece in zip(PIECES, made)]


def homeward(value, k):
    def move(d):
        y = (2 * d["h"] + d["l"] - k * (1 - 2 * d["c"])) % 4
        d["l"], d["h"], d["c"] = y % 2, d["c"], y // 2
        return d

    axes = ("l", "c", "h")
    return lax.ppermute(value, axes, pairs(axes, move))


def add(one, other, join=False):
    count = len(one)
    n = one[0].shape[1]

    def kernel(*refs):
        for i in range(count):
            total = bf(fl(refs[i][...]) + fl(refs[count + i][...]))
            if join:
                refs[2 * count][:, n * i : n * i + n] = total
            else:
                refs[2 * count + i][...] = total

    outs = [sds((512, n * count))] if join else [sds(a.shape) for a in one]
    return call(kernel, "add", outs, [*one, *other], 1)


def ring_cuts(cuts, axis):
    return [ring(cut, axis) for cut in cuts]


def second_blocks(parts, first, me):
    second = "y" if first == "x" else "x"
    return sum_blocks(parts, jnp.stack([me.source(second, k) for k in PIECES]).astype(jnp.int32))


def second_stage(blocks, first):
    if first == "x":
        return [homeward(block, k) for k, block in zip(PIECES, blocks)]
    return send_pieces(blocks, "x")


def summed(parts, hold):
    return sum(fl(part) for part in after(parts, hold))


def send_z(block):
    return [z_moved(block, step) if step else block for step in Z_STEPS]


def place_tokens(blocks, me):
    def kernel(order_ref, b0, b1, b2, b3, out_ref):
        for k, ref in enumerate((b0, b1, b2, b3)):
            out_ref[pl.ds(pl.multiple_of(order_ref[k] * 128, 128), 128), :] = ref[...]

    return call(kernel, "place_tokens", [sds((512, D))], [me.z_order, *blocks], 1)[0]


def norm_tokens(blocks, gain, me):
    def kernel(order_ref, b0, b1, b2, b3, gain_ref, out_ref):
        for k, ref in enumerate((b0, b1, b2, b3)):
            x = fl(ref[...])
            inverse = lax.rsqrt(jnp.mean(x * x, axis=1, keepdims=True) + eps)
            out_ref[pl.ds(pl.multiple_of(order_ref[k] * 128, 128), 128), :] = bf(x * inverse * gain_ref[...])

    return call(kernel, "norm_tokens", [sds((512, D))], [me.z_order, *blocks, gain], 1)[0]


def gather_z(wide_block):
    whole = lax.all_to_all(wide_block, "z", split_axis=0, concat_axis=0, tiled=True)
    return whole.reshape(512, whole.shape[2])


def arrive_z(sums):
    parts = sums.reshape(4, 128, sums.shape[1])
    return lax.all_to_all(parts, "z", split_axis=0, concat_axis=0, tiled=True)


def partial_sums(pieces, weights):
    count = len(pieces)

    def kernel(*refs):
        for j in range(0, D, 512):
            total = None
            for i in range(count):
                one = dot(refs[i][...], refs[count + i][j : j + 512, :], 1, 1)
                total = one if total is None else total + one
            refs[-1][:, j : j + 512] = bf(total)

    depth = sum(p.shape[1] for p in pieces)
    return call(kernel, "partial_sums", [sds((512, D))], [*pieces, *map(pinned, weights)], 2 * 512 * depth * D)[0]


def chip_sums(own, other, weights):
    received = sibling(partial_sums(other, weights))
    return bf(fl(partial_sums(own, weights)) + fl(received))


def chip_product(own, other, weight, sibling_weight):
    received = sibling(other)
    m = own.shape[1]

    def kernel(a_ref, b_ref, v_ref, w_ref, out_ref):
        for j in range(0, D, 512):
            here = slice(j, j + 512)
            total = dot(a_ref[...], v_ref[here, :m], 1, 1) + dot(b_ref[...], w_ref[here, :m], 1, 1)
            out_ref[:, here] = bf(total)

    args = [own, received, weight, sibling_weight]
    return call(kernel, "chip_product", [sds((512, D))], args, 4 * 512 * m * D)[0]


def project(rows, weights, dtype, width=None):
    width = width or weights[0].shape[1]
    n = width * len(weights)

    def kernel(rows_ref, *refs):
        for i, w_ref in enumerate(refs[:-1]):
            for j in range(0, width, 256):
                product = dot(rows_ref[...], w_ref[:, j : j + 256], 1, 0)
                refs[-1][:, i * width + j : i * width + j + 256] = product.astype(dtype)

    return call(kernel, "project", [sds((512, n), dtype)], [rows, *weights], 2 * 512 * D * n)[0]


def down_products(rows, weights):
    def kernel(rows_ref, w0, w1, *out_refs):
        for j in range(0, D, 512):
            here = slice(j, j + 512)
            total = dot(rows_ref[:, :512], w0[here, :], 1, 1) + dot(rows_ref[:, 512:], w1[here, :], 1, 1)
            out_refs[j // 1024][:, j % 1024 : j % 1024 + 512] = bf(total)

    args = [rows, *map(pinned, weights)]
    return call(kernel, "down_products", [sds((512, D // 2))] * 2, args, 2 * 512 * 1024 * D)


def join_sums(one, other):
    def kernel(a0, a1, b0, b1, out_ref):
        out_ref[:, :1024] = bf(fl(a0[...]) + fl(b0[...]))
        out_ref[:, 1024:] = bf(fl(a1[...]) + fl(b1[...]))

    return call(kernel, "join_sums", [sds((512, D))], [*one, *other], 1)[0]


def rope(u, cosine, sine):
    lane = lax.broadcasted_iota(jnp.int32, u.shape, 1)
    turned = jnp.where(lane % DH < DH // 2, pltpu.roll(u, 96, 1), pltpu.roll(u, 32, 1))
    return u * cosine + turned * sine


def rope_three(u, cosine, sine):
    lane = lax.broadcasted_iota(jnp.int32, cosine.shape, 1)
    last = u[:, 256:]
    return jnp.concatenate(
        [
            rope(u[:, :128], cosine, sine),
            rope(u[:, 128:256], cosine, sine),
            jnp.where(lane < DH, rope(last, cosine, sine), last),
        ],
        axis=1,
    )


def half_at(halves_ref, i):
    return pl.ds(pl.multiple_of(halves_ref[i], 512), 512)


def project_qkv(i, rows, weight, tables, halves):
    def kernel(halves_ref, rows_ref, w_ref, cos_ref, sin_ref, out_ref):
        here = half_at(halves_ref, i)
        product = dot(rows_ref[...], w_ref[:, :384], 1, 0)
        out_ref[...] = bf(rope_three(product, cos_ref[here, :], sin_ref[here, :]))

    args = [halves, rows, weight, *tables]
    return call(kernel, "project_qkv", [sds((512, 384))], args, 2 * 512 * D * 384)[0]


def scores_t(keys, query, q_at):
    s = dot(keys, query, 1, 1)
    key = lax.broadcasted_iota(jnp.int32, (256, 256), 0)
    column = lax.broadcasted_iota(jnp.int32, (256, 256), 1)
    diagonal = jnp.where(key <= column, s[q_at:], -1e30)
    return diagonal if q_at == 0 else jnp.concatenate([s[:q_at], diagonal], axis=0)


def attend(qkv, halves):
    def kernel(halves_ref, q0, q1, own_ref, other_ref, nat_ref, lse_ref, att_ref):
        nat_ref[half_at(halves_ref, 0), :] = q0[...]
        nat_ref[half_at(halves_ref, 1), :] = q1[...]
        kv = nat_ref[:, 256:]
        keys = kv[:, :DH]
        values_t = kv.T[DH:]
        lse_ref[...] = jnp.zeros_like(lse_ref)
        for q_at in range(0, SEQ_LEN, 256):
            end = q_at + 256
            for pair in range(2):
                two = nat_ref[q_at:end, 128 * pair : 128 * pair + 128]
                outs = []
                for i in range(2):
                    s = scores_t(keys[:end], two[:, DH * i : DH * i + DH], q_at)
                    top = jnp.max(s, axis=0, keepdims=True)
                    p = jnp.exp2((s - top) * SCALE2)
                    total = jnp.sum(p, axis=0, keepdims=True)
                    outs.append(dot(values_t[:, :end], bf(p), 1, 0) / total)
                    g = 2 * pair + i
                    lse_ref[g : g + 1, q_at:end] = top * SCALE2 + jnp.log2(total)
                att_ref[q_at:end, 128 * pair : 128 * pair + 128] = bf(jnp.concatenate(outs, axis=0).T)
        own_ref[...] = att_ref[half_at(halves_ref, 0), :]
        other_ref[...] = att_ref[half_at(halves_ref, 1), :]

    outs = [sds((512, 256)), sds((512, 256)), sds((SEQ_LEN, 384)), sds((8, SEQ_LEN), jnp.float32)]
    scratch = [pltpu.VMEM((SEQ_LEN, 256), jnp.bfloat16)]
    return call(kernel, "attend", outs, [halves, *qkv], 20e9, scratch)


def attend_backward(qkv, lse, grad_out, tables, halves):
    def kernel(halves_ref, nat_ref, lse_ref, g0, g1, cos_ref, sin_ref, own_ref, other_ref, go_nat, kv_sum, d_nat):
        go_nat[half_at(halves_ref, 0), :] = g0[...]
        go_nat[half_at(halves_ref, 1), :] = g1[...]
        kv = nat_ref[:, 256:]
        keys = kv[:, :DH]
        values = kv[:, DH:]
        keys_t = kv.T[:DH]
        kv_sum[...] = jnp.zeros_like(kv_sum)
        for q_at in range(0, SEQ_LEN, 256):
            end = q_at + 256
            cosine = cos_ref[q_at:end, :]
            sine = -sin_ref[q_at:end, :]
            for pair in range(2):
                lanes = slice(128 * pair, 128 * pair + 128)
                two = nat_ref[q_at:end, lanes]
                two_grad = go_nat[q_at:end, lanes]
                outs = []
                for i in range(2):
                    query = two[:, DH * i : DH * i + DH]
                    grad = two_grad[:, DH * i : DH * i + DH]
                    g = 2 * pair + i
                    s = scores_t(keys[:end], query, q_at)
                    p = jnp.exp2(s * SCALE2 - lse_ref[g : g + 1, q_at:end])
                    dp = dot(values[:end], grad, 1, 1)
                    delta = jnp.sum(dp * p, axis=0, keepdims=True)
                    ds = bf(p * (dp - delta))
                    kv_sum[:end, :] += jnp.concatenate(
                        [dot(ds, query, 1, 0), dot(bf(p), grad, 1, 0)], axis=1
                    )
                    outs.append(dot(keys_t[:, :end], ds, 1, 0))
                d_query = jnp.concatenate(outs, axis=0).T * SCALE
                d_nat[q_at:end, lanes] = bf(rope(d_query, cosine, sine))
        lane = lax.broadcasted_iota(jnp.int32, (SEQ_LEN, 128), 1)
        total = kv_sum[...]
        turned = rope(total * SCALE, cos_ref[...], -sin_ref[...])
        d_nat[:, 256:] = bf(jnp.where(lane < DH, turned, total))
        own_ref[...] = d_nat[half_at(halves_ref, 0), :]
        other_ref[...] = d_nat[half_at(halves_ref, 1), :]

    scratch = [
        pltpu.VMEM((SEQ_LEN, 256), jnp.bfloat16),
        pltpu.VMEM((SEQ_LEN, 128), jnp.float32),
        pltpu.VMEM((SEQ_LEN, 384), jnp.bfloat16),
    ]
    args = [halves, qkv, lse, *grad_out, *tables]
    return call(kernel, "attend_backward", [sds((512, 384))] * 2, args, 30e9, scratch)


def mlp_step(rows, w_gate, w_up, grad_act):
    width = w_gate.shape[1]

    def kernel(rows_ref, g_ref, u_ref, ga_ref, act_ref, gg_ref, gu_ref):
        for j in range(0, width, 256):
            here = slice(j, j + 256)
            gate = dot(rows_ref[...], g_ref[:, here], 1, 0)
            up = dot(rows_ref[...], u_ref[:, here], 1, 0)
            sig = jax.nn.sigmoid(gate)
            silu = gate * sig
            ga = fl(ga_ref[:, here])
            act_ref[:, here] = bf(silu * up)
            gg_ref[:, here] = bf(ga * up * sig * (1.0 + gate * (1.0 - sig)))
            gu_ref[:, here] = bf(ga * silu)

    args = [rows, pinned(w_gate), pinned(w_up), grad_act]
    return call(kernel, "mlp_step", [sds((512, width))] * 3, args, 4 * 512 * D * width)


def frequencies(head_size):
    pair_index = jnp.arange(head_size // 2).astype(jnp.float32)
    base_freq = 500000.0 ** (-2.0 * pair_index / head_size)
    wavelen = 2.0 * jnp.pi / base_freq
    smooth = (8192.0 / wavelen - 1.0) / 3.0
    blended = (1.0 - smooth) * base_freq / 32.0 + smooth * base_freq
    return jnp.where(
        wavelen < 2048.0, base_freq, jnp.where(wavelen > 8192.0, base_freq / 32.0, blended)
    )


LONG = 60e9


def wide(out_ref, value):
    for k in range(4):
        out_ref[k] = value


def arrived_sum(ref):
    return fl(ref[0]) + fl(ref[1]) + fl(ref[2]) + fl(ref[3])


def mlp_norm(inputs, arrived, gain):
    def kernel(x_ref, a_ref, gain_ref, residual_ref, out_ref):
        residual = fl(x_ref[...]) + arrived_sum(a_ref)
        residual_ref[...] = residual
        inverse = lax.rsqrt(jnp.mean(residual * residual, axis=1, keepdims=True) + eps)
        wide(out_ref, bf(residual * inverse * gain_ref[...]))

    outs = [sds((128, D), jnp.float32), sds((4, 128, D))]
    return call(kernel, "mlp_norm", outs, [inputs, arrived, gain], LONG)


def norm_grad(grad, values, gain):
    inverse = lax.rsqrt(jnp.mean(values * values, axis=1, keepdims=True) + eps)
    unit = values * inverse
    scaled = grad * gain
    return inverse * (scaled - unit * jnp.mean(scaled * unit, axis=1, keepdims=True))


def mlp_norm_backward(upstream, arrived, residual, gain):
    def kernel(g_ref, a_ref, r_ref, gain_ref, grad_ref, out_ref):
        grad = fl(g_ref[...]) + norm_grad(arrived_sum(a_ref), r_ref[...], gain_ref[...])
        grad_ref[...] = grad
        wide(out_ref, bf(grad))

    outs = [sds((128, D), jnp.float32), sds((4, 128, D))]
    return call(kernel, "mlp_norm_backward", outs, [upstream, arrived, residual, gain], LONG)


def attn_norm_backward(grad_residual, arrived, inputs, gain):
    def kernel(g_ref, a_ref, x_ref, gain_ref, out_ref):
        out_ref[...] = bf(g_ref[...] + norm_grad(arrived_sum(a_ref), fl(x_ref[...]), gain_ref[...]))

    return call(kernel, "attn_norm_backward", [sds((128, D))], [grad_residual, arrived, inputs, gain], LONG)[0]


def layer_output(residual, arrived):
    def kernel(r_ref, a_ref, out_ref):
        out_ref[...] = bf(r_ref[...] + arrived_sum(a_ref))

    return call(kernel, "layer_output", [sds((128, D))], [residual, arrived], 1)[0]


def on_device(
    tokens, positions, w_query, w_key, w_value, w_out, attn_gain, w_gate, w_up, w_down, mlp_gain, cotangent
):
    me = Place()
    inputs_b = swapped(tokens)
    places = jnp.concatenate([(positions // 256).reshape(128, 8), (positions % 256).reshape(128, 8)], axis=1)
    extra = jnp.concatenate([attn_gain[:, None], mlp_gain[:, None], bf(places)], axis=1)
    extra = jnp.pad(extra, ((0, 0), (0, 110)))
    part_attn = swapped(jnp.concatenate([w_query, w_key, w_value, extra, w_out.T], axis=1))
    part_attn, inputs_b = lax.optimization_barrier((part_attn, inputs_b))

    blocks_in = send_z(inputs_b)
    w_qkv = gather_plane(part_attn[:, :512])
    w_gate, w_up, w_down, cotangent = after((w_gate, w_up, w_down, cotangent), inputs_b)
    upstream = swapped(cotangent)
    down_rows = w_down.T
    part_ab = swapped(jnp.concatenate([w_gate, down_rows[:, :512], w_up, down_rows[:, 512:]], axis=1))

    place = fl(part_attn[:, 386:402])
    seq_positions = (256.0 * place[:, :8] + place[:, 8:]).reshape(SEQ_LEN)
    freq = jnp.tile(frequencies(DH), 4)
    angles = seq_positions[:, None] * freq[None, :]
    sign = jnp.where(jnp.arange(128) % DH < DH // 2, -1.0, 1.0)
    tables = (jnp.cos(angles), jnp.sin(angles) * sign[None, :])
    pick = bf(jnp.arange(128)[None, :] == jnp.arange(8)[:, None])
    gain_rows = dot(pick, w_qkv[:, 384:], 1, 1)
    gain_attn, gain_mlp = gain_rows[:1], gain_rows[1:2]

    blocks_in = after(blocks_in, *tables, upstream, part_ab)
    own_normed = norm_tokens(blocks_in, gain_attn, me)
    normed_attn = [own_normed, sibling(own_normed)]
    own_qkv = project_qkv(0, normed_attn[0], w_qkv, tables, me.halves)
    projected = [own_qkv, project_qkv(1, normed_attn[1], w_qkv, tables, me.halves)]

    (own_up,) = after((upstream,), own_normed)
    blocks_up = send_z(own_up)
    (part_out,) = after((part_attn[:, 512:],), own_qkv)
    w_out_t = gather_plane(part_out)

    projected = after(projected, *blocks_up[1:3])
    attended, other_attended, qkv, lse = attend(projected, me.halves)
    (w_out_t,) = after((w_out_t,), attended, blocks_up[3])
    out_sums = chip_product(attended, other_attended, w_out_t, sibling(w_out_t))
    (out_sums,) = after((out_sums,), *blocks_up)

    (part_ab,) = after((part_ab,), own_normed)
    part_a, part_b = part_ab[:, :1536], part_ab[:, 1536:]
    holds = (projected[1], attended, out_sums)
    stage_a, stage_b = (jnp.concatenate(chain(p, axis, holds), axis=0) for p, axis in ((part_a, "x"), (part_b, "y")))

    own_up = place_tokens(blocks_up, me)
    rows_up = [own_up, sibling(own_up)]
    arrived = arrive_z(out_sums)

    parts_a, parts_b = chain(stage_a, "y", (None, None, None)), chain(stage_b, "x", (None, None, None))
    full_gate, down_a = place_rows(parts_a, me.blocks["x"], (1024, 512))
    full_up, down_b = place_rows(parts_b, me.blocks["y"], (1024, 512))
    full_down = [down_a, down_b]

    (arrived,) = after((arrived,), parts_a[2], parts_b[2], *rows_up)
    residual, normed_mlp = mlp_norm(inputs_b, arrived, gain_mlp)
    own_mlp = gather_z(normed_mlp)
    up_held = after(rows_up, normed_mlp)
    grad_act = [project(r, [pinned(w) for w in full_down], jnp.bfloat16) for r in up_held]
    (own_mlp,) = after((own_mlp,), full_gate, full_up, grad_act[0])
    rows_mlp = [own_mlp, sibling(own_mlp)]
    steps = [mlp_step(r, full_gate, full_up, g) for r, g in zip(rows_mlp, grad_act)]
    activated, grad_gate_pre, grad_up_pre = zip(*steps)

    gate_up = list(zip(grad_gate_pre, grad_up_pre))
    mlp_sums = chip_sums(gate_up[0], gate_up[1], [full_gate, full_up])
    arrived = arrive_z(mlp_sums)

    gg, gu = after((grad_gate_pre, grad_up_pre), mlp_sums)
    made_a = weight_product([(rows_mlp, gg, 0, 1024), (rows_up, activated, 0, 512)], "x", me, 2)
    made_b = weight_product([(rows_mlp, gu, 0, 1024), (rows_up, activated, 512, 1024)], "y", me, 2)
    sums = [made_a[0], made_b[0]]
    rings = [ring_cuts(total, axis) for total, axis in zip(sums, "xy")]
    (arrived,) = after((arrived,), made_a[-1][0], made_b[-1][0])
    grad_residual, grad_residual_b = mlp_norm_backward(upstream, arrived, residual, gain_mlp)

    own_gr = gather_z(grad_residual_b)
    rings = [after(cuts, grad_residual_b) for cuts in rings]
    sums = [add(received, made[1]) for received, made in zip(rings, (made_a, made_b))]
    rings = [ring_cuts(total, axis) for total, axis in zip(sums, "xy")]
    acts = after(activated, *sums[0], *sums[1])
    down_other = down_products(acts[1], full_down)
    down_own = down_products(acts[0], full_down)
    down_arrived = [sibling(half) for half in down_other]
    (own_gr,) = after((own_gr,), *down_own, *down_arrived, *rings[0], *rings[1])
    rows_gr = [own_gr, sibling(own_gr)]
    rings = [after(cuts, own_gr) for cuts in rings]
    sums = [add(received, made[2], True) for received, made in zip(rings, (made_a, made_b))]
    rings = [ring_cuts(total, axis) for total, axis in zip(sums, "xy")]
    down_sums = join_sums(after(down_own, sums[0][0], sums[1][0]), down_arrived)
    arrived = arrive_z(down_sums)
    grad_attended = [project(r, [w_out_t], jnp.bfloat16) for r in after(rows_gr, sums[0][0], sums[1][0])]
    grad_qkv, other_grad_qkv = attend_backward(qkv, lse, grad_attended, tables, me.halves)
    blocks_a = second_blocks([after(rings[0], grad_qkv), made_a[3]], "x", me)
    attn_sums = chip_product(grad_qkv, other_grad_qkv, w_qkv, sibling(w_qkv))
    (attn_sums,) = after((attn_sums,), arrived, blocks_a[0])
    grad_arrived = arrive_z(attn_sums)

    d_qkv = after((grad_qkv, other_grad_qkv), attn_sums)
    terms = [(normed_attn, d_qkv, 0, 384), (rows_gr, (attended, other_attended), 0, 256)]
    made_attn = [cut for (cut,) in weight_product(terms, "x", me)]
    sent_attn = send_pieces(made_attn, "x")
    blocks_b = second_blocks([after(rings[1], made_attn[-1]), made_b[3]], "y", me)
    (arrived,) = after((arrived,), blocks_b[0])
    layer_out = layer_output(residual, arrived)
    (grad_arrived,) = after((grad_arrived,), layer_out)
    grad_tokens = attn_norm_backward(grad_residual, grad_arrived, inputs_b, gain_attn)
    (layer_out,) = after((layer_out,), grad_tokens)
    blocks_a = list(after(blocks_a, made_attn[-1]))
    blocks_a[2:] = after(blocks_a[2:], grad_tokens)
    parts_a = second_stage(blocks_a, "x")
    parts_b = second_stage(after(blocks_b, grad_tokens), "y")
    *sent_attn, parts_a[0], parts_a[1] = after([*sent_attn, *parts_a[:2]], grad_tokens)
    blocks_attn = second_blocks([[part] for part in after(sent_attn, *parts_b)], "x", me)
    share_b = fl(swapped(bf(summed(parts_b, blocks_attn[0]))))
    share_attn = summed(second_stage(blocks_attn, "x"), grad_tokens)
    share_a = summed(parts_a, grad_tokens)

    def gain_sum(*terms):
        return sum(jnp.sum(fl(w) * g, axis=1) for w, g in terms)

    gain_sums = jnp.stack(
        [
            gain_sum((jnp.concatenate([w_query, w_key, w_value], axis=1), share_attn[:, :384])),
            gain_sum((w_gate, share_a[:, :1024]), (w_up, share_b[:, :1024])),
        ]
    )
    gain_sums = gain_sums / fl(jnp.stack([attn_gain, mlp_gain]))
    gain_sums = gain_sums + z_moved(gain_sums, 1) + z_moved(gain_sums, 2) + z_moved(gain_sums, 3)
    gain_sums = gain_sums + h_flipped(gain_sums)
    return (
        swapped(layer_out),
        swapped(grad_tokens),
        share_attn[:, :256],
        share_attn[:, 256:320],
        share_attn[:, 320:384],
        share_attn[:, 384:].T,
        gain_sums[0],
        share_a[:, :1024],
        share_b[:, :1024],
        jnp.concatenate([share_a[:, 1024:], share_b[:, 1024:]], axis=1).T,
        gain_sums[1],
    )


def solution(mesh):
    split = Mesh(mesh.devices.reshape(4, 2, 2, 2, 4), AXES)
    dp, tensor = ("x", "l", "c"), ("h", "z")
    both = P(AXES, None)
    weight, turned, vector = P(dp, tensor), P(tensor, dp), P(dp)
    in_specs = (
        both, vector, weight, weight, weight, turned, vector, weight, weight, turned, vector, both,
    )
    out_specs = (
        both, both, weight, weight, weight, turned, vector, weight, weight, turned, vector,
    )
    return jax.shard_map(on_device, mesh=split, in_specs=in_specs, out_specs=out_specs, check_vma=False)
```

```python
import functools
import itertools
import math

import jax
import jax.numpy as jnp
from jax import lax
from jax.experimental import pallas as pl
from jax.experimental.pallas import tpu as pltpu
from jax.sharding import Mesh, PartitionSpec as P

H = 32
KV = 8
DH = 64
SEQ_LEN = 1024
D = 2048
eps = 1e-05

SIZES = dict(x=4, l=2, c=2, h=2, z=4)
AXES = ("x", "l", "c", "h", "z")

SCALE = DH ** (-0.5)
SCALE2 = SCALE * math.log2(math.e)
VMEM_LIMIT = 14 * 1024 * 1024


def pairs(axes, move):
    def place(index):
        at = 0
        for a in axes:
            at = at * SIZES[a] + index[a]
        return at

    out = []
    for index in itertools.product(*[range(SIZES[a]) for a in axes]):
        here = dict(zip(axes, index))
        out.append((place(here), place(move(dict(here)))))
    return out


def to_swapped(d):
    d["c"], d["h"] = d["h"], d["c"]
    return d


def to_sibling(d):
    d["c"] = 1 - d["c"]
    return d


def along(axis):
    def move(d):
        step = 1 - 2 * d["c"]
        if axis == "y":
            y = (2 * d["h"] + d["l"] + step) % 4
            d["h"], d["l"] = y // 2, y % 2
        else:
            d[axis] = (d[axis] + step) % 4
        return d

    return move


RING_AXES = dict(x=("x", "c"), y=("l", "c", "h"))
Z_STEPS = (0, 1, 3, 2)
PIECES = (1, 2, 3, 0)


def ring(value, axis):
    axes = RING_AXES[axis]
    return lax.ppermute(value, axes, pairs(axes, along(axis)))


def swapped(value):
    return lax.ppermute(value, ("c", "h"), pairs(("c", "h"), to_swapped))


def sibling(value):
    return lax.ppermute(value, ("c",), pairs(("c",), to_sibling))


def z_moved(value, step):
    def move(d):
        d["z"] = (d["z"] + step) % 4
        return d

    return lax.ppermute(value, ("z",), pairs(("z",), move))


def h_flipped(value):
    def move(d):
        d["h"] = 1 - d["h"]
        return d

    return lax.ppermute(value, ("h",), pairs(("h",), move))


def after(values, *earlier):
    held = lax.optimization_barrier((tuple(values), tuple(earlier)))
    return held[0]


def dot(a, b, ca, cb):
    return lax.dot_general(a, b, (((ca,), (cb,)), ((), ())), preferred_element_type=jnp.float32)


def bf(v):
    return v.astype(jnp.bfloat16)


def fl(v):
    return v.astype(jnp.float32)


def sds(shape, dtype=jnp.bfloat16):
    return jax.ShapeDtypeStruct(shape, dtype)


def cost(flops):
    return pl.CostEstimate(flops=int(flops), bytes_accessed=1, transcendentals=0)


PARAMS = pltpu.CompilerParams(vmem_limit_bytes=VMEM_LIMIT)
ANY = pl.BlockSpec(memory_space=pl.ANY)
WHOLE = pl.BlockSpec(memory_space=pltpu.VMEM)


class Place:
    def __init__(self):
        self.c = lax.axis_index("c")
        self.x = lax.axis_index("x")
        self.h = lax.axis_index("h")
        self.y = 2 * self.h + lax.axis_index("l")
        self.step = 1 - 2 * self.c
        self.halves = jnp.stack([512 * self.c, 512 * (1 - self.c)]).astype(jnp.int32)
        z = lax.axis_index("z")
        self.z_order = jnp.stack([lax.rem(z - step + 4, 4) for step in Z_STEPS]).astype(jnp.int32)
        self.blocks = {}
        for first, second in (("x", "y"), ("y", "x")):
            out = []
            for k2 in range(4):
                for k1 in range(4):
                    a, b = self.source(first, k1), self.source(second, k2)
                    out.append(4 * a + b if first == "x" else 4 * b + a)
            self.blocks[first] = jnp.stack(out).astype(jnp.int32)

    def source(self, axis, k):
        at = lax.rem(dict(x=self.x, y=self.y)[axis] - self.step * k + 4, 4)
        if axis == "y":
            at = 2 * lax.rem(at, 2) + lax.div(at, 2)
        return at


SMEM = pl.BlockSpec(memory_space=pltpu.SMEM)


def pinned(value):
    return pltpu.with_memory_space_constraint(value, pltpu.VMEM)


def place_rows(parts, blocks, widths):
    def kernel(blocks_ref, p0, p1, p2, p3, *rest):
        sems = rest[-1]
        copies = []
        for k2, part in enumerate((p0, p1, p2, p3)):
            for k1 in range(4):
                at = pl.multiple_of(blocks_ref[4 * k2 + k1] * 128, 128)
                low = 0
                for i, width in enumerate(widths):
                    copies.append(
                        pltpu.make_async_copy(
                            part.at[pl.ds(128 * k1, 128), pl.ds(low, width)],
                            rest[i].at[pl.ds(at, 128)],
                            sems.at[len(widths) * (4 * k2 + k1) + i],
                        )
                    )
                    low += width
        for copy in copies:
            copy.start()
        for copy in copies:
            copy.wait()

    return pl.pallas_call(
        kernel,
        out_shape=[pltpu.VMEM((D, width), jnp.bfloat16) for width in widths],
        in_specs=[SMEM] + [ANY] * 4,
        out_specs=[WHOLE] * len(widths),
        scratch_shapes=[pltpu.SemaphoreType.DMA((16 * len(widths),))],
        compiler_params=PARAMS,
        cost_estimate=cost(1),
        name="place_rows",
    )(blocks, *parts)


def stepped(value, axis, steps):
    def move(d):
        for _ in range(steps):
            d = along(axis)(d)
        return d

    axes = RING_AXES[axis]
    return lax.ppermute(value, axes, pairs(axes, move))


def chain(block, axis, holds):
    parts = [block]
    for hold in holds:
        part = ring(parts[-1], axis)
        parts.append(part if hold is None else after((part,), hold)[0])
    return parts


def gather_plane(block):
    wide = jnp.broadcast_to(block[None], (16,) + block.shape)
    return lax.all_to_all(wide, ("x", "l", "h"), split_axis=0, concat_axis=0, tiled=True).reshape(D, block.shape[1])


def call(kernel, name, outs, args, flops, scratch=(), limit=VMEM_LIMIT):
    return pl.pallas_call(
        kernel,
        out_shape=outs,
        in_specs=[SMEM if a.dtype == jnp.int32 else WHOLE for a in args],
        out_specs=[WHOLE] * len(outs),
        scratch_shapes=list(scratch),
        compiler_params=pltpu.CompilerParams(vmem_limit_bytes=limit),
        cost_estimate=cost(flops),
        name=name,
    )(*args)


def weight_product(terms, first, me):
    order = jnp.stack([me.source(first, k) for k in PIECES]).astype(jnp.int32)
    n = sum(high - low for _, _, low, high in terms)
    args = [order]
    for rows, right, _, _ in terms:
        args += [*rows, *right]

    def kernel(order_ref, *refs):
        for p in range(4):
            at = 0
            for t, (_, _, low, high) in enumerate(terms):
                rows, right = refs[4 * t : 4 * t + 2], refs[4 * t + 2 : 4 * t + 4]
                left = []
                for r in rows:
                    lanes = []
                    for j in range(4):
                        block = 4 * order_ref[p] + j if first == "x" else 4 * j + order_ref[p]
                        lanes.append(r[:, pl.ds(pl.multiple_of(block * 128, 128), 128)])
                    left.append(jnp.concatenate(lanes, axis=1))
                for j in range(low, high, 256):
                    end = min(j + 256, high)
                    total = dot(left[0], right[0][:, j:end], 0, 0) + dot(left[1], right[1][:, j:end], 0, 0)
                    refs[4 * len(terms) + p][:, at : at + end - j] = bf(total)
                    at += end - j

    return call(
        kernel, "weight_product", [sds((512, n))] * 4, args, 2 * D * SEQ_LEN * n, limit=28 * 1024 * 1024
    )


def sum_blocks(parts, order):
    n = parts[0].shape[1]

    def kernel(order_ref, *refs):
        for k in range(4):
            at = pl.ds(pl.multiple_of(order_ref[k] * 128, 128), 128)
            refs[len(parts) + k][...] = bf(sum(fl(ref[at, :]) for ref in refs[: len(parts)]))

    return call(kernel, "sum_blocks", [sds((128, n))] * 4, [order, *parts], 1)


def send_pieces(made, first):
    return [stepped(piece, first, 4 - k) if k else piece for k, piece in zip(PIECES, made)]


def homeward(value, k):
    def move(d):
        y = (2 * d["h"] + d["l"] - k * (1 - 2 * d["c"])) % 4
        d["l"], d["h"], d["c"] = y % 2, d["c"], y // 2
        return d

    axes = ("l", "c", "h")
    return lax.ppermute(value, axes, pairs(axes, move))


def add(one, other):
    def kernel(a_ref, b_ref, out_ref):
        out_ref[...] = bf(fl(a_ref[...]) + fl(b_ref[...]))

    return call(kernel, "add", [sds(one.shape)], [one, other], 1)[0]


def second_blocks(parts, first, me):
    second = "y" if first == "x" else "x"
    return sum_blocks(parts, jnp.stack([me.source(second, k) for k in PIECES]).astype(jnp.int32))


def second_stage(blocks, first):
    if first == "x":
        return [homeward(block, k) for k, block in zip(PIECES, blocks)]
    return send_pieces(blocks, "x")


def summed(parts, hold):
    return sum(fl(part) for part in after(parts, hold))


def send_z(block):
    return [z_moved(block, step) if step else block for step in Z_STEPS]


def place_tokens(blocks, me):
    def kernel(order_ref, b0, b1, b2, b3, out_ref):
        for k, ref in enumerate((b0, b1, b2, b3)):
            out_ref[pl.ds(pl.multiple_of(order_ref[k] * 128, 128), 128), :] = ref[...]

    return call(kernel, "place_tokens", [sds((512, D))], [me.z_order, *blocks], 1)[0]


def norm_tokens(blocks, gain, me):
    def kernel(order_ref, b0, b1, b2, b3, gain_ref, out_ref):
        for k, ref in enumerate((b0, b1, b2, b3)):
            x = fl(ref[...])
            inverse = lax.rsqrt(jnp.mean(x * x, axis=1, keepdims=True) + eps)
            out_ref[pl.ds(pl.multiple_of(order_ref[k] * 128, 128), 128), :] = bf(x * inverse * gain_ref[...])

    return call(kernel, "norm_tokens", [sds((512, D))], [me.z_order, *blocks, gain], 1)[0]


def gather_z(wide_block):
    whole = lax.all_to_all(wide_block, "z", split_axis=0, concat_axis=0, tiled=True)
    return whole.reshape(512, whole.shape[2])


def arrive_z(sums):
    parts = sums.reshape(4, 128, sums.shape[1])
    return lax.all_to_all(parts, "z", split_axis=0, concat_axis=0, tiled=True)


def partial_sums(pieces, weights):
    count = len(pieces)

    def kernel(*refs):
        for j in range(0, D, 512):
            total = None
            for i in range(count):
                one = dot(refs[i][...], refs[count + i][j : j + 512, :], 1, 1)
                total = one if total is None else total + one
            refs[-1][:, j : j + 512] = bf(total)

    depth = sum(p.shape[1] for p in pieces)
    return call(kernel, "partial_sums", [sds((512, D))], [*pieces, *map(pinned, weights)], 2 * 512 * depth * D)[0]


def chip_sums(own, other, weights):
    received = sibling(partial_sums(other, weights))
    return bf(fl(partial_sums(own, weights)) + fl(received))


def chip_product(own, other, weight, sibling_weight):
    received = sibling(other)
    m = own.shape[1]

    def kernel(a_ref, b_ref, v_ref, w_ref, out_ref):
        for j in range(0, D, 512):
            here = slice(j, j + 512)
            total = dot(a_ref[...], v_ref[here, :m], 1, 1) + dot(b_ref[...], w_ref[here, :m], 1, 1)
            out_ref[:, here] = bf(total)

    args = [own, received, weight, sibling_weight]
    return call(kernel, "chip_product", [sds((512, D))], args, 4 * 512 * m * D)[0]


def project(rows, weights, dtype, width=None):
    width = width or weights[0].shape[1]
    n = width * len(weights)

    def kernel(rows_ref, *refs):
        for i, w_ref in enumerate(refs[:-1]):
            for j in range(0, width, 256):
                product = dot(rows_ref[...], w_ref[:, j : j + 256], 1, 0)
                refs[-1][:, i * width + j : i * width + j + 256] = product.astype(dtype)

    return call(kernel, "project", [sds((512, n), dtype)], [rows, *weights], 2 * 512 * D * n)[0]


def down_products(rows, weights):
    def kernel(rows_ref, w0, w1, out_ref):
        for j in range(0, D, 512):
            here = slice(j, j + 512)
            total = dot(rows_ref[:, :512], w0[here, :], 1, 1) + dot(rows_ref[:, 512:], w1[here, :], 1, 1)
            out_ref[:, here] = bf(total)

    return call(kernel, "down_products", [sds((512, D))], [rows, *map(pinned, weights)], 2 * 512 * 1024 * D)[0]


def rope(u, cosine, sine):
    lane = lax.broadcasted_iota(jnp.int32, u.shape, 1)
    turned = jnp.where(lane % DH < DH // 2, pltpu.roll(u, 96, 1), pltpu.roll(u, 32, 1))
    return u * cosine + turned * sine


def rope_three(u, cosine, sine):
    lane = lax.broadcasted_iota(jnp.int32, cosine.shape, 1)
    last = u[:, 256:]
    return jnp.concatenate(
        [
            rope(u[:, :128], cosine, sine),
            rope(u[:, 128:256], cosine, sine),
            jnp.where(lane < DH, rope(last, cosine, sine), last),
        ],
        axis=1,
    )


def half_at(halves_ref, i):
    return pl.ds(pl.multiple_of(halves_ref[i], 512), 512)


def project_qkv(i, rows, weight, tables, halves):
    def kernel(halves_ref, rows_ref, w_ref, cos_ref, sin_ref, out_ref):
        here = half_at(halves_ref, i)
        product = dot(rows_ref[...], w_ref[:, :384], 1, 0)
        out_ref[...] = bf(rope_three(product, cos_ref[here, :], sin_ref[here, :]))

    args = [halves, rows, weight, *tables]
    return call(kernel, "project_qkv", [sds((512, 384))], args, 2 * 512 * D * 384)[0]


def scores_t(keys, query, q_at):
    s = dot(keys, query, 1, 1)
    key = lax.broadcasted_iota(jnp.int32, (256, 256), 0)
    column = lax.broadcasted_iota(jnp.int32, (256, 256), 1)
    diagonal = jnp.where(key <= column, s[q_at:], -1e30)
    return diagonal if q_at == 0 else jnp.concatenate([s[:q_at], diagonal], axis=0)


def attend(qkv, halves):
    def kernel(halves_ref, q0, q1, own_ref, other_ref, nat_ref, lse_ref, att_ref):
        nat_ref[half_at(halves_ref, 0), :] = q0[...]
        nat_ref[half_at(halves_ref, 1), :] = q1[...]
        kv = nat_ref[:, 256:]
        keys = kv[:, :DH]
        values_t = kv.T[DH:]
        lse_ref[...] = jnp.zeros_like(lse_ref)
        for q_at in range(0, SEQ_LEN, 256):
            end = q_at + 256
            for pair in range(2):
                two = nat_ref[q_at:end, 128 * pair : 128 * pair + 128]
                outs = []
                for i in range(2):
                    s = scores_t(keys[:end], two[:, DH * i : DH * i + DH], q_at)
                    top = jnp.max(s, axis=0, keepdims=True)
                    p = jnp.exp2((s - top) * SCALE2)
                    total = jnp.sum(p, axis=0, keepdims=True)
                    outs.append(dot(values_t[:, :end], bf(p), 1, 0) / total)
                    g = 2 * pair + i
                    lse_ref[g : g + 1, q_at:end] = top * SCALE2 + jnp.log2(total)
                att_ref[q_at:end, 128 * pair : 128 * pair + 128] = bf(jnp.concatenate(outs, axis=0).T)
        own_ref[...] = att_ref[half_at(halves_ref, 0), :]
        other_ref[...] = att_ref[half_at(halves_ref, 1), :]

    outs = [sds((512, 256)), sds((512, 256)), sds((SEQ_LEN, 384)), sds((8, SEQ_LEN), jnp.float32)]
    scratch = [pltpu.VMEM((SEQ_LEN, 256), jnp.bfloat16)]
    return call(kernel, "attend", outs, [halves, *qkv], 20e9, scratch)


def attend_backward(qkv, lse, grad_out, tables, halves):
    def kernel(halves_ref, nat_ref, lse_ref, g0, g1, cos_ref, sin_ref, own_ref, other_ref, go_nat, kv_sum, d_nat):
        go_nat[half_at(halves_ref, 0), :] = g0[...]
        go_nat[half_at(halves_ref, 1), :] = g1[...]
        kv = nat_ref[:, 256:]
        keys = kv[:, :DH]
        values = kv[:, DH:]
        keys_t = kv.T[:DH]
        kv_sum[...] = jnp.zeros_like(kv_sum)
        for q_at in range(0, SEQ_LEN, 256):
            end = q_at + 256
            cosine = cos_ref[q_at:end, :]
            sine = -sin_ref[q_at:end, :]
            for pair in range(2):
                lanes = slice(128 * pair, 128 * pair + 128)
                two = nat_ref[q_at:end, lanes]
                two_grad = go_nat[q_at:end, lanes]
                outs = []
                for i in range(2):
                    query = two[:, DH * i : DH * i + DH]
                    grad = two_grad[:, DH * i : DH * i + DH]
                    g = 2 * pair + i
                    s = scores_t(keys[:end], query, q_at)
                    p = jnp.exp2(s * SCALE2 - lse_ref[g : g + 1, q_at:end])
                    dp = dot(values[:end], grad, 1, 1)
                    delta = jnp.sum(dp * p, axis=0, keepdims=True)
                    ds = bf(p * (dp - delta))
                    kv_sum[:end, :] += jnp.concatenate(
                        [dot(ds, query, 1, 0), dot(bf(p), grad, 1, 0)], axis=1
                    )
                    outs.append(dot(keys_t[:, :end], ds, 1, 0))
                d_query = jnp.concatenate(outs, axis=0).T * SCALE
                d_nat[q_at:end, lanes] = bf(rope(d_query, cosine, sine))
        lane = lax.broadcasted_iota(jnp.int32, (SEQ_LEN, 128), 1)
        total = kv_sum[...]
        turned = rope(total * SCALE, cos_ref[...], -sin_ref[...])
        d_nat[:, 256:] = bf(jnp.where(lane < DH, turned, total))
        own_ref[...] = d_nat[half_at(halves_ref, 0), :]
        other_ref[...] = d_nat[half_at(halves_ref, 1), :]

    scratch = [
        pltpu.VMEM((SEQ_LEN, 256), jnp.bfloat16),
        pltpu.VMEM((SEQ_LEN, 128), jnp.float32),
        pltpu.VMEM((SEQ_LEN, 384), jnp.bfloat16),
    ]
    args = [halves, qkv, lse, *grad_out, *tables]
    return call(kernel, "attend_backward", [sds((512, 384))] * 2, args, 30e9, scratch)


def mlp_step(rows, w_gate, w_up, grad_act):
    width = w_gate.shape[1]

    def kernel(rows_ref, g_ref, u_ref, ga_ref, act_ref, gg_ref, gu_ref):
        for j in range(0, width, 256):
            here = slice(j, j + 256)
            gate = dot(rows_ref[...], g_ref[:, here], 1, 0)
            up = dot(rows_ref[...], u_ref[:, here], 1, 0)
            sig = jax.nn.sigmoid(gate)
            silu = gate * sig
            ga = ga_ref[:, here]
            act_ref[:, here] = bf(silu * up)
            gg_ref[:, here] = bf(ga * up * sig * (1.0 + gate * (1.0 - sig)))
            gu_ref[:, here] = bf(ga * silu)

    args = [rows, pinned(w_gate), pinned(w_up), grad_act]
    return call(kernel, "mlp_step", [sds((512, width))] * 3, args, 4 * 512 * D * width)


def frequencies(head_size):
    pair_index = jnp.arange(head_size // 2).astype(jnp.float32)
    base_freq = 500000.0 ** (-2.0 * pair_index / head_size)
    wavelen = 2.0 * jnp.pi / base_freq
    smooth = (8192.0 / wavelen - 1.0) / 3.0
    blended = (1.0 - smooth) * base_freq / 32.0 + smooth * base_freq
    return jnp.where(
        wavelen < 2048.0, base_freq, jnp.where(wavelen > 8192.0, base_freq / 32.0, blended)
    )


LONG = 60e9


def wide(out_ref, value):
    for k in range(4):
        out_ref[k] = value


def arrived_sum(ref):
    return fl(ref[0]) + fl(ref[1]) + fl(ref[2]) + fl(ref[3])


def mlp_norm(inputs, arrived, gain):
    def kernel(x_ref, a_ref, gain_ref, residual_ref, out_ref):
        residual = fl(x_ref[...]) + arrived_sum(a_ref)
        residual_ref[...] = residual
        inverse = lax.rsqrt(jnp.mean(residual * residual, axis=1, keepdims=True) + eps)
        wide(out_ref, bf(residual * inverse * gain_ref[...]))

    outs = [sds((128, D), jnp.float32), sds((4, 128, D))]
    return call(kernel, "mlp_norm", outs, [inputs, arrived, gain], LONG)


def norm_grad(grad, values, gain):
    inverse = lax.rsqrt(jnp.mean(values * values, axis=1, keepdims=True) + eps)
    unit = values * inverse
    scaled = grad * gain
    return inverse * (scaled - unit * jnp.mean(scaled * unit, axis=1, keepdims=True))


def mlp_norm_backward(upstream, arrived, residual, gain):
    def kernel(g_ref, a_ref, r_ref, gain_ref, grad_ref, out_ref):
        grad = fl(g_ref[...]) + norm_grad(arrived_sum(a_ref), r_ref[...], gain_ref[...])
        grad_ref[...] = grad
        wide(out_ref, bf(grad))

    outs = [sds((128, D), jnp.float32), sds((4, 128, D))]
    return call(kernel, "mlp_norm_backward", outs, [upstream, arrived, residual, gain], LONG)


def attn_norm_backward(grad_residual, arrived, inputs, gain):
    def kernel(g_ref, a_ref, x_ref, gain_ref, out_ref):
        out_ref[...] = bf(g_ref[...] + norm_grad(arrived_sum(a_ref), fl(x_ref[...]), gain_ref[...]))

    return call(kernel, "attn_norm_backward", [sds((128, D))], [grad_residual, arrived, inputs, gain], LONG)[0]


def layer_output(residual, arrived):
    def kernel(r_ref, a_ref, out_ref):
        out_ref[...] = bf(r_ref[...] + arrived_sum(a_ref))

    return call(kernel, "layer_output", [sds((128, D))], [residual, arrived], 1)[0]


def on_device(
    tokens, positions, w_query, w_key, w_value, w_out, attn_gain, w_gate, w_up, w_down, mlp_gain, cotangent
):
    me = Place()
    inputs_b = swapped(tokens)
    places = jnp.concatenate([(positions // 256).reshape(128, 8), (positions % 256).reshape(128, 8)], axis=1)
    extra = jnp.concatenate([attn_gain[:, None], mlp_gain[:, None], bf(places)], axis=1)
    extra = jnp.pad(extra, ((0, 0), (0, 110)))
    part_attn = swapped(jnp.concatenate([w_query, w_key, w_value, extra, w_out.T], axis=1))
    part_attn, inputs_b = lax.optimization_barrier((part_attn, inputs_b))

    blocks_in = send_z(inputs_b)
    w_qkv = gather_plane(part_attn[:, :512])
    (cotangent,) = after((cotangent,), inputs_b)
    upstream = swapped(cotangent)
    w_gate, w_up, w_down = after((w_gate, w_up, w_down), w_qkv)
    down_rows = w_down.T
    part_ab = swapped(jnp.concatenate([w_gate, down_rows[:, :512], w_up, down_rows[:, 512:]], axis=1))

    place = fl(part_attn[:, 386:402])
    seq_positions = (256.0 * place[:, :8] + place[:, 8:]).reshape(SEQ_LEN)
    freq = jnp.tile(frequencies(DH), 4)
    angles = seq_positions[:, None] * freq[None, :]
    sign = jnp.where(jnp.arange(128) % DH < DH // 2, -1.0, 1.0)
    tables = (jnp.cos(angles), jnp.sin(angles) * sign[None, :])
    pick = bf(jnp.arange(128)[None, :] == jnp.arange(8)[:, None])
    gain_rows = dot(pick, w_qkv[:, 384:], 1, 1)
    gain_attn, gain_mlp = gain_rows[:1], gain_rows[1:2]

    blocks_in = after(blocks_in, *tables, upstream)
    own_normed = norm_tokens(blocks_in, gain_attn, me)
    normed_attn = [own_normed, sibling(own_normed)]
    own_qkv = project_qkv(0, normed_attn[0], w_qkv, tables, me.halves)
    projected = [own_qkv, project_qkv(1, normed_attn[1], w_qkv, tables, me.halves)]

    (own_up,) = after((upstream,), own_normed)
    blocks_up = send_z(own_up)
    (part_out,) = after((part_attn[:, 512:],), own_qkv)
    w_out_t = gather_plane(part_out)

    projected = after(projected, *blocks_up[1:3])
    attended, other_attended, qkv, lse = attend(projected, me.halves)
    (w_out_t,) = after((w_out_t,), attended, blocks_up[3])
    out_sums = chip_product(attended, other_attended, w_out_t, sibling(w_out_t))
    (out_sums,) = after((out_sums,), *blocks_up)

    (part_ab,) = after((part_ab,), projected[1])
    part_a, part_b = part_ab[:, :1536], part_ab[:, 1536:]
    holds = (attended, out_sums, None)
    stage_a, stage_b = (jnp.concatenate(chain(p, axis, holds), axis=0) for p, axis in ((part_a, "x"), (part_b, "y")))

    own_up = place_tokens(blocks_up, me)
    rows_up = [own_up, sibling(own_up)]
    arrived = arrive_z(out_sums)

    parts_a, parts_b = chain(stage_a, "y", (None, None, None)), chain(stage_b, "x", (None, None, None))
    full_gate, down_a = place_rows(parts_a, me.blocks["x"], (1024, 512))
    full_up, down_b = place_rows(parts_b, me.blocks["y"], (1024, 512))
    full_down = [down_a, down_b]

    (arrived,) = after((arrived,), parts_a[2], parts_b[2], *rows_up)
    residual, normed_mlp = mlp_norm(inputs_b, arrived, gain_mlp)
    own_mlp = gather_z(normed_mlp)
    up_held = after(rows_up, normed_mlp)
    grad_act = [project(r, [pinned(w) for w in full_down], jnp.float32) for r in up_held]
    (own_mlp,) = after((own_mlp,), full_gate, full_up, grad_act[0])
    rows_mlp = [own_mlp, sibling(own_mlp)]
    steps = [mlp_step(r, full_gate, full_up, g) for r, g in zip(rows_mlp, grad_act)]
    activated, grad_gate_pre, grad_up_pre = zip(*steps)

    gate_up = list(zip(grad_gate_pre, grad_up_pre))
    mlp_sums = chip_sums(gate_up[0], gate_up[1], [full_gate, full_up])
    arrived = arrive_z(mlp_sums)

    gg, gu = after((grad_gate_pre, grad_up_pre), mlp_sums)
    made_a = weight_product([(rows_mlp, gg, 0, 1024), (rows_up, activated, 0, 512)], "x", me)
    made_b = weight_product([(rows_mlp, gu, 0, 1024), (rows_up, activated, 512, 1024)], "y", me)
    sums = [made_a[0], made_b[0]]
    rings = [ring(total, axis) for total, axis in zip(sums, "xy")]
    acts = after(activated, made_a[-1], made_b[-1])
    down_other = down_products(acts[1], full_down)
    down_own = down_products(acts[0], full_down)
    (arrived,) = after((arrived,), down_own)
    grad_residual, grad_residual_b = mlp_norm_backward(upstream, arrived, residual, gain_mlp)

    own_gr = gather_z(grad_residual_b)
    (down_arrived,) = after((sibling(down_other),), grad_residual_b)
    down_sums = bf(fl(down_own) + fl(down_arrived))
    rings = after(rings, grad_residual_b)
    sums = [add(received, made[1]) for received, made in zip(rings, (made_a, made_b))]
    rings = [ring(total, axis) for total, axis in zip(sums, "xy")]
    (own_gr,) = after((own_gr,), down_sums, *rings)
    rows_gr = [own_gr, sibling(own_gr)]
    (down_sums,) = after((down_sums,), own_gr)
    arrived = arrive_z(down_sums)

    rings = after(rings, own_gr)
    sums = [add(received, made[2]) for received, made in zip(rings, (made_a, made_b))]
    rings = [ring(total, axis) for total, axis in zip(sums, "xy")]
    grad_attended = [project(r, [w_out_t], jnp.bfloat16) for r in after(rows_gr, *sums)]
    grad_qkv, other_grad_qkv = attend_backward(qkv, lse, grad_attended, tables, me.halves)
    rings = after(rings, grad_qkv)
    blocks_a, blocks_b = (
        second_blocks([received, made[3]], first, me)
        for received, made, first in zip(rings, (made_a, made_b), "xy")
    )
    parts_b = second_stage(blocks_b, "y")
    attn_sums = chip_product(grad_qkv, other_grad_qkv, w_qkv, sibling(w_qkv))
    (attn_sums,) = after((attn_sums,), arrived, blocks_a[0], blocks_b[0])
    grad_arrived = arrive_z(attn_sums)

    (arrived,) = after((arrived,), attn_sums)
    layer_out = layer_output(residual, arrived)
    parts_a = second_stage(after(blocks_a, layer_out), "x")
    d_qkv = after((grad_qkv, other_grad_qkv), attn_sums)
    made_in = weight_product([(normed_attn, d_qkv, 0, 384)], "x", me)
    sent_in = send_pieces(made_in, "x")
    att = after((attended, other_attended), made_in[-1])
    made_out = weight_product([(rows_gr, att, 0, 256)], "y", me)
    sent_out = send_pieces(made_out, "y")
    (grad_arrived,) = after((grad_arrived,), made_out[-1], layer_out)
    grad_tokens = attn_norm_backward(grad_residual, grad_arrived, inputs_b, gain_attn)
    (layer_out,) = after((layer_out,), grad_tokens)
    share_a, share_b = summed(parts_a, attn_sums), summed(parts_b, attn_sums)
    share_b = fl(swapped(bf(share_b)))
    blocks_in = second_blocks(after(sent_in, grad_tokens), "x", me)
    share_in = summed(second_stage(blocks_in, "x"), grad_tokens)
    blocks_out = second_blocks(after(sent_out, grad_tokens), "y", me)
    share_out = fl(swapped(bf(summed(second_stage(blocks_out, "y"), grad_tokens))))

    def gain_sum(*terms):
        return sum(jnp.sum(fl(w) * g, axis=1) for w, g in terms)

    gain_sums = jnp.stack(
        [
            gain_sum((jnp.concatenate([w_query, w_key, w_value], axis=1), share_in)),
            gain_sum((w_gate, share_a[:, :1024]), (w_up, share_b[:, :1024])),
        ]
    )
    gain_sums = gain_sums / fl(jnp.stack([attn_gain, mlp_gain]))
    gain_sums = gain_sums + z_moved(gain_sums, 1) + z_moved(gain_sums, 2) + z_moved(gain_sums, 3)
    gain_sums = gain_sums + h_flipped(gain_sums)
    return (
        swapped(layer_out),
        swapped(grad_tokens),
        share_in[:, :256],
        share_in[:, 256:320],
        share_in[:, 320:384],
        share_out.T,
        gain_sums[0],
        share_a[:, :1024],
        share_b[:, :1024],
        jnp.concatenate([share_a[:, 1024:], share_b[:, 1024:]], axis=1).T,
        gain_sums[1],
    )


def solution(mesh):
    split = Mesh(mesh.devices.reshape(4, 2, 2, 2, 4), AXES)
    dp, tensor = ("x", "l", "c"), ("h", "z")
    both = P(AXES, None)
    weight, turned, vector = P(dp, tensor), P(tensor, dp), P(dp)
    in_specs = (
        both, vector, weight, weight, weight, turned, vector, weight, weight, turned, vector, both,
    )
    out_specs = (
        both, both, weight, weight, weight, turned, vector, weight, weight, turned, vector,
    )
    return jax.shard_map(on_device, mesh=split, in_specs=in_specs, out_specs=out_specs, check_vma=False)
```
